32 devices in a mesh: context: 16 (over z, y, core), tensor: 2 (over x).
Axes of the slice: x: 2, y: 2, z: 4, core: 2. Of those that a mesh axis runs over, the one named last changes fastest.
Arguments:
- hidden_rows: bfloat16 [2048, 4096], P(('context', 'tensor')), may hold values from -6 to 6
- norm_gain: bfloat16 [4096], replicated, may hold values from 0.25 to 1.75
- w_qkv: bfloat16 [4096, 1536], P('context', 'tensor')
- w_out: bfloat16 [1024, 4096], P('tensor', 'context'), may hold values from -0.1875 to 0.1875
- doc_lengths: int32 [16], replicated, may hold values from 1 to 512, 2048 in all
- span_order: int32 [32], replicated, may hold values from 0 to 31, each once
Outputs:
- attended: bfloat16 [2048, 4096], P(('context', 'tensor'))
The draws below stay inside these ranges and needn't reach their ends.
Inputs may be any that keep to these rules, and one draw needn't show every extreme that they name: `doc_lengths`: the lengths sum to 2048; the longest is exactly 512. `span_order`: each initial span appears once.
All inputs are finite; a program needn't handle non-finite values.
Results may differ from the reference program's by a relative error of at most 0.02.
The reference program's roundings to bfloat16 on the way count: a program that leaves them out, or rounds other values in their place, can miss the bound.
Values may be sent and summed in bfloat16 or wider, within the bound.
No kernel may reach another device: no remote copies, remote signals or barrier semaphores. Data moves between devices by JAX's collectives and lax.ppermute only.
A program may use at most 64 MiB of HBM per device.

```python
import math
import jax
import jax.numpy as jnp
import numpy as np
from jax import lax

D = 4096
HD = 128
QH_DEV = 4
NDOCS = 16
HEADS = 8
QKV_COLS = 768
TOKENS = 2048
SPAN = 64
MOST = 512
N_CONTEXT = 16
N_TENSOR = 2


def draw_w_qkv(key, part):
    key = jax.random.fold_in(key, 7)
    base = jax.random.normal(key, (D, N_TENSOR * QKV_COLS), jnp.float32) / D ** 0.5
    return base.astype(jnp.bfloat16)


def levels(stream_key, extent, shards, low, high):
    def one(dim, parts):
        steps = jax.random.uniform(jax.random.fold_in(jax.random.fold_in(stream_key, 6), dim), (parts,), jnp.float32, low / len(shards), high / len(shards))
        return jnp.repeat(jnp.exp(steps), extent[dim] // parts).reshape((-1,) + (1,) * (len(extent) - dim - 1))

    factor_of = one(*shards[0])
    for cut in shards[1:]:
        factor_of = factor_of * one(*cut)
    return factor_of


def split_up(number_of, total, reach, lean):
    loads = [(1 << 20) // math.isqrt(standing ** lean) + 1 for standing in range(2, number_of + 1)]
    spare, holding = total - reach - (number_of - 1), [1] * (number_of - 1)
    while spare > 0:
        free = [i for i in range(number_of - 1) if holding[i] < reach]
        pool, budget = sum([loads[i] for i in free]), spare
        for i in free:
            addition = min(reach - holding[i], max(1, budget * loads[i] // pool), spare)
            holding[i] = holding[i] + addition
            spare = spare - addition
    return np.array([reach] + holding)


def ragged(stream_key, count, total, limit, skew):
    if count == 2:
        one = jax.random.randint(stream_key, (), max(1, total - limit), min(limit, total - 1) + 1)
        return jnp.stack([one, total - one])
    sizes = jnp.asarray(split_up(count, total, limit, skew), jnp.int32)
    couples = (count - 1) // 2
    giver, taker = sizes[1:1 + 2 * couples:2], sizes[2:2 + 2 * couples:2]
    slack = jnp.minimum(giver - 1, limit - taker)
    shifted = jax.random.randint(jax.random.fold_in(stream_key, 1), (couples,), 0, 1 << 20) % (slack + 1)
    sizes = sizes.at[1:1 + 2 * couples:2].set(giver - shifted).at[2:2 + 2 * couples:2].set(taker + shifted)
    return sizes[jax.random.permutation(jax.random.fold_in(stream_key, 2), count)]


def scatter_about(key, dims, deviation, most, pieces=(), held_as=jnp.bfloat16):
    result = jax.random.normal(key, dims, jnp.float32) * deviation
    if len(pieces) > 0:
        result = levels(key, dims, pieces, -0.22, 0.18) * result
    return jnp.clip(result, min=-most, max=most).astype(held_as)


def setup_inputs(seed: int = 0) -> dict:
    arg_keys = jax.random.split(jax.random.key(seed), 7)
    return {
        "hidden_rows": scatter_about(arg_keys[0], (TOKENS, D), 1.0, 6.0, ((0, 32),)),
        "norm_gain": jnp.clip(1.0 + 0.15 * jax.random.normal(arg_keys[1], (D,), jnp.float32), 0.25, 1.75).astype(jnp.bfloat16),
        "w_qkv": draw_w_qkv(jax.random.fold_in(arg_keys[6], 71), 0),
        "w_out": scatter_about(arg_keys[3], (HEADS * HD, D), (HEADS * HD) ** -0.5, 0.1875, ((0, 2), (1, 16))),
        "doc_lengths": ragged(arg_keys[4], NDOCS, TOKENS, MOST, 2).astype(jnp.int32),
        "span_order": jax.random.permutation(arg_keys[5], 2 * N_CONTEXT).astype(jnp.int32),
    }


rope_theta = 500000.0

def locate(layout_rows, span_order, doc_ends):
    span_index = layout_rows // SPAN
    matches = span_index[:, None] == jnp.arange(span_order.shape[0], dtype=jnp.int32)[None, :]
    source_span = lax.optimization_barrier(jnp.sum(jnp.where(matches, span_order[None, :], 0), axis=1)).astype(jnp.int32)
    initial = (source_span * SPAN + layout_rows % SPAN).astype(jnp.int32)
    document = lax.optimization_barrier(jnp.sum((initial[:, None] >= doc_ends[None, :]).astype(jnp.int32), axis=1)).astype(jnp.int32)
    doc_start = lax.optimization_barrier(jnp.max(jnp.where(doc_ends[None, :] <= initial[:, None], doc_ends[None, :], 0), axis=1))
    return (initial, document, (initial - doc_start).astype(jnp.int32))

def rotate(values, position):
    half = values.shape[-1] // 2
    freq = rope_theta ** (-(jnp.arange(half, dtype=jnp.float32) * 2.0 / values.shape[-1]))
    angle = position.astype(jnp.float32)[:, None, None] * freq[None, None, :]
    cosine = jnp.cos(angle)
    sine = jnp.sin(angle)
    first_half = values[..., :half]
    second_half = values[..., half:]
    return jnp.concatenate([first_half * cosine - second_half * sine, second_half * cosine + first_half * sine], axis=-1)

def reference(hidden_rows, norm_gain, w_qkv, w_out, doc_lengths, span_order):
    doc_ends = jnp.cumsum(doc_lengths).astype(jnp.int32)
    layout_rows = jnp.arange(TOKENS, dtype=jnp.int32)
    initial, document, position = locate(layout_rows, span_order, doc_ends)
    wide = hidden_rows.astype(jnp.float32)
    meansq = lax.optimization_barrier(jnp.mean(wide * wide, axis=-1, keepdims=True))
    normed = (wide * lax.rsqrt(meansq + 1e-05) * norm_gain.astype(jnp.float32)[None, :]).astype(jnp.bfloat16)
    qkv = jnp.dot(normed, w_qkv, preferred_element_type=jnp.float32).reshape(TOKENS, N_TENSOR, QKV_COLS)
    queries = qkv[:, :, :QH_DEV * HD].reshape(TOKENS, HEADS, HD)
    queries = rotate(queries, position).astype(jnp.bfloat16).transpose(1, 0, 2)
    keys = qkv[:, :, QH_DEV * HD:(QH_DEV + 1) * HD]
    keys = rotate(keys, position).astype(jnp.bfloat16).transpose(1, 0, 2)
    values = qkv[:, :, (QH_DEV + 1) * HD:].astype(jnp.bfloat16).transpose(1, 0, 2)
    allowed = (document[:, None] == document[None, :]) & (initial[None, :] <= initial[:, None])
    scale = 1.0 / HD ** 0.5

    def head_output(head):
        group = head // QH_DEV
        query_head = lax.dynamic_index_in_dim(queries, head, 0, keepdims=False)
        key_head = lax.dynamic_index_in_dim(keys, group, 0, keepdims=False)
        value_head = lax.dynamic_index_in_dim(values, group, 0, keepdims=False)
        scores = jnp.dot(query_head, key_head.T, preferred_element_type=jnp.float32) * scale
        scores = jnp.where(allowed, scores, -1e+30)
        top = lax.optimization_barrier(jnp.max(scores, axis=1, keepdims=True))
        expo = jnp.where(allowed, jnp.exp(scores - top), 0.0)
        totals = lax.optimization_barrier(jnp.sum(expo, axis=1, keepdims=True))
        weighted = jnp.dot(expo.astype(jnp.bfloat16), value_head, preferred_element_type=jnp.float32)
        return (weighted / totals).astype(jnp.bfloat16)
    mixed = lax.map(head_output, jnp.arange(HEADS, dtype=jnp.int32))
    mixed = mixed.transpose(1, 0, 2).reshape(TOKENS, HEADS * HD)
    return jnp.dot(mixed, w_out, preferred_element_type=jnp.float32).astype(jnp.bfloat16)
```

```python
import functools

import jax
import jax.numpy as jnp
from jax import lax
from jax.experimental import pallas as pl
from jax.experimental.pallas import tpu as pltpu
from jax.sharding import PartitionSpec as P

HD = 128
QH_DEV = 4
SPAN = 64
HEAD_COLS = QH_DEV * HD
VMEM_LIMIT = 48 * 1024 * 1024

rope_theta = 500000.0


def ring_of_chips(count):
    wide = 1
    while (wide * 2) * (wide * 2) <= count:
        wide *= 2
    tall = count // wide
    if wide < 2:
        return list(range(count))
    ring = [(z, 0) for z in range(tall)]
    for z in range(tall - 1, -1, -1):
        row = list(range(1, wide))
        ring += [(z, y) for y in (row if (tall - 1 - z) % 2 == 0 else row[::-1])]
    if (tall - 1) % 2 == 0 or wide == 2:
        return [z * wide + y for z, y in ring]
    return [z * wide + y for z, y in ring]


def locate(layout_rows, span_order, doc_ends):
    span_index = layout_rows // SPAN
    matches = span_index[:, None] == jnp.arange(span_order.shape[0], dtype=jnp.int32)[None, :]
    source_span = jnp.sum(jnp.where(matches, span_order[None, :], 0), axis=1)
    initial = source_span * SPAN + layout_rows % SPAN
    doc_start = jnp.max(
        jnp.where(doc_ends[None, :] <= initial[:, None], doc_ends[None, :], 0), axis=1
    )
    return (initial, doc_start)


def vmem_specs(count):
    return [pl.BlockSpec(memory_space=pltpu.VMEM)] * count


def compute_params():
    return pltpu.CompilerParams(vmem_limit_bytes=VMEM_LIMIT)


def norm_kernel(place, chips, where_ref, hidden_ref, gain_ref, own_ref, other_ref):
    at, core = where_ref[0], where_ref[1]
    wide = hidden_ref[...].astype(jnp.float32)
    meansq = jnp.mean(wide * wide, axis=-1, keepdims=True)
    normed = (wide * lax.rsqrt(meansq + 1e-05) * gain_ref[...].astype(jnp.float32)).astype(
        jnp.bfloat16
    )
    block = own_ref.shape[2]
    for chip in range(chips):
        slot = lax.rem(place[chip] + chips - at, chips)
        first = normed[:, (2 * chip) * block : (2 * chip + 1) * block]
        second = normed[:, (2 * chip + 1) * block : (2 * chip + 2) * block]

        @pl.when(core == 0)
        def _():
            own_ref[slot] = first
            other_ref[slot] = second

        @pl.when(core != 0)
        def _():
            own_ref[slot] = second
            other_ref[slot] = first


def take_ring(refs, chips):
    refs = list(refs)
    if chips % 2:
        return [(ref,) for ref in refs]
    half = chips // 2
    return [(r,) for r in refs[:half]] + [tuple(refs[half : half + 2])] + [
        (r,) for r in refs[half + 2 :]
    ]


def project_kernel(chips, groups, *refs):
    rows_refs, refs = refs[:groups], refs[groups:]
    weight_refs, (mine_ref, theirs_ref) = refs[:-2], refs[-2:]
    weights = take_ring(weight_refs, chips)
    total = None
    for slot in range(chips):
        rows = jnp.concatenate([ref[slot] for ref in rows_refs], axis=0)
        start = 0
        for ref in weights[slot]:
            depth = ref.shape[0]
            part = jnp.dot(
                rows[:, start : start + depth], ref[...], preferred_element_type=jnp.float32
            )
            total = part if total is None else total + part
            start += depth
    half = mine_ref.shape[0]
    mine_ref[...] = total[:half]
    theirs_ref[...] = total[half:]


def turn(values, cosine, sine):
    return values * cosine + pltpu.roll(values, HD // 2, 1) * sine


def keys_kernel(mine_ref, theirs_ref, cosine_ref, sine_ref, out_ref):
    total = mine_ref[...] + theirs_ref[...]
    out_ref[:, :HD] = turn(total[:, :HD], cosine_ref[...], sine_ref[...]).astype(jnp.bfloat16)
    out_ref[:, HD:] = total[:, HD:].astype(jnp.bfloat16)


def attend_kernel(mine_ref, theirs_ref, cosine_ref, sine_ref, low_ref, high_ref, orig_ref, *refs):
    block_refs, (out_ref, keys_ref, values_ref) = refs[:-3], refs[-3:]
    start = 0
    for ref in block_refs:
        keys_ref[start : start + ref.shape[0], :] = ref[:, :HD]
        values_ref[start : start + ref.shape[0], :] = ref[:, HD:]
        start += ref.shape[0]
    keys = keys_ref[...]
    values = values_ref[...]
    orig = orig_ref[...]
    allowed = (orig >= low_ref[...]) & (orig <= high_ref[...])
    scale = 1.0 / HD**0.5
    for head in range(QH_DEV):
        columns = slice(head * HD, (head + 1) * HD)
        query = turn(
            mine_ref[:, columns] + theirs_ref[:, columns], cosine_ref[...], sine_ref[...]
        ).astype(jnp.bfloat16)
        scores = lax.dot_general(
            query, keys, (((1,), (1,)), ((), ())), preferred_element_type=jnp.float32
        )
        scores = jnp.where(allowed, scores * scale, -1e30)
        top = jnp.max(scores, axis=-1, keepdims=True)
        expo = jnp.where(allowed, jnp.exp(scores - top), 0.0)
        total = jnp.sum(expo, axis=-1, keepdims=True)
        product = jnp.dot(expo.astype(jnp.bfloat16), values, preferred_element_type=jnp.float32)
        out_ref[:, columns] = (product / total).astype(jnp.bfloat16)


def output_kernel(chips, groups, mine_ref, theirs_ref, *refs):
    weight_refs, out_refs = refs[:-groups], refs[-groups:]
    weights = take_ring(weight_refs, chips)
    mixed = jnp.concatenate([mine_ref[...], theirs_ref[...]], axis=0)
    rows = mixed.shape[0] // groups
    for slot in range(chips):
        start, total = 0, None
        for ref in weights[slot]:
            depth = ref.shape[0]
            part = jnp.dot(
                mixed[:, start : start + depth], ref[...], preferred_element_type=jnp.float32
            )
            total = part if total is None else total + part
            start += depth
        total = total.astype(jnp.bfloat16)
        for group in range(groups):
            out_refs[group][slot] = total[group * rows : (group + 1) * rows]


def sum_kernel(place, chips, groups, where_ref, *refs):
    part_refs, out_ref = refs[:groups], refs[groups]
    at, core = where_ref[0], where_ref[1]
    block = part_refs[0].shape[2]
    half = groups // 2

    def added(part, slot):
        total = part_refs[part * half][slot].astype(jnp.float32)
        for ref in part_refs[part * half + 1 : (part + 1) * half]:
            total += ref[slot].astype(jnp.float32)
        return total.astype(jnp.bfloat16)

    for chip in range(chips):
        slot = lax.rem(place[chip] + chips - at, chips)
        first = slice((2 * chip) * block, (2 * chip + 1) * block)
        second = slice((2 * chip + 1) * block, (2 * chip + 2) * block)

        @pl.when(core == 0)
        def _():
            out_ref[:, first] = added(0, slot)
            out_ref[:, second] = added(1, slot)

        @pl.when(core != 0)
        def _():
            out_ref[:, first] = added(1, slot)
            out_ref[:, second] = added(0, slot)


def per_device(n_context, n_tensor, hidden_rows, norm_gain, w_qkv, w_out, doc_lengths, span_order):
    chips = n_context // 2
    ring = ring_of_chips(chips)
    place = [ring.index(chip) for chip in range(chips)]
    groups = 2 * n_tensor
    rows_here, width = hidden_rows.shape
    tokens_here = rows_here * n_tensor
    block = width // n_context
    context = lax.axis_index("context")
    tensor = lax.axis_index("tensor")
    core = context % 2
    at = jnp.sum(
        jnp.where(jnp.arange(chips) == context // 2, jnp.asarray(place, jnp.int32), 0)
    ).astype(jnp.int32)
    where = jnp.stack([at, core]).astype(jnp.int32)

    ahead = [
        (ring[i] * 2 + k, ring[(i + 1) % chips] * 2 + k) for i in range(chips) for k in range(2)
    ]
    back = [(b, a) for a, b in ahead]
    sibling = [(c, c ^ 1) for c in range(n_context)]

    def ring_gather(mine):
        up, down = mine, mine
        behind, before = [], []
        for _ in range((chips - 1) // 2):
            up = lax.ppermute(up, "context", ahead)
            down = lax.ppermute(down, "context", back)
            behind.append(up)
            before.append(down)
        middle = []
        if chips % 2 == 0:
            half = mine.shape[0] // 2
            middle = [
                lax.ppermute(up[:half], "context", ahead),
                lax.ppermute(down[half:], "context", back),
            ]
        return [mine] + before + middle + behind[::-1]

    def member(e, d):
        return [
            (c * n_tensor + t, (c ^ e) * n_tensor + (t - d) % n_tensor)
            for c in range(n_context)
            for t in range(n_tensor)
        ]

    keys_blocks = ring_gather(w_qkv[:, HEAD_COLS:])
    query_blocks = ring_gather(w_qkv[:, :HEAD_COLS])
    out_blocks = ring_gather(w_out)

    smem = pl.BlockSpec(memory_space=pltpu.SMEM)
    normed_shape = jax.ShapeDtypeStruct((chips, rows_here, block), jnp.bfloat16)
    normed_own, normed_other = pl.pallas_call(
        functools.partial(norm_kernel, place, chips),
        out_shape=[normed_shape] * 2,
        in_specs=[smem] + vmem_specs(2),
        out_specs=vmem_specs(2),
        compiler_params=compute_params(),
        name="norm",
    )(where, hidden_rows, norm_gain[None, :])
    normed = []
    for e in range(2):
        for d in range(n_tensor):
            rows = normed_own if e == 0 else normed_other
            if e or d:
                rows = lax.ppermute(rows, ("context", "tensor"), member(e, d))
            normed.append(rows)

    def project(blocks, name):
        columns = blocks[0].shape[1]
        mine, theirs = pl.pallas_call(
            functools.partial(project_kernel, chips, groups),
            out_shape=[jax.ShapeDtypeStruct((tokens_here, columns), jnp.float32)] * 2,
            in_specs=vmem_specs(groups + len(blocks)),
            out_specs=vmem_specs(2),
            compiler_params=compute_params(),
            name=name,
        )(*normed, *blocks)
        return mine, lax.ppermute(theirs, "context", sibling)

    doc_ends = jnp.cumsum(doc_lengths)
    inside = (
        (tensor + jnp.arange(n_tensor, dtype=jnp.int32)) % n_tensor * rows_here
    )[:, None] + jnp.arange(rows_here, dtype=jnp.int32)[None, :]
    inside = inside.reshape(-1)
    query_orig, query_start = locate(context * tokens_here + inside, span_order, doc_ends)
    half = HD // 2
    freq = rope_theta ** (-(jnp.arange(half, dtype=jnp.float32) * 2.0 / HD))
    angle = (query_orig - query_start).astype(jnp.float32)[:, None] * freq[None, :]
    cosine, sine = jnp.cos(angle), jnp.sin(angle)
    cosine = jnp.concatenate([cosine, cosine], axis=1)
    sine = jnp.concatenate([-sine, sine], axis=1)
    chip_of_slot = jnp.sum(
        jnp.where(
            ((jnp.arange(chips) + at) % chips)[:, None] == jnp.arange(chips)[None, :],
            jnp.asarray(ring, jnp.int32)[None, :],
            0,
        ),
        axis=1,
    ).astype(jnp.int32)
    owner = jnp.concatenate([chip_of_slot * 2 + core, chip_of_slot * 2 + (1 - core)])
    key_rows = (owner[:, None] * tokens_here + inside[None, :]).reshape(-1).astype(jnp.int32)
    key_orig, _ = locate(key_rows, span_order, doc_ends)

    mine, theirs = project(keys_blocks, "project_keys")
    kv = pl.pallas_call(
        keys_kernel,
        out_shape=jax.ShapeDtypeStruct((tokens_here, 2 * HD), jnp.bfloat16),
        in_specs=vmem_specs(4),
        out_specs=vmem_specs(1)[0],
        compiler_params=compute_params(),
        name="keys",
    )(mine, theirs, cosine, sine)
    kv_blocks = ring_gather(kv)
    kv_blocks = kv_blocks + [lax.ppermute(b, "context", sibling) for b in kv_blocks]

    mine, theirs = project(query_blocks, "project_queries")
    count = n_context * tokens_here
    mixed = pl.pallas_call(
        attend_kernel,
        out_shape=jax.ShapeDtypeStruct((tokens_here, HEAD_COLS), jnp.bfloat16),
        in_specs=vmem_specs(7 + len(kv_blocks)),
        out_specs=vmem_specs(1)[0],
        scratch_shapes=[pltpu.VMEM((count, HD), jnp.bfloat16)] * 2,
        compiler_params=compute_params(),
        name="attend",
    )(
        mine,
        theirs,
        cosine,
        sine,
        query_start[:, None],
        query_orig[:, None],
        key_orig[None, :],
        *kv_blocks,
    )
    mixed_theirs = lax.ppermute(mixed, "context", sibling)

    out_block = w_out.shape[1]
    parts = pl.pallas_call(
        functools.partial(output_kernel, chips, groups),
        out_shape=[jax.ShapeDtypeStruct((chips, rows_here, out_block), jnp.bfloat16)] * groups,
        in_specs=vmem_specs(2 + len(out_blocks)),
        out_specs=vmem_specs(groups),
        compiler_params=compute_params(),
        name="output",
    )(mixed, mixed_theirs, *out_blocks)
    arrived = []
    for e in range(2):
        for d in range(n_tensor):
            part = parts[e * n_tensor + d]
            if e or d:
                part = lax.ppermute(part, ("context", "tensor"), member(e, -d))
            arrived.append(part)
    return pl.pallas_call(
        functools.partial(sum_kernel, place, chips, groups),
        out_shape=jax.ShapeDtypeStruct((rows_here, n_context * out_block), jnp.bfloat16),
        in_specs=[smem] + vmem_specs(groups),
        out_specs=vmem_specs(1)[0],
        compiler_params=compute_params(),
        name="sum",
    )(where, *arrived)


def solution(mesh):
    placed = (
        P(("context", "tensor"), None),
        P(),
        P("context", "tensor"),
        P("tensor", "context"),
        P(),
        P(),
    )
    return jax.shard_map(
        functools.partial(per_device, mesh.shape["context"], mesh.shape["tensor"]),
        mesh=mesh,
        in_specs=placed,
        out_specs=P(("context", "tensor"), None),
        check_vma=False,
    )
```

```python
import functools

import jax
import jax.numpy as jnp
from jax import lax
from jax.experimental import pallas as pl
from jax.experimental.pallas import tpu as pltpu
from jax.sharding import PartitionSpec as P

HD = 128
QH_DEV = 4
SPAN = 64
HEAD_COLS = QH_DEV * HD
VMEM_LIMIT = 48 * 1024 * 1024

rope_theta = 500000.0


def ring_of_chips(count):
    wide = 1
    while (wide * 2) * (wide * 2) <= count:
        wide *= 2
    tall = count // wide
    if wide < 2:
        return list(range(count))
    ring = [(z, 0) for z in range(tall)]
    for z in range(tall - 1, -1, -1):
        row = list(range(1, wide))
        ring += [(z, y) for y in (row if (tall - 1 - z) % 2 == 0 else row[::-1])]
    if (tall - 1) % 2 == 0 or wide == 2:
        return [z * wide + y for z, y in ring]
    return [z * wide + y for z, y in ring]


def locate(layout_rows, span_order, doc_ends):
    span_index = layout_rows // SPAN
    matches = span_index[:, None] == jnp.arange(span_order.shape[0], dtype=jnp.int32)[None, :]
    source_span = jnp.sum(jnp.where(matches, span_order[None, :], 0), axis=1)
    initial = source_span * SPAN + layout_rows % SPAN
    doc_start = jnp.max(
        jnp.where(doc_ends[None, :] <= initial[:, None], doc_ends[None, :], 0), axis=1
    )
    return (initial, doc_start)


def vmem_specs(count):
    return [pl.BlockSpec(memory_space=pltpu.VMEM)] * count


def compute_params():
    return pltpu.CompilerParams(vmem_limit_bytes=VMEM_LIMIT)


def norm_kernel(place, chips, where_ref, hidden_ref, gain_ref, own_ref, other_ref):
    at, core = where_ref[0], where_ref[1]
    wide = hidden_ref[...].astype(jnp.float32)
    meansq = jnp.mean(wide * wide, axis=-1, keepdims=True)
    normed = (wide * lax.rsqrt(meansq + 1e-05) * gain_ref[...].astype(jnp.float32)).astype(
        jnp.bfloat16
    )
    block = own_ref.shape[2]
    for chip in range(chips):
        slot = lax.rem(place[chip] + chips - at, chips)
        first = normed[:, (2 * chip) * block : (2 * chip + 1) * block]
        second = normed[:, (2 * chip + 1) * block : (2 * chip + 2) * block]

        @pl.when(core == 0)
        def _():
            own_ref[slot] = first
            other_ref[slot] = second

        @pl.when(core != 0)
        def _():
            own_ref[slot] = second
            other_ref[slot] = first


def take_ring(refs, chips):
    refs = list(refs)
    if chips % 2:
        return [(ref,) for ref in refs]
    half = chips // 2
    return [(r,) for r in refs[:half]] + [tuple(refs[half : half + 2])] + [
        (r,) for r in refs[half + 2 :]
    ]


def project_kernel(chips, groups, outs, *refs):
    rows_refs, refs = refs[:groups], refs[groups:]
    weight_refs, out_refs = refs[:-outs], refs[-outs:]
    weights = take_ring(weight_refs, chips)
    total = None
    for slot in range(chips):
        rows = jnp.concatenate([ref[slot] for ref in rows_refs], axis=0)
        start = 0
        for ref in weights[slot]:
            depth = ref.shape[0]
            part = jnp.dot(
                rows[:, start : start + depth], ref[...], preferred_element_type=jnp.float32
            )
            total = part if total is None else total + part
            start += depth
    start = 0
    for ref in out_refs:
        ref[...] = total[start : start + ref.shape[0]]
        start += ref.shape[0]


def turn(values, cosine, sine):
    return values * cosine + pltpu.roll(values, HD // 2, 1) * sine


def keys_kernel(mine_ref, theirs_ref, cosine_ref, sine_ref, out_ref):
    rows = out_ref.shape[0]
    cosine, sine = cosine_ref[:rows, :], sine_ref[:rows, :]
    total = mine_ref[...] + theirs_ref[...]
    out_ref[:, :HD] = turn(total[:, :HD], cosine, sine).astype(jnp.bfloat16)
    out_ref[:, HD:] = total[:, HD:].astype(jnp.bfloat16)


def attend_kernel(mine_ref, theirs_ref, cosine_ref, sine_ref, low_ref, high_ref, orig_ref, *refs):
    block_refs, (out_ref, keys_ref, values_ref) = refs[:-3], refs[-3:]
    start = 0
    for ref in block_refs:
        keys_ref[start : start + ref.shape[0], :] = ref[:, :HD]
        values_ref[start : start + ref.shape[0], :] = ref[:, HD:]
        start += ref.shape[0]
    keys = keys_ref[...]
    values = values_ref[...]
    orig = orig_ref[...]
    allowed = (orig >= low_ref[...]) & (orig <= high_ref[...])
    scale = 1.0 / HD**0.5
    rows = out_ref.shape[0]
    half = rows // 2
    lane = lax.broadcasted_iota(jnp.int32, (rows, HD), 1)
    stats = jnp.zeros((rows, HD), jnp.float32)
    for head in range(QH_DEV):
        columns = slice(head * HD, (head + 1) * HD)
        query = jnp.concatenate(
            [
                mine_ref[:half, columns] + theirs_ref[half:, columns],
                mine_ref[half:, columns] + theirs_ref[:half, columns],
            ],
            axis=0,
        )
        query = turn(query, cosine_ref[...], sine_ref[...]).astype(jnp.bfloat16)
        scores = lax.dot_general(
            query, keys, (((1,), (1,)), ((), ())), preferred_element_type=jnp.float32
        )
        scores = jnp.where(allowed, scores * scale, -1e30)
        top = jnp.max(scores, axis=-1, keepdims=True)
        expo = jnp.where(allowed, jnp.exp(scores - top), 0.0)
        total = jnp.sum(expo, axis=-1, keepdims=True)
        out_ref[:, columns] = jnp.dot(
            expo.astype(jnp.bfloat16), values, preferred_element_type=jnp.float32
        )
        stats = jnp.where(lane == 2 * head, total, stats)
        stats = jnp.where(lane == 2 * head + 1, top, stats)
    out_ref[:, HEAD_COLS:] = stats


def output_kernel(chips, groups, mine_ref, theirs_ref, *refs):
    weight_refs, out_refs = refs[:-groups], refs[-groups:]
    weights = take_ring(weight_refs, chips)
    chip_rows = mine_ref.shape[0]
    half = chip_rows // 2

    def swapped(columns):
        return jnp.concatenate([theirs_ref[half:, columns], theirs_ref[:half, columns]], axis=0)

    pieces = []
    for head in range(QH_DEV):
        columns = slice(head * HD, (head + 1) * HD)
        at = HEAD_COLS + 2 * head
        total, top = mine_ref[:, at : at + 1], mine_ref[:, at + 1 : at + 2]
        other_total, other_top = swapped(slice(at, at + 1)), swapped(slice(at + 1, at + 2))
        peak = jnp.maximum(top, other_top)
        factor, other_factor = jnp.exp(top - peak), jnp.exp(other_top - peak)
        product = mine_ref[:, columns] * factor + swapped(columns) * other_factor
        pieces.append(
            (product / (total * factor + other_total * other_factor)).astype(jnp.bfloat16)
        )
    mixed = jnp.concatenate(pieces, axis=1)
    rows = chip_rows // groups
    for slot in range(chips):
        start, total = 0, None
        for ref in weights[slot]:
            depth = ref.shape[0]
            part = jnp.dot(
                mixed[:, start : start + depth], ref[...], preferred_element_type=jnp.float32
            )
            total = part if total is None else total + part
            start += depth
        total = total.astype(jnp.bfloat16)
        for group in range(groups):
            out_refs[group][slot] = total[group * rows : (group + 1) * rows]


def sum_kernel(place, chips, groups, where_ref, *refs):
    part_refs, out_ref = refs[:groups], refs[groups]
    at, core = where_ref[0], where_ref[1]
    block = part_refs[0].shape[2]
    half = groups // 2

    def added(part, slot):
        total = part_refs[part * half][slot].astype(jnp.float32)
        for ref in part_refs[part * half + 1 : (part + 1) * half]:
            total += ref[slot].astype(jnp.float32)
        return total.astype(jnp.bfloat16)

    for chip in range(chips):
        slot = lax.rem(place[chip] + chips - at, chips)
        first = slice((2 * chip) * block, (2 * chip + 1) * block)
        second = slice((2 * chip + 1) * block, (2 * chip + 2) * block)

        @pl.when(core == 0)
        def _():
            out_ref[:, first] = added(0, slot)
            out_ref[:, second] = added(1, slot)

        @pl.when(core != 0)
        def _():
            out_ref[:, first] = added(1, slot)
            out_ref[:, second] = added(0, slot)


def per_device(n_context, n_tensor, hidden_rows, norm_gain, w_qkv, w_out, doc_lengths, span_order):
    chips = n_context // 2
    ring = ring_of_chips(chips)
    place = [ring.index(chip) for chip in range(chips)]
    groups = 2 * n_tensor
    rows_here, width = hidden_rows.shape
    tokens_here = rows_here * n_tensor
    block = width // n_context
    context = lax.axis_index("context")
    tensor = lax.axis_index("tensor")
    core = context % 2
    at = jnp.sum(
        jnp.where(jnp.arange(chips) == context // 2, jnp.asarray(place, jnp.int32), 0)
    ).astype(jnp.int32)
    where = jnp.stack([at, core]).astype(jnp.int32)

    ahead = [
        (ring[i] * 2 + k, ring[(i + 1) % chips] * 2 + k) for i in range(chips) for k in range(2)
    ]
    back = [(b, a) for a, b in ahead]
    sibling = [(c, c ^ 1) for c in range(n_context)]

    def after(value, *earlier):
        return lax.optimization_barrier((value, *earlier))[0]

    class Ring:
        def __init__(self, mine):
            self.mine = mine
            self.up, self.down = [mine], [mine]
            self.middle = []

        def step(self, *earlier):
            up, down = self.up[-1], self.down[-1]
            if earlier:
                up, down = lax.optimization_barrier((up, down, *earlier))[:2]
            if len(self.up) <= (chips - 1) // 2:
                self.up.append(lax.ppermute(up, "context", ahead))
                self.down.append(lax.ppermute(down, "context", back))
            elif chips % 2 == 0 and not self.middle:
                half = up.shape[0] // 2
                self.middle = [
                    lax.ppermute(up[:half], "context", ahead),
                    lax.ppermute(down[half:], "context", back),
                ]

        def last(self):
            return self.middle or [self.up[-1], self.down[-1]]

        def finish(self):
            while len(self.up) <= (chips - 1) // 2 or (chips % 2 == 0 and not self.middle):
                self.step()
            return self.down + self.middle + self.up[:0:-1]

    def member(e, d):
        return [
            (c * n_tensor + t, (c ^ e) * n_tensor + (t - d) % n_tensor)
            for c in range(n_context)
            for t in range(n_tensor)
        ]

    keys_ring = Ring(w_qkv[:, HEAD_COLS:])
    query_ring = Ring(w_qkv[:, :HEAD_COLS])
    out_ring = Ring(w_out)
    keys_ring.step()
    query_ring.step()

    smem = pl.BlockSpec(memory_space=pltpu.SMEM)
    normed_shape = jax.ShapeDtypeStruct((chips, rows_here, block), jnp.bfloat16)
    normed_own, normed_other = pl.pallas_call(
        functools.partial(norm_kernel, place, chips),
        out_shape=[normed_shape] * 2,
        in_specs=[smem] + vmem_specs(2),
        out_specs=vmem_specs(2),
        compiler_params=compute_params(),
        name="norm",
    )(where, hidden_rows, norm_gain[None, :])
    normed = []
    for e in range(2):
        for d in range(n_tensor):
            rows = normed_own if e == 0 else normed_other
            if e or d:
                rows = lax.ppermute(rows, ("context", "tensor"), member(e, d))
            normed.append(rows)

    def project(blocks, outs, name):
        columns = blocks[0].shape[1]
        return pl.pallas_call(
            functools.partial(project_kernel, chips, groups, outs),
            out_shape=[jax.ShapeDtypeStruct((2 * tokens_here // outs, columns), jnp.float32)]
            * outs,
            in_specs=vmem_specs(groups + len(blocks)),
            out_specs=vmem_specs(outs),
            compiler_params=compute_params(),
            name=name,
        )(*normed, *blocks)

    doc_ends = jnp.cumsum(doc_lengths)
    inside = (
        (tensor + jnp.arange(n_tensor, dtype=jnp.int32)) % n_tensor * rows_here
    )[:, None] + jnp.arange(rows_here, dtype=jnp.int32)[None, :]
    inside = inside.reshape(-1)
    both = jnp.concatenate([context * tokens_here + inside, (context ^ 1) * tokens_here + inside])
    query_orig, query_start = locate(both, span_order, doc_ends)
    half = HD // 2
    freq = rope_theta ** (-(jnp.arange(half, dtype=jnp.float32) * 2.0 / HD))
    angle = (query_orig - query_start).astype(jnp.float32)[:, None] * freq[None, :]
    cosine, sine = jnp.cos(angle), jnp.sin(angle)
    cosine = jnp.concatenate([cosine, cosine], axis=1)
    sine = jnp.concatenate([-sine, sine], axis=1)
    chip_of_slot = jnp.sum(
        jnp.where(
            ((jnp.arange(chips) + at) % chips)[:, None] == jnp.arange(chips)[None, :],
            jnp.asarray(ring, jnp.int32)[None, :],
            0,
        ),
        axis=1,
    ).astype(jnp.int32)
    owner = chip_of_slot * 2 + core
    key_rows = (owner[:, None] * tokens_here + inside[None, :]).reshape(-1).astype(jnp.int32)
    key_orig, _ = locate(key_rows, span_order, doc_ends)

    for _ in range(2):
        keys_ring.step(*keys_ring.last())
        query_ring.step(*query_ring.last())
    keys_ring.step()
    out_ring.step(*keys_ring.up[1:], *keys_ring.down[1:])
    query_ring.step()
    mine, theirs = project(keys_ring.finish(), 2, "project_keys")
    theirs = lax.ppermute(theirs, "context", sibling)
    kv = pl.pallas_call(
        keys_kernel,
        out_shape=jax.ShapeDtypeStruct((tokens_here, 2 * HD), jnp.bfloat16),
        in_specs=vmem_specs(4),
        out_specs=vmem_specs(1)[0],
        compiler_params=compute_params(),
        name="keys",
    )(mine, theirs, cosine, sine)
    kv_ring = Ring(kv)
    kv_ring.step()
    (mine,) = project(query_ring.finish(), 1, "project_queries")
    theirs = lax.ppermute(mine, "context", sibling)
    for _ in range(2):
        kv_ring.step()
        out_ring.step(*kv_ring.last())
    kv_blocks = kv_ring.finish()

    count = chips * tokens_here
    mixed = pl.pallas_call(
        attend_kernel,
        out_shape=jax.ShapeDtypeStruct((2 * tokens_here, HEAD_COLS + HD), jnp.float32),
        in_specs=vmem_specs(7 + len(kv_blocks)),
        out_specs=vmem_specs(1)[0],
        scratch_shapes=[pltpu.VMEM((count, HD), jnp.bfloat16)] * 2,
        compiler_params=compute_params(),
        name="attend",
    )(
        mine,
        theirs,
        cosine,
        sine,
        query_start[:, None],
        query_orig[:, None],
        key_orig[None, :],
        *kv_blocks,
    )
    mixed_theirs = lax.ppermute(mixed, "context", sibling)
    out_blocks = out_ring.finish()

    out_block = w_out.shape[1]
    parts = pl.pallas_call(
        functools.partial(output_kernel, chips, groups),
        out_shape=[jax.ShapeDtypeStruct((chips, rows_here, out_block), jnp.bfloat16)] * groups,
        in_specs=vmem_specs(2 + len(out_blocks)),
        out_specs=vmem_specs(groups),
        compiler_params=compute_params(),
        name="output",
    )(mixed, mixed_theirs, *out_blocks)
    arrived = []
    for e in range(2):
        for d in range(n_tensor):
            part = parts[e * n_tensor + d]
            if e or d:
                part = lax.ppermute(part, ("context", "tensor"), member(e, -d))
            arrived.append(part)
    return pl.pallas_call(
        functools.partial(sum_kernel, place, chips, groups),
        out_shape=jax.ShapeDtypeStruct((rows_here, n_context * out_block), jnp.bfloat16),
        in_specs=[smem] + vmem_specs(groups),
        out_specs=vmem_specs(1)[0],
        compiler_params=compute_params(),
        name="sum",
    )(where, *arrived)


def solution(mesh):
    placed = (
        P(("context", "tensor"), None),
        P(),
        P("context", "tensor"),
        P("tensor", "context"),
        P(),
        P(),
    )
    return jax.shard_map(
        functools.partial(per_device, mesh.shape["context"], mesh.shape["tensor"]),
        mesh=mesh,
        in_specs=placed,
        out_specs=P(("context", "tensor"), None),
        check_vma=False,
    )
```

```python
import functools

import jax
import jax.numpy as jnp
from jax import lax
from jax.experimental import pallas as pl
from jax.experimental.pallas import tpu as pltpu
from jax.sharding import PartitionSpec as P

HD = 128
QH_DEV = 4
SPAN = 64
HEAD_COLS = QH_DEV * HD
VMEM_LIMIT = 48 * 1024 * 1024

rope_theta = 500000.0


def ring_of_chips(count):
    wide = 1
    while (wide * 2) * (wide * 2) <= count:
        wide *= 2
    tall = count // wide
    if wide < 2:
        return list(range(count))
    ring = [(z, 0) for z in range(tall)]
    for z in range(tall - 1, -1, -1):
        row = list(range(1, wide))
        ring += [(z, y) for y in (row if (tall - 1 - z) % 2 == 0 else row[::-1])]
    if (tall - 1) % 2 == 0 or wide == 2:
        return [z * wide + y for z, y in ring]
    return [z * wide + y for z, y in ring]


def locate(layout_rows, span_order, doc_ends):
    span_index = layout_rows // SPAN
    matches = span_index[:, None] == jnp.arange(span_order.shape[0], dtype=jnp.int32)[None, :]
    source_span = jnp.sum(jnp.where(matches, span_order[None, :], 0), axis=1)
    initial = source_span * SPAN + layout_rows % SPAN
    doc_start = jnp.max(
        jnp.where(doc_ends[None, :] <= initial[:, None], doc_ends[None, :], 0), axis=1
    )
    return (initial, doc_start)


def vmem_specs(count):
    return [pl.BlockSpec(memory_space=pltpu.VMEM)] * count


def compute_params():
    return pltpu.CompilerParams(vmem_limit_bytes=VMEM_LIMIT)


def norm_kernel(place, chips, where_ref, hidden_ref, gain_ref, own_ref, other_ref):
    at, core = where_ref[0], where_ref[1]
    wide = hidden_ref[...].astype(jnp.float32)
    meansq = jnp.mean(wide * wide, axis=-1, keepdims=True)
    normed = (wide * lax.rsqrt(meansq + 1e-05) * gain_ref[...].astype(jnp.float32)).astype(
        jnp.bfloat16
    )
    block = own_ref.shape[2]
    for chip in range(chips):
        slot = lax.rem(place[chip] + chips - at, chips)
        first = normed[:, (2 * chip) * block : (2 * chip + 1) * block]
        second = normed[:, (2 * chip + 1) * block : (2 * chip + 2) * block]

        @pl.when(core == 0)
        def _():
            own_ref[slot] = first
            other_ref[slot] = second

        @pl.when(core != 0)
        def _():
            own_ref[slot] = second
            other_ref[slot] = first


def take_ring(refs, chips):
    refs = list(refs)
    if chips % 2:
        return [(ref,) for ref in refs]
    half = chips // 2
    return [(r,) for r in refs[:half]] + [tuple(refs[half : half + 2])] + [
        (r,) for r in refs[half + 2 :]
    ]


def project_kernel(chips, groups, outs, *refs):
    rows_refs, refs = refs[:groups], refs[groups:]
    weight_refs, out_refs = refs[:-outs], refs[-outs:]
    weights = take_ring(weight_refs, chips)
    total = None
    for slot in range(chips):
        rows = jnp.concatenate([ref[slot] for ref in rows_refs], axis=0)
        start = 0
        for ref in weights[slot]:
            depth = ref.shape[0]
            part = jnp.dot(
                rows[:, start : start + depth], ref[...], preferred_element_type=jnp.float32
            )
            total = part if total is None else total + part
            start += depth
    start = 0
    for ref in out_refs:
        ref[...] = total[start : start + ref.shape[0]]
        start += ref.shape[0]


def turn(values, cosine, sine):
    return values * cosine + pltpu.roll(values, HD // 2, 1) * sine


def keys_kernel(mine_ref, theirs_ref, cosine_ref, sine_ref, out_ref):
    rows = out_ref.shape[0]
    cosine, sine = cosine_ref[:rows, :], sine_ref[:rows, :]
    total = mine_ref[...] + theirs_ref[...]
    out_ref[:, :HD] = turn(total[:, :HD], cosine, sine).astype(jnp.bfloat16)
    out_ref[:, HD:] = total[:, HD:].astype(jnp.bfloat16)


def attend_kernel(
    mine_ref, theirs_ref, cosine_ref, sine_ref, low_ref, high_ref, orig_ref, *refs
):
    block_refs, (out_ref, keys_ref, values_ref) = refs[:-3], refs[-3:]
    start = 0
    for ref in block_refs:
        keys_ref[start : start + ref.shape[0], :] = ref[:, :HD]
        values_ref[start : start + ref.shape[0], :] = ref[:, HD:]
        start += ref.shape[0]
    keys = keys_ref[...]
    values = values_ref[...]
    orig = orig_ref[...]
    allowed = (orig >= low_ref[...]) & (orig <= high_ref[...])
    scale = 1.0 / HD**0.5
    rows = out_ref.shape[0]
    half = rows // 2
    lane = lax.broadcasted_iota(jnp.int32, (rows, HD), 1)
    stats = jnp.zeros((rows, HD), jnp.float32)
    for head in range(QH_DEV):
        columns = slice(head * HD, (head + 1) * HD)
        query = jnp.concatenate(
            [
                mine_ref[:half, columns] + theirs_ref[half:, columns],
                mine_ref[half:, columns] + theirs_ref[:half, columns],
            ],
            axis=0,
        )
        query = turn(query, cosine_ref[...], sine_ref[...]).astype(jnp.bfloat16)
        scores = lax.dot_general(
            query, keys, (((1,), (1,)), ((), ())), preferred_element_type=jnp.float32
        )
        scores = jnp.where(allowed, scores * scale, -1e30)
        top = jnp.max(scores, axis=-1, keepdims=True)
        expo = jnp.where(allowed, jnp.exp(scores - top), 0.0)
        total = jnp.sum(expo, axis=-1, keepdims=True)
        out_ref[:, columns] = jnp.dot(
            expo.astype(jnp.bfloat16), values, preferred_element_type=jnp.float32
        )
        stats = jnp.where(lane == 2 * head, total, stats)
        stats = jnp.where(lane == 2 * head + 1, top, stats)
    out_ref[:, HEAD_COLS:] = stats


def output_kernel(chips, groups, mine_ref, theirs_ref, weight_ref, *out_refs):
    chip_rows = mine_ref.shape[0]
    half = chip_rows // 2

    def swapped(columns):
        return jnp.concatenate([theirs_ref[half:, columns], theirs_ref[:half, columns]], axis=0)

    pieces = []
    for head in range(QH_DEV):
        columns = slice(head * HD, (head + 1) * HD)
        at = HEAD_COLS + 2 * head
        total, top = mine_ref[:, at : at + 1], mine_ref[:, at + 1 : at + 2]
        other_total, other_top = swapped(slice(at, at + 1)), swapped(slice(at + 1, at + 2))
        peak = jnp.maximum(top, other_top)
        factor, other_factor = jnp.exp(top - peak), jnp.exp(other_top - peak)
        product = mine_ref[:, columns] * factor + swapped(columns) * other_factor
        pieces.append(
            (product / (total * factor + other_total * other_factor)).astype(jnp.bfloat16)
        )
    mixed = jnp.concatenate(pieces, axis=1)
    rows = chip_rows // groups
    for chip in range(chips):
        total = jnp.dot(mixed, weight_ref[chip], preferred_element_type=jnp.float32)
        total = total.astype(jnp.bfloat16)
        for group in range(groups):
            out_refs[group][chip] = total[group * rows : (group + 1) * rows]


def sum_kernel(chips, groups, where_ref, *refs):
    part_refs, out_ref = refs[:groups], refs[groups]
    core = where_ref[1]
    block = part_refs[0].shape[2]
    half = groups // 2

    def added(part, chip):
        total = part_refs[part * half][chip].astype(jnp.float32)
        for ref in part_refs[part * half + 1 : (part + 1) * half]:
            total += ref[chip].astype(jnp.float32)
        return total.astype(jnp.bfloat16)

    for even in range(2):

        @pl.when(core == even)
        def _():
            for chip in range(chips):
                first = slice((2 * chip) * block, (2 * chip + 1) * block)
                second = slice((2 * chip + 1) * block, (2 * chip + 2) * block)
                out_ref[:, first] = added(even, chip)
                out_ref[:, second] = added(1 - even, chip)


def per_device(n_context, n_tensor, hidden_rows, norm_gain, w_qkv, w_out, doc_lengths, span_order):
    chips = n_context // 2
    ring = ring_of_chips(chips)
    place = [ring.index(chip) for chip in range(chips)]
    groups = 2 * n_tensor
    rows_here, width = hidden_rows.shape
    tokens_here = rows_here * n_tensor
    block = width // n_context
    context = lax.axis_index("context")
    tensor = lax.axis_index("tensor")
    core = context % 2
    at = jnp.sum(
        jnp.where(jnp.arange(chips) == context // 2, jnp.asarray(place, jnp.int32), 0)
    ).astype(jnp.int32)
    where = jnp.stack([at, core]).astype(jnp.int32)

    ahead = [
        (ring[i] * 2 + k, ring[(i + 1) % chips] * 2 + k) for i in range(chips) for k in range(2)
    ]
    back = [(b, a) for a, b in ahead]
    sibling = [(c, c ^ 1) for c in range(n_context)]

    def after(value, *earlier):
        return lax.optimization_barrier((value, *earlier))[0]

    class Ring:
        def __init__(self, mine):
            self.mine = mine
            self.up, self.down = [mine], [mine]
            self.middle = []

        def step(self, *earlier):
            up, down = self.up[-1], self.down[-1]
            if earlier:
                up, down = lax.optimization_barrier((up, down, *earlier))[:2]
            if len(self.up) <= (chips - 1) // 2:
                self.up.append(lax.ppermute(up, "context", ahead))
                self.down.append(lax.ppermute(down, "context", back))
            elif chips % 2 == 0 and not self.middle:
                half = up.shape[0] // 2
                self.middle = [
                    lax.ppermute(up[:half], "context", ahead),
                    lax.ppermute(down[half:], "context", back),
                ]

        def done(self):
            return len(self.up) > (chips - 1) // 2 and (chips % 2 == 1 or bool(self.middle))

        def last(self):
            return self.middle or [self.up[-1], self.down[-1]]

        def finish(self):
            return self.down + self.middle + self.up[:0:-1]

    same_core = [[2 * chip + k for chip in range(chips)] for k in range(2)]

    def from_chips(mine):
        return lax.all_gather(mine, "context", axis_index_groups=same_core)

    def member(e, d):
        return [
            (c * n_tensor + t, (c ^ e) * n_tensor + (t - d) % n_tensor)
            for c in range(n_context)
            for t in range(n_tensor)
        ]

    keys_ring = Ring(w_qkv[:, HEAD_COLS:])
    query_ring = Ring(w_qkv[:, :HEAD_COLS])
    out_blocks = from_chips(w_out)
    keys_ring.step()
    query_ring.step()

    smem = pl.BlockSpec(memory_space=pltpu.SMEM)
    normed_shape = jax.ShapeDtypeStruct((chips, rows_here, block), jnp.bfloat16)
    normed_own, normed_other = pl.pallas_call(
        functools.partial(norm_kernel, place, chips),
        out_shape=[normed_shape] * 2,
        in_specs=[smem] + vmem_specs(2),
        out_specs=vmem_specs(2),
        compiler_params=compute_params(),
        name="norm",
    )(where, hidden_rows, norm_gain[None, :])
    normed = []
    for e in range(2):
        for d in range(n_tensor):
            rows = normed_own if e == 0 else normed_other
            if e or d:
                rows = lax.ppermute(rows, ("context", "tensor"), member(e, d))
            normed.append(rows)

    def project(blocks, outs, name):
        columns = blocks[0].shape[1]
        return pl.pallas_call(
            functools.partial(project_kernel, chips, groups, outs),
            out_shape=[jax.ShapeDtypeStruct((2 * tokens_here // outs, columns), jnp.float32)]
            * outs,
            in_specs=vmem_specs(groups + len(blocks)),
            out_specs=vmem_specs(outs),
            compiler_params=compute_params(),
            name=name,
        )(*normed, *blocks)

    doc_ends = jnp.cumsum(doc_lengths)
    inside = (
        (tensor + jnp.arange(n_tensor, dtype=jnp.int32)) % n_tensor * rows_here
    )[:, None] + jnp.arange(rows_here, dtype=jnp.int32)[None, :]
    inside = inside.reshape(-1)
    both = jnp.concatenate([context * tokens_here + inside, (context ^ 1) * tokens_here + inside])
    query_orig, query_start = locate(both, span_order, doc_ends)
    half = HD // 2
    freq = rope_theta ** (-(jnp.arange(half, dtype=jnp.float32) * 2.0 / HD))
    angle = (query_orig - query_start).astype(jnp.float32)[:, None] * freq[None, :]
    cosine, sine = jnp.cos(angle), jnp.sin(angle)
    cosine = jnp.concatenate([cosine, cosine], axis=1)
    sine = jnp.concatenate([-sine, sine], axis=1)
    chip_of_slot = jnp.sum(
        jnp.where(
            ((jnp.arange(chips) + at) % chips)[:, None] == jnp.arange(chips)[None, :],
            jnp.asarray(ring, jnp.int32)[None, :],
            0,
        ),
        axis=1,
    ).astype(jnp.int32)
    owner = chip_of_slot * 2 + core
    key_rows = (owner[:, None] * tokens_here + inside[None, :]).reshape(-1).astype(jnp.int32)
    key_orig, _ = locate(key_rows, span_order, doc_ends)

    queries_before = []
    while not keys_ring.done():
        keys_now, queries_now = keys_ring.last(), query_ring.last()
        keys_ring.step(*queries_before)
        query_ring.step(*keys_now)
        queries_before = queries_now
    mine, theirs = project(keys_ring.finish(), 2, "project_keys")
    theirs = lax.ppermute(theirs, "context", sibling)
    kv = pl.pallas_call(
        keys_kernel,
        out_shape=jax.ShapeDtypeStruct((tokens_here, 2 * HD), jnp.bfloat16),
        in_specs=vmem_specs(4),
        out_specs=vmem_specs(1)[0],
        compiler_params=compute_params(),
        name="keys",
    )(mine, theirs, cosine, sine)
    kv_ring = Ring(kv)
    kv_ring.step()
    (mine,) = project(query_ring.finish(), 1, "project_queries")
    theirs = lax.ppermute(mine, "context", sibling)
    while not kv_ring.done():
        kv_ring.step(*kv_ring.last())
    kv_blocks = kv_ring.finish()
    count = chips * tokens_here

    mixed = pl.pallas_call(
        attend_kernel,
        out_shape=jax.ShapeDtypeStruct((2 * tokens_here, HEAD_COLS + HD), jnp.float32),
        in_specs=vmem_specs(7 + len(kv_blocks)),
        out_specs=vmem_specs(1)[0],
        scratch_shapes=[pltpu.VMEM((count, HD), jnp.bfloat16)] * 2,
        compiler_params=compute_params(),
        name="attend",
    )(
        mine,
        theirs,
        cosine,
        sine,
        query_start[:, None],
        query_orig[:, None],
        key_orig[None, :],
        *kv_blocks,
    )
    mixed_theirs = lax.ppermute(mixed, "context", sibling)

    out_block = w_out.shape[1]
    parts = pl.pallas_call(
        functools.partial(output_kernel, chips, groups),
        out_shape=[jax.ShapeDtypeStruct((chips, rows_here, out_block), jnp.bfloat16)] * groups,
        in_specs=vmem_specs(3),
        out_specs=vmem_specs(groups),
        compiler_params=compute_params(),
        name="output",
    )(mixed, mixed_theirs, out_blocks)
    arrived = []
    for e in range(2):
        for d in range(n_tensor):
            part = parts[e * n_tensor + d]
            if e or d:
                part = lax.ppermute(part, ("context", "tensor"), member(e, -d))
            arrived.append(part)
    return pl.pallas_call(
        functools.partial(sum_kernel, chips, groups),
        out_shape=jax.ShapeDtypeStruct((rows_here, n_context * out_block), jnp.bfloat16),
        in_specs=[smem] + vmem_specs(groups),
        out_specs=vmem_specs(1)[0],
        compiler_params=compute_params(),
        name="sum",
    )(where, *arrived)


def solution(mesh):
    placed = (
        P(("context", "tensor"), None),
        P(),
        P("context", "tensor"),
        P("tensor", "context"),
        P(),
        P(),
    )
    return jax.shard_map(
        functools.partial(per_device, mesh.shape["context"], mesh.shape["tensor"]),
        mesh=mesh,
        in_specs=placed,
        out_specs=P(("context", "tensor"), None),
        check_vma=False,
    )
```

```python
import functools

import jax
import jax.numpy as jnp
from jax import lax
from jax.experimental import pallas as pl
from jax.experimental.pallas import tpu as pltpu
from jax.sharding import PartitionSpec as P

HD = 128
QH_DEV = 4
SPAN = 64
HEAD_COLS = QH_DEV * HD
VMEM_LIMIT = 48 * 1024 * 1024

rope_theta = 500000.0


def ring_of_chips(count):
    wide = 1
    while (wide * 2) * (wide * 2) <= count:
        wide *= 2
    tall = count // wide
    if wide < 2:
        return list(range(count))
    ring = [(z, 0) for z in range(tall)]
    for z in range(tall - 1, -1, -1):
        row = list(range(1, wide))
        ring += [(z, y) for y in (row if (tall - 1 - z) % 2 == 0 else row[::-1])]
    if (tall - 1) % 2 == 0 or wide == 2:
        return [z * wide + y for z, y in ring]
    return [z * wide + y for z, y in ring]


def locate(layout_rows, span_order, doc_ends):
    span_index = layout_rows // SPAN
    matches = span_index[:, None] == jnp.arange(span_order.shape[0], dtype=jnp.int32)[None, :]
    source_span = jnp.sum(jnp.where(matches, span_order[None, :], 0), axis=1)
    initial = source_span * SPAN + layout_rows % SPAN
    doc_start = jnp.max(
        jnp.where(doc_ends[None, :] <= initial[:, None], doc_ends[None, :], 0), axis=1
    )
    return (initial, doc_start)


def vmem_specs(count):
    return [pl.BlockSpec(memory_space=pltpu.VMEM)] * count


def compute_params():
    return pltpu.CompilerParams(vmem_limit_bytes=VMEM_LIMIT)


def place_of(place):
    context = lax.axis_index("context")
    at = jnp.int32(0)
    for chip, spot in enumerate(place):
        at = jnp.where(context // 2 == chip, jnp.int32(spot), at)
    return at, context % 2


def norm_kernel(place, chips, hidden_ref, gain_ref, own_ref, other_ref):
    at, core = place_of(place)
    wide = hidden_ref[...].astype(jnp.float32)
    meansq = jnp.mean(wide * wide, axis=-1, keepdims=True)
    normed = (wide * lax.rsqrt(meansq + 1e-05) * gain_ref[...].astype(jnp.float32)).astype(
        jnp.bfloat16
    )
    block = own_ref.shape[2]
    for even in range(2):

        @pl.when(core == even)
        def _():
            for chip in range(chips):
                slot = lax.rem(place[chip] + chips - at, chips)
                for side in range(2):
                    column = (2 * chip + side) * block
                    ref = own_ref if side == even else other_ref
                    ref[slot] = normed[:, column : column + block]


def take_ring(refs, chips):
    refs = list(refs)
    if chips % 2:
        return [(ref,) for ref in refs]
    half = chips // 2
    return [(r,) for r in refs[:half]] + [tuple(refs[half : half + 2])] + [
        (r,) for r in refs[half + 2 :]
    ]


def project_kernel(chips, groups, outs, *refs):
    rows_refs, refs = refs[:groups], refs[groups:]
    weight_refs, out_refs = refs[:-outs], refs[-outs:]
    weights = take_ring(weight_refs, chips)
    total = None
    for slot in range(chips):
        rows = jnp.concatenate([ref[slot] for ref in rows_refs], axis=0)
        start = 0
        for ref in weights[slot]:
            depth = ref.shape[0]
            part = jnp.dot(
                rows[:, start : start + depth], ref[...], preferred_element_type=jnp.float32
            )
            total = part if total is None else total + part
            start += depth
    start = 0
    for ref in out_refs:
        ref[...] = total[start : start + ref.shape[0]]
        start += ref.shape[0]


def turn(values, cosine, sine):
    return values * cosine + pltpu.roll(values, HD // 2, 1) * sine


def keys_kernel(mine_ref, theirs_ref, cosine_ref, sine_ref, out_ref):
    rows = out_ref.shape[0]
    cosine, sine = cosine_ref[:rows, :], sine_ref[:rows, :]
    total = mine_ref[...] + theirs_ref[...]
    out_ref[:, :HD] = turn(total[:, :HD], cosine, sine).astype(jnp.bfloat16)
    out_ref[:, HD:] = total[:, HD:].astype(jnp.bfloat16)


def attend_kernel(mine_ref, theirs_ref, cosine_ref, sine_ref, low_ref, high_ref, orig_ref, *refs):
    block_refs, (out_ref, keys_ref, values_ref) = refs[:-3], refs[-3:]
    start = 0
    for ref in block_refs:
        keys_ref[start : start + ref.shape[0], :] = ref[:, :HD]
        values_ref[start : start + ref.shape[0], :] = ref[:, HD:]
        start += ref.shape[0]
    keys = keys_ref[...]
    values = values_ref[...]
    orig = orig_ref[...]
    allowed = (orig >= low_ref[...]) & (orig <= high_ref[...])
    scale = 1.0 / HD**0.5
    rows = out_ref.shape[0]
    half = rows // 2
    lane = lax.broadcasted_iota(jnp.int32, (rows, HD), 1)
    stats = jnp.zeros((rows, HD), jnp.float32)
    for head in range(QH_DEV):
        columns = slice(head * HD, (head + 1) * HD)
        query = jnp.concatenate(
            [
                mine_ref[:half, columns] + theirs_ref[half:, columns],
                mine_ref[half:, columns] + theirs_ref[:half, columns],
            ],
            axis=0,
        )
        query = turn(query, cosine_ref[...], sine_ref[...]).astype(jnp.bfloat16)
        scores = lax.dot_general(
            query, keys, (((1,), (1,)), ((), ())), preferred_element_type=jnp.float32
        )
        scores = jnp.where(allowed, scores * scale, -1e30)
        top = jnp.max(scores, axis=-1, keepdims=True)
        expo = jnp.where(allowed, jnp.exp(scores - top), 0.0)
        total = jnp.sum(expo, axis=-1, keepdims=True)
        out_ref[:, columns] = jnp.dot(
            expo.astype(jnp.bfloat16), values, preferred_element_type=jnp.float32
        )
        stats = jnp.where(lane == 2 * head, total, stats)
        stats = jnp.where(lane == 2 * head + 1, top, stats)
    out_ref[:, HEAD_COLS:] = stats


def output_kernel(chips, groups, mine_ref, theirs_ref, *refs):
    weight_refs, out_refs = refs[:-groups], refs[-groups:]
    weights = take_ring(weight_refs, chips)
    chip_rows = mine_ref.shape[0]
    half = chip_rows // 2

    def swapped(columns):
        return jnp.concatenate([theirs_ref[half:, columns], theirs_ref[:half, columns]], axis=0)

    pieces = []
    for head in range(QH_DEV):
        columns = slice(head * HD, (head + 1) * HD)
        at = HEAD_COLS + 2 * head
        total, top = mine_ref[:, at : at + 1], mine_ref[:, at + 1 : at + 2]
        other_total, other_top = swapped(slice(at, at + 1)), swapped(slice(at + 1, at + 2))
        peak = jnp.maximum(top, other_top)
        factor, other_factor = jnp.exp(top - peak), jnp.exp(other_top - peak)
        product = mine_ref[:, columns] * factor + swapped(columns) * other_factor
        pieces.append(
            (product / (total * factor + other_total * other_factor)).astype(jnp.bfloat16)
        )
    mixed = jnp.concatenate(pieces, axis=1)
    rows = chip_rows // groups
    for slot in range(chips):
        start, total = 0, None
        for ref in weights[slot]:
            depth = ref.shape[0]
            part = jnp.dot(
                mixed[:, start : start + depth], ref[...], preferred_element_type=jnp.float32
            )
            total = part if total is None else total + part
            start += depth
        total = total.astype(jnp.bfloat16)
        for group in range(groups):
            out_refs[group][slot] = total[group * rows : (group + 1) * rows]


def sum_kernel(place, chips, groups, token_ref, *refs):
    part_refs, out_ref = refs[:groups], refs[groups]
    at, core = place_of(place)
    block = part_refs[0].shape[2]
    half = groups // 2

    def added(part, slot):
        total = part_refs[part * half][slot].astype(jnp.float32)
        for ref in part_refs[part * half + 1 : (part + 1) * half]:
            total += ref[slot].astype(jnp.float32)
        return total.astype(jnp.bfloat16)

    for even in range(2):

        @pl.when(core == even)
        def _():
            for chip in range(chips):
                slot = lax.rem(place[chip] + chips - at, chips)
                for side in range(2):
                    column = (2 * chip + side) * block
                    out_ref[:, column : column + block] = added(side ^ even, slot)


def per_device(n_context, n_tensor, hidden_rows, norm_gain, w_qkv, w_out, doc_lengths, span_order):
    chips = n_context // 2
    ring = ring_of_chips(chips)
    place = [ring.index(chip) for chip in range(chips)]
    groups = 2 * n_tensor
    rows_here, width = hidden_rows.shape
    tokens_here = rows_here * n_tensor
    block = width // n_context
    context = lax.axis_index("context")
    tensor = lax.axis_index("tensor")
    ahead = [
        (ring[i] * 2 + k, ring[(i + 1) % chips] * 2 + k) for i in range(chips) for k in range(2)
    ]
    back = [(b, a) for a, b in ahead]
    sibling = [(c, c ^ 1) for c in range(n_context)]

    token = [doc_lengths]

    def ordered(values):
        held = lax.optimization_barrier((*values, token[0]))
        token[0] = held[-1]
        return list(held[:-1])

    class Ring:
        def __init__(self, mine):
            self.up, self.down = [mine], [mine]
            self.middle = []

        def step(self, earlier=()):
            up, down, *earlier = ordered((self.up[-1], self.down[-1], *earlier))
            if len(self.up) <= (chips - 1) // 2:
                self.up.append(lax.ppermute(up, "context", ahead))
                self.down.append(lax.ppermute(down, "context", back))
            elif chips % 2 == 0 and not self.middle:
                half = up.shape[0] // 2
                self.middle = [
                    lax.ppermute(up[:half], "context", ahead),
                    lax.ppermute(down[half:], "context", back),
                ]
            return earlier

        def done(self):
            return len(self.up) > (chips - 1) // 2 and (chips % 2 == 1 or bool(self.middle))

        def finish(self):
            while not self.done():
                self.step()
            return self.down + self.middle + self.up[:0:-1]

    def member(e, d):
        return [
            (c * n_tensor + t, (c ^ e) * n_tensor + (t - d) % n_tensor)
            for c in range(n_context)
            for t in range(n_tensor)
        ]

    keys_ring = Ring(w_qkv[:, HEAD_COLS:])
    keys_ring.step()

    normed_shape = jax.ShapeDtypeStruct((chips, rows_here, block), jnp.bfloat16)
    normed_own, normed_other = pl.pallas_call(
        functools.partial(norm_kernel, place, chips),
        out_shape=[normed_shape] * 2,
        in_specs=vmem_specs(2),
        out_specs=vmem_specs(2),
        compiler_params=compute_params(),
        name="norm",
    )(hidden_rows, norm_gain[None, :])
    normed_own, normed_other = ordered((normed_own, normed_other))
    normed = []
    for e in range(2):
        for d in range(n_tensor):
            rows = normed_own if e == 0 else normed_other
            if e or d:
                rows = lax.ppermute(rows, ("context", "tensor"), member(e, d))
            normed.append(rows)

    keys_ring.step()
    query_ring = Ring(ordered((w_qkv,))[0][:, :HEAD_COLS])
    query_ring.step()
    keys_ring.step()
    normed = keys_ring.step(normed)
    while not keys_ring.done():
        keys_ring.step()
    query_ring.step()
    out_ring = Ring(w_out)

    def project(blocks, outs, name):
        columns = blocks[0].shape[1]
        return pl.pallas_call(
            functools.partial(project_kernel, chips, groups, outs),
            out_shape=[jax.ShapeDtypeStruct((2 * tokens_here // outs, columns), jnp.float32)]
            * outs,
            in_specs=vmem_specs(groups + len(blocks)),
            out_specs=vmem_specs(outs),
            compiler_params=compute_params(),
            name=name,
        )(*ordered((*normed, *blocks)))

    doc_ends = jnp.cumsum(doc_lengths)
    inside = (
        (tensor + jnp.arange(n_tensor, dtype=jnp.int32)) % n_tensor * rows_here
    )[:, None] + jnp.arange(rows_here, dtype=jnp.int32)[None, :]
    inside = inside.reshape(-1)
    both = jnp.concatenate([context * tokens_here + inside, (context ^ 1) * tokens_here + inside])
    query_orig, query_start = locate(both, span_order, doc_ends)
    half = HD // 2
    freq = rope_theta ** (-(jnp.arange(half, dtype=jnp.float32) * 2.0 / HD))
    angle = (query_orig - query_start).astype(jnp.float32)[:, None] * freq[None, :]
    cosine, sine = jnp.cos(angle), jnp.sin(angle)
    cosine = jnp.concatenate([cosine, cosine], axis=1)
    sine = jnp.concatenate([-sine, sine], axis=1)
    at = jnp.sum(
        jnp.where(jnp.arange(chips) == context // 2, jnp.asarray(place, jnp.int32), 0)
    ).astype(jnp.int32)
    chip_of_slot = jnp.sum(
        jnp.where(
            ((jnp.arange(chips) + at) % chips)[:, None] == jnp.arange(chips)[None, :],
            jnp.asarray(ring, jnp.int32)[None, :],
            0,
        ),
        axis=1,
    ).astype(jnp.int32)
    owner = chip_of_slot * 2 + context % 2
    key_rows = (owner[:, None] * tokens_here + inside[None, :]).reshape(-1).astype(jnp.int32)
    key_orig, _ = locate(key_rows, span_order, doc_ends)

    mine, theirs = project(keys_ring.finish(), 2, "project_keys")
    theirs = lax.ppermute(theirs, "context", sibling)
    out_ring.step()
    mine, theirs = ordered((mine, theirs))
    kv = pl.pallas_call(
        keys_kernel,
        out_shape=jax.ShapeDtypeStruct((tokens_here, 2 * HD), jnp.bfloat16),
        in_specs=vmem_specs(4),
        out_specs=vmem_specs(1)[0],
        compiler_params=compute_params(),
        name="keys",
    )(mine, theirs, cosine, sine)
    kv_ring = Ring(kv)
    kv_ring.step()
    query_ring.step()
    kv_ring.step()
    out_ring.step()
    kv_ring.step()
    while not query_ring.done():
        query_ring.step()
    while not kv_ring.done():
        kv_ring.step()
    out_ring.step()
    (mine,) = project(query_ring.finish(), 1, "project_queries")
    theirs = lax.ppermute(mine, "context", sibling)
    kv_blocks = kv_ring.finish()

    count = chips * tokens_here
    mixed = pl.pallas_call(
        attend_kernel,
        out_shape=jax.ShapeDtypeStruct((2 * tokens_here, HEAD_COLS + HD), jnp.float32),
        in_specs=vmem_specs(7 + len(kv_blocks)),
        out_specs=vmem_specs(1)[0],
        scratch_shapes=[pltpu.VMEM((count, HD), jnp.bfloat16)] * 2,
        compiler_params=compute_params(),
        name="attend",
    )(
        mine,
        theirs,
        cosine,
        sine,
        query_start[:, None],
        query_orig[:, None],
        key_orig[None, :],
        *kv_blocks,
    )
    (mixed,) = ordered((mixed,))
    mixed_theirs = lax.ppermute(mixed, "context", sibling)
    out_blocks = out_ring.finish()

    out_block = w_out.shape[1]
    parts = pl.pallas_call(
        functools.partial(output_kernel, chips, groups),
        out_shape=[jax.ShapeDtypeStruct((chips, rows_here, out_block), jnp.bfloat16)] * groups,
        in_specs=vmem_specs(2 + len(out_blocks)),
        out_specs=vmem_specs(groups),
        compiler_params=compute_params(),
        name="output",
    )(mixed, mixed_theirs, *out_blocks)
    arrived = []
    for e in range(2):
        for d in range(n_tensor):
            part = parts[e * n_tensor + d]
            if e or d:
                part = lax.ppermute(part, ("context", "tensor"), member(e, -d))
            arrived.append(part)
    return pl.pallas_call(
        functools.partial(sum_kernel, place, chips, groups),
        out_shape=jax.ShapeDtypeStruct((rows_here, n_context * out_block), jnp.bfloat16),
        in_specs=[pl.BlockSpec(memory_space=pl.ANY)] + vmem_specs(groups),
        out_specs=vmem_specs(1)[0],
        compiler_params=compute_params(),
        name="sum",
    )(token[0], *arrived)


def solution(mesh):
    placed = (
        P(("context", "tensor"), None),
        P(),
        P("context", "tensor"),
        P("tensor", "context"),
        P(),
        P(),
    )
    return jax.shard_map(
        functools.partial(per_device, mesh.shape["context"], mesh.shape["tensor"]),
        mesh=mesh,
        in_specs=placed,
        out_specs=P(("context", "tensor"), None),
        check_vma=False,
    )
```

```python
import functools

import jax
import jax.numpy as jnp
from jax import lax
from jax.experimental import pallas as pl
from jax.experimental.pallas import tpu as pltpu
from jax.sharding import PartitionSpec as P

HD = 128
QH_DEV = 4
SPAN = 64
HEAD_COLS = QH_DEV * HD
VMEM_LIMIT = 24 * 1024 * 1024

rope_theta = 500000.0


def ring_of_chips(count):
    wide = 1
    while (wide * 2) * (wide * 2) <= count:
        wide *= 2
    tall = count // wide
    if wide < 2:
        return list(range(count))
    ring = [(z, 0) for z in range(tall)]
    for z in range(tall - 1, -1, -1):
        row = list(range(1, wide))
        ring += [(z, y) for y in (row if (tall - 1 - z) % 2 == 0 else row[::-1])]
    if (tall - 1) % 2 == 0 or wide == 2:
        return [z * wide + y for z, y in ring]
    return [z * wide + y for z, y in ring]


def locate(layout_rows, span_order, doc_ends):
    span_index = layout_rows // SPAN
    matches = span_index[:, None] == jnp.arange(span_order.shape[0], dtype=jnp.int32)[None, :]
    source_span = jnp.sum(jnp.where(matches, span_order[None, :], 0), axis=1)
    initial = source_span * SPAN + layout_rows % SPAN
    doc_start = jnp.max(
        jnp.where(doc_ends[None, :] <= initial[:, None], doc_ends[None, :], 0), axis=1
    )
    return (initial, doc_start)


def vmem_specs(count):
    return [pl.BlockSpec(memory_space=pltpu.VMEM)] * count


def compute_params():
    return pltpu.CompilerParams(vmem_limit_bytes=VMEM_LIMIT)


def place_of(place):
    context = lax.axis_index("context")
    at = jnp.int32(0)
    for chip, spot in enumerate(place):
        at = jnp.where(context // 2 == chip, jnp.int32(spot), at)
    return at, context % 2


def norm_kernel(place, chips, hidden_ref, gain_ref, own_ref, other_ref):
    at, core = place_of(place)
    wide = hidden_ref[...].astype(jnp.float32)
    meansq = jnp.mean(wide * wide, axis=-1, keepdims=True)
    normed = (wide * lax.rsqrt(meansq + 1e-05) * gain_ref[...].astype(jnp.float32)).astype(
        jnp.bfloat16
    )
    block = own_ref.shape[2]
    for even in range(2):

        @pl.when(core == even)
        def _():
            for chip in range(chips):
                slot = lax.rem(place[chip] + chips - at, chips)
                for side in range(2):
                    column = (2 * chip + side) * block
                    ref = own_ref if side == even else other_ref
                    ref[slot] = normed[:, column : column + block]


def take_ring(refs, chips):
    refs = list(refs)
    if chips % 2:
        return [(ref,) for ref in refs]
    half = chips // 2
    return [(r,) for r in refs[:half]] + [tuple(refs[half : half + 2])] + [
        (r,) for r in refs[half + 2 :]
    ]


def project_kernel(chips, groups, outs, *refs):
    rows_refs, refs = refs[:groups], refs[groups:]
    weight_refs, out_refs = refs[:-outs], refs[-outs:]
    weights = take_ring(weight_refs, chips)
    total = None
    for slot in range(chips):
        rows = jnp.concatenate([ref[slot] for ref in rows_refs], axis=0)
        start = 0
        for ref in weights[slot]:
            depth = ref.shape[0]
            part = jnp.dot(
                rows[:, start : start + depth], ref[...], preferred_element_type=jnp.float32
            )
            total = part if total is None else total + part
            start += depth
    start = 0
    for ref in out_refs:
        ref[...] = total[start : start + ref.shape[0]]
        start += ref.shape[0]


def turn(values, cosine, sine):
    return values * cosine + pltpu.roll(values, HD // 2, 1) * sine


def keys_kernel(mine_ref, theirs_ref, cosine_ref, sine_ref, out_ref):
    rows = out_ref.shape[0]
    cosine, sine = cosine_ref[:rows, :], sine_ref[:rows, :]
    total = mine_ref[...] + theirs_ref[...]
    out_ref[:, :HD] = turn(total[:, :HD], cosine, sine).astype(jnp.bfloat16)
    out_ref[:, HD:] = total[:, HD:].astype(jnp.bfloat16)


def attend_kernel(mine_ref, theirs_ref, cosine_ref, sine_ref, low_ref, high_ref, orig_ref, *refs):
    block_refs, (out_ref, keys_ref, values_ref) = refs[:-3], refs[-3:]
    start = 0
    for ref in block_refs:
        keys_ref[start : start + ref.shape[0], :] = ref[:, :HD]
        values_ref[start : start + ref.shape[0], :] = ref[:, HD:]
        start += ref.shape[0]
    keys = keys_ref[...]
    values = values_ref[...]
    orig = orig_ref[...]
    allowed = (orig >= low_ref[...]) & (orig <= high_ref[...])
    scale = 1.0 / HD**0.5
    rows = out_ref.shape[0]
    half = rows // 2
    lane = lax.broadcasted_iota(jnp.int32, (rows, HD), 1)
    stats = jnp.zeros((rows, HD), jnp.float32)
    for head in range(QH_DEV):
        columns = slice(head * HD, (head + 1) * HD)
        query = jnp.concatenate(
            [
                mine_ref[:half, columns] + theirs_ref[half:, columns],
                mine_ref[half:, columns] + theirs_ref[:half, columns],
            ],
            axis=0,
        )
        query = turn(query, cosine_ref[...], sine_ref[...]).astype(jnp.bfloat16)
        scores = lax.dot_general(
            query, keys, (((1,), (1,)), ((), ())), preferred_element_type=jnp.float32
        )
        scores = jnp.where(allowed, scores * scale, -1e30)
        top = jnp.max(scores, axis=-1, keepdims=True)
        expo = jnp.where(allowed, jnp.exp(scores - top), 0.0)
        total = jnp.sum(expo, axis=-1, keepdims=True)
        out_ref[:, columns] = jnp.dot(
            expo.astype(jnp.bfloat16), values, preferred_element_type=jnp.float32
        )
        stats = jnp.where(lane == 2 * head, total, stats)
        stats = jnp.where(lane == 2 * head + 1, top, stats)
    out_ref[:, HEAD_COLS:] = stats


def output_kernel(chips, groups, mine_ref, theirs_ref, *refs):
    weight_refs, out_refs = refs[:-groups], refs[-groups:]
    weights = take_ring(weight_refs, chips)
    chip_rows = mine_ref.shape[0]
    half = chip_rows // 2

    def swapped(columns):
        return jnp.concatenate([theirs_ref[half:, columns], theirs_ref[:half, columns]], axis=0)

    pieces = []
    for head in range(QH_DEV):
        columns = slice(head * HD, (head + 1) * HD)
        at = HEAD_COLS + 2 * head
        total, top = mine_ref[:, at : at + 1], mine_ref[:, at + 1 : at + 2]
        other_total, other_top = swapped(slice(at, at + 1)), swapped(slice(at + 1, at + 2))
        peak = jnp.maximum(top, other_top)
        factor, other_factor = jnp.exp(top - peak), jnp.exp(other_top - peak)
        product = mine_ref[:, columns] * factor + swapped(columns) * other_factor
        pieces.append(
            (product / (total * factor + other_total * other_factor)).astype(jnp.bfloat16)
        )
    mixed = jnp.concatenate(pieces, axis=1)
    rows = chip_rows // groups
    for slot in range(chips):
        start, total = 0, None
        for ref in weights[slot]:
            depth = ref.shape[0]
            part = jnp.dot(
                mixed[:, start : start + depth], ref[...], preferred_element_type=jnp.float32
            )
            total = part if total is None else total + part
            start += depth
        total = total.astype(jnp.bfloat16)
        for group in range(groups):
            out_refs[group][slot] = total[group * rows : (group + 1) * rows]


def sum_kernel(place, chips, groups, token_ref, *refs):
    part_refs, out_ref = refs[:groups], refs[groups]
    at, core = place_of(place)
    block = part_refs[0].shape[2]
    half = groups // 2

    def added(part, slot):
        total = part_refs[part * half][slot].astype(jnp.float32)
        for ref in part_refs[part * half + 1 : (part + 1) * half]:
            total += ref[slot].astype(jnp.float32)
        return total.astype(jnp.bfloat16)

    for even in range(2):

        @pl.when(core == even)
        def _():
            for chip in range(chips):
                slot = lax.rem(place[chip] + chips - at, chips)
                for side in range(2):
                    column = (2 * chip + side) * block
                    out_ref[:, column : column + block] = added(side ^ even, slot)


def per_device(n_context, n_tensor, hidden_rows, norm_gain, w_qkv, w_out, doc_lengths, span_order):
    chips = n_context // 2
    ring = ring_of_chips(chips)
    place = [ring.index(chip) for chip in range(chips)]
    groups = 2 * n_tensor
    rows_here, width = hidden_rows.shape
    tokens_here = rows_here * n_tensor
    block = width // n_context
    context = lax.axis_index("context")
    tensor = lax.axis_index("tensor")
    ahead = [
        (ring[i] * 2 + k, ring[(i + 1) % chips] * 2 + k) for i in range(chips) for k in range(2)
    ]
    back = [(b, a) for a, b in ahead]
    sibling = [(c, c ^ 1) for c in range(n_context)]

    token = [doc_lengths]

    def ordered(values):
        held = lax.optimization_barrier((*values, token[0]))
        token[0] = held[-1]
        return list(held[:-1])

    class Ring:
        def __init__(self, mine):
            self.up, self.down = [mine], [mine]
            self.middle = []

        def step(self, earlier=()):
            up, down, *earlier = ordered((self.up[-1], self.down[-1], *earlier))
            if len(self.up) <= (chips - 1) // 2:
                self.up.append(lax.ppermute(up, "context", ahead))
                self.down.append(lax.ppermute(down, "context", back))
            elif chips % 2 == 0 and not self.middle:
                half = up.shape[0] // 2
                self.middle = [
                    lax.ppermute(up[:half], "context", ahead),
                    lax.ppermute(down[half:], "context", back),
                ]
            return earlier

        def done(self):
            return len(self.up) > (chips - 1) // 2 and (chips % 2 == 1 or bool(self.middle))

        def finish(self):
            while not self.done():
                self.step()
            return self.down + self.middle + self.up[:0:-1]

    def member(e, d):
        return [
            (c * n_tensor + t, (c ^ e) * n_tensor + (t - d) % n_tensor)
            for c in range(n_context)
            for t in range(n_tensor)
        ]

    keys_ring = Ring(w_qkv[:, HEAD_COLS:])
    keys_ring.step()
    query_ring = Ring(w_qkv[:, :HEAD_COLS])
    query_ring.step()

    normed_shape = jax.ShapeDtypeStruct((chips, rows_here, block), jnp.bfloat16)
    normed_own, normed_other = pl.pallas_call(
        functools.partial(norm_kernel, place, chips),
        out_shape=[normed_shape] * 2,
        in_specs=vmem_specs(2),
        out_specs=vmem_specs(2),
        compiler_params=compute_params(),
        name="norm",
    )(hidden_rows, norm_gain[None, :])
    keys_ring.step()
    normed_own, normed_other = ordered((normed_own, normed_other))
    normed = []
    for e in range(2):
        for d in range(n_tensor):
            rows = normed_own if e == 0 else normed_other
            if e or d:
                rows = lax.ppermute(rows, ("context", "tensor"), member(e, d))
            normed.append(rows)

    query_ring.step()
    keys_ring.step()
    query_ring.step()
    while not keys_ring.done():
        normed = keys_ring.step(normed)
        query_ring.step()

    def project(blocks, outs, name):
        columns = blocks[0].shape[1]
        return pl.pallas_call(
            functools.partial(project_kernel, chips, groups, outs),
            out_shape=[jax.ShapeDtypeStruct((2 * tokens_here // outs, columns), jnp.float32)]
            * outs,
            in_specs=vmem_specs(groups + len(blocks)),
            out_specs=vmem_specs(outs),
            compiler_params=compute_params(),
            name=name,
        )(*ordered((*normed, *blocks)))

    doc_ends = jnp.cumsum(doc_lengths)
    inside = (
        (tensor + jnp.arange(n_tensor, dtype=jnp.int32)) % n_tensor * rows_here
    )[:, None] + jnp.arange(rows_here, dtype=jnp.int32)[None, :]
    inside = inside.reshape(-1)
    both = jnp.concatenate([context * tokens_here + inside, (context ^ 1) * tokens_here + inside])
    query_orig, query_start = locate(both, span_order, doc_ends)
    half = HD // 2
    freq = rope_theta ** (-(jnp.arange(half, dtype=jnp.float32) * 2.0 / HD))
    angle = (query_orig - query_start).astype(jnp.float32)[:, None] * freq[None, :]
    cosine, sine = jnp.cos(angle), jnp.sin(angle)
    cosine = jnp.concatenate([cosine, cosine], axis=1)
    sine = jnp.concatenate([-sine, sine], axis=1)
    at, core = place_of(place)
    spot = (jnp.arange(chips, dtype=jnp.int32) + at) % chips
    chip_of_slot = jnp.zeros((chips,), jnp.int32)
    for i, chip in enumerate(ring):
        chip_of_slot = jnp.where(spot == i, jnp.int32(chip), chip_of_slot)
    owner = chip_of_slot * 2 + core
    key_rows = (owner[:, None] * tokens_here + inside[None, :]).reshape(-1).astype(jnp.int32)
    key_orig, _ = locate(key_rows, span_order, doc_ends)

    mine, theirs = project(keys_ring.finish(), 2, "project_keys")
    theirs = lax.ppermute(theirs, "context", sibling)
    out_ring = Ring(w_out)
    out_ring.step()
    mine, theirs = ordered((mine, theirs))
    kv = pl.pallas_call(
        keys_kernel,
        out_shape=jax.ShapeDtypeStruct((tokens_here, 2 * HD), jnp.bfloat16),
        in_specs=vmem_specs(4),
        out_specs=vmem_specs(1)[0],
        compiler_params=compute_params(),
        name="keys",
    )(mine, theirs, cosine, sine)
    kv_ring = Ring(kv)
    kv_ring.step()
    (mine,) = project(query_ring.finish(), 1, "project_queries")
    theirs = lax.ppermute(mine, "context", sibling)
    while not kv_ring.done():
        out_ring.step()
        kv_ring.step()
    kv_blocks = kv_ring.finish()

    count = chips * tokens_here
    mixed = pl.pallas_call(
        attend_kernel,
        out_shape=jax.ShapeDtypeStruct((2 * tokens_here, HEAD_COLS + HD), jnp.float32),
        in_specs=vmem_specs(7 + len(kv_blocks)),
        out_specs=vmem_specs(1)[0],
        scratch_shapes=[pltpu.VMEM((count, HD), jnp.bfloat16)] * 2,
        compiler_params=compute_params(),
        name="attend",
    )(
        mine,
        theirs,
        cosine,
        sine,
        query_start[:, None],
        query_orig[:, None],
        key_orig[None, :],
        *kv_blocks,
    )
    (mixed,) = ordered((mixed,))
    mixed_theirs = lax.ppermute(mixed, "context", sibling)
    out_blocks = out_ring.finish()

    out_block = w_out.shape[1]
    parts = pl.pallas_call(
        functools.partial(output_kernel, chips, groups),
        out_shape=[jax.ShapeDtypeStruct((chips, rows_here, out_block), jnp.bfloat16)] * groups,
        in_specs=vmem_specs(2 + len(out_blocks)),
        out_specs=vmem_specs(groups),
        compiler_params=compute_params(),
        name="output",
    )(mixed, mixed_theirs, *out_blocks)
    arrived = []
    for e in range(2):
        for d in range(n_tensor):
            part = parts[e * n_tensor + d]
            if e or d:
                part = lax.ppermute(part, ("context", "tensor"), member(e, -d))
            arrived.append(part)
    return pl.pallas_call(
        functools.partial(sum_kernel, place, chips, groups),
        out_shape=jax.ShapeDtypeStruct((rows_here, n_context * out_block), jnp.bfloat16),
        in_specs=[pl.BlockSpec(memory_space=pl.ANY)] + vmem_specs(groups),
        out_specs=vmem_specs(1)[0],
        compiler_params=compute_params(),
        name="sum",
    )(token[0], *arrived)


def solution(mesh):
    placed = (
        P(("context", "tensor"), None),
        P(),
        P("context", "tensor"),
        P("tensor", "context"),
        P(),
        P(),
    )
    return jax.shard_map(
        functools.partial(per_device, mesh.shape["context"], mesh.shape["tensor"]),
        mesh=mesh,
        in_specs=placed,
        out_specs=P(("context", "tensor"), None),
        check_vma=False,
    )
```

```python
import functools

import jax
import jax.numpy as jnp
from jax import lax
from jax.experimental import pallas as pl
from jax.experimental.pallas import tpu as pltpu
from jax.sharding import PartitionSpec as P

HD = 128
QH_DEV = 4
SPAN = 64
HEAD_COLS = QH_DEV * HD
VMEM_LIMIT = 24 * 1024 * 1024

rope_theta = 500000.0


def ring_of_chips(count):
    wide = 1
    while (wide * 2) * (wide * 2) <= count:
        wide *= 2
    tall = count // wide
    if wide < 2:
        return list(range(count))
    ring = [(z, 0) for z in range(tall)]
    for z in range(tall - 1, -1, -1):
        row = list(range(1, wide))
        ring += [(z, y) for y in (row if (tall - 1 - z) % 2 == 0 else row[::-1])]
    if (tall - 1) % 2 == 0 or wide == 2:
        return [z * wide + y for z, y in ring]
    return [z * wide + y for z, y in ring]


def locate(layout_rows, span_order, doc_ends):
    span_index = layout_rows // SPAN
    matches = span_index[:, None] == jnp.arange(span_order.shape[0], dtype=jnp.int32)[None, :]
    source_span = jnp.sum(jnp.where(matches, span_order[None, :], 0), axis=1)
    initial = source_span * SPAN + layout_rows % SPAN
    doc_start = jnp.max(
        jnp.where(doc_ends[None, :] <= initial[:, None], doc_ends[None, :], 0), axis=1
    )
    return (initial, doc_start)


def vmem_specs(count):
    return [pl.BlockSpec(memory_space=pltpu.VMEM)] * count


def compute_params():
    return pltpu.CompilerParams(vmem_limit_bytes=VMEM_LIMIT)


def place_of(place):
    context = lax.axis_index("context")
    at = jnp.int32(0)
    for chip, spot in enumerate(place):
        at = jnp.where(context // 2 == chip, jnp.int32(spot), at)
    return at, context % 2


def norm_kernel(place, chips, hidden_ref, gain_ref, own_ref, other_ref):
    at, core = place_of(place)
    wide = hidden_ref[...].astype(jnp.float32)
    meansq = jnp.mean(wide * wide, axis=-1, keepdims=True)
    normed = (wide * lax.rsqrt(meansq + 1e-05) * gain_ref[...].astype(jnp.float32)).astype(
        jnp.bfloat16
    )
    block = own_ref.shape[2]
    for even in range(2):

        @pl.when(core == even)
        def _():
            for chip in range(chips):
                slot = lax.rem(place[chip] + chips - at, chips)
                for side in range(2):
                    column = (2 * chip + side) * block
                    ref = own_ref if side == even else other_ref
                    ref[slot] = normed[:, column : column + block]


def take_ring(refs, chips):
    refs = list(refs)
    if chips % 2:
        return [(ref,) for ref in refs]
    half = chips // 2
    return [(r,) for r in refs[:half]] + [tuple(refs[half : half + 2])] + [
        (r,) for r in refs[half + 2 :]
    ]


def project_kernel(chips, groups, outs, *refs):
    rows_refs, refs = refs[:groups], refs[groups:]
    weight_refs, out_refs = refs[:-outs], refs[-outs:]
    weights = take_ring(weight_refs, chips)
    total = None
    for slot in range(chips):
        rows = jnp.concatenate([ref[slot] for ref in rows_refs], axis=0)
        start = 0
        for ref in weights[slot]:
            depth = ref.shape[0]
            part = jnp.dot(
                rows[:, start : start + depth], ref[...], preferred_element_type=jnp.float32
            )
            total = part if total is None else total + part
            start += depth
    start = 0
    for ref in out_refs:
        ref[...] = total[start : start + ref.shape[0]]
        start += ref.shape[0]


def turn(values, cosine, sine):
    return values * cosine + pltpu.roll(values, HD // 2, 1) * sine


def keys_kernel(mine_ref, theirs_ref, cosine_ref, sine_ref, out_ref):
    rows = out_ref.shape[0]
    cosine, sine = cosine_ref[:rows, :], sine_ref[:rows, :]
    total = mine_ref[...] + theirs_ref[...]
    out_ref[:, :HD] = turn(total[:, :HD], cosine, sine).astype(jnp.bfloat16)
    out_ref[:, HD:] = total[:, HD:].astype(jnp.bfloat16)


def attend_kernel(mine_ref, theirs_ref, cosine_ref, sine_ref, low_ref, high_ref, orig_ref, *refs):
    block_refs, (out_ref, keys_ref, values_ref) = refs[:-3], refs[-3:]
    start = 0
    for ref in block_refs:
        keys_ref[start : start + ref.shape[0], :] = ref[:, :HD]
        values_ref[start : start + ref.shape[0], :] = ref[:, HD:]
        start += ref.shape[0]
    keys = keys_ref[...]
    values = values_ref[...]
    orig = orig_ref[...]
    allowed = (orig >= low_ref[...]) & (orig <= high_ref[...])
    scale = 1.0 / HD**0.5
    rows = out_ref.shape[0]
    half = rows // 2
    lane = lax.broadcasted_iota(jnp.int32, (rows, HD), 1)
    stats = jnp.zeros((rows, HD), jnp.float32)
    for head in range(QH_DEV):
        columns = slice(head * HD, (head + 1) * HD)
        query = jnp.concatenate(
            [
                mine_ref[:half, columns] + theirs_ref[half:, columns],
                mine_ref[half:, columns] + theirs_ref[:half, columns],
            ],
            axis=0,
        )
        query = turn(query, cosine_ref[...], sine_ref[...]).astype(jnp.bfloat16)
        scores = lax.dot_general(
            query, keys, (((1,), (1,)), ((), ())), preferred_element_type=jnp.float32
        )
        scores = jnp.where(allowed, scores * scale, -1e30)
        top = jnp.max(scores, axis=-1, keepdims=True)
        expo = jnp.where(allowed, jnp.exp(scores - top), 0.0)
        total = jnp.sum(expo, axis=-1, keepdims=True)
        out_ref[:, columns] = jnp.dot(
            expo.astype(jnp.bfloat16), values, preferred_element_type=jnp.float32
        )
        stats = jnp.where(lane == 2 * head, total, stats)
        stats = jnp.where(lane == 2 * head + 1, top, stats)
    out_ref[:, HEAD_COLS:] = stats


def output_kernel(chips, groups, mine_ref, theirs_ref, *refs):
    weight_refs, out_refs = refs[:-groups], refs[-groups:]
    weights = take_ring(weight_refs, chips)
    chip_rows = mine_ref.shape[0]
    half = chip_rows // 2

    def swapped(columns):
        return jnp.concatenate([theirs_ref[half:, columns], theirs_ref[:half, columns]], axis=0)

    pieces = []
    for head in range(QH_DEV):
        columns = slice(head * HD, (head + 1) * HD)
        at = HEAD_COLS + 2 * head
        total, top = mine_ref[:, at : at + 1], mine_ref[:, at + 1 : at + 2]
        other_total, other_top = swapped(slice(at, at + 1)), swapped(slice(at + 1, at + 2))
        peak = jnp.maximum(top, other_top)
        factor, other_factor = jnp.exp(top - peak), jnp.exp(other_top - peak)
        product = mine_ref[:, columns] * factor + swapped(columns) * other_factor
        pieces.append(
            (product / (total * factor + other_total * other_factor)).astype(jnp.bfloat16)
        )
    mixed = jnp.concatenate(pieces, axis=1)
    rows = chip_rows // groups
    for slot in range(chips):
        start, total = 0, None
        for ref in weights[slot]:
            depth = ref.shape[0]
            part = jnp.dot(
                mixed[:, start : start + depth], ref[...], preferred_element_type=jnp.float32
            )
            total = part if total is None else total + part
            start += depth
        total = total.astype(jnp.bfloat16)
        for group in range(groups):
            out_refs[group][slot] = total[group * rows : (group + 1) * rows]


def sum_kernel(place, chips, groups, token_ref, *refs):
    part_refs, out_ref = refs[:groups], refs[groups]
    at, core = place_of(place)
    block = part_refs[0].shape[2]
    half = groups // 2

    def added(part, slot):
        total = part_refs[part * half][slot].astype(jnp.float32)
        for ref in part_refs[part * half + 1 : (part + 1) * half]:
            total += ref[slot].astype(jnp.float32)
        return total.astype(jnp.bfloat16)

    for even in range(2):

        @pl.when(core == even)
        def _():
            for chip in range(chips):
                slot = lax.rem(place[chip] + chips - at, chips)
                for side in range(2):
                    column = (2 * chip + side) * block
                    out_ref[:, column : column + block] = added(side ^ even, slot)


def per_device(n_context, n_tensor, hidden_rows, norm_gain, w_qkv, w_out, doc_lengths, span_order):
    chips = n_context // 2
    ring = ring_of_chips(chips)
    place = [ring.index(chip) for chip in range(chips)]
    groups = 2 * n_tensor
    rows_here, width = hidden_rows.shape
    tokens_here = rows_here * n_tensor
    block = width // n_context
    context = lax.axis_index("context")
    tensor = lax.axis_index("tensor")
    ahead = [
        (ring[i] * 2 + k, ring[(i + 1) % chips] * 2 + k) for i in range(chips) for k in range(2)
    ]
    back = [(b, a) for a, b in ahead]
    sibling = [(c, c ^ 1) for c in range(n_context)]

    token = [doc_lengths]

    def ordered(values):
        held = lax.optimization_barrier((*values, token[0]))
        token[0] = held[-1]
        return list(held[:-1])

    class Ring:
        def __init__(self, mine):
            self.up, self.down = [mine], [mine]
            self.middle = []

        def step(self, earlier=()):
            up, down, *earlier = ordered((self.up[-1], self.down[-1], *earlier))
            if len(self.up) <= (chips - 1) // 2:
                self.up.append(lax.ppermute(up, "context", ahead))
                self.down.append(lax.ppermute(down, "context", back))
            elif chips % 2 == 0 and not self.middle:
                half = up.shape[0] // 2
                self.middle = [
                    lax.ppermute(up[:half], "context", ahead),
                    lax.ppermute(down[half:], "context", back),
                ]
            return earlier

        def done(self):
            return len(self.up) > (chips - 1) // 2 and (chips % 2 == 1 or bool(self.middle))

        def finish(self):
            while not self.done():
                self.step()
            return self.down + self.middle + self.up[:0:-1]

    def member(e, d):
        return [
            (c * n_tensor + t, (c ^ e) * n_tensor + (t - d) % n_tensor)
            for c in range(n_context)
            for t in range(n_tensor)
        ]

    keys_ring = Ring(w_qkv[:, HEAD_COLS:])
    keys_ring.step()

    normed_shape = jax.ShapeDtypeStruct((chips, rows_here, block), jnp.bfloat16)
    normed_own, normed_other = pl.pallas_call(
        functools.partial(norm_kernel, place, chips),
        out_shape=[normed_shape] * 2,
        in_specs=vmem_specs(2),
        out_specs=vmem_specs(2),
        compiler_params=compute_params(),
        name="norm",
    )(hidden_rows, norm_gain[None, :])
    normed_own, normed_other = ordered((normed_own, normed_other))
    normed = []
    for e in range(2):
        for d in range(n_tensor):
            rows = normed_own if e == 0 else normed_other
            if e or d:
                rows = lax.ppermute(rows, ("context", "tensor"), member(e, d))
            normed.append(rows)

    query_ring = Ring(w_qkv[:, :HEAD_COLS])
    query_ring.step()
    keys_ring.step()
    query_ring.step()
    normed = keys_ring.step(normed)
    query_ring.step()
    while not keys_ring.done():
        keys_ring.step()

    def project(blocks, outs, name):
        columns = blocks[0].shape[1]
        return pl.pallas_call(
            functools.partial(project_kernel, chips, groups, outs),
            out_shape=[jax.ShapeDtypeStruct((2 * tokens_here // outs, columns), jnp.float32)]
            * outs,
            in_specs=vmem_specs(groups + len(blocks)),
            out_specs=vmem_specs(outs),
            compiler_params=compute_params(),
            name=name,
        )(*ordered((*normed, *blocks)))

    doc_ends = jnp.cumsum(doc_lengths)
    inside = (
        (tensor + jnp.arange(n_tensor, dtype=jnp.int32)) % n_tensor * rows_here
    )[:, None] + jnp.arange(rows_here, dtype=jnp.int32)[None, :]
    inside = inside.reshape(-1)
    both = jnp.concatenate([context * tokens_here + inside, (context ^ 1) * tokens_here + inside])
    query_orig, query_start = locate(both, span_order, doc_ends)
    half = HD // 2
    freq = rope_theta ** (-(jnp.arange(half, dtype=jnp.float32) * 2.0 / HD))
    angle = (query_orig - query_start).astype(jnp.float32)[:, None] * freq[None, :]
    cosine, sine = jnp.cos(angle), jnp.sin(angle)
    cosine = jnp.concatenate([cosine, cosine], axis=1)
    sine = jnp.concatenate([-sine, sine], axis=1)
    at, core = place_of(place)
    spot = (jnp.arange(chips, dtype=jnp.int32) + at) % chips
    chip_of_slot = jnp.zeros((chips,), jnp.int32)
    for i, chip in enumerate(ring):
        chip_of_slot = jnp.where(spot == i, jnp.int32(chip), chip_of_slot)
    owner = chip_of_slot * 2 + core
    key_rows = (owner[:, None] * tokens_here + inside[None, :]).reshape(-1).astype(jnp.int32)
    key_orig, _ = locate(key_rows, span_order, doc_ends)

    mine, theirs = project(keys_ring.finish(), 2, "project_keys")
    theirs = lax.ppermute(theirs, "context", sibling)
    query_ring.step()
    out_ring = Ring(w_out)
    out_ring.step()
    mine, theirs = ordered((mine, theirs))
    kv = pl.pallas_call(
        keys_kernel,
        out_shape=jax.ShapeDtypeStruct((tokens_here, 2 * HD), jnp.bfloat16),
        in_specs=vmem_specs(4),
        out_specs=vmem_specs(1)[0],
        compiler_params=compute_params(),
        name="keys",
    )(mine, theirs, cosine, sine)
    kv_ring = Ring(kv)
    kv_ring.step()
    (mine,) = project(query_ring.finish(), 1, "project_queries")
    theirs = lax.ppermute(mine, "context", sibling)
    while not kv_ring.done():
        kv_ring.step()
        out_ring.step()
    kv_blocks = kv_ring.finish()

    count = chips * tokens_here
    mixed = pl.pallas_call(
        attend_kernel,
        out_shape=jax.ShapeDtypeStruct((2 * tokens_here, HEAD_COLS + HD), jnp.float32),
        in_specs=vmem_specs(7 + len(kv_blocks)),
        out_specs=vmem_specs(1)[0],
        scratch_shapes=[pltpu.VMEM((count, HD), jnp.bfloat16)] * 2,
        compiler_params=compute_params(),
        name="attend",
    )(
        mine,
        theirs,
        cosine,
        sine,
        query_start[:, None],
        query_orig[:, None],
        key_orig[None, :],
        *kv_blocks,
    )
    (mixed,) = ordered((mixed,))
    mixed_theirs = lax.ppermute(mixed, "context", sibling)
    out_blocks = out_ring.finish()

    out_block = w_out.shape[1]
    parts = pl.pallas_call(
        functools.partial(output_kernel, chips, groups),
        out_shape=[jax.ShapeDtypeStruct((chips, rows_here, out_block), jnp.bfloat16)] * groups,
        in_specs=vmem_specs(2 + len(out_blocks)),
        out_specs=vmem_specs(groups),
        compiler_params=compute_params(),
        name="output",
    )(mixed, mixed_theirs, *out_blocks)
    arrived = []
    for e in range(2):
        for d in range(n_tensor):
            part = parts[e * n_tensor + d]
            if e or d:
                part = lax.ppermute(part, ("context", "tensor"), member(e, -d))
            arrived.append(part)
    return pl.pallas_call(
        functools.partial(sum_kernel, place, chips, groups),
        out_shape=jax.ShapeDtypeStruct((rows_here, n_context * out_block), jnp.bfloat16),
        in_specs=[pl.BlockSpec(memory_space=pl.ANY)] + vmem_specs(groups),
        out_specs=vmem_specs(1)[0],
        compiler_params=compute_params(),
        name="sum",
    )(token[0], *arrived)


def solution(mesh):
    placed = (
        P(("context", "tensor"), None),
        P(),
        P("context", "tensor"),
        P("tensor", "context"),
        P(),
        P(),
    )
    return jax.shard_map(
        functools.partial(per_device, mesh.shape["context"], mesh.shape["tensor"]),
        mesh=mesh,
        in_specs=placed,
        out_specs=P(("context", "tensor"), None),
        check_vma=False,
    )
```

```python
import functools

import jax
import jax.numpy as jnp
from jax import lax
from jax.experimental import pallas as pl
from jax.experimental.pallas import tpu as pltpu
from jax.sharding import PartitionSpec as P

HD = 128
QH_DEV = 4
SPAN = 64
HEAD_COLS = QH_DEV * HD
VMEM_LIMIT = 24 * 1024 * 1024

rope_theta = 500000.0


def ring_of_chips(count):
    wide = 1
    while (wide * 2) * (wide * 2) <= count:
        wide *= 2
    tall = count // wide
    if wide < 2:
        return list(range(count))
    ring = [(z, 0) for z in range(tall)]
    for z in range(tall - 1, -1, -1):
        row = list(range(1, wide))
        ring += [(z, y) for y in (row if (tall - 1 - z) % 2 == 0 else row[::-1])]
    if (tall - 1) % 2 == 0 or wide == 2:
        return [z * wide + y for z, y in ring]
    return [z * wide + y for z, y in ring]


def locate(layout_rows, span_order, doc_ends):
    span_index = layout_rows // SPAN
    matches = span_index[:, None] == jnp.arange(span_order.shape[0], dtype=jnp.int32)[None, :]
    source_span = jnp.sum(jnp.where(matches, span_order[None, :], 0), axis=1)
    initial = source_span * SPAN + layout_rows % SPAN
    doc_start = jnp.max(
        jnp.where(doc_ends[None, :] <= initial[:, None], doc_ends[None, :], 0), axis=1
    )
    return (initial, doc_start)


def vmem_specs(count):
    return [pl.BlockSpec(memory_space=pltpu.VMEM)] * count


def compute_params():
    return pltpu.CompilerParams(vmem_limit_bytes=VMEM_LIMIT)


def place_of(place):
    context = lax.axis_index("context")
    at = jnp.int32(0)
    for chip, spot in enumerate(place):
        at = jnp.where(context // 2 == chip, jnp.int32(spot), at)
    return at, context % 2


def norm_kernel(place, chips, hidden_ref, gain_ref, own_ref, other_ref):
    at, core = place_of(place)
    wide = hidden_ref[...].astype(jnp.float32)
    meansq = jnp.mean(wide * wide, axis=-1, keepdims=True)
    normed = (wide * lax.rsqrt(meansq + 1e-05) * gain_ref[...].astype(jnp.float32)).astype(
        jnp.bfloat16
    )
    block = own_ref.shape[2]
    for even in range(2):

        @pl.when(core == even)
        def _():
            for chip in range(chips):
                slot = lax.rem(place[chip] + chips - at, chips)
                for side in range(2):
                    column = (2 * chip + side) * block
                    ref = own_ref if side == even else other_ref
                    ref[slot] = normed[:, column : column + block]


def take_ring(refs, chips):
    refs = list(refs)
    if chips % 2:
        return [(ref,) for ref in refs]
    half = chips // 2
    return [(r,) for r in refs[:half]] + [tuple(refs[half : half + 2])] + [
        (r,) for r in refs[half + 2 :]
    ]


def project_kernel(chips, groups, outs, *refs):
    rows_refs, refs = refs[:groups], refs[groups:]
    weight_refs, out_refs = refs[:-outs], refs[-outs:]
    weights = take_ring(weight_refs, chips)
    total = None
    for slot in range(chips):
        rows = jnp.concatenate([ref[slot] for ref in rows_refs], axis=0)
        start = 0
        for ref in weights[slot]:
            depth = ref.shape[0]
            part = jnp.dot(
                rows[:, start : start + depth], ref[...], preferred_element_type=jnp.float32
            )
            total = part if total is None else total + part
            start += depth
    start = 0
    for ref in out_refs:
        ref[...] = total[start : start + ref.shape[0]]
        start += ref.shape[0]


def turn(values, cosine, sine):
    return values * cosine + pltpu.roll(values, HD // 2, 1) * sine


def keys_kernel(chips, mine_ref, theirs_ref, cosine_ref, sine_ref, out_ref):
    rows = out_ref.shape[0] // chips
    cosine, sine = cosine_ref[:rows, :], sine_ref[:rows, :]
    total = mine_ref[...] + theirs_ref[...]
    keys = turn(total[:, :HD], cosine, sine).astype(jnp.bfloat16)
    values = total[:, HD:].astype(jnp.bfloat16)
    for chip in range(chips):
        out_ref[chip * rows : (chip + 1) * rows, :HD] = keys
        out_ref[chip * rows : (chip + 1) * rows, HD:] = values


def attend_kernel(
    mine_ref, theirs_ref, cosine_ref, sine_ref, low_ref, high_ref, orig_ref, kv_ref, out_ref
):
    keys = kv_ref[:, :HD]
    values = kv_ref[:, HD:]
    orig = orig_ref[...]
    allowed = (orig >= low_ref[...]) & (orig <= high_ref[...])
    scale = 1.0 / HD**0.5
    rows = out_ref.shape[0]
    half = rows // 2
    lane = lax.broadcasted_iota(jnp.int32, (rows, HD), 1)
    stats = jnp.zeros((rows, HD), jnp.float32)
    for head in range(QH_DEV):
        columns = slice(head * HD, (head + 1) * HD)
        query = jnp.concatenate(
            [
                mine_ref[:half, columns] + theirs_ref[half:, columns],
                mine_ref[half:, columns] + theirs_ref[:half, columns],
            ],
            axis=0,
        )
        query = turn(query, cosine_ref[...], sine_ref[...]).astype(jnp.bfloat16)
        scores = lax.dot_general(
            query, keys, (((1,), (1,)), ((), ())), preferred_element_type=jnp.float32
        )
        scores = jnp.where(allowed, scores * scale, -1e30)
        top = jnp.max(scores, axis=-1, keepdims=True)
        expo = jnp.where(allowed, jnp.exp(scores - top), 0.0)
        total = jnp.sum(expo, axis=-1, keepdims=True)
        out_ref[:, columns] = jnp.dot(
            expo.astype(jnp.bfloat16), values, preferred_element_type=jnp.float32
        )
        stats = jnp.where(lane == 2 * head, total, stats)
        stats = jnp.where(lane == 2 * head + 1, top, stats)
    out_ref[:, HEAD_COLS:] = stats


def output_kernel(chips, groups, mine_ref, theirs_ref, *refs):
    weight_refs, out_refs = refs[:-groups], refs[-groups:]
    weights = take_ring(weight_refs, chips)
    chip_rows = mine_ref.shape[0]
    half = chip_rows // 2

    def swapped(columns):
        return jnp.concatenate([theirs_ref[half:, columns], theirs_ref[:half, columns]], axis=0)

    pieces = []
    for head in range(QH_DEV):
        columns = slice(head * HD, (head + 1) * HD)
        at = HEAD_COLS + 2 * head
        total, top = mine_ref[:, at : at + 1], mine_ref[:, at + 1 : at + 2]
        other_total, other_top = swapped(slice(at, at + 1)), swapped(slice(at + 1, at + 2))
        peak = jnp.maximum(top, other_top)
        factor, other_factor = jnp.exp(top - peak), jnp.exp(other_top - peak)
        product = mine_ref[:, columns] * factor + swapped(columns) * other_factor
        pieces.append(
            (product / (total * factor + other_total * other_factor)).astype(jnp.bfloat16)
        )
    mixed = jnp.concatenate(pieces, axis=1)
    rows = chip_rows // groups
    for slot in range(chips):
        start, total = 0, None
        for ref in weights[slot]:
            depth = ref.shape[0]
            part = jnp.dot(
                mixed[:, start : start + depth], ref[...], preferred_element_type=jnp.float32
            )
            total = part if total is None else total + part
            start += depth
        total = total.astype(jnp.bfloat16)
        for group in range(groups):
            out_refs[group][slot] = total[group * rows : (group + 1) * rows]


def sum_kernel(place, chips, groups, token_ref, *refs):
    part_refs, out_ref = refs[:groups], refs[groups]
    at, core = place_of(place)
    block = part_refs[0].shape[2]
    half = groups // 2

    def added(part, slot):
        total = part_refs[part * half][slot].astype(jnp.float32)
        for ref in part_refs[part * half + 1 : (part + 1) * half]:
            total += ref[slot].astype(jnp.float32)
        return total.astype(jnp.bfloat16)

    for even in range(2):

        @pl.when(core == even)
        def _():
            for chip in range(chips):
                slot = lax.rem(place[chip] + chips - at, chips)
                for side in range(2):
                    column = (2 * chip + side) * block
                    out_ref[:, column : column + block] = added(side ^ even, slot)


def per_device(n_context, n_tensor, hidden_rows, norm_gain, w_qkv, w_out, doc_lengths, span_order):
    chips = n_context // 2
    ring = ring_of_chips(chips)
    place = [ring.index(chip) for chip in range(chips)]
    groups = 2 * n_tensor
    rows_here, width = hidden_rows.shape
    tokens_here = rows_here * n_tensor
    block = width // n_context
    context = lax.axis_index("context")
    tensor = lax.axis_index("tensor")
    ahead = [
        (ring[i] * 2 + k, ring[(i + 1) % chips] * 2 + k) for i in range(chips) for k in range(2)
    ]
    back = [(b, a) for a, b in ahead]
    sibling = [(c, c ^ 1) for c in range(n_context)]

    same_core = [[2 * chip + k for chip in range(chips)] for k in range(2)]
    token = [doc_lengths]

    def ordered(values):
        held = lax.optimization_barrier((*values, token[0]))
        token[0] = held[-1]
        return list(held[:-1])

    class Ring:
        def __init__(self, mine):
            self.up, self.down = [mine], [mine]
            self.middle = []

        def step(self, earlier=()):
            up, down, *earlier = ordered((self.up[-1], self.down[-1], *earlier))
            if len(self.up) <= (chips - 1) // 2:
                self.up.append(lax.ppermute(up, "context", ahead))
                self.down.append(lax.ppermute(down, "context", back))
            elif chips % 2 == 0 and not self.middle:
                half = up.shape[0] // 2
                self.middle = [
                    lax.ppermute(up[:half], "context", ahead),
                    lax.ppermute(down[half:], "context", back),
                ]
            return earlier

        def done(self):
            return len(self.up) > (chips - 1) // 2 and (chips % 2 == 1 or bool(self.middle))

        def finish(self):
            while not self.done():
                self.step()
            return self.down + self.middle + self.up[:0:-1]

    def member(e, d):
        return [
            (c * n_tensor + t, (c ^ e) * n_tensor + (t - d) % n_tensor)
            for c in range(n_context)
            for t in range(n_tensor)
        ]

    keys_ring = Ring(w_qkv[:, HEAD_COLS:])
    keys_ring.step()

    normed_shape = jax.ShapeDtypeStruct((chips, rows_here, block), jnp.bfloat16)
    normed_own, normed_other = pl.pallas_call(
        functools.partial(norm_kernel, place, chips),
        out_shape=[normed_shape] * 2,
        in_specs=vmem_specs(2),
        out_specs=vmem_specs(2),
        compiler_params=compute_params(),
        name="norm",
    )(hidden_rows, norm_gain[None, :])
    normed_own, normed_other = ordered((normed_own, normed_other))
    normed = []
    for e in range(2):
        for d in range(n_tensor):
            rows = normed_own if e == 0 else normed_other
            if e or d:
                rows = lax.ppermute(rows, ("context", "tensor"), member(e, d))
            normed.append(rows)

    query_ring = Ring(w_qkv[:, :HEAD_COLS])
    query_ring.step()
    keys_ring.step()
    query_ring.step()
    normed = keys_ring.step(normed)
    query_ring.step()
    while not keys_ring.done():
        keys_ring.step()

    def project(blocks, outs, name):
        columns = blocks[0].shape[1]
        return pl.pallas_call(
            functools.partial(project_kernel, chips, groups, outs),
            out_shape=[jax.ShapeDtypeStruct((2 * tokens_here // outs, columns), jnp.float32)]
            * outs,
            in_specs=vmem_specs(groups + len(blocks)),
            out_specs=vmem_specs(outs),
            compiler_params=compute_params(),
            name=name,
        )(*ordered((*normed, *blocks)))

    doc_ends = jnp.cumsum(doc_lengths)
    inside = (
        (tensor + jnp.arange(n_tensor, dtype=jnp.int32)) % n_tensor * rows_here
    )[:, None] + jnp.arange(rows_here, dtype=jnp.int32)[None, :]
    inside = inside.reshape(-1)
    both = jnp.concatenate([context * tokens_here + inside, (context ^ 1) * tokens_here + inside])
    query_orig, query_start = locate(both, span_order, doc_ends)
    half = HD // 2
    freq = rope_theta ** (-(jnp.arange(half, dtype=jnp.float32) * 2.0 / HD))
    angle = (query_orig - query_start).astype(jnp.float32)[:, None] * freq[None, :]
    cosine, sine = jnp.cos(angle), jnp.sin(angle)
    cosine = jnp.concatenate([cosine, cosine], axis=1)
    sine = jnp.concatenate([-sine, sine], axis=1)
    owner = 2 * jnp.arange(chips, dtype=jnp.int32) + context % 2
    key_rows = (owner[:, None] * tokens_here + inside[None, :]).reshape(-1).astype(jnp.int32)
    key_orig, _ = locate(key_rows, span_order, doc_ends)

    mine, theirs = project(keys_ring.finish(), 2, "project_keys")
    theirs = lax.ppermute(theirs, "context", sibling)
    query_ring.step()
    out_ring = Ring(w_out)
    out_ring.step()
    mine, theirs = ordered((mine, theirs))
    kv = pl.pallas_call(
        functools.partial(keys_kernel, chips),
        out_shape=jax.ShapeDtypeStruct((chips * tokens_here, 2 * HD), jnp.bfloat16),
        in_specs=vmem_specs(4),
        out_specs=vmem_specs(1)[0],
        compiler_params=compute_params(),
        name="keys",
    )(mine, theirs, cosine, sine)
    (kv,) = ordered((kv,))
    kv = lax.all_to_all(
        kv, "context", split_axis=0, concat_axis=0, axis_index_groups=same_core, tiled=True
    )
    (mine,) = project(query_ring.finish(), 1, "project_queries")
    theirs = lax.ppermute(mine, "context", sibling)
    out_ring.step()

    mixed = pl.pallas_call(
        attend_kernel,
        out_shape=jax.ShapeDtypeStruct((2 * tokens_here, HEAD_COLS + HD), jnp.float32),
        in_specs=vmem_specs(8),
        out_specs=vmem_specs(1)[0],
        compiler_params=compute_params(),
        name="attend",
    )(
        mine,
        theirs,
        cosine,
        sine,
        query_start[:, None],
        query_orig[:, None],
        key_orig[None, :],
        kv,
    )
    (mixed,) = ordered((mixed,))
    mixed_theirs = lax.ppermute(mixed, "context", sibling)
    out_blocks = out_ring.finish()

    out_block = w_out.shape[1]
    parts = pl.pallas_call(
        functools.partial(output_kernel, chips, groups),
        out_shape=[jax.ShapeDtypeStruct((chips, rows_here, out_block), jnp.bfloat16)] * groups,
        in_specs=vmem_specs(2 + len(out_blocks)),
        out_specs=vmem_specs(groups),
        compiler_params=compute_params(),
        name="output",
    )(mixed, mixed_theirs, *out_blocks)
    arrived = []
    for e in range(2):
        for d in range(n_tensor):
            part = parts[e * n_tensor + d]
            if e or d:
                part = lax.ppermute(part, ("context", "tensor"), member(e, -d))
            arrived.append(part)
    return pl.pallas_call(
        functools.partial(sum_kernel, place, chips, groups),
        out_shape=jax.ShapeDtypeStruct((rows_here, n_context * out_block), jnp.bfloat16),
        in_specs=[pl.BlockSpec(memory_space=pl.ANY)] + vmem_specs(groups),
        out_specs=vmem_specs(1)[0],
        compiler_params=compute_params(),
        name="sum",
    )(token[0], *arrived)


def solution(mesh):
    placed = (
        P(("context", "tensor"), None),
        P(),
        P("context", "tensor"),
        P("tensor", "context"),
        P(),
        P(),
    )
    return jax.shard_map(
        functools.partial(per_device, mesh.shape["context"], mesh.shape["tensor"]),
        mesh=mesh,
        in_specs=placed,
        out_specs=P(("context", "tensor"), None),
        check_vma=False,
    )
```

```python
import functools

import jax
import jax.numpy as jnp
from jax import lax
from jax.experimental import pallas as pl
from jax.experimental.pallas import tpu as pltpu
from jax.sharding import PartitionSpec as P

HD = 128
QH_DEV = 4
SPAN = 64
HEAD_COLS = QH_DEV * HD
VMEM_LIMIT = 24 * 1024 * 1024

rope_theta = 500000.0


def ring_of_chips(count):
    wide = 1
    while (wide * 2) * (wide * 2) <= count:
        wide *= 2
    tall = count // wide
    if wide < 2:
        return list(range(count))
    ring = [(z, 0) for z in range(tall)]
    for z in range(tall - 1, -1, -1):
        row = list(range(1, wide))
        ring += [(z, y) for y in (row if (tall - 1 - z) % 2 == 0 else row[::-1])]
    if (tall - 1) % 2 == 0 or wide == 2:
        return [z * wide + y for z, y in ring]
    return [z * wide + y for z, y in ring]


def locate(layout_rows, span_order, doc_ends):
    span_index = layout_rows // SPAN
    matches = span_index[:, None] == jnp.arange(span_order.shape[0], dtype=jnp.int32)[None, :]
    source_span = jnp.sum(jnp.where(matches, span_order[None, :], 0), axis=1)
    initial = source_span * SPAN + layout_rows % SPAN
    doc_start = jnp.max(
        jnp.where(doc_ends[None, :] <= initial[:, None], doc_ends[None, :], 0), axis=1
    )
    return (initial, doc_start)


def vmem_specs(count):
    return [pl.BlockSpec(memory_space=pltpu.VMEM)] * count


def compute_params():
    return pltpu.CompilerParams(vmem_limit_bytes=VMEM_LIMIT)


def place_of(place):
    context = lax.axis_index("context")
    at = jnp.int32(0)
    for chip, spot in enumerate(place):
        at = jnp.where(context // 2 == chip, jnp.int32(spot), at)
    return at, context % 2


def norm_kernel(place, chips, hidden_ref, gain_ref, own_ref, other_ref):
    at, core = place_of(place)
    wide = hidden_ref[...].astype(jnp.float32)
    meansq = jnp.mean(wide * wide, axis=-1, keepdims=True)
    normed = (wide * lax.rsqrt(meansq + 1e-05) * gain_ref[...].astype(jnp.float32)).astype(
        jnp.bfloat16
    )
    block = own_ref.shape[2]
    for even in range(2):

        @pl.when(core == even)
        def _():
            for chip in range(chips):
                slot = lax.rem(place[chip] + chips - at, chips)
                for side in range(2):
                    column = (2 * chip + side) * block
                    ref = own_ref if side == even else other_ref
                    ref[slot] = normed[:, column : column + block]


def take_ring(refs, chips):
    refs = list(refs)
    if chips % 2:
        return [(ref,) for ref in refs]
    half = chips // 2
    return [(r,) for r in refs[:half]] + [tuple(refs[half : half + 2])] + [
        (r,) for r in refs[half + 2 :]
    ]


def project_kernel(chips, groups, *refs):
    rows_refs, refs = refs[:groups], refs[groups:]
    weight_refs, (mine_ref, theirs_ref, queries_ref) = refs[:-3], refs[-3:]
    weights = take_ring(weight_refs, chips)
    total = None
    for slot in range(chips):
        rows = jnp.concatenate([ref[slot] for ref in rows_refs], axis=0)
        start = 0
        for ref in weights[slot]:
            depth = ref.shape[0]
            part = jnp.dot(
                rows[:, start : start + depth], ref[...], preferred_element_type=jnp.float32
            )
            total = part if total is None else total + part
            start += depth
    half = mine_ref.shape[0]
    mine_ref[...] = total[:half, HEAD_COLS:]
    theirs_ref[...] = total[half:, HEAD_COLS:]
    queries_ref[...] = total[:, :HEAD_COLS]


def turn(values, cosine, sine):
    return values * cosine + pltpu.roll(values, HD // 2, 1) * sine


def keys_kernel(chips, mine_ref, theirs_ref, cosine_ref, sine_ref, out_ref):
    rows = out_ref.shape[0] // chips
    cosine, sine = cosine_ref[:rows, :], sine_ref[:rows, :]
    total = mine_ref[...] + theirs_ref[...]
    keys = turn(total[:, :HD], cosine, sine).astype(jnp.bfloat16)
    values = total[:, HD:].astype(jnp.bfloat16)
    for chip in range(chips):
        out_ref[chip * rows : (chip + 1) * rows, :HD] = keys
        out_ref[chip * rows : (chip + 1) * rows, HD:] = values


def attend_kernel(
    mine_ref, theirs_ref, cosine_ref, sine_ref, low_ref, high_ref, orig_ref, kv_ref, out_ref
):
    keys = kv_ref[:, :HD]
    values = kv_ref[:, HD:]
    orig = orig_ref[...]
    allowed = (orig >= low_ref[...]) & (orig <= high_ref[...])
    scale = 1.0 / HD**0.5
    rows = out_ref.shape[0]
    half = rows // 2
    lane = lax.broadcasted_iota(jnp.int32, (rows, HD), 1)
    stats = jnp.zeros((rows, HD), jnp.float32)
    for head in range(QH_DEV):
        columns = slice(head * HD, (head + 1) * HD)
        query = jnp.concatenate(
            [
                mine_ref[:half, columns] + theirs_ref[half:, columns],
                mine_ref[half:, columns] + theirs_ref[:half, columns],
            ],
            axis=0,
        )
        query = turn(query, cosine_ref[...], sine_ref[...]).astype(jnp.bfloat16)
        scores = lax.dot_general(
            query, keys, (((1,), (1,)), ((), ())), preferred_element_type=jnp.float32
        )
        scores = jnp.where(allowed, scores * scale, -1e30)
        top = jnp.max(scores, axis=-1, keepdims=True)
        expo = jnp.where(allowed, jnp.exp(scores - top), 0.0)
        total = jnp.sum(expo, axis=-1, keepdims=True)
        out_ref[:, columns] = jnp.dot(
            expo.astype(jnp.bfloat16), values, preferred_element_type=jnp.float32
        )
        stats = jnp.where(lane == 2 * head, total, stats)
        stats = jnp.where(lane == 2 * head + 1, top, stats)
    out_ref[:, HEAD_COLS:] = stats


def output_kernel(chips, groups, mine_ref, theirs_ref, *refs):
    weight_refs, out_refs = refs[:-groups], refs[-groups:]
    weights = take_ring(weight_refs, chips)
    chip_rows = mine_ref.shape[0]
    half = chip_rows // 2

    def swapped(columns):
        return jnp.concatenate([theirs_ref[half:, columns], theirs_ref[:half, columns]], axis=0)

    pieces = []
    for head in range(QH_DEV):
        columns = slice(head * HD, (head + 1) * HD)
        at = HEAD_COLS + 2 * head
        total, top = mine_ref[:, at : at + 1], mine_ref[:, at + 1 : at + 2]
        other_total, other_top = swapped(slice(at, at + 1)), swapped(slice(at + 1, at + 2))
        peak = jnp.maximum(top, other_top)
        factor, other_factor = jnp.exp(top - peak), jnp.exp(other_top - peak)
        product = mine_ref[:, columns] * factor + swapped(columns) * other_factor
        pieces.append(
            (product / (total * factor + other_total * other_factor)).astype(jnp.bfloat16)
        )
    mixed = jnp.concatenate(pieces, axis=1)
    rows = chip_rows // groups
    for slot in range(chips):
        start, total = 0, None
        for ref in weights[slot]:
            depth = ref.shape[0]
            part = jnp.dot(
                mixed[:, start : start + depth], ref[...], preferred_element_type=jnp.float32
            )
            total = part if total is None else total + part
            start += depth
        total = total.astype(jnp.bfloat16)
        for group in range(groups):
            out_refs[group][slot] = total[group * rows : (group + 1) * rows]


def sum_kernel(place, chips, groups, token_ref, *refs):
    part_refs, out_ref = refs[:groups], refs[groups]
    at, core = place_of(place)
    block = part_refs[0].shape[2]
    half = groups // 2

    def added(part, slot):
        total = part_refs[part * half][slot].astype(jnp.float32)
        for ref in part_refs[part * half + 1 : (part + 1) * half]:
            total += ref[slot].astype(jnp.float32)
        return total.astype(jnp.bfloat16)

    for even in range(2):

        @pl.when(core == even)
        def _():
            for chip in range(chips):
                slot = lax.rem(place[chip] + chips - at, chips)
                for side in range(2):
                    column = (2 * chip + side) * block
                    out_ref[:, column : column + block] = added(side ^ even, slot)


def per_device(n_context, n_tensor, hidden_rows, norm_gain, w_qkv, w_out, doc_lengths, span_order):
    chips = n_context // 2
    ring = ring_of_chips(chips)
    place = [ring.index(chip) for chip in range(chips)]
    groups = 2 * n_tensor
    rows_here, width = hidden_rows.shape
    tokens_here = rows_here * n_tensor
    block = width // n_context
    context = lax.axis_index("context")
    tensor = lax.axis_index("tensor")
    ahead = [
        (ring[i] * 2 + k, ring[(i + 1) % chips] * 2 + k) for i in range(chips) for k in range(2)
    ]
    back = [(b, a) for a, b in ahead]
    sibling = [(c, c ^ 1) for c in range(n_context)]

    same_core = [[2 * chip + k for chip in range(chips)] for k in range(2)]
    token = [doc_lengths]

    def ordered(values):
        held = lax.optimization_barrier((*values, token[0]))
        token[0] = held[-1]
        return list(held[:-1])

    class Ring:
        def __init__(self, mine):
            self.up, self.down = [mine], [mine]
            self.middle = []

        def step(self, earlier=()):
            up, down, *earlier = ordered((self.up[-1], self.down[-1], *earlier))
            if len(self.up) <= (chips - 1) // 2:
                self.up.append(lax.ppermute(up, "context", ahead))
                self.down.append(lax.ppermute(down, "context", back))
            elif chips % 2 == 0 and not self.middle:
                half = up.shape[0] // 2
                self.middle = [
                    lax.ppermute(up[:half], "context", ahead),
                    lax.ppermute(down[half:], "context", back),
                ]
            return earlier

        def done(self):
            return len(self.up) > (chips - 1) // 2 and (chips % 2 == 1 or bool(self.middle))

        def finish(self):
            while not self.done():
                self.step()
            return self.down + self.middle + self.up[:0:-1]

    def member(e, d):
        return [
            (c * n_tensor + t, (c ^ e) * n_tensor + (t - d) % n_tensor)
            for c in range(n_context)
            for t in range(n_tensor)
        ]

    qkv_ring = Ring(w_qkv)
    qkv_ring.step()

    normed_shape = jax.ShapeDtypeStruct((chips, rows_here, block), jnp.bfloat16)
    normed_own, normed_other = pl.pallas_call(
        functools.partial(norm_kernel, place, chips),
        out_shape=[normed_shape] * 2,
        in_specs=vmem_specs(2),
        out_specs=vmem_specs(2),
        compiler_params=compute_params(),
        name="norm",
    )(hidden_rows, norm_gain[None, :])
    normed_own, normed_other = ordered((normed_own, normed_other))
    normed = []
    for e in range(2):
        for d in range(n_tensor):
            rows = normed_own if e == 0 else normed_other
            if e or d:
                rows = lax.ppermute(rows, ("context", "tensor"), member(e, d))
            normed.append(rows)

    out_ring = Ring(w_out)
    out_ring.step()
    qkv_ring.step()
    out_ring.step()
    normed = qkv_ring.step(normed)
    out_ring.step()
    while not qkv_ring.done():
        qkv_ring.step()
    mine, theirs, queries = pl.pallas_call(
        functools.partial(project_kernel, chips, groups),
        out_shape=[
            jax.ShapeDtypeStruct((tokens_here, 2 * HD), jnp.float32),
            jax.ShapeDtypeStruct((tokens_here, 2 * HD), jnp.float32),
            jax.ShapeDtypeStruct((2 * tokens_here, HEAD_COLS), jnp.float32),
        ],
        in_specs=vmem_specs(groups + len(qkv_ring.finish())),
        out_specs=vmem_specs(3),
        compiler_params=compute_params(),
        name="project",
    )(*ordered((*normed, *qkv_ring.finish())))
    theirs = lax.ppermute(theirs, "context", sibling)

    doc_ends = jnp.cumsum(doc_lengths)
    inside = (
        (tensor + jnp.arange(n_tensor, dtype=jnp.int32)) % n_tensor * rows_here
    )[:, None] + jnp.arange(rows_here, dtype=jnp.int32)[None, :]
    inside = inside.reshape(-1)
    both = jnp.concatenate([context * tokens_here + inside, (context ^ 1) * tokens_here + inside])
    query_orig, query_start = locate(both, span_order, doc_ends)
    half = HD // 2
    freq = rope_theta ** (-(jnp.arange(half, dtype=jnp.float32) * 2.0 / HD))
    angle = (query_orig - query_start).astype(jnp.float32)[:, None] * freq[None, :]
    cosine, sine = jnp.cos(angle), jnp.sin(angle)
    cosine = jnp.concatenate([cosine, cosine], axis=1)
    sine = jnp.concatenate([-sine, sine], axis=1)
    owner = 2 * jnp.arange(chips, dtype=jnp.int32) + context % 2
    key_rows = (owner[:, None] * tokens_here + inside[None, :]).reshape(-1).astype(jnp.int32)
    key_orig, _ = locate(key_rows, span_order, doc_ends)

    mine, theirs = ordered((mine, theirs))
    kv = pl.pallas_call(
        functools.partial(keys_kernel, chips),
        out_shape=jax.ShapeDtypeStruct((chips * tokens_here, 2 * HD), jnp.bfloat16),
        in_specs=vmem_specs(4),
        out_specs=vmem_specs(1)[0],
        compiler_params=compute_params(),
        name="keys",
    )(mine, theirs, cosine, sine)
    (kv,) = ordered((kv,))
    kv = lax.all_to_all(
        kv, "context", split_axis=0, concat_axis=0, axis_index_groups=same_core, tiled=True
    )
    queries_theirs = lax.ppermute(queries, "context", sibling)
    while not out_ring.done():
        out_ring.step()

    mixed = pl.pallas_call(
        attend_kernel,
        out_shape=jax.ShapeDtypeStruct((2 * tokens_here, HEAD_COLS + HD), jnp.float32),
        in_specs=vmem_specs(8),
        out_specs=vmem_specs(1)[0],
        compiler_params=compute_params(),
        name="attend",
    )(
        queries,
        queries_theirs,
        cosine,
        sine,
        query_start[:, None],
        query_orig[:, None],
        key_orig[None, :],
        kv,
    )
    (mixed,) = ordered((mixed,))
    mixed_theirs = lax.ppermute(mixed, "context", sibling)
    out_blocks = out_ring.finish()

    out_block = w_out.shape[1]
    parts = pl.pallas_call(
        functools.partial(output_kernel, chips, groups),
        out_shape=[jax.ShapeDtypeStruct((chips, rows_here, out_block), jnp.bfloat16)] * groups,
        in_specs=vmem_specs(2 + len(out_blocks)),
        out_specs=vmem_specs(groups),
        compiler_params=compute_params(),
        name="output",
    )(mixed, mixed_theirs, *out_blocks)
    arrived = []
    for e in range(2):
        for d in range(n_tensor):
            part = parts[e * n_tensor + d]
            if e or d:
                part = lax.ppermute(part, ("context", "tensor"), member(e, -d))
            arrived.append(part)
    return pl.pallas_call(
        functools.partial(sum_kernel, place, chips, groups),
        out_shape=jax.ShapeDtypeStruct((rows_here, n_context * out_block), jnp.bfloat16),
        in_specs=[pl.BlockSpec(memory_space=pl.ANY)] + vmem_specs(groups),
        out_specs=vmem_specs(1)[0],
        compiler_params=compute_params(),
        name="sum",
    )(token[0], *arrived)


def solution(mesh):
    placed = (
        P(("context", "tensor"), None),
        P(),
        P("context", "tensor"),
        P("tensor", "context"),
        P(),
        P(),
    )
    return jax.shard_map(
        functools.partial(per_device, mesh.shape["context"], mesh.shape["tensor"]),
        mesh=mesh,
        in_specs=placed,
        out_specs=P(("context", "tensor"), None),
        check_vma=False,
    )
```

```python
import functools

import jax
import jax.numpy as jnp
from jax import lax
from jax.experimental import pallas as pl
from jax.experimental.pallas import tpu as pltpu
from jax.sharding import PartitionSpec as P

HD = 128
QH_DEV = 4
SPAN = 64
HEAD_COLS = QH_DEV * HD
VMEM_LIMIT = 24 * 1024 * 1024

rope_theta = 500000.0


def ring_of_chips(count):
    wide = 1
    while (wide * 2) * (wide * 2) <= count:
        wide *= 2
    tall = count // wide
    if wide < 2:
        return list(range(count))
    ring = [(z, 0) for z in range(tall)]
    for z in range(tall - 1, -1, -1):
        row = list(range(1, wide))
        ring += [(z, y) for y in (row if (tall - 1 - z) % 2 == 0 else row[::-1])]
    if (tall - 1) % 2 == 0 or wide == 2:
        return [z * wide + y for z, y in ring]
    return [z * wide + y for z, y in ring]


def locate(layout_rows, span_order, doc_ends):
    span_index = layout_rows // SPAN
    matches = span_index[:, None] == jnp.arange(span_order.shape[0], dtype=jnp.int32)[None, :]
    source_span = jnp.sum(jnp.where(matches, span_order[None, :], 0), axis=1)
    initial = source_span * SPAN + layout_rows % SPAN
    doc_start = jnp.max(
        jnp.where(doc_ends[None, :] <= initial[:, None], doc_ends[None, :], 0), axis=1
    )
    return (initial, doc_start)


def vmem_specs(count):
    return [pl.BlockSpec(memory_space=pltpu.VMEM)] * count


def compute_params():
    return pltpu.CompilerParams(vmem_limit_bytes=VMEM_LIMIT)


def place_of(place):
    context = lax.axis_index("context")
    at = jnp.int32(0)
    for chip, spot in enumerate(place):
        at = jnp.where(context // 2 == chip, jnp.int32(spot), at)
    return at, context % 2


def norm_kernel(place, chips, hidden_ref, gain_ref, own_ref, other_ref):
    at, core = place_of(place)
    wide = hidden_ref[...].astype(jnp.float32)
    meansq = jnp.mean(wide * wide, axis=-1, keepdims=True)
    normed = (wide * lax.rsqrt(meansq + 1e-05) * gain_ref[...].astype(jnp.float32)).astype(
        jnp.bfloat16
    )
    block = own_ref.shape[2]
    for even in range(2):

        @pl.when(core == even)
        def _():
            for chip in range(chips):
                slot = lax.rem(place[chip] + chips - at, chips)
                for side in range(2):
                    column = (2 * chip + side) * block
                    ref = own_ref if side == even else other_ref
                    ref[slot] = normed[:, column : column + block]


def take_ring(refs, chips):
    refs = list(refs)
    if chips % 2:
        return [(ref,) for ref in refs]
    half = chips // 2
    return [(r,) for r in refs[:half]] + [tuple(refs[half : half + 2])] + [
        (r,) for r in refs[half + 2 :]
    ]


def project_kernel(chips, groups, outs, *refs):
    rows_refs, refs = refs[:groups], refs[groups:]
    weight_refs, out_refs = refs[: -len(outs)], refs[-len(outs) :]
    weights = take_ring(weight_refs, chips)
    total = None
    for slot in range(chips):
        rows = jnp.concatenate([ref[slot] for ref in rows_refs], axis=0)
        start = 0
        for ref in weights[slot]:
            depth = ref.shape[0]
            part = jnp.dot(
                rows[:, start : start + depth], ref[...], preferred_element_type=jnp.float32
            )
            total = part if total is None else total + part
            start += depth
    for ref, (rows, columns) in zip(out_refs, outs):
        ref[...] = total[rows, columns]


def turn(values, cosine, sine):
    return values * cosine + pltpu.roll(values, HD // 2, 1) * sine


def keys_kernel(chips, mine_ref, theirs_ref, cosine_ref, sine_ref, out_ref):
    rows = out_ref.shape[0] // chips
    cosine, sine = cosine_ref[:rows, :], sine_ref[:rows, :]
    total = mine_ref[...] + theirs_ref[...]
    keys = turn(total[:, :HD], cosine, sine).astype(jnp.bfloat16)
    values = total[:, HD:].astype(jnp.bfloat16)
    for chip in range(chips):
        out_ref[chip * rows : (chip + 1) * rows, :HD] = keys
        out_ref[chip * rows : (chip + 1) * rows, HD:] = values


def attend_kernel(
    first_ref,
    first_theirs_ref,
    last_ref,
    last_theirs_ref,
    cosine_ref,
    sine_ref,
    low_ref,
    high_ref,
    orig_ref,
    kv_ref,
    out_ref,
):
    keys = kv_ref[:, :HD]
    values = kv_ref[:, HD:]
    orig = orig_ref[...]
    allowed = (orig >= low_ref[...]) & (orig <= high_ref[...])
    scale = 1.0 / HD**0.5
    rows = out_ref.shape[0]
    half = rows // 2
    lane = lax.broadcasted_iota(jnp.int32, (rows, HD), 1)
    stats = jnp.zeros((rows, HD), jnp.float32)
    for head in range(QH_DEV):
        if head < QH_DEV - 1:
            mine_ref, theirs_ref = first_ref, first_theirs_ref
            columns = slice(head * HD, (head + 1) * HD)
        else:
            mine_ref, theirs_ref = last_ref, last_theirs_ref
            columns = slice(0, HD)
        query = jnp.concatenate(
            [
                mine_ref[:half, columns] + theirs_ref[half:, columns],
                mine_ref[half:, columns] + theirs_ref[:half, columns],
            ],
            axis=0,
        )
        query = turn(query, cosine_ref[...], sine_ref[...]).astype(jnp.bfloat16)
        scores = lax.dot_general(
            query, keys, (((1,), (1,)), ((), ())), preferred_element_type=jnp.float32
        )
        scores = jnp.where(allowed, scores * scale, -1e30)
        top = jnp.max(scores, axis=-1, keepdims=True)
        expo = jnp.where(allowed, jnp.exp(scores - top), 0.0)
        total = jnp.sum(expo, axis=-1, keepdims=True)
        out_ref[:, head * HD : (head + 1) * HD] = jnp.dot(
            expo.astype(jnp.bfloat16), values, preferred_element_type=jnp.float32
        )
        stats = jnp.where(lane == 2 * head, total, stats)
        stats = jnp.where(lane == 2 * head + 1, top, stats)
    out_ref[:, HEAD_COLS:] = stats


def output_kernel(chips, groups, mine_ref, theirs_ref, *refs):
    weight_refs, out_refs = refs[:-groups], refs[-groups:]
    count = len(weight_refs) // 2
    upper = take_ring(weight_refs[:count], chips)
    lower = take_ring(weight_refs[count:], chips)
    weights = [a + b for a, b in zip(upper, lower)]
    chip_rows = mine_ref.shape[0]
    half = chip_rows // 2

    def swapped(columns):
        return jnp.concatenate([theirs_ref[half:, columns], theirs_ref[:half, columns]], axis=0)

    pieces = []
    for head in range(QH_DEV):
        columns = slice(head * HD, (head + 1) * HD)
        at = HEAD_COLS + 2 * head
        total, top = mine_ref[:, at : at + 1], mine_ref[:, at + 1 : at + 2]
        other_total, other_top = swapped(slice(at, at + 1)), swapped(slice(at + 1, at + 2))
        peak = jnp.maximum(top, other_top)
        factor, other_factor = jnp.exp(top - peak), jnp.exp(other_top - peak)
        product = mine_ref[:, columns] * factor + swapped(columns) * other_factor
        pieces.append(
            (product / (total * factor + other_total * other_factor)).astype(jnp.bfloat16)
        )
    mixed = jnp.concatenate(pieces, axis=1)
    rows = chip_rows // groups
    for slot in range(chips):
        start, total = 0, None
        for ref in weights[slot]:
            depth = ref.shape[0]
            part = jnp.dot(
                mixed[:, start : start + depth], ref[...], preferred_element_type=jnp.float32
            )
            total = part if total is None else total + part
            start += depth
        total = total.astype(jnp.bfloat16)
        for group in range(groups):
            out_refs[group][slot] = total[group * rows : (group + 1) * rows]


def sum_kernel(place, chips, groups, token_ref, *refs):
    part_refs, out_ref = refs[:groups], refs[groups]
    at, core = place_of(place)
    block = part_refs[0].shape[2]
    half = groups // 2

    def added(part, slot):
        total = part_refs[part * half][slot].astype(jnp.float32)
        for ref in part_refs[part * half + 1 : (part + 1) * half]:
            total += ref[slot].astype(jnp.float32)
        return total.astype(jnp.bfloat16)

    for even in range(2):

        @pl.when(core == even)
        def _():
            for chip in range(chips):
                slot = lax.rem(place[chip] + chips - at, chips)
                for side in range(2):
                    column = (2 * chip + side) * block
                    out_ref[:, column : column + block] = added(side ^ even, slot)


def per_device(n_context, n_tensor, hidden_rows, norm_gain, w_qkv, w_out, doc_lengths, span_order):
    chips = n_context // 2
    ring = ring_of_chips(chips)
    place = [ring.index(chip) for chip in range(chips)]
    groups = 2 * n_tensor
    rows_here, width = hidden_rows.shape
    tokens_here = rows_here * n_tensor
    block = width // n_context
    context = lax.axis_index("context")
    tensor = lax.axis_index("tensor")
    ahead = [
        (ring[i] * 2 + k, ring[(i + 1) % chips] * 2 + k) for i in range(chips) for k in range(2)
    ]
    back = [(b, a) for a, b in ahead]
    sibling = [(c, c ^ 1) for c in range(n_context)]

    same_core = [[2 * chip + k for chip in range(chips)] for k in range(2)]
    token = [doc_lengths]

    def ordered(values):
        held = lax.optimization_barrier((*values, token[0]))
        token[0] = held[-1]
        return list(held[:-1])

    class Ring:
        def __init__(self, mine):
            self.up, self.down = [mine], [mine]
            self.middle = []

        def step(self, earlier=()):
            up, down, *earlier = ordered((self.up[-1], self.down[-1], *earlier))
            if len(self.up) <= (chips - 1) // 2:
                self.up.append(lax.ppermute(up, "context", ahead))
                self.down.append(lax.ppermute(down, "context", back))
            elif chips % 2 == 0 and not self.middle:
                half = up.shape[0] // 2
                self.middle = [
                    lax.ppermute(up[:half], "context", ahead),
                    lax.ppermute(down[half:], "context", back),
                ]
            return earlier

        def done(self):
            return len(self.up) > (chips - 1) // 2 and (chips % 2 == 1 or bool(self.middle))

        def finish(self):
            while not self.done():
                self.step()
            return self.down + self.middle + self.up[:0:-1]

    def member(e, d):
        return [
            (c * n_tensor + t, (c ^ e) * n_tensor + (t - d) % n_tensor)
            for c in range(n_context)
            for t in range(n_tensor)
        ]

    split = (QH_DEV - 1) * HD

    normed_shape = jax.ShapeDtypeStruct((chips, rows_here, block), jnp.bfloat16)
    normed_own, normed_other = pl.pallas_call(
        functools.partial(norm_kernel, place, chips),
        out_shape=[normed_shape] * 2,
        in_specs=vmem_specs(2),
        out_specs=vmem_specs(2),
        compiler_params=compute_params(),
        name="norm",
    )(hidden_rows, norm_gain[None, :])
    last_ring = Ring(w_qkv[:, split:])
    first_ring = Ring(w_qkv[:, :split])
    normed_own, normed_other, last_ring.up[0] = ordered(
        (normed_own, normed_other, last_ring.up[0])
    )
    last_ring.down[0] = last_ring.up[0]
    last_ring.step()
    first_ring.step()
    normed = []
    for e in range(2):
        for d in range(n_tensor):
            rows = normed_own if e == 0 else normed_other
            if e or d:
                rows = lax.ppermute(rows, ("context", "tensor"), member(e, d))
            normed.append(rows)

    last_ring.step()
    first_ring.step()
    normed = last_ring.step(normed)
    first_ring.step()
    while not last_ring.done():
        last_ring.step()
    while not first_ring.done():
        first_ring.step()
    half = w_out.shape[0] // 2
    upper_ring, lower_ring = Ring(w_out[:half]), Ring(w_out[half:])
    upper_ring.step()
    lower_ring.step()

    def project(blocks, outs, name):
        shapes = [
            jax.ShapeDtypeStruct((rows.stop - rows.start, columns.stop - columns.start), jnp.float32)
            for rows, columns in outs
        ]
        return pl.pallas_call(
            functools.partial(project_kernel, chips, groups, outs),
            out_shape=shapes,
            in_specs=vmem_specs(groups + len(blocks)),
            out_specs=vmem_specs(len(outs)),
            compiler_params=compute_params(),
            name=name,
        )(*ordered((*normed, *blocks)))

    doc_ends = jnp.cumsum(doc_lengths)
    inside = (
        (tensor + jnp.arange(n_tensor, dtype=jnp.int32)) % n_tensor * rows_here
    )[:, None] + jnp.arange(rows_here, dtype=jnp.int32)[None, :]
    inside = inside.reshape(-1)
    both = jnp.concatenate([context * tokens_here + inside, (context ^ 1) * tokens_here + inside])
    query_orig, query_start = locate(both, span_order, doc_ends)
    half = HD // 2
    freq = rope_theta ** (-(jnp.arange(half, dtype=jnp.float32) * 2.0 / HD))
    angle = (query_orig - query_start).astype(jnp.float32)[:, None] * freq[None, :]
    cosine, sine = jnp.cos(angle), jnp.sin(angle)
    cosine = jnp.concatenate([cosine, cosine], axis=1)
    sine = jnp.concatenate([-sine, sine], axis=1)
    owner = 2 * jnp.arange(chips, dtype=jnp.int32) + context % 2
    key_rows = (owner[:, None] * tokens_here + inside[None, :]).reshape(-1).astype(jnp.int32)
    key_orig, _ = locate(key_rows, span_order, doc_ends)

    ours, siblings = slice(0, tokens_here), slice(tokens_here, 2 * tokens_here)
    both_rows, kv_columns = slice(0, 2 * tokens_here), slice(HD, 3 * HD)
    mine, theirs, last = project(
        last_ring.finish(),
        [(ours, kv_columns), (siblings, kv_columns), (both_rows, slice(0, HD))],
        "project_keys",
    )
    theirs = lax.ppermute(theirs, "context", sibling)
    upper_ring.step()
    lower_ring.step()
    mine, theirs = ordered((mine, theirs))
    kv = pl.pallas_call(
        functools.partial(keys_kernel, chips),
        out_shape=jax.ShapeDtypeStruct((chips * tokens_here, 2 * HD), jnp.bfloat16),
        in_specs=vmem_specs(4),
        out_specs=vmem_specs(1)[0],
        compiler_params=compute_params(),
        name="keys",
    )(mine, theirs, cosine, sine)
    (kv,) = ordered((kv,))
    kv = lax.all_to_all(
        kv, "context", split_axis=0, concat_axis=0, axis_index_groups=same_core, tiled=True
    )
    (first,) = project(first_ring.finish(), [(both_rows, slice(0, split))], "project_queries")
    first_theirs = lax.ppermute(first, "context", sibling)
    last_theirs = lax.ppermute(last, "context", sibling)
    while not lower_ring.done():
        upper_ring.step()
        lower_ring.step()
    (kv,) = ordered((kv,))

    mixed = pl.pallas_call(
        attend_kernel,
        out_shape=jax.ShapeDtypeStruct((2 * tokens_here, HEAD_COLS + HD), jnp.float32),
        in_specs=vmem_specs(10),
        out_specs=vmem_specs(1)[0],
        compiler_params=compute_params(),
        name="attend",
    )(
        first,
        first_theirs,
        last,
        last_theirs,
        cosine,
        sine,
        query_start[:, None],
        query_orig[:, None],
        key_orig[None, :],
        kv,
    )
    (mixed,) = ordered((mixed,))
    mixed_theirs = lax.ppermute(mixed, "context", sibling)
    out_blocks = upper_ring.finish() + lower_ring.finish()

    out_block = w_out.shape[1]
    parts = pl.pallas_call(
        functools.partial(output_kernel, chips, groups),
        out_shape=[jax.ShapeDtypeStruct((chips, rows_here, out_block), jnp.bfloat16)] * groups,
        in_specs=vmem_specs(2 + len(out_blocks)),
        out_specs=vmem_specs(groups),
        compiler_params=compute_params(),
        name="output",
    )(mixed, mixed_theirs, *out_blocks)
    arrived = []
    for e in range(2):
        for d in range(n_tensor):
            part = parts[e * n_tensor + d]
            if e or d:
                part = lax.ppermute(part, ("context", "tensor"), member(e, -d))
            arrived.append(part)
    return pl.pallas_call(
        functools.partial(sum_kernel, place, chips, groups),
        out_shape=jax.ShapeDtypeStruct((rows_here, n_context * out_block), jnp.bfloat16),
        in_specs=[pl.BlockSpec(memory_space=pl.ANY)] + vmem_specs(groups),
        out_specs=vmem_specs(1)[0],
        compiler_params=compute_params(),
        name="sum",
    )(token[0], *arrived)


def solution(mesh):
    placed = (
        P(("context", "tensor"), None),
        P(),
        P("context", "tensor"),
        P("tensor", "context"),
        P(),
        P(),
    )
    return jax.shard_map(
        functools.partial(per_device, mesh.shape["context"], mesh.shape["tensor"]),
        mesh=mesh,
        in_specs=placed,
        out_specs=P(("context", "tensor"), None),
        check_vma=False,
    )
```

```python
import functools

import jax
import jax.numpy as jnp
from jax import lax
from jax.experimental import pallas as pl
from jax.experimental.pallas import tpu as pltpu
from jax.sharding import PartitionSpec as P

HD = 128
QH_DEV = 4
SPAN = 64
HEAD_COLS = QH_DEV * HD
VMEM_LIMIT = 24 * 1024 * 1024

rope_theta = 500000.0


def ring_of_chips(count):
    wide = 1
    while (wide * 2) * (wide * 2) <= count:
        wide *= 2
    tall = count // wide
    if wide < 2:
        return list(range(count))
    ring = [(z, 0) for z in range(tall)]
    for z in range(tall - 1, -1, -1):
        row = list(range(1, wide))
        ring += [(z, y) for y in (row if (tall - 1 - z) % 2 == 0 else row[::-1])]
    if (tall - 1) % 2 == 0 or wide == 2:
        return [z * wide + y for z, y in ring]
    return [z * wide + y for z, y in ring]


def locate(layout_rows, span_order, doc_ends):
    span_index = layout_rows // SPAN
    matches = span_index[:, None] == jnp.arange(span_order.shape[0], dtype=jnp.int32)[None, :]
    source_span = jnp.sum(jnp.where(matches, span_order[None, :], 0), axis=1)
    initial = source_span * SPAN + layout_rows % SPAN
    doc_start = jnp.max(
        jnp.where(doc_ends[None, :] <= initial[:, None], doc_ends[None, :], 0), axis=1
    )
    return (initial, doc_start)


def vmem_specs(count):
    return [pl.BlockSpec(memory_space=pltpu.VMEM)] * count


def compute_params():
    return pltpu.CompilerParams(vmem_limit_bytes=VMEM_LIMIT)


def place_of(place):
    context = lax.axis_index("context")
    at = jnp.int32(0)
    for chip, spot in enumerate(place):
        at = jnp.where(context // 2 == chip, jnp.int32(spot), at)
    return at, context % 2


def norm_kernel(place, chips, hidden_ref, gain_ref, own_ref, other_ref):
    at, core = place_of(place)
    wide = hidden_ref[...].astype(jnp.float32)
    meansq = jnp.mean(wide * wide, axis=-1, keepdims=True)
    scaled = wide * lax.rsqrt(meansq + 1e-05)
    lanes = gain_ref.shape[1]
    normed = jnp.concatenate(
        [
            (
                scaled[:, i * lanes : (i + 1) * lanes]
                * gain_ref[i : i + 1, :].astype(jnp.float32)
            ).astype(jnp.bfloat16)
            for i in range(gain_ref.shape[0])
        ],
        axis=1,
    )
    block = own_ref.shape[2]
    for even in range(2):

        @pl.when(core == even)
        def _():
            for chip in range(chips):
                slot = lax.rem(place[chip] + chips - at, chips)
                for side in range(2):
                    column = (2 * chip + side) * block
                    ref = own_ref if side == even else other_ref
                    ref[slot] = normed[:, column : column + block]


def take_ring(refs, chips):
    refs = list(refs)
    if chips % 2:
        return [(ref,) for ref in refs]
    half = chips // 2
    return [(r,) for r in refs[:half]] + [tuple(refs[half : half + 2])] + [
        (r,) for r in refs[half + 2 :]
    ]


def project_kernel(chips, groups, outs, *refs):
    rows_refs, refs = refs[:groups], refs[groups:]
    weight_refs, out_refs = refs[: -len(outs)], refs[-len(outs) :]
    weights = take_ring(weight_refs, chips)
    total = None
    for slot in range(chips):
        rows = jnp.concatenate([ref[slot] for ref in rows_refs], axis=0)
        start = 0
        for ref in weights[slot]:
            depth = ref.shape[0]
            part = jnp.dot(
                rows[:, start : start + depth], ref[...], preferred_element_type=jnp.float32
            )
            total = part if total is None else total + part
            start += depth
    for ref, (rows, columns) in zip(out_refs, outs):
        ref[...] = total[rows, columns]


def turn(values, cosine, sine):
    return values * cosine + pltpu.roll(values, HD // 2, 1) * sine


def keys_kernel(chips, mine_ref, theirs_ref, cosine_ref, sine_ref, out_ref):
    rows = out_ref.shape[0] // chips
    cosine, sine = cosine_ref[:rows, :], sine_ref[:rows, :]
    total = mine_ref[...] + theirs_ref[...]
    keys = turn(total[:, :HD], cosine, sine).astype(jnp.bfloat16)
    values = total[:, HD:].astype(jnp.bfloat16)
    for chip in range(chips):
        out_ref[chip * rows : (chip + 1) * rows, :HD] = keys
        out_ref[chip * rows : (chip + 1) * rows, HD:] = values


def attend_kernel(
    first_ref,
    first_theirs_ref,
    last_ref,
    last_theirs_ref,
    cosine_ref,
    sine_ref,
    low_ref,
    high_ref,
    orig_ref,
    kv_ref,
    out_ref,
):
    keys = kv_ref[:, :HD]
    values = kv_ref[:, HD:]
    orig = orig_ref[...]
    allowed = (orig >= low_ref[...]) & (orig <= high_ref[...])
    scale = 1.0 / HD**0.5
    rows = out_ref.shape[0]
    half = rows // 2
    lane = lax.broadcasted_iota(jnp.int32, (rows, HD), 1)
    stats = jnp.zeros((rows, HD), jnp.float32)
    for head in range(QH_DEV):
        if head < QH_DEV - 1:
            mine_ref, theirs_ref = first_ref, first_theirs_ref
            columns = slice(head * HD, (head + 1) * HD)
        else:
            mine_ref, theirs_ref = last_ref, last_theirs_ref
            columns = slice(0, HD)
        query = jnp.concatenate(
            [
                mine_ref[:half, columns] + theirs_ref[half:, columns],
                mine_ref[half:, columns] + theirs_ref[:half, columns],
            ],
            axis=0,
        )
        query = turn(query, cosine_ref[...], sine_ref[...]).astype(jnp.bfloat16)
        scores = lax.dot_general(
            query, keys, (((1,), (1,)), ((), ())), preferred_element_type=jnp.float32
        )
        scores = jnp.where(allowed, scores * scale, -1e30)
        top = jnp.max(scores, axis=-1, keepdims=True)
        expo = jnp.where(allowed, jnp.exp(scores - top), 0.0)
        total = jnp.sum(expo, axis=-1, keepdims=True)
        out_ref[:, head * HD : (head + 1) * HD] = jnp.dot(
            expo.astype(jnp.bfloat16), values, preferred_element_type=jnp.float32
        )
        stats = jnp.where(lane == 2 * head, total, stats)
        stats = jnp.where(lane == 2 * head + 1, top, stats)
    out_ref[:, HEAD_COLS:] = stats


def output_kernel(chips, groups, mine_ref, theirs_ref, *refs):
    weight_refs, out_refs = refs[:-groups], refs[-groups:]
    weights = take_ring(weight_refs, chips)
    chip_rows = mine_ref.shape[0]
    half = chip_rows // 2

    def swapped(columns):
        return jnp.concatenate([theirs_ref[half:, columns], theirs_ref[:half, columns]], axis=0)

    pieces = []
    for head in range(QH_DEV):
        columns = slice(head * HD, (head + 1) * HD)
        at = HEAD_COLS + 2 * head
        total, top = mine_ref[:, at : at + 1], mine_ref[:, at + 1 : at + 2]
        other_total, other_top = swapped(slice(at, at + 1)), swapped(slice(at + 1, at + 2))
        peak = jnp.maximum(top, other_top)
        factor, other_factor = jnp.exp(top - peak), jnp.exp(other_top - peak)
        product = mine_ref[:, columns] * factor + swapped(columns) * other_factor
        pieces.append(
            (product / (total * factor + other_total * other_factor)).astype(jnp.bfloat16)
        )
    mixed = jnp.concatenate(pieces, axis=1)
    rows = chip_rows // groups
    for slot in range(chips):
        start, total = 0, None
        for ref in weights[slot]:
            depth = ref.shape[0]
            part = jnp.dot(
                mixed[:, start : start + depth], ref[...], preferred_element_type=jnp.float32
            )
            total = part if total is None else total + part
            start += depth
        total = total.astype(jnp.bfloat16)
        for group in range(groups):
            out_refs[group][slot] = total[group * rows : (group + 1) * rows]


def sum_kernel(place, chips, groups, token_ref, *refs):
    part_refs, out_ref = refs[:groups], refs[groups]
    at, core = place_of(place)
    block = part_refs[0].shape[2]
    half = groups // 2

    def added(part, slot):
        total = part_refs[part * half][slot].astype(jnp.float32)
        for ref in part_refs[part * half + 1 : (part + 1) * half]:
            total += ref[slot].astype(jnp.float32)
        return total.astype(jnp.bfloat16)

    for even in range(2):

        @pl.when(core == even)
        def _():
            for chip in range(chips):
                slot = lax.rem(place[chip] + chips - at, chips)
                for side in range(2):
                    column = (2 * chip + side) * block
                    out_ref[:, column : column + block] = added(side ^ even, slot)


def per_device(n_context, n_tensor, hidden_rows, norm_gain, w_qkv, w_out, doc_lengths, span_order):
    chips = n_context // 2
    ring = ring_of_chips(chips)
    place = [ring.index(chip) for chip in range(chips)]
    groups = 2 * n_tensor
    rows_here, width = hidden_rows.shape
    tokens_here = rows_here * n_tensor
    block = width // n_context
    context = lax.axis_index("context")
    tensor = lax.axis_index("tensor")
    ahead = [
        (ring[i] * 2 + k, ring[(i + 1) % chips] * 2 + k) for i in range(chips) for k in range(2)
    ]
    back = [(b, a) for a, b in ahead]
    sibling = [(c, c ^ 1) for c in range(n_context)]

    same_core = [[2 * chip + k for chip in range(chips)] for k in range(2)]
    token = [doc_lengths]

    def ordered(values):
        held = lax.optimization_barrier((*values, token[0]))
        token[0] = held[-1]
        return list(held[:-1])

    class Ring:
        def __init__(self, mine):
            self.up, self.down = [mine], [mine]
            self.middle = []

        def step(self, earlier=()):
            up, down, *earlier = ordered((self.up[-1], self.down[-1], *earlier))
            if len(self.up) <= (chips - 1) // 2:
                self.up.append(lax.ppermute(up, "context", ahead))
                self.down.append(lax.ppermute(down, "context", back))
            elif chips % 2 == 0 and not self.middle:
                half = up.shape[0] // 2
                self.middle = [
                    lax.ppermute(up[:half], "context", ahead),
                    lax.ppermute(down[half:], "context", back),
                ]
            return earlier

        def done(self):
            return len(self.up) > (chips - 1) // 2 and (chips % 2 == 1 or bool(self.middle))

        def finish(self):
            while not self.done():
                self.step()
            return self.down + self.middle + self.up[:0:-1]

    def member(e, d):
        return [
            (c * n_tensor + t, (c ^ e) * n_tensor + (t - d) % n_tensor)
            for c in range(n_context)
            for t in range(n_tensor)
        ]

    split = (QH_DEV - 1) * HD

    normed_shape = jax.ShapeDtypeStruct((chips, rows_here, block), jnp.bfloat16)
    normed_own, normed_other = pl.pallas_call(
        functools.partial(norm_kernel, place, chips),
        out_shape=[normed_shape] * 2,
        in_specs=vmem_specs(2),
        out_specs=vmem_specs(2),
        compiler_params=compute_params(),
        name="norm",
    )(hidden_rows, norm_gain.reshape(-1, HD))
    last_ring = Ring(w_qkv[:, split:])
    first_ring = Ring(w_qkv[:, :split])
    normed_own, normed_other, last_ring.up[0] = ordered(
        (normed_own, normed_other, last_ring.up[0])
    )
    last_ring.down[0] = last_ring.up[0]
    last_ring.step()
    first_ring.step()
    normed = []
    for e in range(2):
        for d in range(n_tensor):
            rows = normed_own if e == 0 else normed_other
            if e or d:
                rows = lax.ppermute(rows, ("context", "tensor"), member(e, d))
            normed.append(rows)

    last_ring.step()
    normed = first_ring.step(normed)
    while not last_ring.done():
        last_ring.step()
        first_ring.step()
    out_ring = Ring(w_out)
    out_ring.step()

    def project(blocks, outs, name):
        shapes = [
            jax.ShapeDtypeStruct((rows.stop - rows.start, columns.stop - columns.start), jnp.float32)
            for rows, columns in outs
        ]
        return pl.pallas_call(
            functools.partial(project_kernel, chips, groups, outs),
            out_shape=shapes,
            in_specs=vmem_specs(groups + len(blocks)),
            out_specs=vmem_specs(len(outs)),
            compiler_params=compute_params(),
            name=name,
        )(*ordered((*normed, *blocks)))

    doc_ends = jnp.cumsum(doc_lengths)
    inside = (
        (tensor + jnp.arange(n_tensor, dtype=jnp.int32)) % n_tensor * rows_here
    )[:, None] + jnp.arange(rows_here, dtype=jnp.int32)[None, :]
    inside = inside.reshape(-1)
    both = jnp.concatenate([context * tokens_here + inside, (context ^ 1) * tokens_here + inside])
    query_orig, query_start = locate(both, span_order, doc_ends)
    half = HD // 2
    freq = rope_theta ** (-(jnp.arange(half, dtype=jnp.float32) * 2.0 / HD))
    angle = (query_orig - query_start).astype(jnp.float32)[:, None] * freq[None, :]
    cosine, sine = jnp.cos(angle), jnp.sin(angle)
    cosine = jnp.concatenate([cosine, cosine], axis=1)
    sine = jnp.concatenate([-sine, sine], axis=1)
    owner = 2 * jnp.arange(chips, dtype=jnp.int32) + context % 2
    key_rows = (owner[:, None] * tokens_here + inside[None, :]).reshape(-1).astype(jnp.int32)
    key_orig, _ = locate(key_rows, span_order, doc_ends)

    ours, siblings = slice(0, tokens_here), slice(tokens_here, 2 * tokens_here)
    both_rows, kv_columns = slice(0, 2 * tokens_here), slice(HD, 3 * HD)
    mine, theirs, last = project(
        last_ring.finish(),
        [(ours, kv_columns), (siblings, kv_columns), (both_rows, slice(0, HD))],
        "project_keys",
    )
    theirs = lax.ppermute(theirs, "context", sibling)
    out_ring.step()
    out_ring.step()
    mine, theirs = ordered((mine, theirs))
    kv = pl.pallas_call(
        functools.partial(keys_kernel, chips),
        out_shape=jax.ShapeDtypeStruct((chips * tokens_here, 2 * HD), jnp.bfloat16),
        in_specs=vmem_specs(4),
        out_specs=vmem_specs(1)[0],
        compiler_params=compute_params(),
        name="keys",
    )(mine, theirs, cosine, sine)
    (kv,) = ordered((kv,))
    kv = lax.all_to_all(
        kv, "context", split_axis=0, concat_axis=0, axis_index_groups=same_core, tiled=True
    )
    (first,) = project(first_ring.finish(), [(both_rows, slice(0, split))], "project_queries")
    first_theirs = lax.ppermute(first, "context", sibling)
    last_theirs = lax.ppermute(last, "context", sibling)
    out_ring.step()
    (kv,) = ordered((kv,))

    mixed = pl.pallas_call(
        attend_kernel,
        out_shape=jax.ShapeDtypeStruct((2 * tokens_here, HEAD_COLS + HD), jnp.float32),
        in_specs=vmem_specs(10),
        out_specs=vmem_specs(1)[0],
        compiler_params=compute_params(),
        name="attend",
    )(
        first,
        first_theirs,
        last,
        last_theirs,
        cosine,
        sine,
        query_start[:, None],
        query_orig[:, None],
        key_orig[None, :],
        kv,
    )
    (mixed,) = ordered((mixed,))
    mixed_theirs = lax.ppermute(mixed, "context", sibling)
    while not out_ring.done():
        out_ring.step()
    out_blocks = out_ring.finish()

    out_block = w_out.shape[1]
    parts = pl.pallas_call(
        functools.partial(output_kernel, chips, groups),
        out_shape=[jax.ShapeDtypeStruct((chips, rows_here, out_block), jnp.bfloat16)] * groups,
        in_specs=vmem_specs(2 + len(out_blocks)),
        out_specs=vmem_specs(groups),
        compiler_params=compute_params(),
        name="output",
    )(mixed, mixed_theirs, *out_blocks)
    arrived = []
    for e in range(2):
        for d in range(n_tensor):
            part = parts[e * n_tensor + d]
            if e or d:
                part = lax.ppermute(part, ("context", "tensor"), member(e, -d))
            arrived.append(part)
    return pl.pallas_call(
        functools.partial(sum_kernel, place, chips, groups),
        out_shape=jax.ShapeDtypeStruct((rows_here, n_context * out_block), jnp.bfloat16),
        in_specs=[pl.BlockSpec(memory_space=pl.ANY)] + vmem_specs(groups),
        out_specs=vmem_specs(1)[0],
        compiler_params=compute_params(),
        name="sum",
    )(token[0], *arrived)


def solution(mesh):
    placed = (
        P(("context", "tensor"), None),
        P(),
        P("context", "tensor"),
        P("tensor", "context"),
        P(),
        P(),
    )
    return jax.shard_map(
        functools.partial(per_device, mesh.shape["context"], mesh.shape["tensor"]),
        mesh=mesh,
        in_specs=placed,
        out_specs=P(("context", "tensor"), None),
        check_vma=False,
    )
```

```python
import functools

import jax
import jax.numpy as jnp
from jax import lax
from jax.experimental import pallas as pl
from jax.experimental.pallas import tpu as pltpu
from jax.sharding import PartitionSpec as P

HD = 128
QH_DEV = 4
SPAN = 64
HEAD_COLS = QH_DEV * HD
VMEM_LIMIT = 24 * 1024 * 1024

rope_theta = 500000.0


def ring_of_chips(count):
    wide = 1
    while (wide * 2) * (wide * 2) <= count:
        wide *= 2
    tall = count // wide
    if wide < 2:
        return list(range(count))
    ring = [(z, 0) for z in range(tall)]
    for z in range(tall - 1, -1, -1):
        row = list(range(1, wide))
        ring += [(z, y) for y in (row if (tall - 1 - z) % 2 == 0 else row[::-1])]
    if (tall - 1) % 2 == 0 or wide == 2:
        return [z * wide + y for z, y in ring]
    return [z * wide + y for z, y in ring]


def locate(layout_rows, span_order, doc_ends):
    span_index = layout_rows // SPAN
    matches = span_index[:, None] == jnp.arange(span_order.shape[0], dtype=jnp.int32)[None, :]
    source_span = jnp.sum(jnp.where(matches, span_order[None, :], 0), axis=1)
    initial = source_span * SPAN + layout_rows % SPAN
    doc_start = jnp.max(
        jnp.where(doc_ends[None, :] <= initial[:, None], doc_ends[None, :], 0), axis=1
    )
    return (initial, doc_start)


def vmem_specs(count):
    return [pl.BlockSpec(memory_space=pltpu.VMEM)] * count


def compute_params():
    return pltpu.CompilerParams(vmem_limit_bytes=VMEM_LIMIT)


def place_of(place):
    context = lax.axis_index("context")
    at = jnp.int32(0)
    for chip, spot in enumerate(place):
        at = jnp.where(context // 2 == chip, jnp.int32(spot), at)
    return at, context % 2


def norm_kernel(hidden_ref, gain_ref, out_ref):
    wide = hidden_ref[...].astype(jnp.float32)
    meansq = jnp.mean(wide * wide, axis=-1, keepdims=True)
    scaled = wide * lax.rsqrt(meansq + 1e-05)
    lanes = gain_ref.shape[1]
    normed = jnp.concatenate(
        [
            (
                scaled[:, i * lanes : (i + 1) * lanes]
                * gain_ref[i : i + 1, :].astype(jnp.float32)
            ).astype(jnp.bfloat16)
            for i in range(gain_ref.shape[0])
        ],
        axis=1,
    )
    block = out_ref.shape[2]
    for owner in range(out_ref.shape[0]):
        out_ref[owner] = normed[:, owner * block : (owner + 1) * block]


def take_ring(refs, chips):
    refs = list(refs)
    if chips % 2:
        return [(ref,) for ref in refs]
    half = chips // 2
    return [(r,) for r in refs[:half]] + [tuple(refs[half : half + 2])] + [
        (r,) for r in refs[half + 2 :]
    ]


def project_kernel(place, chips, n_tensor, outs, ring_ref, rows_ref, *refs):
    weight_refs, out_refs = refs[: -len(outs)], refs[-len(outs) :]
    at, core = place_of(place)
    tensor = lax.axis_index("tensor")
    members = [
        (core ^ e) * n_tensor + lax.rem(tensor + d, n_tensor)
        for e in range(2)
        for d in range(n_tensor)
    ]
    weights = take_ring(weight_refs, chips)
    total = None
    for slot in range(chips):
        owner = 2 * ring_ref[lax.rem(at + slot, chips)] + core
        rows = jnp.concatenate([rows_ref[member, owner] for member in members], axis=0)
        start = 0
        for ref in weights[slot]:
            depth = ref.shape[0]
            part = jnp.dot(
                rows[:, start : start + depth], ref[...], preferred_element_type=jnp.float32
            )
            total = part if total is None else total + part
            start += depth
    for ref, (rows, columns) in zip(out_refs, outs):
        ref[...] = total[rows, columns]


def turn(values, cosine, sine):
    return values * cosine + pltpu.roll(values, HD // 2, 1) * sine


def keys_kernel(chips, mine_ref, theirs_ref, cosine_ref, sine_ref, out_ref):
    rows = out_ref.shape[0] // chips
    cosine, sine = cosine_ref[:rows, :], sine_ref[:rows, :]
    total = mine_ref[...] + theirs_ref[...]
    keys = turn(total[:, :HD], cosine, sine).astype(jnp.bfloat16)
    values = total[:, HD:].astype(jnp.bfloat16)
    for chip in range(chips):
        out_ref[chip * rows : (chip + 1) * rows, :HD] = keys
        out_ref[chip * rows : (chip + 1) * rows, HD:] = values


def attend_kernel(
    first_ref,
    first_theirs_ref,
    last_ref,
    last_theirs_ref,
    cosine_ref,
    sine_ref,
    low_ref,
    high_ref,
    orig_ref,
    kv_ref,
    out_ref,
):
    keys = kv_ref[:, :HD]
    values = kv_ref[:, HD:]
    orig = orig_ref[...]
    allowed = (orig >= low_ref[...]) & (orig <= high_ref[...])
    scale = 1.0 / HD**0.5
    rows = out_ref.shape[0]
    half = rows // 2
    lane = lax.broadcasted_iota(jnp.int32, (rows, HD), 1)
    stats = jnp.zeros((rows, HD), jnp.float32)
    for head in range(QH_DEV):
        if head < QH_DEV - 1:
            mine_ref, theirs_ref = first_ref, first_theirs_ref
            columns = slice(head * HD, (head + 1) * HD)
        else:
            mine_ref, theirs_ref = last_ref, last_theirs_ref
            columns = slice(0, HD)
        query = jnp.concatenate(
            [
                mine_ref[:half, columns] + theirs_ref[half:, columns],
                mine_ref[half:, columns] + theirs_ref[:half, columns],
            ],
            axis=0,
        )
        query = turn(query, cosine_ref[...], sine_ref[...]).astype(jnp.bfloat16)
        scores = lax.dot_general(
            query, keys, (((1,), (1,)), ((), ())), preferred_element_type=jnp.float32
        )
        scores = jnp.where(allowed, scores * scale, -1e30)
        top = jnp.max(scores, axis=-1, keepdims=True)
        expo = jnp.where(allowed, jnp.exp(scores - top), 0.0)
        total = jnp.sum(expo, axis=-1, keepdims=True)
        out_ref[:, head * HD : (head + 1) * HD] = jnp.dot(
            expo.astype(jnp.bfloat16), values, preferred_element_type=jnp.float32
        )
        stats = jnp.where(lane == 2 * head, total, stats)
        stats = jnp.where(lane == 2 * head + 1, top, stats)
    out_ref[:, HEAD_COLS:] = stats


def output_kernel(groups, pieces_of, mine_ref, theirs_ref, *refs):
    weight_refs, out_refs = refs[:-groups], refs[-groups:]
    chip_rows = mine_ref.shape[0]
    half = chip_rows // 2

    def swapped(columns):
        return jnp.concatenate([theirs_ref[half:, columns], theirs_ref[:half, columns]], axis=0)

    pieces = []
    for head in range(QH_DEV):
        columns = slice(head * HD, (head + 1) * HD)
        at = HEAD_COLS + 2 * head
        total, top = mine_ref[:, at : at + 1], mine_ref[:, at + 1 : at + 2]
        other_total, other_top = swapped(slice(at, at + 1)), swapped(slice(at + 1, at + 2))
        peak = jnp.maximum(top, other_top)
        factor, other_factor = jnp.exp(top - peak), jnp.exp(other_top - peak)
        product = mine_ref[:, columns] * factor + swapped(columns) * other_factor
        pieces.append(
            (product / (total * factor + other_total * other_factor)).astype(jnp.bfloat16)
        )
    mixed = jnp.concatenate(pieces, axis=1)
    rows = chip_rows // groups
    weight_refs = iter(weight_refs)
    for slot, pieces in enumerate(pieces_of):
        start, total = 0, None
        for _ in range(pieces):
            ref = next(weight_refs)
            depth = ref.shape[0]
            part = jnp.dot(
                mixed[:, start : start + depth], ref[...], preferred_element_type=jnp.float32
            )
            total = part if total is None else total + part
            start += depth
        total = total.astype(jnp.bfloat16)
        for group in range(groups):
            out_refs[group][slot] = total[group * rows : (group + 1) * rows]


def sum_kernel(place, chips, groups, near, token_ref, *refs):
    near_refs, far_refs, out_ref = refs[:groups], refs[groups : 2 * groups], refs[2 * groups]
    at, core = place_of(place)
    block = near_refs[0].shape[2]
    half = groups // 2

    def added(part, slot):
        turn_at = lax.rem(slot + near // 2, chips)
        total = None
        for group in range(part * half, (part + 1) * half):
            rows = jnp.where(
                turn_at < near,
                near_refs[group][jnp.minimum(turn_at, near - 1)].astype(jnp.float32),
                far_refs[group][jnp.maximum(turn_at - near, 0)].astype(jnp.float32),
            )
            total = rows if total is None else total + rows
        return total.astype(jnp.bfloat16)

    for even in range(2):

        @pl.when(core == even)
        def _():
            for chip in range(chips):
                slot = lax.rem(place[chip] + chips - at, chips)
                for side in range(2):
                    column = (2 * chip + side) * block
                    out_ref[:, column : column + block] = added(side ^ even, slot)


def per_device(n_context, n_tensor, hidden_rows, norm_gain, w_qkv, w_out, doc_lengths, span_order):
    chips = n_context // 2
    ring = ring_of_chips(chips)
    place = [ring.index(chip) for chip in range(chips)]
    groups = 2 * n_tensor
    rows_here, width = hidden_rows.shape
    tokens_here = rows_here * n_tensor
    block = width // n_context
    context = lax.axis_index("context")
    tensor = lax.axis_index("tensor")
    ahead = [
        (ring[i] * 2 + k, ring[(i + 1) % chips] * 2 + k) for i in range(chips) for k in range(2)
    ]
    back = [(b, a) for a, b in ahead]
    sibling = [(c, c ^ 1) for c in range(n_context)]

    same_core = [[2 * chip + k for chip in range(chips)] for k in range(2)]
    token = [doc_lengths]

    def ordered(values):
        held = lax.optimization_barrier((*values, token[0]))
        token[0] = held[-1]
        return list(held[:-1])

    class Ring:
        def __init__(self, mine):
            self.up, self.down = [mine], [mine]
            self.middle = []

        def step(self, earlier=()):
            up, down, *earlier = ordered((self.up[-1], self.down[-1], *earlier))
            if len(self.up) <= (chips - 1) // 2:
                self.up.append(lax.ppermute(up, "context", ahead))
                self.down.append(lax.ppermute(down, "context", back))
            elif chips % 2 == 0 and not self.middle:
                half = up.shape[0] // 2
                self.middle = [
                    lax.ppermute(up[:half], "context", ahead),
                    lax.ppermute(down[half:], "context", back),
                ]
            return earlier

        def done(self):
            return len(self.up) > (chips - 1) // 2 and (chips % 2 == 1 or bool(self.middle))

        def finish(self):
            while not self.done():
                self.step()
            return self.down + self.middle + self.up[:0:-1]

        def block(self, slot):
            slot %= chips
            if chips % 2 == 0 and slot == chips // 2:
                return tuple(self.middle)
            return (self.down[slot] if slot <= chips // 2 else self.up[chips - slot],)

    def member(e, d):
        return [
            (c * n_tensor + t, (c ^ e) * n_tensor + (t - d) % n_tensor)
            for c in range(n_context)
            for t in range(n_tensor)
        ]

    split = (QH_DEV - 1) * HD

    normed = pl.pallas_call(
        norm_kernel,
        out_shape=jax.ShapeDtypeStruct((n_context, rows_here, block), jnp.bfloat16),
        in_specs=vmem_specs(2),
        out_specs=vmem_specs(1)[0],
        compiler_params=compute_params(),
        name="norm",
    )(hidden_rows, norm_gain.reshape(-1, HD))
    sharers = [
        [(2 * chip + k) * n_tensor + t for k in range(2) for t in range(n_tensor)]
        for chip in range(chips)
    ]
    normed = lax.all_gather(normed, ("context", "tensor"), axis_index_groups=sharers)
    last_ring = Ring(w_qkv[:, split:])
    first_ring = Ring(w_qkv[:, :split])
    last_ring.step()
    first_ring.step()
    while not last_ring.done():
        last_ring.step()
        first_ring.step()

    def project(blocks, outs, name):
        shapes = [
            jax.ShapeDtypeStruct((rows.stop - rows.start, columns.stop - columns.start), jnp.float32)
            for rows, columns in outs
        ]
        return pl.pallas_call(
            functools.partial(project_kernel, place, chips, n_tensor, outs),
            out_shape=shapes,
            in_specs=[pl.BlockSpec(memory_space=pltpu.SMEM)] + vmem_specs(1 + len(blocks)),
            out_specs=vmem_specs(len(outs)),
            compiler_params=compute_params(),
            name=name,
        )(jnp.asarray(ring, jnp.int32), *ordered((normed, *blocks)))

    doc_ends = jnp.cumsum(doc_lengths)
    inside = (
        (tensor + jnp.arange(n_tensor, dtype=jnp.int32)) % n_tensor * rows_here
    )[:, None] + jnp.arange(rows_here, dtype=jnp.int32)[None, :]
    inside = inside.reshape(-1)
    both = jnp.concatenate([context * tokens_here + inside, (context ^ 1) * tokens_here + inside])
    query_orig, query_start = locate(both, span_order, doc_ends)
    half = HD // 2
    freq = rope_theta ** (-(jnp.arange(half, dtype=jnp.float32) * 2.0 / HD))
    angle = (query_orig - query_start).astype(jnp.float32)[:, None] * freq[None, :]
    cosine, sine = jnp.cos(angle), jnp.sin(angle)
    cosine = jnp.concatenate([cosine, cosine], axis=1)
    sine = jnp.concatenate([-sine, sine], axis=1)
    owner = 2 * jnp.arange(chips, dtype=jnp.int32) + context % 2
    key_rows = (owner[:, None] * tokens_here + inside[None, :]).reshape(-1).astype(jnp.int32)
    key_orig, _ = locate(key_rows, span_order, doc_ends)

    ours, siblings = slice(0, tokens_here), slice(tokens_here, 2 * tokens_here)
    both_rows, kv_columns = slice(0, 2 * tokens_here), slice(HD, 3 * HD)
    mine, theirs, last = project(
        last_ring.finish(),
        [(ours, kv_columns), (siblings, kv_columns), (both_rows, slice(0, HD))],
        "project_keys",
    )
    theirs = lax.ppermute(theirs, "context", sibling)
    out_ring = Ring(w_out)
    out_ring.step()
    (first,) = project(first_ring.finish(), [(both_rows, slice(0, split))], "project_queries")
    first_theirs = lax.ppermute(first, "context", sibling)
    last_theirs = lax.ppermute(last, "context", sibling)
    out_ring.step()
    mine, theirs = ordered((mine, theirs))
    kv = pl.pallas_call(
        functools.partial(keys_kernel, chips),
        out_shape=jax.ShapeDtypeStruct((chips * tokens_here, 2 * HD), jnp.bfloat16),
        in_specs=vmem_specs(4),
        out_specs=vmem_specs(1)[0],
        compiler_params=compute_params(),
        name="keys",
    )(mine, theirs, cosine, sine)
    (kv,) = ordered((kv,))
    kv = lax.all_to_all(
        kv, "context", split_axis=0, concat_axis=0, axis_index_groups=same_core, tiled=True
    )
    (kv,) = ordered((kv,))

    mixed = pl.pallas_call(
        attend_kernel,
        out_shape=jax.ShapeDtypeStruct((2 * tokens_here, HEAD_COLS + HD), jnp.float32),
        in_specs=vmem_specs(10),
        out_specs=vmem_specs(1)[0],
        compiler_params=compute_params(),
        name="attend",
    )(
        first,
        first_theirs,
        last,
        last_theirs,
        cosine,
        sine,
        query_start[:, None],
        query_orig[:, None],
        key_orig[None, :],
        kv,
    )
    out_ring.step()
    (mixed,) = ordered((mixed,))
    mixed_theirs = lax.ppermute(mixed, "context", sibling)

    out_block = w_out.shape[1]

    def output(slots, name):
        blocks = [out_ring.block(slot) for slot in slots]
        flat = [piece for pieces in blocks for piece in pieces]
        parts = pl.pallas_call(
            functools.partial(output_kernel, groups, [len(pieces) for pieces in blocks]),
            out_shape=[jax.ShapeDtypeStruct((len(slots), rows_here, out_block), jnp.bfloat16)]
            * groups,
            in_specs=vmem_specs(2 + len(flat)),
            out_specs=vmem_specs(groups),
            compiler_params=compute_params(),
            name=name,
        )(mixed, mixed_theirs, *flat)
        parts = ordered(parts)
        arrived = []
        for e in range(2):
            for d in range(n_tensor):
                part = parts[e * n_tensor + d]
                if e or d:
                    part = lax.ppermute(part, ("context", "tensor"), member(e, -d))
                arrived.append(part)
        return arrived

    reach = max(chips // 2 - 2, 0)
    while len(out_ring.up) <= reach:
        out_ring.step()
    near = 2 * reach + 1
    arrived = output(list(range(-reach, reach + 1)), "output_near")
    while not out_ring.done():
        out_ring.step()
    arrived += output(list(range(reach + 1, chips - reach)), "output_far")
    return pl.pallas_call(
        functools.partial(sum_kernel, place, chips, groups, near),
        out_shape=jax.ShapeDtypeStruct((rows_here, n_context * out_block), jnp.bfloat16),
        in_specs=[pl.BlockSpec(memory_space=pl.ANY)] + vmem_specs(2 * groups),
        out_specs=vmem_specs(1)[0],
        compiler_params=compute_params(),
        name="sum",
    )(token[0], *arrived)


def solution(mesh):
    placed = (
        P(("context", "tensor"), None),
        P(),
        P("context", "tensor"),
        P("tensor", "context"),
        P(),
        P(),
    )
    return jax.shard_map(
        functools.partial(per_device, mesh.shape["context"], mesh.shape["tensor"]),
        mesh=mesh,
        in_specs=placed,
        out_specs=P(("context", "tensor"), None),
        check_vma=False,
    )
```

```python
import functools

import jax
import jax.numpy as jnp
from jax import lax
from jax.experimental import pallas as pl
from jax.experimental.pallas import tpu as pltpu
from jax.sharding import PartitionSpec as P

HD = 128
QH_DEV = 4
SPAN = 64
HEAD_COLS = QH_DEV * HD
VMEM_LIMIT = 24 * 1024 * 1024

rope_theta = 500000.0


def ring_of_chips(count):
    wide = 1
    while (wide * 2) * (wide * 2) <= count:
        wide *= 2
    tall = count // wide
    if wide < 2:
        return list(range(count))
    ring = [(z, 0) for z in range(tall)]
    for z in range(tall - 1, -1, -1):
        row = list(range(1, wide))
        ring += [(z, y) for y in (row if (tall - 1 - z) % 2 == 0 else row[::-1])]
    if (tall - 1) % 2 == 0 or wide == 2:
        return [z * wide + y for z, y in ring]
    return [z * wide + y for z, y in ring]


def locate(layout_rows, span_order, doc_ends):
    span_index = layout_rows // SPAN
    matches = span_index[:, None] == jnp.arange(span_order.shape[0], dtype=jnp.int32)[None, :]
    source_span = jnp.sum(jnp.where(matches, span_order[None, :], 0), axis=1)
    initial = source_span * SPAN + layout_rows % SPAN
    doc_start = jnp.max(
        jnp.where(doc_ends[None, :] <= initial[:, None], doc_ends[None, :], 0), axis=1
    )
    return (initial, doc_start)


def vmem_specs(count):
    return [pl.BlockSpec(memory_space=pltpu.VMEM)] * count


def compute_params():
    return pltpu.CompilerParams(vmem_limit_bytes=VMEM_LIMIT)


def place_of(place):
    context = lax.axis_index("context")
    at = jnp.int32(0)
    for chip, spot in enumerate(place):
        at = jnp.where(context // 2 == chip, jnp.int32(spot), at)
    return at, context % 2


def norm_kernel(place, chips, hidden_ref, gain_ref, out_ref):
    at, core = place_of(place)
    wide = hidden_ref[...].astype(jnp.float32)
    meansq = jnp.mean(wide * wide, axis=-1, keepdims=True)
    scaled = wide * lax.rsqrt(meansq + 1e-05)
    lanes = gain_ref.shape[1]
    normed = jnp.concatenate(
        [
            (
                scaled[:, i * lanes : (i + 1) * lanes]
                * gain_ref[i : i + 1, :].astype(jnp.float32)
            ).astype(jnp.bfloat16)
            for i in range(gain_ref.shape[0])
        ],
        axis=1,
    )
    block = out_ref.shape[3]
    for even in range(2):

        @pl.when(core == even)
        def _():
            for chip in range(chips):
                slot = lax.rem(place[chip] + chips - at, chips)
                for side in range(2):
                    column = (2 * chip + side) * block
                    out_ref[side ^ even, slot] = normed[:, column : column + block]


def take_ring(refs, chips):
    refs = list(refs)
    if chips % 2:
        return [(ref,) for ref in refs]
    half = chips // 2
    return [(r,) for r in refs[:half]] + [tuple(refs[half : half + 2])] + [
        (r,) for r in refs[half + 2 :]
    ]


def project_kernel(chips, groups, *refs):
    rows_refs, refs = refs[:groups], refs[groups:]
    weight_refs, (mine_ref, theirs_ref, queries_ref) = refs[:-3], refs[-3:]
    half = groups // 2
    weights = take_ring(weight_refs, chips)
    total = None
    for slot in range(chips):
        rows = jnp.concatenate(
            [ref[group // half, slot] for group, ref in enumerate(rows_refs)], axis=0
        )
        start = 0
        for ref in weights[slot]:
            depth = ref.shape[0]
            part = jnp.dot(
                rows[:, start : start + depth], ref[...], preferred_element_type=jnp.float32
            )
            total = part if total is None else total + part
            start += depth
    count = mine_ref.shape[0]
    mine_ref[...] = total[:count, HEAD_COLS:]
    theirs_ref[...] = total[count:, HEAD_COLS:]
    queries_ref[...] = total[:, :HEAD_COLS]


def turn(values, cosine, sine):
    return values * cosine + pltpu.roll(values, HD // 2, 1) * sine


def keys_kernel(chips, mine_ref, theirs_ref, cosine_ref, sine_ref, out_ref):
    rows = out_ref.shape[0] // chips
    cosine, sine = cosine_ref[:rows, :], sine_ref[:rows, :]
    total = mine_ref[...] + theirs_ref[...]
    keys = turn(total[:, :HD], cosine, sine).astype(jnp.bfloat16)
    values = total[:, HD:].astype(jnp.bfloat16)
    for chip in range(chips):
        out_ref[chip * rows : (chip + 1) * rows, :HD] = keys
        out_ref[chip * rows : (chip + 1) * rows, HD:] = values


def attend_kernel(
    mine_ref,
    theirs_ref,
    cosine_ref,
    sine_ref,
    low_ref,
    high_ref,
    orig_ref,
    kv_ref,
    out_ref,
):
    keys = kv_ref[:, :HD]
    values = kv_ref[:, HD:]
    orig = orig_ref[...]
    allowed = (orig >= low_ref[...]) & (orig <= high_ref[...])
    scale = 1.0 / HD**0.5
    rows = out_ref.shape[0]
    half = rows // 2
    lane = lax.broadcasted_iota(jnp.int32, (rows, HD), 1)
    stats = jnp.zeros((rows, HD), jnp.float32)
    for head in range(QH_DEV):
        columns = slice(head * HD, (head + 1) * HD)
        query = jnp.concatenate(
            [
                mine_ref[:half, columns] + theirs_ref[half:, columns],
                mine_ref[half:, columns] + theirs_ref[:half, columns],
            ],
            axis=0,
        )
        query = turn(query, cosine_ref[...], sine_ref[...]).astype(jnp.bfloat16)
        scores = lax.dot_general(
            query, keys, (((1,), (1,)), ((), ())), preferred_element_type=jnp.float32
        )
        scores = jnp.where(allowed, scores * scale, -1e30)
        top = jnp.max(scores, axis=-1, keepdims=True)
        expo = jnp.where(allowed, jnp.exp(scores - top), 0.0)
        total = jnp.sum(expo, axis=-1, keepdims=True)
        out_ref[:, columns] = jnp.dot(
            expo.astype(jnp.bfloat16), values, preferred_element_type=jnp.float32
        )
        stats = jnp.where(lane == 2 * head, total, stats)
        stats = jnp.where(lane == 2 * head + 1, top, stats)
    out_ref[:, HEAD_COLS:] = stats


def output_kernel(groups, pieces_of, mine_ref, theirs_ref, *refs):
    weight_refs, out_refs = refs[:-groups], refs[-groups:]
    chip_rows = mine_ref.shape[0]
    half = chip_rows // 2

    def swapped(columns):
        return jnp.concatenate([theirs_ref[half:, columns], theirs_ref[:half, columns]], axis=0)

    pieces = []
    for head in range(QH_DEV):
        columns = slice(head * HD, (head + 1) * HD)
        at = HEAD_COLS + 2 * head
        total, top = mine_ref[:, at : at + 1], mine_ref[:, at + 1 : at + 2]
        other_total, other_top = swapped(slice(at, at + 1)), swapped(slice(at + 1, at + 2))
        peak = jnp.maximum(top, other_top)
        factor, other_factor = jnp.exp(top - peak), jnp.exp(other_top - peak)
        product = mine_ref[:, columns] * factor + swapped(columns) * other_factor
        pieces.append(
            (product / (total * factor + other_total * other_factor)).astype(jnp.bfloat16)
        )
    mixed = jnp.concatenate(pieces, axis=1)
    rows = chip_rows // groups
    weight_refs = iter(weight_refs)
    for slot, pieces in enumerate(pieces_of):
        start, total = 0, None
        for _ in range(pieces):
            ref = next(weight_refs)
            depth = ref.shape[0]
            part = jnp.dot(
                mixed[:, start : start + depth], ref[...], preferred_element_type=jnp.float32
            )
            total = part if total is None else total + part
            start += depth
        total = total.astype(jnp.bfloat16)
        for group in range(groups):
            out_refs[group][slot] = total[group * rows : (group + 1) * rows]


def sum_kernel(place, chips, groups, near, token_ref, *refs):
    near_refs, far_refs, out_ref = refs[:groups], refs[groups : 2 * groups], refs[2 * groups]
    at, core = place_of(place)
    block = near_refs[0].shape[2]
    half = groups // 2

    def added(part, slot):
        turn_at = lax.rem(slot + near // 2, chips)
        total = None
        for group in range(part * half, (part + 1) * half):
            rows = jnp.where(
                turn_at < near,
                near_refs[group][jnp.minimum(turn_at, near - 1)].astype(jnp.float32),
                far_refs[group][jnp.maximum(turn_at - near, 0)].astype(jnp.float32),
            )
            total = rows if total is None else total + rows
        return total.astype(jnp.bfloat16)

    for even in range(2):

        @pl.when(core == even)
        def _():
            for chip in range(chips):
                slot = lax.rem(place[chip] + chips - at, chips)
                for side in range(2):
                    column = (2 * chip + side) * block
                    out_ref[:, column : column + block] = added(side ^ even, slot)


def per_device(n_context, n_tensor, hidden_rows, norm_gain, w_qkv, w_out, doc_lengths, span_order):
    chips = n_context // 2
    ring = ring_of_chips(chips)
    place = [ring.index(chip) for chip in range(chips)]
    groups = 2 * n_tensor
    rows_here, width = hidden_rows.shape
    tokens_here = rows_here * n_tensor
    block = width // n_context
    context = lax.axis_index("context")
    tensor = lax.axis_index("tensor")
    ahead = [
        (ring[i] * 2 + k, ring[(i + 1) % chips] * 2 + k) for i in range(chips) for k in range(2)
    ]
    back = [(b, a) for a, b in ahead]
    sibling = [(c, c ^ 1) for c in range(n_context)]

    same_core = [[2 * chip + k for chip in range(chips)] for k in range(2)]
    token = [doc_lengths]

    def ordered(values):
        held = lax.optimization_barrier((*values, token[0]))
        token[0] = held[-1]
        return list(held[:-1])

    class Ring:
        def __init__(self, mine):
            self.up, self.down = [mine], [mine]
            self.middle = []

        def step(self, earlier=()):
            up, down, *earlier = ordered((self.up[-1], self.down[-1], *earlier))
            if len(self.up) <= (chips - 1) // 2:
                self.up.append(lax.ppermute(up, "context", ahead))
                self.down.append(lax.ppermute(down, "context", back))
            elif chips % 2 == 0 and not self.middle:
                half = up.shape[0] // 2
                self.middle = [
                    lax.ppermute(up[:half], "context", ahead),
                    lax.ppermute(down[half:], "context", back),
                ]
            return earlier

        def done(self):
            return len(self.up) > (chips - 1) // 2 and (chips % 2 == 1 or bool(self.middle))

        def finish(self):
            while not self.done():
                self.step()
            return self.down + self.middle + self.up[:0:-1]

        def block(self, slot):
            slot %= chips
            if chips % 2 == 0 and slot == chips // 2:
                return tuple(self.middle)
            return (self.down[slot] if slot <= chips // 2 else self.up[chips - slot],)

    def member(e, d):
        return [
            (c * n_tensor + t, (c ^ e) * n_tensor + (t - d) % n_tensor)
            for c in range(n_context)
            for t in range(n_tensor)
        ]

    qkv_ring = Ring(w_qkv)
    qkv_ring.step()
    normed = pl.pallas_call(
        functools.partial(norm_kernel, place, chips),
        out_shape=jax.ShapeDtypeStruct((2, chips, rows_here, block), jnp.bfloat16),
        in_specs=vmem_specs(2),
        out_specs=vmem_specs(1)[0],
        compiler_params=compute_params(),
        name="norm",
    )(hidden_rows, norm_gain.reshape(-1, HD))
    normed = [normed] + [
        lax.ppermute(
            normed, "tensor", [(t, (t - d) % n_tensor) for t in range(n_tensor)]
        )
        for d in range(1, n_tensor)
    ]
    normed += [lax.ppermute(rows, "context", sibling) for rows in normed]

    qkv_ring.step()
    qkv_ring.step()
    normed = qkv_ring.step(normed)
    while not qkv_ring.done():
        qkv_ring.step()

    doc_ends = jnp.cumsum(doc_lengths)
    inside = (
        (tensor + jnp.arange(n_tensor, dtype=jnp.int32)) % n_tensor * rows_here
    )[:, None] + jnp.arange(rows_here, dtype=jnp.int32)[None, :]
    inside = inside.reshape(-1)
    both = jnp.concatenate([context * tokens_here + inside, (context ^ 1) * tokens_here + inside])
    query_orig, query_start = locate(both, span_order, doc_ends)
    half = HD // 2
    freq = rope_theta ** (-(jnp.arange(half, dtype=jnp.float32) * 2.0 / HD))
    angle = (query_orig - query_start).astype(jnp.float32)[:, None] * freq[None, :]
    cosine, sine = jnp.cos(angle), jnp.sin(angle)
    cosine = jnp.concatenate([cosine, cosine], axis=1)
    sine = jnp.concatenate([-sine, sine], axis=1)
    owner = 2 * jnp.arange(chips, dtype=jnp.int32) + context % 2
    key_rows = (owner[:, None] * tokens_here + inside[None, :]).reshape(-1).astype(jnp.int32)
    key_orig, _ = locate(key_rows, span_order, doc_ends)

    out_ring = Ring(w_out)
    out_ring.step()
    blocks = qkv_ring.finish()
    mine, theirs, queries = pl.pallas_call(
        functools.partial(project_kernel, chips, groups),
        out_shape=[
            jax.ShapeDtypeStruct((tokens_here, 2 * HD), jnp.float32),
            jax.ShapeDtypeStruct((tokens_here, 2 * HD), jnp.float32),
            jax.ShapeDtypeStruct((2 * tokens_here, HEAD_COLS), jnp.float32),
        ],
        in_specs=vmem_specs(groups + len(blocks)),
        out_specs=vmem_specs(3),
        compiler_params=compute_params(),
        name="project",
    )(*ordered((*normed, *blocks)))
    theirs = lax.ppermute(theirs, "context", sibling)
    queries_theirs = lax.ppermute(queries, "context", sibling)
    out_ring.step()
    mine, theirs = ordered((mine, theirs))
    kv = pl.pallas_call(
        functools.partial(keys_kernel, chips),
        out_shape=jax.ShapeDtypeStruct((chips * tokens_here, 2 * HD), jnp.bfloat16),
        in_specs=vmem_specs(4),
        out_specs=vmem_specs(1)[0],
        compiler_params=compute_params(),
        name="keys",
    )(mine, theirs, cosine, sine)
    (kv,) = ordered((kv,))
    kv = lax.all_to_all(
        kv, "context", split_axis=0, concat_axis=0, axis_index_groups=same_core, tiled=True
    )
    (kv,) = ordered((kv,))

    mixed = pl.pallas_call(
        attend_kernel,
        out_shape=jax.ShapeDtypeStruct((2 * tokens_here, HEAD_COLS + HD), jnp.float32),
        in_specs=vmem_specs(8),
        out_specs=vmem_specs(1)[0],
        compiler_params=compute_params(),
        name="attend",
    )(
        queries,
        queries_theirs,
        cosine,
        sine,
        query_start[:, None],
        query_orig[:, None],
        key_orig[None, :],
        kv,
    )
    out_ring.step()
    (mixed,) = ordered((mixed,))
    mixed_theirs = lax.ppermute(mixed, "context", sibling)

    out_block = w_out.shape[1]

    def output(slots, name):
        blocks = [out_ring.block(slot) for slot in slots]
        flat = [piece for pieces in blocks for piece in pieces]
        parts = pl.pallas_call(
            functools.partial(output_kernel, groups, [len(pieces) for pieces in blocks]),
            out_shape=[jax.ShapeDtypeStruct((len(slots), rows_here, out_block), jnp.bfloat16)]
            * groups,
            in_specs=vmem_specs(2 + len(flat)),
            out_specs=vmem_specs(groups),
            compiler_params=compute_params(),
            name=name,
        )(mixed, mixed_theirs, *flat)
        parts = ordered(parts)
        arrived = []
        for e in range(2):
            for d in range(n_tensor):
                part = parts[e * n_tensor + d]
                if e or d:
                    part = lax.ppermute(part, ("context", "tensor"), member(e, -d))
                arrived.append(part)
        return arrived

    reach = max(chips // 2 - 2, 0)
    while len(out_ring.up) <= reach:
        out_ring.step()
    near = 2 * reach + 1
    arrived = output(list(range(-reach, reach + 1)), "output_near")
    while not out_ring.done():
        out_ring.step()
    arrived += output(list(range(reach + 1, chips - reach)), "output_far")
    return pl.pallas_call(
        functools.partial(sum_kernel, place, chips, groups, near),
        out_shape=jax.ShapeDtypeStruct((rows_here, n_context * out_block), jnp.bfloat16),
        in_specs=[pl.BlockSpec(memory_space=pl.ANY)] + vmem_specs(2 * groups),
        out_specs=vmem_specs(1)[0],
        compiler_params=compute_params(),
        name="sum",
    )(token[0], *arrived)


def solution(mesh):
    placed = (
        P(("context", "tensor"), None),
        P(),
        P("context", "tensor"),
        P("tensor", "context"),
        P(),
        P(),
    )
    return jax.shard_map(
        functools.partial(per_device, mesh.shape["context"], mesh.shape["tensor"]),
        mesh=mesh,
        in_specs=placed,
        out_specs=P(("context", "tensor"), None),
        check_vma=False,
    )
```

```python
import functools

import jax
import jax.numpy as jnp
from jax import lax
from jax.experimental import pallas as pl
from jax.experimental.pallas import tpu as pltpu
from jax.sharding import PartitionSpec as P

HD = 128
QH_DEV = 4
SPAN = 64
HEAD_COLS = QH_DEV * HD
VMEM_LIMIT = 24 * 1024 * 1024

rope_theta = 500000.0


def ring_of_chips(count):
    wide = 1
    while (wide * 2) * (wide * 2) <= count:
        wide *= 2
    tall = count // wide
    if wide < 2:
        return list(range(count))
    ring = [(z, 0) for z in range(tall)]
    for z in range(tall - 1, -1, -1):
        row = list(range(1, wide))
        ring += [(z, y) for y in (row if (tall - 1 - z) % 2 == 0 else row[::-1])]
    if (tall - 1) % 2 == 0 or wide == 2:
        return [z * wide + y for z, y in ring]
    return [z * wide + y for z, y in ring]


def locate(layout_rows, span_order, doc_ends):
    span_index = layout_rows // SPAN
    matches = span_index[:, None] == jnp.arange(span_order.shape[0], dtype=jnp.int32)[None, :]
    source_span = jnp.sum(jnp.where(matches, span_order[None, :], 0), axis=1)
    initial = source_span * SPAN + layout_rows % SPAN
    doc_start = jnp.max(
        jnp.where(doc_ends[None, :] <= initial[:, None], doc_ends[None, :], 0), axis=1
    )
    return (initial, doc_start)


def vmem_specs(count):
    return [pl.BlockSpec(memory_space=pltpu.VMEM)] * count


def compute_params():
    return pltpu.CompilerParams(vmem_limit_bytes=VMEM_LIMIT)


def place_of(place):
    context = lax.axis_index("context")
    at = jnp.int32(0)
    for chip, spot in enumerate(place):
        at = jnp.where(context // 2 == chip, jnp.int32(spot), at)
    return at, context % 2


def norm_kernel(place, chips, hidden_ref, gain_ref, out_ref):
    at, core = place_of(place)
    wide = hidden_ref[...].astype(jnp.float32)
    meansq = jnp.mean(wide * wide, axis=-1, keepdims=True)
    scaled = wide * lax.rsqrt(meansq + 1e-05)
    lanes = gain_ref.shape[1]
    normed = jnp.concatenate(
        [
            (
                scaled[:, i * lanes : (i + 1) * lanes]
                * gain_ref[i : i + 1, :].astype(jnp.float32)
            ).astype(jnp.bfloat16)
            for i in range(gain_ref.shape[0])
        ],
        axis=1,
    )
    block = out_ref.shape[3]
    for even in range(2):

        @pl.when(core == even)
        def _():
            for chip in range(chips):
                slot = lax.rem(place[chip] + chips - at, chips)
                for side in range(2):
                    column = (2 * chip + side) * block
                    out_ref[side ^ even, slot] = normed[:, column : column + block]


def take_ring(refs, chips):
    refs = list(refs)
    if chips % 2:
        return [(ref,) for ref in refs]
    half = chips // 2
    return [(r,) for r in refs[:half]] + [tuple(refs[half : half + 2])] + [
        (r,) for r in refs[half + 2 :]
    ]


def project_kernel(chips, groups, *refs):
    rows_refs, refs = refs[:groups], refs[groups:]
    weight_refs, (mine_ref, theirs_ref, queries_ref) = refs[:-3], refs[-3:]
    half = groups // 2
    weights = take_ring(weight_refs, chips)
    total = None
    for slot in range(chips):
        rows = jnp.concatenate(
            [ref[group // half, slot] for group, ref in enumerate(rows_refs)], axis=0
        )
        start = 0
        for ref in weights[slot]:
            depth = ref.shape[0]
            part = jnp.dot(
                rows[:, start : start + depth], ref[...], preferred_element_type=jnp.float32
            )
            total = part if total is None else total + part
            start += depth
    count = mine_ref.shape[0]
    mine_ref[...] = total[:count, HEAD_COLS:]
    theirs_ref[...] = total[count:, HEAD_COLS:]
    queries_ref[...] = total[:, :HEAD_COLS]


def turn(values, cosine, sine):
    return values * cosine + pltpu.roll(values, HD // 2, 1) * sine


def keys_kernel(chips, mine_ref, theirs_ref, cosine_ref, sine_ref, out_ref):
    rows = out_ref.shape[0] // chips
    cosine, sine = cosine_ref[:rows, :], sine_ref[:rows, :]
    total = mine_ref[...] + theirs_ref[...]
    keys = turn(total[:, :HD], cosine, sine).astype(jnp.bfloat16)
    values = total[:, HD:].astype(jnp.bfloat16)
    for chip in range(chips):
        out_ref[chip * rows : (chip + 1) * rows, :HD] = keys
        out_ref[chip * rows : (chip + 1) * rows, HD:] = values


def attend_kernel(
    mine_ref,
    theirs_ref,
    cosine_ref,
    sine_ref,
    low_ref,
    high_ref,
    orig_ref,
    kv_ref,
    out_ref,
):
    keys = kv_ref[:, :HD]
    values = kv_ref[:, HD:]
    orig = orig_ref[...]
    allowed = (orig >= low_ref[...]) & (orig <= high_ref[...])
    scale = 1.0 / HD**0.5
    rows = out_ref.shape[0]
    half = rows // 2
    lane = lax.broadcasted_iota(jnp.int32, (rows, HD), 1)
    stats = jnp.zeros((rows, HD), jnp.float32)
    for head in range(QH_DEV):
        columns = slice(head * HD, (head + 1) * HD)
        query = jnp.concatenate(
            [
                mine_ref[:half, columns] + theirs_ref[half:, columns],
                mine_ref[half:, columns] + theirs_ref[:half, columns],
            ],
            axis=0,
        )
        query = turn(query, cosine_ref[...], sine_ref[...]).astype(jnp.bfloat16)
        scores = lax.dot_general(
            query, keys, (((1,), (1,)), ((), ())), preferred_element_type=jnp.float32
        )
        scores = jnp.where(allowed, scores * scale, -1e30)
        top = jnp.max(scores, axis=-1, keepdims=True)
        expo = jnp.where(allowed, jnp.exp(scores - top), 0.0)
        total = jnp.sum(expo, axis=-1, keepdims=True)
        out_ref[:, columns] = jnp.dot(
            expo.astype(jnp.bfloat16), values, preferred_element_type=jnp.float32
        )
        stats = jnp.where(lane == 2 * head, total, stats)
        stats = jnp.where(lane == 2 * head + 1, top, stats)
    out_ref[:, HEAD_COLS:] = stats


def output_kernel(chips, groups, mine_ref, theirs_ref, *refs):
    weight_refs, out_refs = refs[:-groups], refs[-groups:]
    weights = take_ring(weight_refs, chips)
    chip_rows = mine_ref.shape[0]
    half = chip_rows // 2

    def swapped(columns):
        return jnp.concatenate([theirs_ref[half:, columns], theirs_ref[:half, columns]], axis=0)

    pieces = []
    for head in range(QH_DEV):
        columns = slice(head * HD, (head + 1) * HD)
        at = HEAD_COLS + 2 * head
        total, top = mine_ref[:, at : at + 1], mine_ref[:, at + 1 : at + 2]
        other_total, other_top = swapped(slice(at, at + 1)), swapped(slice(at + 1, at + 2))
        peak = jnp.maximum(top, other_top)
        factor, other_factor = jnp.exp(top - peak), jnp.exp(other_top - peak)
        product = mine_ref[:, columns] * factor + swapped(columns) * other_factor
        pieces.append(
            (product / (total * factor + other_total * other_factor)).astype(jnp.bfloat16)
        )
    mixed = jnp.concatenate(pieces, axis=1)
    rows = chip_rows // groups
    for slot in range(chips):
        start, total = 0, None
        for ref in weights[slot]:
            depth = ref.shape[0]
            part = jnp.dot(
                mixed[:, start : start + depth], ref[...], preferred_element_type=jnp.float32
            )
            total = part if total is None else total + part
            start += depth
        total = total.astype(jnp.bfloat16)
        for group in range(groups):
            out_refs[group][slot] = total[group * rows : (group + 1) * rows]


def sum_kernel(place, chips, groups, token_ref, *refs):
    part_refs, out_ref = refs[:groups], refs[groups]
    at, core = place_of(place)
    block = part_refs[0].shape[2]
    half = groups // 2

    def added(part, slot):
        total = part_refs[part * half][slot].astype(jnp.float32)
        for ref in part_refs[part * half + 1 : (part + 1) * half]:
            total += ref[slot].astype(jnp.float32)
        return total.astype(jnp.bfloat16)

    for even in range(2):

        @pl.when(core == even)
        def _():
            for chip in range(chips):
                slot = lax.rem(place[chip] + chips - at, chips)
                for side in range(2):
                    column = (2 * chip + side) * block
                    out_ref[:, column : column + block] = added(side ^ even, slot)


def per_device(n_context, n_tensor, hidden_rows, norm_gain, w_qkv, w_out, doc_lengths, span_order):
    chips = n_context // 2
    ring = ring_of_chips(chips)
    place = [ring.index(chip) for chip in range(chips)]
    groups = 2 * n_tensor
    rows_here, width = hidden_rows.shape
    tokens_here = rows_here * n_tensor
    block = width // n_context
    context = lax.axis_index("context")
    tensor = lax.axis_index("tensor")
    ahead = [
        (ring[i] * 2 + k, ring[(i + 1) % chips] * 2 + k) for i in range(chips) for k in range(2)
    ]
    back = [(b, a) for a, b in ahead]
    sibling = [(c, c ^ 1) for c in range(n_context)]

    same_core = [[2 * chip + k for chip in range(chips)] for k in range(2)]
    token = [doc_lengths]

    def ordered(values):
        held = lax.optimization_barrier((*values, token[0]))
        token[0] = held[-1]
        return list(held[:-1])

    class Ring:
        def __init__(self, mine):
            self.up, self.down = [mine], [mine]
            self.middle = []

        def step(self, earlier=()):
            up, down, *earlier = ordered((self.up[-1], self.down[-1], *earlier))
            if len(self.up) <= (chips - 1) // 2:
                self.up.append(lax.ppermute(up, "context", ahead))
                self.down.append(lax.ppermute(down, "context", back))
            elif chips % 2 == 0 and not self.middle:
                half = up.shape[0] // 2
                self.middle = [
                    lax.ppermute(up[:half], "context", ahead),
                    lax.ppermute(down[half:], "context", back),
                ]
            return earlier

        def done(self):
            return len(self.up) > (chips - 1) // 2 and (chips % 2 == 1 or bool(self.middle))

        def finish(self):
            while not self.done():
                self.step()
            return self.down + self.middle + self.up[:0:-1]

    def member(e, d):
        return [
            (c * n_tensor + t, (c ^ e) * n_tensor + (t - d) % n_tensor)
            for c in range(n_context)
            for t in range(n_tensor)
        ]

    qkv_ring = Ring(w_qkv)
    qkv_ring.step()
    normed = pl.pallas_call(
        functools.partial(norm_kernel, place, chips),
        out_shape=jax.ShapeDtypeStruct((2, chips, rows_here, block), jnp.bfloat16),
        in_specs=vmem_specs(2),
        out_specs=vmem_specs(1)[0],
        compiler_params=compute_params(),
        name="norm",
    )(hidden_rows, norm_gain.reshape(-1, HD))
    normed = [normed] + [
        lax.ppermute(
            normed, "tensor", [(t, (t - d) % n_tensor) for t in range(n_tensor)]
        )
        for d in range(1, n_tensor)
    ]
    normed += [lax.ppermute(rows, "context", sibling) for rows in normed]

    while len(qkv_ring.up) <= (chips - 1) // 2:
        qkv_ring.step()
    out_ring = Ring(w_out)
    out_ring.step()
    *normed, out_ring.up[-1], out_ring.down[-1] = qkv_ring.step(
        (*normed, out_ring.up[-1], out_ring.down[-1])
    )

    doc_ends = jnp.cumsum(doc_lengths)
    inside = (
        (tensor + jnp.arange(n_tensor, dtype=jnp.int32)) % n_tensor * rows_here
    )[:, None] + jnp.arange(rows_here, dtype=jnp.int32)[None, :]
    inside = inside.reshape(-1)
    both = jnp.concatenate([context * tokens_here + inside, (context ^ 1) * tokens_here + inside])
    query_orig, query_start = locate(both, span_order, doc_ends)
    half = HD // 2
    freq = rope_theta ** (-(jnp.arange(half, dtype=jnp.float32) * 2.0 / HD))
    angle = (query_orig - query_start).astype(jnp.float32)[:, None] * freq[None, :]
    cosine, sine = jnp.cos(angle), jnp.sin(angle)
    cosine = jnp.concatenate([cosine, cosine], axis=1)
    sine = jnp.concatenate([-sine, sine], axis=1)
    owner = 2 * jnp.arange(chips, dtype=jnp.int32) + context % 2
    key_rows = (owner[:, None] * tokens_here + inside[None, :]).reshape(-1).astype(jnp.int32)
    key_orig, _ = locate(key_rows, span_order, doc_ends)

    out_ring.step()
    blocks = qkv_ring.finish()
    mine, theirs, queries = pl.pallas_call(
        functools.partial(project_kernel, chips, groups),
        out_shape=[
            jax.ShapeDtypeStruct((tokens_here, 2 * HD), jnp.float32),
            jax.ShapeDtypeStruct((tokens_here, 2 * HD), jnp.float32),
            jax.ShapeDtypeStruct((2 * tokens_here, HEAD_COLS), jnp.float32),
        ],
        in_specs=vmem_specs(groups + len(blocks)),
        out_specs=vmem_specs(3),
        compiler_params=compute_params(),
        name="project",
    )(*ordered((*normed, *blocks)))
    theirs = lax.ppermute(theirs, "context", sibling)
    queries_theirs = lax.ppermute(queries, "context", sibling)
    out_ring.step()
    mine, theirs = ordered((mine, theirs))
    kv = pl.pallas_call(
        functools.partial(keys_kernel, chips),
        out_shape=jax.ShapeDtypeStruct((chips * tokens_here, 2 * HD), jnp.bfloat16),
        in_specs=vmem_specs(4),
        out_specs=vmem_specs(1)[0],
        compiler_params=compute_params(),
        name="keys",
    )(mine, theirs, cosine, sine)
    (kv,) = ordered((kv,))
    kv = lax.all_to_all(
        kv, "context", split_axis=0, concat_axis=0, axis_index_groups=same_core, tiled=True
    )
    (kv,) = ordered((kv,))

    mixed = pl.pallas_call(
        attend_kernel,
        out_shape=jax.ShapeDtypeStruct((2 * tokens_here, HEAD_COLS + HD), jnp.float32),
        in_specs=vmem_specs(8),
        out_specs=vmem_specs(1)[0],
        compiler_params=compute_params(),
        name="attend",
    )(
        queries,
        queries_theirs,
        cosine,
        sine,
        query_start[:, None],
        query_orig[:, None],
        key_orig[None, :],
        kv,
    )
    out_ring.step()
    (mixed,) = ordered((mixed,))
    mixed_theirs = lax.ppermute(mixed, "context", sibling)

    out_block = w_out.shape[1]

    while not out_ring.done():
        out_ring.step()
    blocks = out_ring.finish()
    parts = pl.pallas_call(
        functools.partial(output_kernel, chips, groups),
        out_shape=[jax.ShapeDtypeStruct((chips, rows_here, out_block), jnp.bfloat16)] * groups,
        in_specs=vmem_specs(2 + len(blocks)),
        out_specs=vmem_specs(groups),
        compiler_params=compute_params(),
        name="output",
    )(mixed, mixed_theirs, *blocks)
    arrived = []
    for e in range(2):
        for d in range(n_tensor):
            part = parts[e * n_tensor + d]
            if e or d:
                part = lax.ppermute(part, ("context", "tensor"), member(e, -d))
            arrived.append(part)
    return pl.pallas_call(
        functools.partial(sum_kernel, place, chips, groups),
        out_shape=jax.ShapeDtypeStruct((rows_here, n_context * out_block), jnp.bfloat16),
        in_specs=[pl.BlockSpec(memory_space=pl.ANY)] + vmem_specs(groups),
        out_specs=vmem_specs(1)[0],
        compiler_params=compute_params(),
        name="sum",
    )(token[0], *arrived)


def solution(mesh):
    placed = (
        P(("context", "tensor"), None),
        P(),
        P("context", "tensor"),
        P("tensor", "context"),
        P(),
        P(),
    )
    return jax.shard_map(
        functools.partial(per_device, mesh.shape["context"], mesh.shape["tensor"]),
        mesh=mesh,
        in_specs=placed,
        out_specs=P(("context", "tensor"), None),
        check_vma=False,
    )
```

```python
import functools

import jax
import jax.numpy as jnp
import numpy as np
from jax import lax
from jax.experimental import pallas as pl
from jax.experimental.pallas import tpu as pltpu
from jax.sharding import PartitionSpec as P

HD = 128
QH_DEV = 4
SPAN = 64
HEAD_COLS = QH_DEV * HD
VMEM_LIMIT = 24 * 1024 * 1024

rope_theta = 500000.0


def ring_of_chips(count):
    wide = 1
    while (wide * 2) * (wide * 2) <= count:
        wide *= 2
    tall = count // wide
    if wide < 2:
        return list(range(count))
    ring = [(z, 0) for z in range(tall)]
    for z in range(tall - 1, -1, -1):
        row = list(range(1, wide))
        ring += [(z, y) for y in (row if (tall - 1 - z) % 2 == 0 else row[::-1])]
    if (tall - 1) % 2 == 0 or wide == 2:
        return [z * wide + y for z, y in ring]
    return [z * wide + y for z, y in ring]


def vmem_specs(count):
    return [pl.BlockSpec(memory_space=pltpu.VMEM)] * count


def compute_params():
    return pltpu.CompilerParams(vmem_limit_bytes=VMEM_LIMIT)


def place_of(place):
    context = lax.axis_index("context")
    at = jnp.int32(0)
    for chip, spot in enumerate(place):
        at = jnp.where(context // 2 == chip, jnp.int32(spot), at)
    return at, context % 2


def where_kernel(
    n_tensor, rows_here, spans_ref, lengths_ref, freq_ref, cos_ref, sin_ref, low_ref, high_ref, orig_ref
):
    context, tensor = lax.axis_index("context"), lax.axis_index("tensor")
    rows = rows_here * n_tensor
    spans = rows // SPAN

    def shift(values, size):
        return lax.shift_right_logical(values, jnp.int32(size.bit_length() - 1))

    def inside_of(row):
        row = row & (rows - 1)
        turned = (tensor + shift(row, rows_here)) & (n_tensor - 1)
        return turned * rows_here + (row & (rows_here - 1))

    def initial(owner, inside):
        source = jnp.zeros_like(inside)
        for k in range(spans):
            source = jnp.where(shift(inside, SPAN) == k, spans_ref[owner * spans + k], source)
        return source * SPAN + (inside & (SPAN - 1))

    row = lax.broadcasted_iota(jnp.int32, cos_ref.shape, 0)
    inside = inside_of(row)
    orig = jnp.where(row < rows, initial(context, inside), initial(context ^ 1, inside))
    start, end = jnp.zeros_like(orig), jnp.int32(0)
    for i in range(lengths_ref.shape[0]):
        end = end + lengths_ref[i]
        start = jnp.where(orig >= end, end, start)
    low_ref[...] = start[:, :1]
    high_ref[...] = orig[:, :1]
    angle = (orig - start).astype(jnp.float32) * freq_ref[...]
    lane = lax.broadcasted_iota(jnp.int32, cos_ref.shape, 1)
    cos_ref[...] = jnp.cos(angle)
    sine = jnp.sin(angle)
    sin_ref[...] = jnp.where(lane < HD // 2, -sine, sine)
    inside = inside_of(lax.broadcasted_iota(jnp.int32, (1, rows), 1))
    for chip in range(orig_ref.shape[1] // rows):
        owner = 2 * chip + context % 2
        orig_ref[:, chip * rows : (chip + 1) * rows] = initial(owner, inside)


def norm_kernel(place, chips, hidden_ref, gain_ref, out_ref):
    at, core = place_of(place)
    wide = hidden_ref[...].astype(jnp.float32)
    meansq = jnp.mean(wide * wide, axis=-1, keepdims=True)
    scaled = wide * lax.rsqrt(meansq + 1e-05)
    lanes = gain_ref.shape[1]
    normed = jnp.concatenate(
        [
            (
                scaled[:, i * lanes : (i + 1) * lanes]
                * gain_ref[i : i + 1, :].astype(jnp.float32)
            ).astype(jnp.bfloat16)
            for i in range(gain_ref.shape[0])
        ],
        axis=1,
    )
    block = out_ref.shape[3]
    for even in range(2):

        @pl.when(core == even)
        def _():
            for chip in range(chips):
                slot = lax.rem(place[chip] + chips - at, chips)
                for side in range(2):
                    column = (2 * chip + side) * block
                    out_ref[side ^ even, slot] = normed[:, column : column + block]


def take_ring(refs, chips):
    refs = list(refs)
    if chips % 2:
        return [(ref,) for ref in refs]
    half = chips // 2
    return [(r,) for r in refs[:half]] + [tuple(refs[half : half + 2])] + [
        (r,) for r in refs[half + 2 :]
    ]


def project_kernel(chips, groups, *refs):
    rows_refs, refs = refs[:groups], refs[groups:]
    weight_refs, (mine_ref, theirs_ref, queries_ref) = refs[:-3], refs[-3:]
    half = groups // 2
    weights = take_ring(weight_refs, chips)
    total = None
    for slot in range(chips):
        rows = jnp.concatenate(
            [ref[group // half, slot] for group, ref in enumerate(rows_refs)], axis=0
        )
        start = 0
        for ref in weights[slot]:
            depth = ref.shape[0]
            part = jnp.dot(
                rows[:, start : start + depth], ref[...], preferred_element_type=jnp.float32
            )
            total = part if total is None else total + part
            start += depth
    count = mine_ref.shape[0]
    mine_ref[...] = total[:count, HEAD_COLS:]
    theirs_ref[...] = total[count:, HEAD_COLS:]
    queries_ref[...] = total[:, :HEAD_COLS]


def turn(values, cosine, sine):
    return values * cosine + pltpu.roll(values, HD // 2, 1) * sine


def keys_kernel(chips, mine_ref, theirs_ref, cosine_ref, sine_ref, out_ref):
    rows = out_ref.shape[0] // chips
    cosine, sine = cosine_ref[:rows, :], sine_ref[:rows, :]
    total = mine_ref[...] + theirs_ref[...]
    keys = turn(total[:, :HD], cosine, sine).astype(jnp.bfloat16)
    values = total[:, HD:].astype(jnp.bfloat16)
    for chip in range(chips):
        out_ref[chip * rows : (chip + 1) * rows, :HD] = keys
        out_ref[chip * rows : (chip + 1) * rows, HD:] = values


def attend_kernel(
    mine_ref,
    theirs_ref,
    cosine_ref,
    sine_ref,
    low_ref,
    high_ref,
    orig_ref,
    kv_ref,
    out_ref,
):
    keys = kv_ref[:, :HD]
    values = kv_ref[:, HD:]
    orig = orig_ref[...]
    allowed = (orig >= low_ref[...]) & (orig <= high_ref[...])
    scale = 1.0 / HD**0.5
    rows = out_ref.shape[0]
    half = rows // 2
    lane = lax.broadcasted_iota(jnp.int32, (rows, HD), 1)
    stats = jnp.zeros((rows, HD), jnp.float32)
    for head in range(QH_DEV):
        columns = slice(head * HD, (head + 1) * HD)
        query = jnp.concatenate(
            [
                mine_ref[:half, columns] + theirs_ref[half:, columns],
                mine_ref[half:, columns] + theirs_ref[:half, columns],
            ],
            axis=0,
        )
        query = turn(query, cosine_ref[...], sine_ref[...]).astype(jnp.bfloat16)
        scores = lax.dot_general(
            query, keys, (((1,), (1,)), ((), ())), preferred_element_type=jnp.float32
        )
        scores = jnp.where(allowed, scores * scale, -1e30)
        top = jnp.max(scores, axis=-1, keepdims=True)
        expo = jnp.where(allowed, jnp.exp(scores - top), 0.0)
        total = jnp.sum(expo, axis=-1, keepdims=True)
        out_ref[:, columns] = jnp.dot(
            expo.astype(jnp.bfloat16), values, preferred_element_type=jnp.float32
        )
        stats = jnp.where(lane == 2 * head, total, stats)
        stats = jnp.where(lane == 2 * head + 1, top, stats)
    out_ref[:, HEAD_COLS:] = stats


def output_kernel(groups, pieces_of, mine_ref, theirs_ref, *refs):
    weight_refs, out_refs = refs[:-groups], refs[-groups:]
    chip_rows = mine_ref.shape[0]
    half = chip_rows // 2

    def swapped(columns):
        return jnp.concatenate([theirs_ref[half:, columns], theirs_ref[:half, columns]], axis=0)

    pieces = []
    for head in range(QH_DEV):
        columns = slice(head * HD, (head + 1) * HD)
        at = HEAD_COLS + 2 * head
        total, top = mine_ref[:, at : at + 1], mine_ref[:, at + 1 : at + 2]
        other_total, other_top = swapped(slice(at, at + 1)), swapped(slice(at + 1, at + 2))
        peak = jnp.maximum(top, other_top)
        factor, other_factor = jnp.exp(top - peak), jnp.exp(other_top - peak)
        product = mine_ref[:, columns] * factor + swapped(columns) * other_factor
        pieces.append(
            (product / (total * factor + other_total * other_factor)).astype(jnp.bfloat16)
        )
    mixed = jnp.concatenate(pieces, axis=1)
    rows = chip_rows // groups
    weight_refs = iter(weight_refs)
    for slot, pieces in enumerate(pieces_of):
        start, total = 0, None
        for _ in range(pieces):
            ref = next(weight_refs)
            depth = ref.shape[0]
            part = jnp.dot(
                mixed[:, start : start + depth], ref[...], preferred_element_type=jnp.float32
            )
            total = part if total is None else total + part
            start += depth
        total = total.astype(jnp.bfloat16)
        for group in range(groups):
            out_refs[group][slot] = total[group * rows : (group + 1) * rows]


def sum_kernel(place, chips, groups, near, token_ref, *refs):
    near_refs, far_refs, out_ref = refs[:groups], refs[groups : 2 * groups], refs[2 * groups]
    at, core = place_of(place)
    block = near_refs[0].shape[2]
    half = groups // 2

    def added(part, slot):
        turn_at = lax.rem(slot + near // 2, chips)
        total = None
        for group in range(part * half, (part + 1) * half):
            rows = jnp.where(
                turn_at < near,
                near_refs[group][jnp.minimum(turn_at, near - 1)].astype(jnp.float32),
                far_refs[group][jnp.maximum(turn_at - near, 0)].astype(jnp.float32),
            )
            total = rows if total is None else total + rows
        return total.astype(jnp.bfloat16)

    for even in range(2):

        @pl.when(core == even)
        def _():
            for chip in range(chips):
                slot = lax.rem(place[chip] + chips - at, chips)
                for side in range(2):
                    column = (2 * chip + side) * block
                    out_ref[:, column : column + block] = added(side ^ even, slot)


def per_device(n_context, n_tensor, hidden_rows, norm_gain, w_qkv, w_out, doc_lengths, span_order):
    chips = n_context // 2
    ring = ring_of_chips(chips)
    place = [ring.index(chip) for chip in range(chips)]
    groups = 2 * n_tensor
    rows_here, width = hidden_rows.shape
    tokens_here = rows_here * n_tensor
    block = width // n_context
    context = lax.axis_index("context")
    tensor = lax.axis_index("tensor")
    ahead = [
        (ring[i] * 2 + k, ring[(i + 1) % chips] * 2 + k) for i in range(chips) for k in range(2)
    ]
    back = [(b, a) for a, b in ahead]
    sibling = [(c, c ^ 1) for c in range(n_context)]

    same_core = [[2 * chip + k for chip in range(chips)] for k in range(2)]
    token = [doc_lengths]

    def ordered(values):
        held = lax.optimization_barrier((*values, token[0]))
        token[0] = held[-1]
        return list(held[:-1])

    class Ring:
        def __init__(self, mine):
            self.up, self.down = [mine], [mine]
            self.middle = []

        def step(self, earlier=()):
            up, down, *earlier = ordered((self.up[-1], self.down[-1], *earlier))
            if len(self.up) <= (chips - 1) // 2:
                self.up.append(lax.ppermute(up, "context", ahead))
                self.down.append(lax.ppermute(down, "context", back))
            elif chips % 2 == 0 and not self.middle:
                half = up.shape[0] // 2
                self.middle = [
                    lax.ppermute(up[:half], "context", ahead),
                    lax.ppermute(down[half:], "context", back),
                ]
            return earlier

        def done(self):
            return len(self.up) > (chips - 1) // 2 and (chips % 2 == 1 or bool(self.middle))

        def finish(self):
            while not self.done():
                self.step()
            return self.down + self.middle + self.up[:0:-1]

        def block(self, slot):
            slot %= chips
            if chips % 2 == 0 and slot == chips // 2:
                return tuple(self.middle)
            return (self.down[slot] if slot <= chips // 2 else self.up[chips - slot],)

    def member(e, d):
        return [
            (c * n_tensor + t, (c ^ e) * n_tensor + (t - d) % n_tensor)
            for c in range(n_context)
            for t in range(n_tensor)
        ]

    smem, vmem = pl.BlockSpec(memory_space=pltpu.SMEM), pl.BlockSpec(memory_space=pltpu.VMEM)
    freq = rope_theta ** (-(np.arange(HD // 2, dtype=np.float64) * 2.0 / HD))
    freq = np.concatenate([freq, freq]).astype(np.float32)[None, :]
    table = jax.ShapeDtypeStruct((2 * tokens_here, HD), jnp.float32)
    bound = jax.ShapeDtypeStruct((2 * tokens_here, 1), jnp.int32)
    cosine, sine, query_start, query_orig, key_orig = pl.pallas_call(
        functools.partial(where_kernel, n_tensor, rows_here),
        out_shape=[
            table,
            table,
            bound,
            bound,
            jax.ShapeDtypeStruct((1, chips * tokens_here), jnp.int32),
        ],
        in_specs=[smem, smem, vmem],
        out_specs=vmem_specs(5),
        compiler_params=compute_params(),
        name="where",
    )(span_order, doc_lengths, jnp.asarray(freq))

    qkv_ring = Ring(w_qkv)
    qkv_ring.step()
    normed = pl.pallas_call(
        functools.partial(norm_kernel, place, chips),
        out_shape=jax.ShapeDtypeStruct((2, chips, rows_here, block), jnp.bfloat16),
        in_specs=vmem_specs(2),
        out_specs=vmem_specs(1)[0],
        compiler_params=compute_params(),
        name="norm",
    )(hidden_rows, norm_gain.reshape(-1, HD))
    normed = [normed] + [
        lax.ppermute(
            normed, "tensor", [(t, (t - d) % n_tensor) for t in range(n_tensor)]
        )
        for d in range(1, n_tensor)
    ]
    normed += [lax.ppermute(rows, "context", sibling) for rows in normed]

    qkv_ring.step()
    qkv_ring.step()
    normed = qkv_ring.step(normed)
    while not qkv_ring.done():
        qkv_ring.step()

    out_ring = Ring(w_out)
    out_ring.step()
    blocks = qkv_ring.finish()
    mine, theirs, queries = pl.pallas_call(
        functools.partial(project_kernel, chips, groups),
        out_shape=[
            jax.ShapeDtypeStruct((tokens_here, 2 * HD), jnp.float32),
            jax.ShapeDtypeStruct((tokens_here, 2 * HD), jnp.float32),
            jax.ShapeDtypeStruct((2 * tokens_here, HEAD_COLS), jnp.float32),
        ],
        in_specs=vmem_specs(groups + len(blocks)),
        out_specs=vmem_specs(3),
        compiler_params=compute_params(),
        name="project",
    )(*ordered((*normed, *blocks)))
    theirs = lax.ppermute(theirs, "context", sibling)
    queries_theirs = lax.ppermute(queries, "context", sibling)
    out_ring.step()
    mine, theirs = ordered((mine, theirs))
    kv = pl.pallas_call(
        functools.partial(keys_kernel, chips),
        out_shape=jax.ShapeDtypeStruct((chips * tokens_here, 2 * HD), jnp.bfloat16),
        in_specs=vmem_specs(4),
        out_specs=vmem_specs(1)[0],
        compiler_params=compute_params(),
        name="keys",
    )(mine, theirs, cosine, sine)
    (kv,) = ordered((kv,))
    kv = lax.all_to_all(
        kv, "context", split_axis=0, concat_axis=0, axis_index_groups=same_core, tiled=True
    )
    out_ring.step()
    (kv,) = ordered((kv,))

    mixed = pl.pallas_call(
        attend_kernel,
        out_shape=jax.ShapeDtypeStruct((2 * tokens_here, HEAD_COLS + HD), jnp.float32),
        in_specs=vmem_specs(8),
        out_specs=vmem_specs(1)[0],
        compiler_params=compute_params(),
        name="attend",
    )(
        queries,
        queries_theirs,
        cosine,
        sine,
        query_start,
        query_orig,
        key_orig,
        kv,
    )
    (mixed,) = ordered((mixed,))
    mixed_theirs = lax.ppermute(mixed, "context", sibling)

    out_block = w_out.shape[1]

    def output(slots, name):
        blocks = [out_ring.block(slot) for slot in slots]
        flat = [piece for pieces in blocks for piece in pieces]
        parts = pl.pallas_call(
            functools.partial(output_kernel, groups, [len(pieces) for pieces in blocks]),
            out_shape=[jax.ShapeDtypeStruct((len(slots), rows_here, out_block), jnp.bfloat16)]
            * groups,
            in_specs=vmem_specs(2 + len(flat)),
            out_specs=vmem_specs(groups),
            compiler_params=compute_params(),
            name=name,
        )(mixed, mixed_theirs, *flat)
        parts = ordered(parts)
        arrived = []
        for e in range(2):
            for d in range(n_tensor):
                part = parts[e * n_tensor + d]
                if e or d:
                    part = lax.ppermute(part, ("context", "tensor"), member(e, -d))
                arrived.append(part)
        return arrived

    reach = max(chips // 2 - 2, 0)
    while len(out_ring.up) <= reach:
        out_ring.step()
    near = 2 * reach + 1
    arrived = output(list(range(-reach, reach + 1)), "output_near")
    while not out_ring.done():
        out_ring.step()
    arrived += output(list(range(reach + 1, chips - reach)), "output_far")
    return pl.pallas_call(
        functools.partial(sum_kernel, place, chips, groups, near),
        out_shape=jax.ShapeDtypeStruct((rows_here, n_context * out_block), jnp.bfloat16),
        in_specs=[pl.BlockSpec(memory_space=pl.ANY)] + vmem_specs(2 * groups),
        out_specs=vmem_specs(1)[0],
        compiler_params=compute_params(),
        name="sum",
    )(token[0], *arrived)


def solution(mesh):
    placed = (
        P(("context", "tensor"), None),
        P(),
        P("context", "tensor"),
        P("tensor", "context"),
        P(),
        P(),
    )
    return jax.shard_map(
        functools.partial(per_device, mesh.shape["context"], mesh.shape["tensor"]),
        mesh=mesh,
        in_specs=placed,
        out_specs=P(("context", "tensor"), None),
        check_vma=False,
    )
```

```python
import functools

import jax
import jax.numpy as jnp
import numpy as np
from jax import lax
from jax.experimental import pallas as pl
from jax.experimental.pallas import tpu as pltpu
from jax.sharding import PartitionSpec as P

HD = 128
QH_DEV = 4
SPAN = 64
HEAD_COLS = QH_DEV * HD
VMEM_LIMIT = 24 * 1024 * 1024

rope_theta = 500000.0


def ring_of_chips(count):
    wide = 1
    while (wide * 2) * (wide * 2) <= count:
        wide *= 2
    tall = count // wide
    if wide < 2:
        return list(range(count))
    ring = [(z, 0) for z in range(tall)]
    for z in range(tall - 1, -1, -1):
        row = list(range(1, wide))
        ring += [(z, y) for y in (row if (tall - 1 - z) % 2 == 0 else row[::-1])]
    if (tall - 1) % 2 == 0 or wide == 2:
        return [z * wide + y for z, y in ring]
    return [z * wide + y for z, y in ring]


def vmem_specs(count):
    return [pl.BlockSpec(memory_space=pltpu.VMEM)] * count


def compute_params():
    return pltpu.CompilerParams(vmem_limit_bytes=VMEM_LIMIT)


def place_of(place):
    context = lax.axis_index("context")
    at = jnp.int32(0)
    for chip, spot in enumerate(place):
        at = jnp.where(context // 2 == chip, jnp.int32(spot), at)
    return at, context % 2


def where_kernel(
    ring,
    place,
    n_tensor,
    rows_here,
    spans_ref,
    lengths_ref,
    freq_ref,
    cos_ref,
    sin_ref,
    low_ref,
    high_ref,
    orig_ref,
):
    context, tensor = lax.axis_index("context"), lax.axis_index("tensor")
    rows = rows_here * n_tensor
    spans = rows // SPAN

    def shift(values, size):
        return lax.shift_right_logical(values, jnp.int32(size.bit_length() - 1))

    def inside_of(row):
        row = row & (rows - 1)
        turned = (tensor + shift(row, rows_here)) & (n_tensor - 1)
        return turned * rows_here + (row & (rows_here - 1))

    def initial(owner, inside):
        source = jnp.zeros_like(inside)
        for k in range(spans):
            source = jnp.where(shift(inside, SPAN) == k, spans_ref[owner * spans + k], source)
        return source * SPAN + (inside & (SPAN - 1))

    row = lax.broadcasted_iota(jnp.int32, cos_ref.shape, 0)
    inside = inside_of(row)
    orig = jnp.where(row < rows, initial(context, inside), initial(context ^ 1, inside))
    start, end = jnp.zeros_like(orig), jnp.int32(0)
    for i in range(lengths_ref.shape[0]):
        end = end + lengths_ref[i]
        start = jnp.where(orig >= end, end, start)
    low_ref[...] = start[:, :1]
    high_ref[...] = orig[:, :1]
    angle = (orig - start).astype(jnp.float32) * freq_ref[...]
    lane = lax.broadcasted_iota(jnp.int32, cos_ref.shape, 1)
    cos_ref[...] = jnp.cos(angle)
    sine = jnp.sin(angle)
    sin_ref[...] = jnp.where(lane < HD // 2, -sine, sine)
    inside = inside_of(lax.broadcasted_iota(jnp.int32, (1, rows), 1))
    at, core = place_of(place)
    for slot in range(len(ring)):
        spot = lax.rem(at + slot, len(ring))
        chip = jnp.int32(0)
        for i, at_spot in enumerate(ring):
            chip = jnp.where(spot == i, jnp.int32(at_spot), chip)
        owner = 2 * chip + core
        orig_ref[:, slot * rows : (slot + 1) * rows] = initial(owner, inside)


def norm_kernel(place, chips, hidden_ref, gain_ref, out_ref):
    at, core = place_of(place)
    wide = hidden_ref[...].astype(jnp.float32)
    meansq = jnp.mean(wide * wide, axis=-1, keepdims=True)
    scaled = wide * lax.rsqrt(meansq + 1e-05)
    lanes = gain_ref.shape[1]
    normed = jnp.concatenate(
        [
            (
                scaled[:, i * lanes : (i + 1) * lanes]
                * gain_ref[i : i + 1, :].astype(jnp.float32)
            ).astype(jnp.bfloat16)
            for i in range(gain_ref.shape[0])
        ],
        axis=1,
    )
    block = out_ref.shape[3]
    for even in range(2):

        @pl.when(core == even)
        def _():
            for chip in range(chips):
                slot = lax.rem(place[chip] + chips - at, chips)
                for side in range(2):
                    column = (2 * chip + side) * block
                    out_ref[side ^ even, slot] = normed[:, column : column + block]


def take_ring(refs, chips):
    refs = list(refs)
    if chips % 2:
        return [(ref,) for ref in refs]
    half = chips // 2
    return [(r,) for r in refs[:half]] + [tuple(refs[half : half + 2])] + [
        (r,) for r in refs[half + 2 :]
    ]


def project_kernel(chips, groups, *refs):
    rows_refs, refs = refs[:groups], refs[groups:]
    weight_refs, (mine_ref, theirs_ref, queries_ref) = refs[:-3], refs[-3:]
    half = groups // 2
    weights = take_ring(weight_refs, chips)
    total = None
    for slot in range(chips):
        rows = jnp.concatenate(
            [ref[group // half, slot] for group, ref in enumerate(rows_refs)], axis=0
        )
        start = 0
        for ref in weights[slot]:
            depth = ref.shape[0]
            part = jnp.dot(
                rows[:, start : start + depth], ref[...], preferred_element_type=jnp.float32
            )
            total = part if total is None else total + part
            start += depth
    count = mine_ref.shape[0]
    mine_ref[...] = total[:count, HEAD_COLS:]
    theirs_ref[...] = total[count:, HEAD_COLS:]
    queries_ref[...] = total[:, :HEAD_COLS]


def turn(values, cosine, sine):
    return values * cosine + pltpu.roll(values, HD // 2, 1) * sine


def keys_kernel(mine_ref, theirs_ref, cosine_ref, sine_ref, out_ref):
    rows = out_ref.shape[0]
    total = mine_ref[...] + theirs_ref[...]
    out_ref[:, :HD] = turn(total[:, :HD], cosine_ref[:rows, :], sine_ref[:rows, :]).astype(
        jnp.bfloat16
    )
    out_ref[:, HD:] = total[:, HD:].astype(jnp.bfloat16)


def attend_kernel(
    mine_ref,
    theirs_ref,
    cosine_ref,
    sine_ref,
    low_ref,
    high_ref,
    orig_ref,
    *refs,
):
    block_refs, (out_ref, keys_ref, values_ref) = refs[:-3], refs[-3:]
    start = 0
    for ref in block_refs:
        keys_ref[start : start + ref.shape[0], :] = ref[:, :HD]
        values_ref[start : start + ref.shape[0], :] = ref[:, HD:]
        start += ref.shape[0]
    keys = keys_ref[...]
    values = values_ref[...]
    orig = orig_ref[...]
    allowed = (orig >= low_ref[...]) & (orig <= high_ref[...])
    scale = 1.0 / HD**0.5
    rows = out_ref.shape[0]
    half = rows // 2
    lane = lax.broadcasted_iota(jnp.int32, (rows, HD), 1)
    stats = jnp.zeros((rows, HD), jnp.float32)
    for head in range(QH_DEV):
        columns = slice(head * HD, (head + 1) * HD)
        query = jnp.concatenate(
            [
                mine_ref[:half, columns] + theirs_ref[half:, columns],
                mine_ref[half:, columns] + theirs_ref[:half, columns],
            ],
            axis=0,
        )
        query = turn(query, cosine_ref[...], sine_ref[...]).astype(jnp.bfloat16)
        scores = lax.dot_general(
            query, keys, (((1,), (1,)), ((), ())), preferred_element_type=jnp.float32
        )
        scores = jnp.where(allowed, scores * scale, -1e30)
        top = jnp.max(scores, axis=-1, keepdims=True)
        expo = jnp.where(allowed, jnp.exp(scores - top), 0.0)
        total = jnp.sum(expo, axis=-1, keepdims=True)
        out_ref[:, columns] = jnp.dot(
            expo.astype(jnp.bfloat16), values, preferred_element_type=jnp.float32
        )
        stats = jnp.where(lane == 2 * head, total, stats)
        stats = jnp.where(lane == 2 * head + 1, top, stats)
    out_ref[:, HEAD_COLS:] = stats


def output_kernel(groups, pieces_of, mine_ref, theirs_ref, *refs):
    weight_refs, out_refs = refs[:-groups], refs[-groups:]
    chip_rows = mine_ref.shape[0]
    half = chip_rows // 2

    def swapped(columns):
        return jnp.concatenate([theirs_ref[half:, columns], theirs_ref[:half, columns]], axis=0)

    pieces = []
    for head in range(QH_DEV):
        columns = slice(head * HD, (head + 1) * HD)
        at = HEAD_COLS + 2 * head
        total, top = mine_ref[:, at : at + 1], mine_ref[:, at + 1 : at + 2]
        other_total, other_top = swapped(slice(at, at + 1)), swapped(slice(at + 1, at + 2))
        peak = jnp.maximum(top, other_top)
        factor, other_factor = jnp.exp(top - peak), jnp.exp(other_top - peak)
        product = mine_ref[:, columns] * factor + swapped(columns) * other_factor
        pieces.append(
            (product / (total * factor + other_total * other_factor)).astype(jnp.bfloat16)
        )
    mixed = jnp.concatenate(pieces, axis=1)
    rows = chip_rows // groups
    weight_refs = iter(weight_refs)
    for slot, pieces in enumerate(pieces_of):
        start, total = 0, None
        for _ in range(pieces):
            ref = next(weight_refs)
            depth = ref.shape[0]
            part = jnp.dot(
                mixed[:, start : start + depth], ref[...], preferred_element_type=jnp.float32
            )
            total = part if total is None else total + part
            start += depth
        total = total.astype(jnp.bfloat16)
        for group in range(groups):
            out_refs[group][slot] = total[group * rows : (group + 1) * rows]


def sum_kernel(place, chips, groups, near, token_ref, *refs):
    near_refs, far_refs, out_ref = refs[:groups], refs[groups : 2 * groups], refs[2 * groups]
    at, core = place_of(place)
    block = near_refs[0].shape[2]
    half = groups // 2

    def added(part, slot):
        turn_at = lax.rem(slot + near // 2, chips)
        total = None
        for group in range(part * half, (part + 1) * half):
            rows = jnp.where(
                turn_at < near,
                near_refs[group][jnp.minimum(turn_at, near - 1)].astype(jnp.float32),
                far_refs[group][jnp.maximum(turn_at - near, 0)].astype(jnp.float32),
            )
            total = rows if total is None else total + rows
        return total.astype(jnp.bfloat16)

    for even in range(2):

        @pl.when(core == even)
        def _():
            for chip in range(chips):
                slot = lax.rem(place[chip] + chips - at, chips)
                for side in range(2):
                    column = (2 * chip + side) * block
                    out_ref[:, column : column + block] = added(side ^ even, slot)


def per_device(n_context, n_tensor, hidden_rows, norm_gain, w_qkv, w_out, doc_lengths, span_order):
    chips = n_context // 2
    ring = ring_of_chips(chips)
    place = [ring.index(chip) for chip in range(chips)]
    groups = 2 * n_tensor
    rows_here, width = hidden_rows.shape
    tokens_here = rows_here * n_tensor
    block = width // n_context
    context = lax.axis_index("context")
    tensor = lax.axis_index("tensor")
    ahead = [
        (ring[i] * 2 + k, ring[(i + 1) % chips] * 2 + k) for i in range(chips) for k in range(2)
    ]
    back = [(b, a) for a, b in ahead]
    sibling = [(c, c ^ 1) for c in range(n_context)]

    token = [doc_lengths]

    def ordered(values):
        held = lax.optimization_barrier((*values, token[0]))
        token[0] = held[-1]
        return list(held[:-1])

    class Ring:
        def __init__(self, mine):
            self.up, self.down = [mine], [mine]
            self.middle = []

        def step(self, earlier=()):
            up, down, *earlier = ordered((self.up[-1], self.down[-1], *earlier))
            if len(self.up) <= (chips - 1) // 2:
                self.up.append(lax.ppermute(up, "context", ahead))
                self.down.append(lax.ppermute(down, "context", back))
            elif chips % 2 == 0 and not self.middle:
                half = up.shape[0] // 2
                self.middle = [
                    lax.ppermute(up[:half], "context", ahead),
                    lax.ppermute(down[half:], "context", back),
                ]
            return earlier

        def done(self):
            return len(self.up) > (chips - 1) // 2 and (chips % 2 == 1 or bool(self.middle))

        def finish(self):
            while not self.done():
                self.step()
            return self.down + self.middle + self.up[:0:-1]

        def block(self, slot):
            slot %= chips
            if chips % 2 == 0 and slot == chips // 2:
                return tuple(self.middle)
            return (self.down[slot] if slot <= chips // 2 else self.up[chips - slot],)

    def member(e, d):
        return [
            (c * n_tensor + t, (c ^ e) * n_tensor + (t - d) % n_tensor)
            for c in range(n_context)
            for t in range(n_tensor)
        ]

    smem, vmem = pl.BlockSpec(memory_space=pltpu.SMEM), pl.BlockSpec(memory_space=pltpu.VMEM)
    freq = rope_theta ** (-(np.arange(HD // 2, dtype=np.float64) * 2.0 / HD))
    freq = np.concatenate([freq, freq]).astype(np.float32)[None, :]
    table = jax.ShapeDtypeStruct((2 * tokens_here, HD), jnp.float32)
    bound = jax.ShapeDtypeStruct((2 * tokens_here, 1), jnp.int32)
    cosine, sine, query_start, query_orig, key_orig = pl.pallas_call(
        functools.partial(where_kernel, ring, place, n_tensor, rows_here),
        out_shape=[
            table,
            table,
            bound,
            bound,
            jax.ShapeDtypeStruct((1, chips * tokens_here), jnp.int32),
        ],
        in_specs=[smem, smem, vmem],
        out_specs=vmem_specs(5),
        compiler_params=compute_params(),
        name="where",
    )(span_order, doc_lengths, jnp.asarray(freq))

    qkv_ring = Ring(w_qkv)
    qkv_ring.step()
    normed = pl.pallas_call(
        functools.partial(norm_kernel, place, chips),
        out_shape=jax.ShapeDtypeStruct((2, chips, rows_here, block), jnp.bfloat16),
        in_specs=vmem_specs(2),
        out_specs=vmem_specs(1)[0],
        compiler_params=compute_params(),
        name="norm",
    )(hidden_rows, norm_gain.reshape(-1, HD))
    normed = [normed] + [
        lax.ppermute(
            normed, "tensor", [(t, (t - d) % n_tensor) for t in range(n_tensor)]
        )
        for d in range(1, n_tensor)
    ]
    normed += [lax.ppermute(rows, "context", sibling) for rows in normed]

    qkv_ring.step()
    cosine, sine, query_start, query_orig, key_orig = ordered(
        (cosine, sine, query_start, query_orig, key_orig)
    )
    qkv_ring.step()
    normed = qkv_ring.step(normed)
    while not qkv_ring.done():
        qkv_ring.step()

    out_ring = Ring(w_out)
    out_ring.step()
    blocks = qkv_ring.finish()
    mine, theirs, queries = pl.pallas_call(
        functools.partial(project_kernel, chips, groups),
        out_shape=[
            jax.ShapeDtypeStruct((tokens_here, 2 * HD), jnp.float32),
            jax.ShapeDtypeStruct((tokens_here, 2 * HD), jnp.float32),
            jax.ShapeDtypeStruct((2 * tokens_here, HEAD_COLS), jnp.float32),
        ],
        in_specs=vmem_specs(groups + len(blocks)),
        out_specs=vmem_specs(3),
        compiler_params=compute_params(),
        name="project",
    )(*ordered((*normed, *blocks)))
    theirs = lax.ppermute(theirs, "context", sibling)
    queries_theirs = lax.ppermute(queries, "context", sibling)
    mine, theirs = ordered((mine, theirs))
    out_ring.step()
    kv = pl.pallas_call(
        keys_kernel,
        out_shape=jax.ShapeDtypeStruct((tokens_here, 2 * HD), jnp.bfloat16),
        in_specs=vmem_specs(4),
        out_specs=vmem_specs(1)[0],
        compiler_params=compute_params(),
        name="keys",
    )(mine, theirs, cosine, sine)
    kv_ring = Ring(kv)
    kv_ring.step()
    kv_ring.step()
    out_ring.step()
    while not kv_ring.done():
        kv_ring.step()
    while not out_ring.done():
        out_ring.step()
    kv_blocks = ordered(kv_ring.finish())

    mixed = pl.pallas_call(
        attend_kernel,
        out_shape=jax.ShapeDtypeStruct((2 * tokens_here, HEAD_COLS + HD), jnp.float32),
        in_specs=vmem_specs(7 + len(kv_blocks)),
        out_specs=vmem_specs(1)[0],
        scratch_shapes=[pltpu.VMEM((chips * tokens_here, HD), jnp.bfloat16)] * 2,
        compiler_params=compute_params(),
        name="attend",
    )(
        queries,
        queries_theirs,
        cosine,
        sine,
        query_start,
        query_orig,
        key_orig,
        *kv_blocks,
    )
    (mixed,) = ordered((mixed,))
    mixed_theirs = lax.ppermute(mixed, "context", sibling)

    out_block = w_out.shape[1]

    def output(slots, name):
        blocks = [out_ring.block(slot) for slot in slots]
        flat = [piece for pieces in blocks for piece in pieces]
        parts = pl.pallas_call(
            functools.partial(output_kernel, groups, [len(pieces) for pieces in blocks]),
            out_shape=[jax.ShapeDtypeStruct((len(slots), rows_here, out_block), jnp.bfloat16)]
            * groups,
            in_specs=vmem_specs(2 + len(flat)),
            out_specs=vmem_specs(groups),
            compiler_params=compute_params(),
            name=name,
        )(mixed, mixed_theirs, *flat)
        parts = ordered(parts)
        arrived = []
        for e in range(2):
            for d in range(n_tensor):
                part = parts[e * n_tensor + d]
                if e or d:
                    part = lax.ppermute(part, ("context", "tensor"), member(e, -d))
                arrived.append(part)
        return arrived

    reach = (chips - 1) // 2
    near = 2 * reach + 1
    arrived = output(list(range(-reach, reach + 1)), "output_near")
    if near < chips:
        arrived += output(list(range(reach + 1, chips - reach)), "output_far")
    return pl.pallas_call(
        functools.partial(sum_kernel, place, chips, groups, near),
        out_shape=jax.ShapeDtypeStruct((rows_here, n_context * out_block), jnp.bfloat16),
        in_specs=[pl.BlockSpec(memory_space=pl.ANY)] + vmem_specs(2 * groups),
        out_specs=vmem_specs(1)[0],
        compiler_params=compute_params(),
        name="sum",
    )(token[0], *arrived)


def solution(mesh):
    placed = (
        P(("context", "tensor"), None),
        P(),
        P("context", "tensor"),
        P("tensor", "context"),
        P(),
        P(),
    )
    return jax.shard_map(
        functools.partial(per_device, mesh.shape["context"], mesh.shape["tensor"]),
        mesh=mesh,
        in_specs=placed,
        out_specs=P(("context", "tensor"), None),
        check_vma=False,
    )
```

```python
import functools

import jax
import jax.numpy as jnp
import numpy as np
from jax import lax
from jax.experimental import pallas as pl
from jax.experimental.pallas import tpu as pltpu
from jax.sharding import PartitionSpec as P

HD = 128
QH_DEV = 4
SPAN = 64
HEAD_COLS = QH_DEV * HD
VMEM_LIMIT = 24 * 1024 * 1024

rope_theta = 500000.0


def ring_of_chips(count):
    wide = 1
    while (wide * 2) * (wide * 2) <= count:
        wide *= 2
    tall = count // wide
    if wide < 2:
        return list(range(count))
    ring = [(z, 0) for z in range(tall)]
    for z in range(tall - 1, -1, -1):
        row = list(range(1, wide))
        ring += [(z, y) for y in (row if (tall - 1 - z) % 2 == 0 else row[::-1])]
    if (tall - 1) % 2 == 0 or wide == 2:
        return [z * wide + y for z, y in ring]
    return [z * wide + y for z, y in ring]


def vmem_specs(count):
    return [pl.BlockSpec(memory_space=pltpu.VMEM)] * count


def compute_params():
    return pltpu.CompilerParams(vmem_limit_bytes=VMEM_LIMIT)


def place_of(place):
    context = lax.axis_index("context")
    at = jnp.int32(0)
    for chip, spot in enumerate(place):
        at = jnp.where(context // 2 == chip, jnp.int32(spot), at)
    return at, context % 2


def where_kernel(
    n_tensor, rows_here, spans_ref, lengths_ref, freq_ref, cos_ref, sin_ref, low_ref, high_ref, orig_ref
):
    context, tensor = lax.axis_index("context"), lax.axis_index("tensor")
    rows = rows_here * n_tensor
    spans = rows // SPAN

    def shift(values, size):
        return lax.shift_right_logical(values, jnp.int32(size.bit_length() - 1))

    def inside_of(row):
        row = row & (rows - 1)
        turned = (tensor + shift(row, rows_here)) & (n_tensor - 1)
        return turned * rows_here + (row & (rows_here - 1))

    def initial(owner, inside):
        source = jnp.zeros_like(inside)
        for k in range(spans):
            source = jnp.where(shift(inside, SPAN) == k, spans_ref[owner * spans + k], source)
        return source * SPAN + (inside & (SPAN - 1))

    row = lax.broadcasted_iota(jnp.int32, cos_ref.shape, 0)
    inside = inside_of(row)
    orig = jnp.where(row < rows, initial(context, inside), initial(context ^ 1, inside))
    start, end = jnp.zeros_like(orig), jnp.int32(0)
    for i in range(lengths_ref.shape[0]):
        end = end + lengths_ref[i]
        start = jnp.where(orig >= end, end, start)
    low_ref[...] = start[:, :1]
    high_ref[...] = orig[:, :1]
    angle = (orig - start).astype(jnp.float32) * freq_ref[...]
    lane = lax.broadcasted_iota(jnp.int32, cos_ref.shape, 1)
    cos_ref[...] = jnp.cos(angle)
    sine = jnp.sin(angle)
    sin_ref[...] = jnp.where(lane < HD // 2, -sine, sine)
    inside = inside_of(lax.broadcasted_iota(jnp.int32, (1, rows), 1))
    for chip in range(orig_ref.shape[1] // rows):
        owner = 2 * chip + context % 2
        orig_ref[:, chip * rows : (chip + 1) * rows] = initial(owner, inside)


def norm_kernel(place, chips, hidden_ref, gain_ref, out_ref):
    at, core = place_of(place)
    wide = hidden_ref[...].astype(jnp.float32)
    meansq = jnp.mean(wide * wide, axis=-1, keepdims=True)
    scaled = wide * lax.rsqrt(meansq + 1e-05)
    lanes = gain_ref.shape[1]
    normed = jnp.concatenate(
        [
            (
                scaled[:, i * lanes : (i + 1) * lanes]
                * gain_ref[i : i + 1, :].astype(jnp.float32)
            ).astype(jnp.bfloat16)
            for i in range(gain_ref.shape[0])
        ],
        axis=1,
    )
    block = out_ref.shape[3]
    for even in range(2):

        @pl.when(core == even)
        def _():
            for chip in range(chips):
                slot = lax.rem(place[chip] + chips - at, chips)
                for side in range(2):
                    column = (2 * chip + side) * block
                    out_ref[side ^ even, slot] = normed[:, column : column + block]


def take_ring(refs, chips):
    refs = list(refs)
    if chips % 2:
        return [(ref,) for ref in refs]
    half = chips // 2
    return [(r,) for r in refs[:half]] + [tuple(refs[half : half + 2])] + [
        (r,) for r in refs[half + 2 :]
    ]


def project_kernel(chips, groups, *refs):
    rows_refs, refs = refs[:groups], refs[groups:]
    weight_refs, (mine_ref, theirs_ref, queries_ref) = refs[:-3], refs[-3:]
    half = groups // 2
    weights = take_ring(weight_refs, chips)
    total = None
    for slot in range(chips):
        rows = jnp.concatenate(
            [ref[group // half, slot] for group, ref in enumerate(rows_refs)], axis=0
        )
        start = 0
        for ref in weights[slot]:
            depth = ref.shape[0]
            part = jnp.dot(
                rows[:, start : start + depth], ref[...], preferred_element_type=jnp.float32
            )
            total = part if total is None else total + part
            start += depth
    count = mine_ref.shape[0]
    mine_ref[...] = total[:count, HEAD_COLS:]
    theirs_ref[...] = total[count:, HEAD_COLS:]
    queries_ref[...] = total[:, :HEAD_COLS]


def turn(values, cosine, sine):
    return values * cosine + pltpu.roll(values, HD // 2, 1) * sine


def keys_kernel(chips, mine_ref, theirs_ref, cosine_ref, sine_ref, out_ref):
    rows = out_ref.shape[0] // chips
    cosine, sine = cosine_ref[:rows, :], sine_ref[:rows, :]
    total = mine_ref[...] + theirs_ref[...]
    keys = turn(total[:, :HD], cosine, sine).astype(jnp.bfloat16)
    values = total[:, HD:].astype(jnp.bfloat16)
    for chip in range(chips):
        out_ref[chip * rows : (chip + 1) * rows, :HD] = keys
        out_ref[chip * rows : (chip + 1) * rows, HD:] = values


def attend_kernel(
    mine_ref,
    theirs_ref,
    cosine_ref,
    sine_ref,
    low_ref,
    high_ref,
    orig_ref,
    kv_ref,
    out_ref,
):
    keys = kv_ref[:, :HD]
    values = kv_ref[:, HD:]
    orig = orig_ref[...]
    allowed = (orig >= low_ref[...]) & (orig <= high_ref[...])
    scale = 1.0 / HD**0.5
    rows = out_ref.shape[0]
    half = rows // 2
    lane = lax.broadcasted_iota(jnp.int32, (rows, HD), 1)
    stats = jnp.zeros((rows, HD), jnp.float32)
    for head in range(QH_DEV):
        columns = slice(head * HD, (head + 1) * HD)
        query = jnp.concatenate(
            [
                mine_ref[:half, columns] + theirs_ref[half:, columns],
                mine_ref[half:, columns] + theirs_ref[:half, columns],
            ],
            axis=0,
        )
        query = turn(query, cosine_ref[...], sine_ref[...]).astype(jnp.bfloat16)
        scores = lax.dot_general(
            query, keys, (((1,), (1,)), ((), ())), preferred_element_type=jnp.float32
        )
        scores = jnp.where(allowed, scores * scale, -1e30)
        top = jnp.max(scores, axis=-1, keepdims=True)
        expo = jnp.where(allowed, jnp.exp(scores - top), 0.0)
        total = jnp.sum(expo, axis=-1, keepdims=True)
        out_ref[:, columns] = jnp.dot(
            expo.astype(jnp.bfloat16), values, preferred_element_type=jnp.float32
        )
        stats = jnp.where(lane == 2 * head, total, stats)
        stats = jnp.where(lane == 2 * head + 1, top, stats)
    out_ref[:, HEAD_COLS:] = stats


def output_kernel(groups, pieces_of, mine_ref, theirs_ref, *refs):
    weight_refs, out_refs = refs[:-groups], refs[-groups:]
    chip_rows = mine_ref.shape[0]
    half = chip_rows // 2

    def swapped(columns):
        return jnp.concatenate([theirs_ref[half:, columns], theirs_ref[:half, columns]], axis=0)

    pieces = []
    for head in range(QH_DEV):
        columns = slice(head * HD, (head + 1) * HD)
        at = HEAD_COLS + 2 * head
        total, top = mine_ref[:, at : at + 1], mine_ref[:, at + 1 : at + 2]
        other_total, other_top = swapped(slice(at, at + 1)), swapped(slice(at + 1, at + 2))
        peak = jnp.maximum(top, other_top)
        factor, other_factor = jnp.exp(top - peak), jnp.exp(other_top - peak)
        product = mine_ref[:, columns] * factor + swapped(columns) * other_factor
        pieces.append(
            (product / (total * factor + other_total * other_factor)).astype(jnp.bfloat16)
        )
    mixed = jnp.concatenate(pieces, axis=1)
    rows = chip_rows // groups
    weight_refs = iter(weight_refs)
    for slot, pieces in enumerate(pieces_of):
        start, total = 0, None
        for _ in range(pieces):
            ref = next(weight_refs)
            depth = ref.shape[0]
            part = jnp.dot(
                mixed[:, start : start + depth], ref[...], preferred_element_type=jnp.float32
            )
            total = part if total is None else total + part
            start += depth
        total = total.astype(jnp.bfloat16)
        for group in range(groups):
            out_refs[group][slot] = total[group * rows : (group + 1) * rows]


def sum_kernel(place, chips, groups, near, token_ref, *refs):
    near_refs, far_refs, out_ref = refs[:groups], refs[groups : 2 * groups], refs[2 * groups]
    at, core = place_of(place)
    block = near_refs[0].shape[2]
    half = groups // 2

    def added(part, slot):
        turn_at = lax.rem(slot + near // 2, chips)
        total = None
        for group in range(part * half, (part + 1) * half):
            rows = jnp.where(
                turn_at < near,
                near_refs[group][jnp.minimum(turn_at, near - 1)].astype(jnp.float32),
                far_refs[group][jnp.maximum(turn_at - near, 0)].astype(jnp.float32),
            )
            total = rows if total is None else total + rows
        return total.astype(jnp.bfloat16)

    for even in range(2):

        @pl.when(core == even)
        def _():
            for chip in range(chips):
                slot = lax.rem(place[chip] + chips - at, chips)
                for side in range(2):
                    column = (2 * chip + side) * block
                    out_ref[:, column : column + block] = added(side ^ even, slot)


def per_device(n_context, n_tensor, hidden_rows, norm_gain, w_qkv, w_out, doc_lengths, span_order):
    chips = n_context // 2
    ring = ring_of_chips(chips)
    place = [ring.index(chip) for chip in range(chips)]
    groups = 2 * n_tensor
    rows_here, width = hidden_rows.shape
    tokens_here = rows_here * n_tensor
    block = width // n_context
    context = lax.axis_index("context")
    tensor = lax.axis_index("tensor")
    ahead = [
        (ring[i] * 2 + k, ring[(i + 1) % chips] * 2 + k) for i in range(chips) for k in range(2)
    ]
    back = [(b, a) for a, b in ahead]
    sibling = [(c, c ^ 1) for c in range(n_context)]

    same_core = [[2 * chip + k for chip in range(chips)] for k in range(2)]
    token = [doc_lengths]

    def ordered(values):
        held = lax.optimization_barrier((*values, token[0]))
        token[0] = held[-1]
        return list(held[:-1])

    class Ring:
        def __init__(self, mine):
            self.up, self.down = [mine], [mine]
            self.middle = []

        def step(self, earlier=()):
            up, down, *earlier = ordered((self.up[-1], self.down[-1], *earlier))
            if len(self.up) <= (chips - 1) // 2:
                self.up.append(lax.ppermute(up, "context", ahead))
                self.down.append(lax.ppermute(down, "context", back))
            elif chips % 2 == 0 and not self.middle:
                half = up.shape[0] // 2
                self.middle = [
                    lax.ppermute(up[:half], "context", ahead),
                    lax.ppermute(down[half:], "context", back),
                ]
            return earlier

        def done(self):
            return len(self.up) > (chips - 1) // 2 and (chips % 2 == 1 or bool(self.middle))

        def finish(self):
            while not self.done():
                self.step()
            return self.down + self.middle + self.up[:0:-1]

        def block(self, slot):
            slot %= chips
            if chips % 2 == 0 and slot == chips // 2:
                return tuple(self.middle)
            return (self.down[slot] if slot <= chips // 2 else self.up[chips - slot],)

    def member(e, d):
        return [
            (c * n_tensor + t, (c ^ e) * n_tensor + (t - d) % n_tensor)
            for c in range(n_context)
            for t in range(n_tensor)
        ]

    smem, vmem = pl.BlockSpec(memory_space=pltpu.SMEM), pl.BlockSpec(memory_space=pltpu.VMEM)
    freq = rope_theta ** (-(np.arange(HD // 2, dtype=np.float64) * 2.0 / HD))
    freq = np.concatenate([freq, freq]).astype(np.float32)[None, :]
    table = jax.ShapeDtypeStruct((2 * tokens_here, HD), jnp.float32)
    bound = jax.ShapeDtypeStruct((2 * tokens_here, 1), jnp.int32)
    cosine, sine, query_start, query_orig, key_orig = pl.pallas_call(
        functools.partial(where_kernel, n_tensor, rows_here),
        out_shape=[
            table,
            table,
            bound,
            bound,
            jax.ShapeDtypeStruct((1, chips * tokens_here), jnp.int32),
        ],
        in_specs=[smem, smem, vmem],
        out_specs=vmem_specs(5),
        compiler_params=compute_params(),
        name="where",
    )(span_order, doc_lengths, jnp.asarray(freq))

    qkv_ring = Ring(w_qkv)
    qkv_ring.step()
    normed = pl.pallas_call(
        functools.partial(norm_kernel, place, chips),
        out_shape=jax.ShapeDtypeStruct((2, chips, rows_here, block), jnp.bfloat16),
        in_specs=vmem_specs(2),
        out_specs=vmem_specs(1)[0],
        compiler_params=compute_params(),
        name="norm",
    )(hidden_rows, norm_gain.reshape(-1, HD))
    normed = [normed] + [
        lax.ppermute(
            normed, "tensor", [(t, (t - d) % n_tensor) for t in range(n_tensor)]
        )
        for d in range(1, n_tensor)
    ]
    normed += [lax.ppermute(rows, "context", sibling) for rows in normed]

    qkv_ring.step()
    cosine, sine, query_start, query_orig, key_orig = ordered(
        (cosine, sine, query_start, query_orig, key_orig)
    )
    qkv_ring.step()
    normed = qkv_ring.step(normed)
    while not qkv_ring.done():
        qkv_ring.step()

    out_ring = Ring(w_out)
    out_ring.step()
    blocks = qkv_ring.finish()
    mine, theirs, queries = pl.pallas_call(
        functools.partial(project_kernel, chips, groups),
        out_shape=[
            jax.ShapeDtypeStruct((tokens_here, 2 * HD), jnp.float32),
            jax.ShapeDtypeStruct((tokens_here, 2 * HD), jnp.float32),
            jax.ShapeDtypeStruct((2 * tokens_here, HEAD_COLS), jnp.float32),
        ],
        in_specs=vmem_specs(groups + len(blocks)),
        out_specs=vmem_specs(3),
        compiler_params=compute_params(),
        name="project",
    )(*ordered((*normed, *blocks)))
    theirs = lax.ppermute(theirs, "context", sibling)
    queries_theirs = lax.ppermute(queries, "context", sibling)
    out_ring.step()
    mine, theirs = ordered((mine, theirs))
    kv = pl.pallas_call(
        functools.partial(keys_kernel, chips),
        out_shape=jax.ShapeDtypeStruct((chips * tokens_here, 2 * HD), jnp.bfloat16),
        in_specs=vmem_specs(4),
        out_specs=vmem_specs(1)[0],
        compiler_params=compute_params(),
        name="keys",
    )(mine, theirs, cosine, sine)
    (kv,) = ordered((kv,))
    kv = lax.all_to_all(
        kv, "context", split_axis=0, concat_axis=0, axis_index_groups=same_core, tiled=True
    )
    out_ring.step()
    (kv,) = ordered((kv,))

    mixed = pl.pallas_call(
        attend_kernel,
        out_shape=jax.ShapeDtypeStruct((2 * tokens_here, HEAD_COLS + HD), jnp.float32),
        in_specs=vmem_specs(8),
        out_specs=vmem_specs(1)[0],
        compiler_params=compute_params(),
        name="attend",
    )(
        queries,
        queries_theirs,
        cosine,
        sine,
        query_start,
        query_orig,
        key_orig,
        kv,
    )
    while not out_ring.done():
        out_ring.step()
    (mixed,) = ordered((mixed,))
    mixed_theirs = lax.ppermute(mixed, "context", sibling)

    out_block = w_out.shape[1]

    def output(slots, name):
        blocks = [out_ring.block(slot) for slot in slots]
        flat = [piece for pieces in blocks for piece in pieces]
        parts = pl.pallas_call(
            functools.partial(output_kernel, groups, [len(pieces) for pieces in blocks]),
            out_shape=[jax.ShapeDtypeStruct((len(slots), rows_here, out_block), jnp.bfloat16)]
            * groups,
            in_specs=vmem_specs(2 + len(flat)),
            out_specs=vmem_specs(groups),
            compiler_params=compute_params(),
            name=name,
        )(mixed, mixed_theirs, *flat)
        parts = ordered(parts)
        arrived = []
        for e in range(2):
            for d in range(n_tensor):
                part = parts[e * n_tensor + d]
                if e or d:
                    part = lax.ppermute(part, ("context", "tensor"), member(e, -d))
                arrived.append(part)
        return arrived

    reach = (chips - 1) // 2
    near = 2 * reach + 1
    arrived = output(list(range(-reach, reach + 1)), "output_near")
    arrived += output(list(range(reach + 1, chips - reach)), "output_far")
    return pl.pallas_call(
        functools.partial(sum_kernel, place, chips, groups, near),
        out_shape=jax.ShapeDtypeStruct((rows_here, n_context * out_block), jnp.bfloat16),
        in_specs=[pl.BlockSpec(memory_space=pl.ANY)] + vmem_specs(2 * groups),
        out_specs=vmem_specs(1)[0],
        compiler_params=compute_params(),
        name="sum",
    )(token[0], *arrived)


def solution(mesh):
    placed = (
        P(("context", "tensor"), None),
        P(),
        P("context", "tensor"),
        P("tensor", "context"),
        P(),
        P(),
    )
    return jax.shard_map(
        functools.partial(per_device, mesh.shape["context"], mesh.shape["tensor"]),
        mesh=mesh,
        in_specs=placed,
        out_specs=P(("context", "tensor"), None),
        check_vma=False,
    )
```

```python
import functools

import jax
import jax.numpy as jnp
import numpy as np
from jax import lax
from jax.experimental import pallas as pl
from jax.experimental.pallas import tpu as pltpu
from jax.sharding import PartitionSpec as P

HD = 128
QH_DEV = 4
SPAN = 64
HEAD_COLS = QH_DEV * HD
VMEM_LIMIT = 24 * 1024 * 1024

rope_theta = 500000.0


def ring_of_chips(count):
    wide = 1
    while (wide * 2) * (wide * 2) <= count:
        wide *= 2
    tall = count // wide
    if wide < 2:
        return list(range(count))
    ring = [(z, 0) for z in range(tall)]
    for z in range(tall - 1, -1, -1):
        row = list(range(1, wide))
        ring += [(z, y) for y in (row if (tall - 1 - z) % 2 == 0 else row[::-1])]
    if (tall - 1) % 2 == 0 or wide == 2:
        return [z * wide + y for z, y in ring]
    return [z * wide + y for z, y in ring]


def vmem_specs(count):
    return [pl.BlockSpec(memory_space=pltpu.VMEM)] * count


def compute_params():
    return pltpu.CompilerParams(vmem_limit_bytes=VMEM_LIMIT)


def place_of(place):
    context = lax.axis_index("context")
    at = jnp.int32(0)
    for chip, spot in enumerate(place):
        at = jnp.where(context // 2 == chip, jnp.int32(spot), at)
    return at, context % 2


def where_kernel(
    n_tensor, rows_here, spans_ref, lengths_ref, freq_ref, cos_ref, sin_ref, low_ref, high_ref, orig_ref
):
    context, tensor = lax.axis_index("context"), lax.axis_index("tensor")
    rows = rows_here * n_tensor
    spans = rows // SPAN

    def shift(values, size):
        return lax.shift_right_logical(values, jnp.int32(size.bit_length() - 1))

    def inside_of(row):
        row = row & (rows - 1)
        turned = (tensor + shift(row, rows_here)) & (n_tensor - 1)
        return turned * rows_here + (row & (rows_here - 1))

    def initial(owner, inside):
        source = jnp.zeros_like(inside)
        for k in range(spans):
            source = jnp.where(shift(inside, SPAN) == k, spans_ref[owner * spans + k], source)
        return source * SPAN + (inside & (SPAN - 1))

    row = lax.broadcasted_iota(jnp.int32, cos_ref.shape, 0)
    inside = inside_of(row)
    orig = jnp.where(row < rows, initial(context, inside), initial(context ^ 1, inside))
    start, end = jnp.zeros_like(orig), jnp.int32(0)
    for i in range(lengths_ref.shape[0]):
        end = end + lengths_ref[i]
        start = jnp.where(orig >= end, end, start)
    low_ref[...] = start[:, :1]
    high_ref[...] = orig[:, :1]
    angle = (orig - start).astype(jnp.float32) * freq_ref[...]
    lane = lax.broadcasted_iota(jnp.int32, cos_ref.shape, 1)
    cos_ref[...] = jnp.cos(angle)
    sine = jnp.sin(angle)
    sin_ref[...] = jnp.where(lane < HD // 2, -sine, sine)
    inside = inside_of(lax.broadcasted_iota(jnp.int32, (1, rows), 1))
    for chip in range(orig_ref.shape[1] // rows):
        owner = 2 * chip + context % 2
        orig_ref[:, chip * rows : (chip + 1) * rows] = initial(owner, inside)


def norm_kernel(place, chips, hidden_ref, gain_ref, out_ref):
    at, core = place_of(place)
    wide = hidden_ref[...].astype(jnp.float32)
    meansq = jnp.mean(wide * wide, axis=-1, keepdims=True)
    scaled = wide * lax.rsqrt(meansq + 1e-05)
    lanes = gain_ref.shape[1]
    normed = jnp.concatenate(
        [
            (
                scaled[:, i * lanes : (i + 1) * lanes]
                * gain_ref[i : i + 1, :].astype(jnp.float32)
            ).astype(jnp.bfloat16)
            for i in range(gain_ref.shape[0])
        ],
        axis=1,
    )
    block = out_ref.shape[3]
    for even in range(2):

        @pl.when(core == even)
        def _():
            for chip in range(chips):
                slot = lax.rem(place[chip] + chips - at, chips)
                for side in range(2):
                    column = (2 * chip + side) * block
                    out_ref[side ^ even, slot] = normed[:, column : column + block]


def take_ring(refs, chips):
    refs = list(refs)
    if chips % 2:
        return [(ref,) for ref in refs]
    half = chips // 2
    return [(r,) for r in refs[:half]] + [tuple(refs[half : half + 2])] + [
        (r,) for r in refs[half + 2 :]
    ]


def project_kernel(chips, groups, *refs):
    rows_refs, refs = refs[:groups], refs[groups:]
    weight_refs, (mine_ref, theirs_ref, queries_ref) = refs[:-3], refs[-3:]
    half = groups // 2
    weights = take_ring(weight_refs, chips)
    total = None
    for slot in range(chips):
        rows = jnp.concatenate(
            [ref[group // half, slot] for group, ref in enumerate(rows_refs)], axis=0
        )
        start = 0
        for ref in weights[slot]:
            depth = ref.shape[0]
            part = jnp.dot(
                rows[:, start : start + depth], ref[...], preferred_element_type=jnp.float32
            )
            total = part if total is None else total + part
            start += depth
    count = mine_ref.shape[0]
    mine_ref[...] = total[:count, HEAD_COLS:]
    theirs_ref[...] = total[count:, HEAD_COLS:]
    queries_ref[...] = total[:, :HEAD_COLS]


def turn(values, cosine, sine):
    return values * cosine + pltpu.roll(values, HD // 2, 1) * sine


def keys_kernel(chips, mine_ref, theirs_ref, cosine_ref, sine_ref, out_ref):
    rows = out_ref.shape[0] // chips
    cosine, sine = cosine_ref[:rows, :], sine_ref[:rows, :]
    total = mine_ref[...] + theirs_ref[...]
    keys = turn(total[:, :HD], cosine, sine).astype(jnp.bfloat16)
    values = total[:, HD:].astype(jnp.bfloat16)
    for chip in range(chips):
        out_ref[chip * rows : (chip + 1) * rows, :HD] = keys
        out_ref[chip * rows : (chip + 1) * rows, HD:] = values


def attend_kernel(
    mine_ref,
    theirs_ref,
    cosine_ref,
    sine_ref,
    low_ref,
    high_ref,
    orig_ref,
    kv_ref,
    out_ref,
    sent_ref,
    stats_ref,
):
    keys = kv_ref[:, :HD]
    values = kv_ref[:, HD:]
    orig = orig_ref[...]
    allowed = (orig >= low_ref[...]) & (orig <= high_ref[...])
    scale = 1.0 / HD**0.5
    rows = out_ref.shape[0]
    half = rows // 2
    lane = lax.broadcasted_iota(jnp.int32, (rows, HD), 1)
    stats = jnp.zeros((rows, HD), jnp.float32)
    for head in range(QH_DEV):
        columns = slice(head * HD, (head + 1) * HD)
        query = jnp.concatenate(
            [
                mine_ref[:half, columns] + theirs_ref[half:, columns],
                mine_ref[half:, columns] + theirs_ref[:half, columns],
            ],
            axis=0,
        )
        query = turn(query, cosine_ref[...], sine_ref[...]).astype(jnp.bfloat16)
        scores = lax.dot_general(
            query, keys, (((1,), (1,)), ((), ())), preferred_element_type=jnp.float32
        )
        scores = jnp.where(allowed, scores * scale, -1e30)
        top = jnp.max(scores, axis=-1, keepdims=True)
        expo = jnp.where(allowed, jnp.exp(scores - top), 0.0)
        total = jnp.sum(expo, axis=-1, keepdims=True)
        product = jnp.dot(expo.astype(jnp.bfloat16), values, preferred_element_type=jnp.float32)
        out_ref[:, columns] = product
        sent_ref[:, columns] = product.astype(jnp.bfloat16)
        stats = jnp.where(lane == 2 * head, total, stats)
        stats = jnp.where(lane == 2 * head + 1, top, stats)
    stats_ref[...] = stats


def output_kernel(
    groups, pieces_of, mine_ref, stats_ref, theirs_ref, their_stats_ref, *refs
):
    weight_refs, out_refs = refs[:-groups], refs[-groups:]
    chip_rows = mine_ref.shape[0]
    half = chip_rows // 2

    def swapped(ref, columns):
        return jnp.concatenate([ref[half:, columns], ref[:half, columns]], axis=0)

    pieces = []
    for head in range(QH_DEV):
        columns = slice(head * HD, (head + 1) * HD)
        sums, tops = slice(2 * head, 2 * head + 1), slice(2 * head + 1, 2 * head + 2)
        total, top = stats_ref[:, sums], stats_ref[:, tops]
        other_total, other_top = swapped(their_stats_ref, sums), swapped(their_stats_ref, tops)
        peak = jnp.maximum(top, other_top)
        factor, other_factor = jnp.exp(top - peak), jnp.exp(other_top - peak)
        other = swapped(theirs_ref, columns).astype(jnp.float32)
        product = mine_ref[:, columns] * factor + other * other_factor
        pieces.append(
            (product / (total * factor + other_total * other_factor)).astype(jnp.bfloat16)
        )
    mixed = jnp.concatenate(pieces, axis=1)
    rows = chip_rows // groups
    weight_refs = iter(weight_refs)
    for slot, pieces in enumerate(pieces_of):
        start, total = 0, None
        for _ in range(pieces):
            ref = next(weight_refs)
            depth = ref.shape[0]
            part = jnp.dot(
                mixed[:, start : start + depth], ref[...], preferred_element_type=jnp.float32
            )
            total = part if total is None else total + part
            start += depth
        total = total.astype(jnp.bfloat16)
        for group in range(groups):
            out_refs[group][slot] = total[group * rows : (group + 1) * rows]


def sum_kernel(place, chips, groups, near, token_ref, *refs):
    near_refs, far_refs, out_ref = refs[:groups], refs[groups : 2 * groups], refs[2 * groups]
    at, core = place_of(place)
    block = near_refs[0].shape[2]
    half = groups // 2

    def added(part, slot):
        turn_at = lax.rem(slot + near // 2, chips)
        total = None
        for group in range(part * half, (part + 1) * half):
            rows = jnp.where(
                turn_at < near,
                near_refs[group][jnp.minimum(turn_at, near - 1)].astype(jnp.float32),
                far_refs[group][jnp.maximum(turn_at - near, 0)].astype(jnp.float32),
            )
            total = rows if total is None else total + rows
        return total.astype(jnp.bfloat16)

    for even in range(2):

        @pl.when(core == even)
        def _():
            for chip in range(chips):
                slot = lax.rem(place[chip] + chips - at, chips)
                for side in range(2):
                    column = (2 * chip + side) * block
                    out_ref[:, column : column + block] = added(side ^ even, slot)


def per_device(n_context, n_tensor, hidden_rows, norm_gain, w_qkv, w_out, doc_lengths, span_order):
    chips = n_context // 2
    ring = ring_of_chips(chips)
    place = [ring.index(chip) for chip in range(chips)]
    groups = 2 * n_tensor
    rows_here, width = hidden_rows.shape
    tokens_here = rows_here * n_tensor
    block = width // n_context
    context = lax.axis_index("context")
    tensor = lax.axis_index("tensor")
    ahead = [
        (ring[i] * 2 + k, ring[(i + 1) % chips] * 2 + k) for i in range(chips) for k in range(2)
    ]
    back = [(b, a) for a, b in ahead]
    sibling = [(c, c ^ 1) for c in range(n_context)]

    same_core = [[2 * chip + k for chip in range(chips)] for k in range(2)]
    token = [doc_lengths]

    def ordered(values):
        held = lax.optimization_barrier((*values, token[0]))
        token[0] = held[-1]
        return list(held[:-1])

    class Ring:
        def __init__(self, mine):
            self.up, self.down = [mine], [mine]
            self.middle = []

        def step(self, earlier=()):
            up, down, *earlier = ordered((self.up[-1], self.down[-1], *earlier))
            if len(self.up) <= (chips - 1) // 2:
                self.up.append(lax.ppermute(up, "context", ahead))
                self.down.append(lax.ppermute(down, "context", back))
            elif chips % 2 == 0 and not self.middle:
                half = up.shape[0] // 2
                self.middle = [
                    lax.ppermute(up[:half], "context", ahead),
                    lax.ppermute(down[half:], "context", back),
                ]
            return earlier

        def done(self):
            return len(self.up) > (chips - 1) // 2 and (chips % 2 == 1 or bool(self.middle))

        def finish(self):
            while not self.done():
                self.step()
            return self.down + self.middle + self.up[:0:-1]

        def block(self, slot):
            slot %= chips
            if chips % 2 == 0 and slot == chips // 2:
                return tuple(self.middle)
            return (self.down[slot] if slot <= chips // 2 else self.up[chips - slot],)

    def member(e, d):
        return [
            (c * n_tensor + t, (c ^ e) * n_tensor + (t - d) % n_tensor)
            for c in range(n_context)
            for t in range(n_tensor)
        ]

    smem, vmem = pl.BlockSpec(memory_space=pltpu.SMEM), pl.BlockSpec(memory_space=pltpu.VMEM)
    freq = rope_theta ** (-(np.arange(HD // 2, dtype=np.float64) * 2.0 / HD))
    freq = np.concatenate([freq, freq]).astype(np.float32)[None, :]
    table = jax.ShapeDtypeStruct((2 * tokens_here, HD), jnp.float32)
    bound = jax.ShapeDtypeStruct((2 * tokens_here, 1), jnp.int32)
    cosine, sine, query_start, query_orig, key_orig = pl.pallas_call(
        functools.partial(where_kernel, n_tensor, rows_here),
        out_shape=[
            table,
            table,
            bound,
            bound,
            jax.ShapeDtypeStruct((1, chips * tokens_here), jnp.int32),
        ],
        in_specs=[smem, smem, vmem],
        out_specs=vmem_specs(5),
        compiler_params=compute_params(),
        name="where",
    )(span_order, doc_lengths, jnp.asarray(freq))

    qkv_ring = Ring(w_qkv)
    qkv_ring.step()
    normed = pl.pallas_call(
        functools.partial(norm_kernel, place, chips),
        out_shape=jax.ShapeDtypeStruct((2, chips, rows_here, block), jnp.bfloat16),
        in_specs=vmem_specs(2),
        out_specs=vmem_specs(1)[0],
        compiler_params=compute_params(),
        name="norm",
    )(hidden_rows, norm_gain.reshape(-1, HD))
    normed = [normed] + [
        lax.ppermute(
            normed, "tensor", [(t, (t - d) % n_tensor) for t in range(n_tensor)]
        )
        for d in range(1, n_tensor)
    ]
    normed += [lax.ppermute(rows, "context", sibling) for rows in normed]

    qkv_ring.step()
    cosine, sine, query_start, query_orig, key_orig = ordered(
        (cosine, sine, query_start, query_orig, key_orig)
    )
    qkv_ring.step()
    normed = qkv_ring.step(normed)
    while not qkv_ring.done():
        qkv_ring.step()

    out_ring = Ring(w_out)
    out_ring.step()
    blocks = qkv_ring.finish()
    mine, theirs, queries = pl.pallas_call(
        functools.partial(project_kernel, chips, groups),
        out_shape=[
            jax.ShapeDtypeStruct((tokens_here, 2 * HD), jnp.float32),
            jax.ShapeDtypeStruct((tokens_here, 2 * HD), jnp.float32),
            jax.ShapeDtypeStruct((2 * tokens_here, HEAD_COLS), jnp.float32),
        ],
        in_specs=vmem_specs(groups + len(blocks)),
        out_specs=vmem_specs(3),
        compiler_params=compute_params(),
        name="project",
    )(*ordered((*normed, *blocks)))
    theirs = lax.ppermute(theirs, "context", sibling)
    queries_theirs = lax.ppermute(queries, "context", sibling)
    out_ring.step()
    mine, theirs = ordered((mine, theirs))
    kv = pl.pallas_call(
        functools.partial(keys_kernel, chips),
        out_shape=jax.ShapeDtypeStruct((chips * tokens_here, 2 * HD), jnp.bfloat16),
        in_specs=vmem_specs(4),
        out_specs=vmem_specs(1)[0],
        compiler_params=compute_params(),
        name="keys",
    )(mine, theirs, cosine, sine)
    (kv,) = ordered((kv,))
    kv = lax.all_to_all(
        kv, "context", split_axis=0, concat_axis=0, axis_index_groups=same_core, tiled=True
    )
    out_ring.step()
    (kv,) = ordered((kv,))

    mixed, sent, stats = pl.pallas_call(
        attend_kernel,
        out_shape=[
            jax.ShapeDtypeStruct((2 * tokens_here, HEAD_COLS), jnp.float32),
            jax.ShapeDtypeStruct((2 * tokens_here, HEAD_COLS), jnp.bfloat16),
            jax.ShapeDtypeStruct((2 * tokens_here, HD), jnp.float32),
        ],
        in_specs=vmem_specs(8),
        out_specs=vmem_specs(3),
        compiler_params=compute_params(),
        name="attend",
    )(
        queries,
        queries_theirs,
        cosine,
        sine,
        query_start,
        query_orig,
        key_orig,
        kv,
    )
    sent, stats = ordered((sent, stats))
    sent = lax.ppermute(sent, "context", sibling)
    their_stats = lax.ppermute(stats, "context", sibling)
    while not out_ring.done():
        out_ring.step()

    out_block = w_out.shape[1]

    def output(slots, name):
        blocks = [out_ring.block(slot) for slot in slots]
        flat = [piece for pieces in blocks for piece in pieces]
        parts = pl.pallas_call(
            functools.partial(output_kernel, groups, [len(pieces) for pieces in blocks]),
            out_shape=[jax.ShapeDtypeStruct((len(slots), rows_here, out_block), jnp.bfloat16)]
            * groups,
            in_specs=vmem_specs(4 + len(flat)),
            out_specs=vmem_specs(groups),
            compiler_params=compute_params(),
            name=name,
        )(mixed, stats, sent, their_stats, *flat)
        parts = ordered(parts)
        arrived = []
        for e in range(2):
            for d in range(n_tensor):
                part = parts[e * n_tensor + d]
                if e or d:
                    part = lax.ppermute(part, ("context", "tensor"), member(e, -d))
                arrived.append(part)
        return arrived

    reach = (chips - 1) // 2
    near = 2 * reach + 1
    arrived = output(list(range(-reach, reach + 1)), "output_near")
    arrived += output(list(range(reach + 1, chips - reach)), "output_far")
    return pl.pallas_call(
        functools.partial(sum_kernel, place, chips, groups, near),
        out_shape=jax.ShapeDtypeStruct((rows_here, n_context * out_block), jnp.bfloat16),
        in_specs=[pl.BlockSpec(memory_space=pl.ANY)] + vmem_specs(2 * groups),
        out_specs=vmem_specs(1)[0],
        compiler_params=compute_params(),
        name="sum",
    )(token[0], *arrived)


def solution(mesh):
    placed = (
        P(("context", "tensor"), None),
        P(),
        P("context", "tensor"),
        P("tensor", "context"),
        P(),
        P(),
    )
    return jax.shard_map(
        functools.partial(per_device, mesh.shape["context"], mesh.shape["tensor"]),
        mesh=mesh,
        in_specs=placed,
        out_specs=P(("context", "tensor"), None),
        check_vma=False,
    )
```

```python
import functools

import jax
import jax.numpy as jnp
import numpy as np
from jax import lax
from jax.experimental import pallas as pl
from jax.experimental.pallas import tpu as pltpu
from jax.sharding import PartitionSpec as P

HD = 128
QH_DEV = 4
SPAN = 64
HEAD_COLS = QH_DEV * HD
VMEM_LIMIT = 24 * 1024 * 1024

rope_theta = 500000.0


def ring_of_chips(count):
    wide = 1
    while (wide * 2) * (wide * 2) <= count:
        wide *= 2
    tall = count // wide
    if wide < 2:
        return list(range(count))
    ring = [(z, 0) for z in range(tall)]
    for z in range(tall - 1, -1, -1):
        row = list(range(1, wide))
        ring += [(z, y) for y in (row if (tall - 1 - z) % 2 == 0 else row[::-1])]
    if (tall - 1) % 2 == 0 or wide == 2:
        return [z * wide + y for z, y in ring]
    return [z * wide + y for z, y in ring]


def vmem_specs(count):
    return [pl.BlockSpec(memory_space=pltpu.VMEM)] * count


def compute_params():
    return pltpu.CompilerParams(vmem_limit_bytes=VMEM_LIMIT)


def place_of(place):
    context = lax.axis_index("context")
    at = jnp.int32(0)
    for chip, spot in enumerate(place):
        at = jnp.where(context // 2 == chip, jnp.int32(spot), at)
    return at, context % 2


def where_kernel(
    n_tensor, rows_here, spans_ref, lengths_ref, freq_ref, cos_ref, sin_ref, low_ref, high_ref, orig_ref
):
    context, tensor = lax.axis_index("context"), lax.axis_index("tensor")
    rows = rows_here * n_tensor
    spans = rows // SPAN

    def shift(values, size):
        return lax.shift_right_logical(values, jnp.int32(size.bit_length() - 1))

    def inside_of(row):
        row = row & (rows - 1)
        turned = (tensor + shift(row, rows_here)) & (n_tensor - 1)
        return turned * rows_here + (row & (rows_here - 1))

    def initial(owner, inside):
        source = jnp.zeros_like(inside)
        for k in range(spans):
            source = jnp.where(shift(inside, SPAN) == k, spans_ref[owner * spans + k], source)
        return source * SPAN + (inside & (SPAN - 1))

    row = lax.broadcasted_iota(jnp.int32, cos_ref.shape, 0)
    inside = inside_of(row)
    orig = jnp.where(row < rows, initial(context, inside), initial(context ^ 1, inside))
    start, end = jnp.zeros_like(orig), jnp.int32(0)
    for i in range(lengths_ref.shape[0]):
        end = end + lengths_ref[i]
        start = jnp.where(orig >= end, end, start)
    low_ref[...] = start[:, :1]
    high_ref[...] = orig[:, :1]
    angle = (orig - start).astype(jnp.float32) * freq_ref[...]
    lane = lax.broadcasted_iota(jnp.int32, cos_ref.shape, 1)
    cos_ref[...] = jnp.cos(angle)
    sine = jnp.sin(angle)
    sin_ref[...] = jnp.where(lane < HD // 2, -sine, sine)
    inside = inside_of(lax.broadcasted_iota(jnp.int32, (1, rows), 1))
    for chip in range(orig_ref.shape[1] // rows):
        owner = 2 * chip + context % 2
        orig_ref[:, chip * rows : (chip + 1) * rows] = initial(owner, inside)


def slot_of(place, chip, side, at):
    chips = len(place)
    ahead = place[chip] - at if side == 0 else at - place[chip]
    return lax.rem(ahead + chips, chips)


def norm_kernel(place, chips, hidden_ref, gain_ref, out_ref):
    at, core = place_of(place)
    wide = hidden_ref[...].astype(jnp.float32)
    meansq = jnp.mean(wide * wide, axis=-1, keepdims=True)
    scaled = wide * lax.rsqrt(meansq + 1e-05)
    lanes = gain_ref.shape[1]
    normed = jnp.concatenate(
        [
            (
                scaled[:, i * lanes : (i + 1) * lanes]
                * gain_ref[i : i + 1, :].astype(jnp.float32)
            ).astype(jnp.bfloat16)
            for i in range(gain_ref.shape[0])
        ],
        axis=1,
    )
    block = out_ref.shape[3]
    for even in range(2):

        @pl.when(core == even)
        def _():
            for chip in range(chips):
                for side in range(2):
                    slot = slot_of(place, chip, side, at)
                    column = (2 * chip + side) * block
                    out_ref[side ^ even, slot] = normed[:, column : column + block]


def take_ring(refs, chips):
    refs = list(refs)
    if chips % 2:
        return [(ref,) for ref in refs]
    half = chips // 2
    return [(r,) for r in refs[:half]] + [tuple(refs[half : half + 2])] + [
        (r,) for r in refs[half + 2 :]
    ]


def project_kernel(chips, groups, *refs):
    rows_refs, refs = refs[:groups], refs[groups:]
    weight_refs, (mine_ref, theirs_ref, queries_ref) = refs[:-3], refs[-3:]
    half = groups // 2
    weights = take_ring(weight_refs, chips)
    total = None
    for slot in range(chips):
        rows = jnp.concatenate(
            [ref[group // half, slot] for group, ref in enumerate(rows_refs)], axis=0
        )
        start = 0
        for ref in weights[slot]:
            depth = ref.shape[0]
            part = jnp.dot(
                rows[:, start : start + depth], ref[...], preferred_element_type=jnp.float32
            )
            total = part if total is None else total + part
            start += depth
    count = mine_ref.shape[0]
    mine_ref[...] = total[:count, HEAD_COLS:]
    theirs_ref[...] = total[count:, HEAD_COLS:]
    queries_ref[...] = total[:, :HEAD_COLS]


def turn(values, cosine, sine):
    return values * cosine + pltpu.roll(values, HD // 2, 1) * sine


def keys_kernel(chips, mine_ref, theirs_ref, cosine_ref, sine_ref, out_ref):
    rows = out_ref.shape[0] // chips
    cosine, sine = cosine_ref[:rows, :], sine_ref[:rows, :]
    total = mine_ref[...] + theirs_ref[...]
    keys = turn(total[:, :HD], cosine, sine).astype(jnp.bfloat16)
    values = total[:, HD:].astype(jnp.bfloat16)
    for chip in range(chips):
        out_ref[chip * rows : (chip + 1) * rows, :HD] = keys
        out_ref[chip * rows : (chip + 1) * rows, HD:] = values


def attend_kernel(
    mine_ref,
    theirs_ref,
    cosine_ref,
    sine_ref,
    low_ref,
    high_ref,
    orig_ref,
    kv_ref,
    out_ref,
):
    keys = kv_ref[:, :HD]
    values = kv_ref[:, HD:]
    orig = orig_ref[...]
    allowed = (orig >= low_ref[...]) & (orig <= high_ref[...])
    scale = 1.0 / HD**0.5
    rows = out_ref.shape[0]
    half = rows // 2
    lane = lax.broadcasted_iota(jnp.int32, (rows, HD), 1)
    stats = jnp.zeros((rows, HD), jnp.float32)
    for head in range(QH_DEV):
        columns = slice(head * HD, (head + 1) * HD)
        query = jnp.concatenate(
            [
                mine_ref[:half, columns] + theirs_ref[half:, columns],
                mine_ref[half:, columns] + theirs_ref[:half, columns],
            ],
            axis=0,
        )
        query = turn(query, cosine_ref[...], sine_ref[...]).astype(jnp.bfloat16)
        scores = lax.dot_general(
            query, keys, (((1,), (1,)), ((), ())), preferred_element_type=jnp.float32
        )
        scores = jnp.where(allowed, scores * scale, -1e30)
        top = jnp.max(scores, axis=-1, keepdims=True)
        expo = jnp.where(allowed, jnp.exp(scores - top), 0.0)
        total = jnp.sum(expo, axis=-1, keepdims=True)
        out_ref[:, columns] = jnp.dot(
            expo.astype(jnp.bfloat16), values, preferred_element_type=jnp.float32
        )
        stats = jnp.where(lane == 2 * head, total, stats)
        stats = jnp.where(lane == 2 * head + 1, top, stats)
    out_ref[:, HEAD_COLS:] = stats


def output_kernel(groups, pieces_of, mine_ref, theirs_ref, *refs):
    weight_refs, out_refs = refs[:-groups], refs[-groups:]
    chip_rows = mine_ref.shape[0]
    half = chip_rows // 2

    def swapped(columns):
        return jnp.concatenate([theirs_ref[half:, columns], theirs_ref[:half, columns]], axis=0)

    pieces = []
    for head in range(QH_DEV):
        columns = slice(head * HD, (head + 1) * HD)
        at = HEAD_COLS + 2 * head
        total, top = mine_ref[:, at : at + 1], mine_ref[:, at + 1 : at + 2]
        other_total, other_top = swapped(slice(at, at + 1)), swapped(slice(at + 1, at + 2))
        peak = jnp.maximum(top, other_top)
        factor, other_factor = jnp.exp(top - peak), jnp.exp(other_top - peak)
        product = mine_ref[:, columns] * factor + swapped(columns) * other_factor
        pieces.append(
            (product / (total * factor + other_total * other_factor)).astype(jnp.bfloat16)
        )
    mixed = jnp.concatenate(pieces, axis=1)
    rows = chip_rows // groups
    weight_refs = iter(weight_refs)
    for slot, pieces in enumerate(pieces_of):
        start, total = 0, None
        for _ in range(pieces):
            ref = next(weight_refs)
            depth = ref.shape[0]
            part = jnp.dot(
                mixed[:, start : start + depth], ref[...], preferred_element_type=jnp.float32
            )
            total = part if total is None else total + part
            start += depth
        total = total.astype(jnp.bfloat16)
        for group in range(groups):
            out_refs[group][slot] = total[group * rows : (group + 1) * rows]


def sum_kernel(place, chips, groups, near, token_ref, *refs):
    near_refs, far_refs, out_ref = refs[:groups], refs[groups : 2 * groups], refs[2 * groups]
    at, core = place_of(place)
    block = near_refs[0].shape[2]
    half = groups // 2

    def added(part, slot):
        turn_at = lax.rem(slot + near // 2, chips)
        total = None
        for group in range(part * half, (part + 1) * half):
            rows = jnp.where(
                turn_at < near,
                near_refs[group][jnp.minimum(turn_at, near - 1)].astype(jnp.float32),
                far_refs[group][jnp.maximum(turn_at - near, 0)].astype(jnp.float32),
            )
            total = rows if total is None else total + rows
        return total.astype(jnp.bfloat16)

    for even in range(2):

        @pl.when(core == even)
        def _():
            for chip in range(chips):
                for side in range(2):
                    slot = slot_of(place, chip, side, at)
                    column = (2 * chip + side) * block
                    out_ref[:, column : column + block] = added(side ^ even, slot)


def per_device(n_context, n_tensor, hidden_rows, norm_gain, w_qkv, w_out, doc_lengths, span_order):
    chips = n_context // 2
    ring = ring_of_chips(chips)
    place = [ring.index(chip) for chip in range(chips)]
    groups = 2 * n_tensor
    rows_here, width = hidden_rows.shape
    tokens_here = rows_here * n_tensor
    block = width // n_context
    context = lax.axis_index("context")
    tensor = lax.axis_index("tensor")
    ahead = [
        (ring[i] * 2 + k, ring[(i + 1 - 2 * k) % chips] * 2 + k)
        for i in range(chips)
        for k in range(2)
    ]
    back = [(b, a) for a, b in ahead]
    sibling = [(c, c ^ 1) for c in range(n_context)]

    same_core = [[2 * chip + k for chip in range(chips)] for k in range(2)]
    token = [doc_lengths]

    def ordered(values):
        held = lax.optimization_barrier((*values, token[0]))
        token[0] = held[-1]
        return list(held[:-1])

    class Ring:
        def __init__(self, mine):
            self.up, self.down = [mine], [mine]
            self.middle = []

        def step(self, earlier=()):
            up, down, *earlier = ordered((self.up[-1], self.down[-1], *earlier))
            if len(self.up) <= (chips - 1) // 2:
                self.up.append(lax.ppermute(up, "context", ahead))
                self.down.append(lax.ppermute(down, "context", back))
            elif chips % 2 == 0 and not self.middle:
                half = up.shape[0] // 2
                self.middle = [
                    lax.ppermute(up[:half], "context", ahead),
                    lax.ppermute(down[half:], "context", back),
                ]
            return earlier

        def done(self):
            return len(self.up) > (chips - 1) // 2 and (chips % 2 == 1 or bool(self.middle))

        def finish(self):
            while not self.done():
                self.step()
            return self.down + self.middle + self.up[:0:-1]

        def block(self, slot):
            slot %= chips
            if chips % 2 == 0 and slot == chips // 2:
                return tuple(self.middle)
            return (self.down[slot] if slot <= chips // 2 else self.up[chips - slot],)

    def member(e, d):
        return [
            (c * n_tensor + t, (c ^ e) * n_tensor + (t - d) % n_tensor)
            for c in range(n_context)
            for t in range(n_tensor)
        ]

    smem, vmem = pl.BlockSpec(memory_space=pltpu.SMEM), pl.BlockSpec(memory_space=pltpu.VMEM)
    freq = rope_theta ** (-(np.arange(HD // 2, dtype=np.float64) * 2.0 / HD))
    freq = np.concatenate([freq, freq]).astype(np.float32)[None, :]
    table = jax.ShapeDtypeStruct((2 * tokens_here, HD), jnp.float32)
    bound = jax.ShapeDtypeStruct((2 * tokens_here, 1), jnp.int32)
    cosine, sine, query_start, query_orig, key_orig = pl.pallas_call(
        functools.partial(where_kernel, n_tensor, rows_here),
        out_shape=[
            table,
            table,
            bound,
            bound,
            jax.ShapeDtypeStruct((1, chips * tokens_here), jnp.int32),
        ],
        in_specs=[smem, smem, vmem],
        out_specs=vmem_specs(5),
        compiler_params=compute_params(),
        name="where",
    )(span_order, doc_lengths, jnp.asarray(freq))

    qkv_ring = Ring(w_qkv)
    qkv_ring.step()
    normed = pl.pallas_call(
        functools.partial(norm_kernel, place, chips),
        out_shape=jax.ShapeDtypeStruct((2, chips, rows_here, block), jnp.bfloat16),
        in_specs=vmem_specs(2),
        out_specs=vmem_specs(1)[0],
        compiler_params=compute_params(),
        name="norm",
    )(hidden_rows, norm_gain.reshape(-1, HD))
    normed = [normed] + [
        lax.ppermute(
            normed, "tensor", [(t, (t - d) % n_tensor) for t in range(n_tensor)]
        )
        for d in range(1, n_tensor)
    ]
    normed += [lax.ppermute(rows, "context", sibling) for rows in normed]

    qkv_ring.step()
    cosine, sine, query_start, query_orig, key_orig = ordered(
        (cosine, sine, query_start, query_orig, key_orig)
    )
    qkv_ring.step()
    normed = qkv_ring.step(normed)
    while not qkv_ring.done():
        qkv_ring.step()

    out_ring = Ring(w_out)
    out_ring.step()
    blocks = qkv_ring.finish()
    mine, theirs, queries = pl.pallas_call(
        functools.partial(project_kernel, chips, groups),
        out_shape=[
            jax.ShapeDtypeStruct((tokens_here, 2 * HD), jnp.float32),
            jax.ShapeDtypeStruct((tokens_here, 2 * HD), jnp.float32),
            jax.ShapeDtypeStruct((2 * tokens_here, HEAD_COLS), jnp.float32),
        ],
        in_specs=vmem_specs(groups + len(blocks)),
        out_specs=vmem_specs(3),
        compiler_params=compute_params(),
        name="project",
    )(*ordered((*normed, *blocks)))
    theirs = lax.ppermute(theirs, "context", sibling)
    queries_theirs = lax.ppermute(queries, "context", sibling)
    out_ring.step()
    mine, theirs = ordered((mine, theirs))
    kv = pl.pallas_call(
        functools.partial(keys_kernel, chips),
        out_shape=jax.ShapeDtypeStruct((chips * tokens_here, 2 * HD), jnp.bfloat16),
        in_specs=vmem_specs(4),
        out_specs=vmem_specs(1)[0],
        compiler_params=compute_params(),
        name="keys",
    )(mine, theirs, cosine, sine)
    (kv,) = ordered((kv,))
    kv = lax.all_to_all(
        kv, "context", split_axis=0, concat_axis=0, axis_index_groups=same_core, tiled=True
    )
    out_ring.step()
    (kv,) = ordered((kv,))

    mixed = pl.pallas_call(
        attend_kernel,
        out_shape=jax.ShapeDtypeStruct((2 * tokens_here, HEAD_COLS + HD), jnp.float32),
        in_specs=vmem_specs(8),
        out_specs=vmem_specs(1)[0],
        compiler_params=compute_params(),
        name="attend",
    )(
        queries,
        queries_theirs,
        cosine,
        sine,
        query_start,
        query_orig,
        key_orig,
        kv,
    )
    (mixed,) = ordered((mixed,))
    mixed_theirs = lax.ppermute(mixed, "context", sibling)

    out_block = w_out.shape[1]

    def output(slots, name):
        blocks = [out_ring.block(slot) for slot in slots]
        flat = [piece for pieces in blocks for piece in pieces]
        parts = pl.pallas_call(
            functools.partial(output_kernel, groups, [len(pieces) for pieces in blocks]),
            out_shape=[jax.ShapeDtypeStruct((len(slots), rows_here, out_block), jnp.bfloat16)]
            * groups,
            in_specs=vmem_specs(2 + len(flat)),
            out_specs=vmem_specs(groups),
            compiler_params=compute_params(),
            name=name,
        )(mixed, mixed_theirs, *flat)
        parts = ordered(parts)
        arrived = []
        for e in range(2):
            for d in range(n_tensor):
                part = parts[e * n_tensor + d]
                if e or d:
                    part = lax.ppermute(part, ("context", "tensor"), member(e, -d))
                arrived.append(part)
        return arrived

    reach = max(chips // 2 - 2, 0)
    while len(out_ring.up) <= reach:
        out_ring.step()
    near = 2 * reach + 1
    arrived = output(list(range(-reach, reach + 1)), "output_near")
    while not out_ring.done():
        out_ring.step()
    arrived += output(list(range(reach + 1, chips - reach)), "output_far")
    return pl.pallas_call(
        functools.partial(sum_kernel, place, chips, groups, near),
        out_shape=jax.ShapeDtypeStruct((rows_here, n_context * out_block), jnp.bfloat16),
        in_specs=[pl.BlockSpec(memory_space=pl.ANY)] + vmem_specs(2 * groups),
        out_specs=vmem_specs(1)[0],
        compiler_params=compute_params(),
        name="sum",
    )(token[0], *arrived)


def solution(mesh):
    placed = (
        P(("context", "tensor"), None),
        P(),
        P("context", "tensor"),
        P("tensor", "context"),
        P(),
        P(),
    )
    return jax.shard_map(
        functools.partial(per_device, mesh.shape["context"], mesh.shape["tensor"]),
        mesh=mesh,
        in_specs=placed,
        out_specs=P(("context", "tensor"), None),
        check_vma=False,
    )
```

```python
import functools

import jax
import jax.numpy as jnp
import numpy as np
from jax import lax
from jax.experimental import pallas as pl
from jax.experimental.pallas import tpu as pltpu
from jax.sharding import PartitionSpec as P

HD = 128
QH_DEV = 4
SPAN = 64
HEAD_COLS = QH_DEV * HD
VMEM_LIMIT = 24 * 1024 * 1024

rope_theta = 500000.0


def ring_of_chips(count):
    wide = 1
    while (wide * 2) * (wide * 2) <= count:
        wide *= 2
    tall = count // wide
    if wide < 2:
        return list(range(count))
    ring = [(z, 0) for z in range(tall)]
    for z in range(tall - 1, -1, -1):
        row = list(range(1, wide))
        ring += [(z, y) for y in (row if (tall - 1 - z) % 2 == 0 else row[::-1])]
    if (tall - 1) % 2 == 0 or wide == 2:
        return [z * wide + y for z, y in ring]
    return [z * wide + y for z, y in ring]


def vmem_specs(count):
    return [pl.BlockSpec(memory_space=pltpu.VMEM)] * count


def compute_params():
    return pltpu.CompilerParams(vmem_limit_bytes=VMEM_LIMIT)


def place_of(place):
    context = lax.axis_index("context")
    at = jnp.int32(0)
    for chip, spot in enumerate(place):
        at = jnp.where(context // 2 == chip, jnp.int32(spot), at)
    return at, context % 2


def where_kernel(
    n_tensor, rows_here, spans_ref, lengths_ref, freq_ref, cos_ref, sin_ref, low_ref, high_ref, orig_ref
):
    context, tensor = lax.axis_index("context"), lax.axis_index("tensor")
    rows = rows_here * n_tensor
    spans = rows // SPAN

    def shift(values, size):
        return lax.shift_right_logical(values, jnp.int32(size.bit_length() - 1))

    def inside_of(row):
        row = row & (rows - 1)
        turned = (tensor + shift(row, rows_here)) & (n_tensor - 1)
        return turned * rows_here + (row & (rows_here - 1))

    def initial(owner, inside):
        source = jnp.zeros_like(inside)
        for k in range(spans):
            source = jnp.where(shift(inside, SPAN) == k, spans_ref[owner * spans + k], source)
        return source * SPAN + (inside & (SPAN - 1))

    row = lax.broadcasted_iota(jnp.int32, cos_ref.shape, 0)
    inside = inside_of(row)
    orig = jnp.where(row < rows, initial(context, inside), initial(context ^ 1, inside))
    start, end = jnp.zeros_like(orig), jnp.int32(0)
    for i in range(lengths_ref.shape[0]):
        end = end + lengths_ref[i]
        start = jnp.where(orig >= end, end, start)
    low_ref[...] = start[:, :1]
    high_ref[...] = orig[:, :1]
    angle = (orig - start).astype(jnp.float32) * freq_ref[...]
    lane = lax.broadcasted_iota(jnp.int32, cos_ref.shape, 1)
    cos_ref[...] = jnp.cos(angle)
    sine = jnp.sin(angle)
    sin_ref[...] = jnp.where(lane < HD // 2, -sine, sine)
    inside = inside_of(lax.broadcasted_iota(jnp.int32, (1, rows), 1))
    for chip in range(orig_ref.shape[1] // rows):
        owner = 2 * chip + context % 2
        orig_ref[:, chip * rows : (chip + 1) * rows] = initial(owner, inside)


def norm_kernel(place, chips, hidden_ref, gain_ref, own_ref, other_ref):
    at, core = place_of(place)
    wide = hidden_ref[...].astype(jnp.float32)
    meansq = jnp.mean(wide * wide, axis=-1, keepdims=True)
    scaled = wide * lax.rsqrt(meansq + 1e-05)
    lanes = gain_ref.shape[1]
    normed = jnp.concatenate(
        [
            (
                scaled[:, i * lanes : (i + 1) * lanes]
                * gain_ref[i : i + 1, :].astype(jnp.float32)
            ).astype(jnp.bfloat16)
            for i in range(gain_ref.shape[0])
        ],
        axis=1,
    )
    block = own_ref.shape[2]
    for even in range(2):

        @pl.when(core == even)
        def _():
            for chip in range(chips):
                slot = lax.rem(place[chip] + chips - at, chips)
                for side in range(2):
                    column = (2 * chip + side) * block
                    ref = own_ref if side == even else other_ref
                    ref[slot] = normed[:, column : column + block]


def take_ring(refs, chips):
    refs = list(refs)
    if chips % 2:
        return [(ref,) for ref in refs]
    half = chips // 2
    return [(r,) for r in refs[:half]] + [tuple(refs[half : half + 2])] + [
        (r,) for r in refs[half + 2 :]
    ]


def project_kernel(chips, groups, *refs):
    rows_refs, refs = refs[:groups], refs[groups:]
    weight_refs, (mine_ref, theirs_ref, queries_ref) = refs[:-3], refs[-3:]
    weights = take_ring(weight_refs, chips)
    total = None
    for slot in range(chips):
        rows = jnp.concatenate([ref[slot] for ref in rows_refs], axis=0)
        start = 0
        for ref in weights[slot]:
            depth = ref.shape[0]
            part = jnp.dot(
                rows[:, start : start + depth], ref[...], preferred_element_type=jnp.float32
            )
            total = part if total is None else total + part
            start += depth
    count = mine_ref.shape[0]
    mine_ref[...] = total[:count, HEAD_COLS:]
    theirs_ref[...] = total[count:, HEAD_COLS:]
    queries_ref[...] = total[:, :HEAD_COLS]


def turn(values, cosine, sine):
    return values * cosine + pltpu.roll(values, HD // 2, 1) * sine


def keys_kernel(chips, mine_ref, theirs_ref, cosine_ref, sine_ref, out_ref):
    rows = out_ref.shape[0] // chips
    cosine, sine = cosine_ref[:rows, :], sine_ref[:rows, :]
    total = mine_ref[...] + theirs_ref[...]
    keys = turn(total[:, :HD], cosine, sine).astype(jnp.bfloat16)
    values = total[:, HD:].astype(jnp.bfloat16)
    for chip in range(chips):
        out_ref[chip * rows : (chip + 1) * rows, :HD] = keys
        out_ref[chip * rows : (chip + 1) * rows, HD:] = values


def attend_kernel(
    mine_ref,
    theirs_ref,
    cosine_ref,
    sine_ref,
    low_ref,
    high_ref,
    orig_ref,
    kv_ref,
    out_ref,
):
    keys = kv_ref[:, :HD]
    values = kv_ref[:, HD:]
    orig = orig_ref[...]
    allowed = (orig >= low_ref[...]) & (orig <= high_ref[...])
    scale = 1.0 / HD**0.5
    rows = out_ref.shape[0]
    half = rows // 2
    lane = lax.broadcasted_iota(jnp.int32, (rows, HD), 1)
    stats = jnp.zeros((rows, HD), jnp.float32)
    for head in range(QH_DEV):
        columns = slice(head * HD, (head + 1) * HD)
        query = jnp.concatenate(
            [
                mine_ref[:half, columns] + theirs_ref[half:, columns],
                mine_ref[half:, columns] + theirs_ref[:half, columns],
            ],
            axis=0,
        )
        query = turn(query, cosine_ref[...], sine_ref[...]).astype(jnp.bfloat16)
        scores = lax.dot_general(
            query, keys, (((1,), (1,)), ((), ())), preferred_element_type=jnp.float32
        )
        scores = jnp.where(allowed, scores * scale, -1e30)
        top = jnp.max(scores, axis=-1, keepdims=True)
        expo = jnp.where(allowed, jnp.exp(scores - top), 0.0)
        total = jnp.sum(expo, axis=-1, keepdims=True)
        out_ref[:, columns] = jnp.dot(
            expo.astype(jnp.bfloat16), values, preferred_element_type=jnp.float32
        )
        stats = jnp.where(lane == 2 * head, total, stats)
        stats = jnp.where(lane == 2 * head + 1, top, stats)
    out_ref[:, HEAD_COLS:] = stats


def output_kernel(groups, pieces_of, mine_ref, theirs_ref, *refs):
    weight_refs, out_refs = refs[:-groups], refs[-groups:]
    chip_rows = mine_ref.shape[0]
    half = chip_rows // 2

    def swapped(columns):
        return jnp.concatenate([theirs_ref[half:, columns], theirs_ref[:half, columns]], axis=0)

    pieces = []
    for head in range(QH_DEV):
        columns = slice(head * HD, (head + 1) * HD)
        at = HEAD_COLS + 2 * head
        total, top = mine_ref[:, at : at + 1], mine_ref[:, at + 1 : at + 2]
        other_total, other_top = swapped(slice(at, at + 1)), swapped(slice(at + 1, at + 2))
        peak = jnp.maximum(top, other_top)
        factor, other_factor = jnp.exp(top - peak), jnp.exp(other_top - peak)
        product = mine_ref[:, columns] * factor + swapped(columns) * other_factor
        pieces.append(
            (product / (total * factor + other_total * other_factor)).astype(jnp.bfloat16)
        )
    mixed = jnp.concatenate(pieces, axis=1)
    rows = chip_rows // groups
    weight_refs = iter(weight_refs)
    for slot, pieces in enumerate(pieces_of):
        start, total = 0, None
        for _ in range(pieces):
            ref = next(weight_refs)
            depth = ref.shape[0]
            part = jnp.dot(
                mixed[:, start : start + depth], ref[...], preferred_element_type=jnp.float32
            )
            total = part if total is None else total + part
            start += depth
        total = total.astype(jnp.bfloat16)
        for group in range(groups):
            out_refs[group][slot] = total[group * rows : (group + 1) * rows]


def sum_kernel(place, chips, groups, near, token_ref, *refs):
    near_refs, far_refs, out_ref = refs[:groups], refs[groups : 2 * groups], refs[2 * groups]
    at, core = place_of(place)
    block = near_refs[0].shape[2]
    half = groups // 2

    def added(part, slot):
        turn_at = lax.rem(slot + near // 2, chips)
        total = None
        for group in range(part * half, (part + 1) * half):
            rows = jnp.where(
                turn_at < near,
                near_refs[group][jnp.minimum(turn_at, near - 1)].astype(jnp.float32),
                far_refs[group][jnp.maximum(turn_at - near, 0)].astype(jnp.float32),
            )
            total = rows if total is None else total + rows
        return total.astype(jnp.bfloat16)

    for even in range(2):

        @pl.when(core == even)
        def _():
            for chip in range(chips):
                slot = lax.rem(place[chip] + chips - at, chips)
                for side in range(2):
                    column = (2 * chip + side) * block
                    out_ref[:, column : column + block] = added(side ^ even, slot)


def per_device(n_context, n_tensor, hidden_rows, norm_gain, w_qkv, w_out, doc_lengths, span_order):
    chips = n_context // 2
    ring = ring_of_chips(chips)
    place = [ring.index(chip) for chip in range(chips)]
    groups = 2 * n_tensor
    rows_here, width = hidden_rows.shape
    tokens_here = rows_here * n_tensor
    block = width // n_context
    context = lax.axis_index("context")
    tensor = lax.axis_index("tensor")
    ahead = [
        (ring[i] * 2 + k, ring[(i + 1) % chips] * 2 + k) for i in range(chips) for k in range(2)
    ]
    back = [(b, a) for a, b in ahead]
    sibling = [(c, c ^ 1) for c in range(n_context)]

    same_core = [[2 * chip + k for chip in range(chips)] for k in range(2)]
    token = [doc_lengths]

    def ordered(values):
        held = lax.optimization_barrier((*values, token[0]))
        token[0] = held[-1]
        return list(held[:-1])

    class Ring:
        def __init__(self, mine):
            self.up, self.down = [mine], [mine]
            self.middle = []

        def step(self, earlier=()):
            up, down, *earlier = ordered((self.up[-1], self.down[-1], *earlier))
            if len(self.up) <= (chips - 1) // 2:
                self.up.append(lax.ppermute(up, "context", ahead))
                self.down.append(lax.ppermute(down, "context", back))
            elif chips % 2 == 0 and not self.middle:
                half = up.shape[0] // 2
                self.middle = [
                    lax.ppermute(up[:half], "context", ahead),
                    lax.ppermute(down[half:], "context", back),
                ]
            return earlier

        def done(self):
            return len(self.up) > (chips - 1) // 2 and (chips % 2 == 1 or bool(self.middle))

        def finish(self):
            while not self.done():
                self.step()
            return self.down + self.middle + self.up[:0:-1]

        def block(self, slot):
            slot %= chips
            if chips % 2 == 0 and slot == chips // 2:
                return tuple(self.middle)
            return (self.down[slot] if slot <= chips // 2 else self.up[chips - slot],)

    def member(e, d):
        return [
            (c * n_tensor + t, (c ^ e) * n_tensor + (t - d) % n_tensor)
            for c in range(n_context)
            for t in range(n_tensor)
        ]

    smem, vmem = pl.BlockSpec(memory_space=pltpu.SMEM), pl.BlockSpec(memory_space=pltpu.VMEM)
    freq = rope_theta ** (-(np.arange(HD // 2, dtype=np.float64) * 2.0 / HD))
    freq = np.concatenate([freq, freq]).astype(np.float32)[None, :]
    table = jax.ShapeDtypeStruct((2 * tokens_here, HD), jnp.float32)
    bound = jax.ShapeDtypeStruct((2 * tokens_here, 1), jnp.int32)
    cosine, sine, query_start, query_orig, key_orig = pl.pallas_call(
        functools.partial(where_kernel, n_tensor, rows_here),
        out_shape=[
            table,
            table,
            bound,
            bound,
            jax.ShapeDtypeStruct((1, chips * tokens_here), jnp.int32),
        ],
        in_specs=[smem, smem, vmem],
        out_specs=vmem_specs(5),
        compiler_params=compute_params(),
        name="where",
    )(span_order, doc_lengths, jnp.asarray(freq))

    qkv_ring = Ring(w_qkv)
    qkv_ring.step()
    own, other = pl.pallas_call(
        functools.partial(norm_kernel, place, chips),
        out_shape=[jax.ShapeDtypeStruct((chips, rows_here, block), jnp.bfloat16)] * 2,
        in_specs=vmem_specs(2),
        out_specs=vmem_specs(2),
        compiler_params=compute_params(),
        name="norm",
    )(hidden_rows, norm_gain.reshape(-1, HD))

    def from_tensor(rows):
        return [rows] + [
            lax.ppermute(rows, "tensor", [(t, (t - d) % n_tensor) for t in range(n_tensor)])
            for d in range(1, n_tensor)
        ]

    other = from_tensor(other)
    normed = from_tensor(own)
    normed += [lax.ppermute(rows, "context", sibling) for rows in other]

    qkv_ring.step()
    cosine, sine, query_start, query_orig, key_orig = ordered(
        (cosine, sine, query_start, query_orig, key_orig)
    )
    qkv_ring.step()
    normed = qkv_ring.step(normed)
    while not qkv_ring.done():
        qkv_ring.step()

    out_ring = Ring(w_out)
    out_ring.step()
    blocks = qkv_ring.finish()
    mine, theirs, queries = pl.pallas_call(
        functools.partial(project_kernel, chips, groups),
        out_shape=[
            jax.ShapeDtypeStruct((tokens_here, 2 * HD), jnp.float32),
            jax.ShapeDtypeStruct((tokens_here, 2 * HD), jnp.float32),
            jax.ShapeDtypeStruct((2 * tokens_here, HEAD_COLS), jnp.float32),
        ],
        in_specs=vmem_specs(groups + len(blocks)),
        out_specs=vmem_specs(3),
        compiler_params=compute_params(),
        name="project",
    )(*ordered((*normed, *blocks)))
    theirs = lax.ppermute(theirs, "context", sibling)
    queries_theirs = lax.ppermute(queries, "context", sibling)
    out_ring.step()
    mine, theirs = ordered((mine, theirs))
    kv = pl.pallas_call(
        functools.partial(keys_kernel, chips),
        out_shape=jax.ShapeDtypeStruct((chips * tokens_here, 2 * HD), jnp.bfloat16),
        in_specs=vmem_specs(4),
        out_specs=vmem_specs(1)[0],
        compiler_params=compute_params(),
        name="keys",
    )(mine, theirs, cosine, sine)
    (kv,) = ordered((kv,))
    kv = lax.all_to_all(
        kv, "context", split_axis=0, concat_axis=0, axis_index_groups=same_core, tiled=True
    )
    out_ring.step()
    (kv,) = ordered((kv,))

    mixed = pl.pallas_call(
        attend_kernel,
        out_shape=jax.ShapeDtypeStruct((2 * tokens_here, HEAD_COLS + HD), jnp.float32),
        in_specs=vmem_specs(8),
        out_specs=vmem_specs(1)[0],
        compiler_params=compute_params(),
        name="attend",
    )(
        queries,
        queries_theirs,
        cosine,
        sine,
        query_start,
        query_orig,
        key_orig,
        kv,
    )
    (mixed,) = ordered((mixed,))
    mixed_theirs = lax.ppermute(mixed, "context", sibling)

    out_block = w_out.shape[1]

    def output(slots, name):
        blocks = [out_ring.block(slot) for slot in slots]
        flat = [piece for pieces in blocks for piece in pieces]
        parts = pl.pallas_call(
            functools.partial(output_kernel, groups, [len(pieces) for pieces in blocks]),
            out_shape=[jax.ShapeDtypeStruct((len(slots), rows_here, out_block), jnp.bfloat16)]
            * groups,
            in_specs=vmem_specs(2 + len(flat)),
            out_specs=vmem_specs(groups),
            compiler_params=compute_params(),
            name=name,
        )(mixed, mixed_theirs, *flat)
        parts = ordered(parts)
        arrived = []
        for e in range(2):
            for d in range(n_tensor):
                part = parts[e * n_tensor + d]
                if e or d:
                    part = lax.ppermute(part, ("context", "tensor"), member(e, -d))
                arrived.append(part)
        return arrived

    reach = max(chips // 2 - 2, 0)
    while len(out_ring.up) <= reach:
        out_ring.step()
    near = 2 * reach + 1
    arrived = output(list(range(-reach, reach + 1)), "output_near")
    while not out_ring.done():
        out_ring.step()
    arrived += output(list(range(reach + 1, chips - reach)), "output_far")
    return pl.pallas_call(
        functools.partial(sum_kernel, place, chips, groups, near),
        out_shape=jax.ShapeDtypeStruct((rows_here, n_context * out_block), jnp.bfloat16),
        in_specs=[pl.BlockSpec(memory_space=pl.ANY)] + vmem_specs(2 * groups),
        out_specs=vmem_specs(1)[0],
        compiler_params=compute_params(),
        name="sum",
    )(token[0], *arrived)


def solution(mesh):
    placed = (
        P(("context", "tensor"), None),
        P(),
        P("context", "tensor"),
        P("tensor", "context"),
        P(),
        P(),
    )
    return jax.shard_map(
        functools.partial(per_device, mesh.shape["context"], mesh.shape["tensor"]),
        mesh=mesh,
        in_specs=placed,
        out_specs=P(("context", "tensor"), None),
        check_vma=False,
    )
```

```python
import functools

import jax
import jax.numpy as jnp
import numpy as np
from jax import lax
from jax.experimental import pallas as pl
from jax.experimental.pallas import tpu as pltpu
from jax.sharding import PartitionSpec as P

HD = 128
QH_DEV = 4
SPAN = 64
HEAD_COLS = QH_DEV * HD
VMEM_LIMIT = 24 * 1024 * 1024

rope_theta = 500000.0


def ring_of_chips(count):
    wide = 1
    while (wide * 2) * (wide * 2) <= count:
        wide *= 2
    tall = count // wide
    if wide < 2:
        return list(range(count))
    ring = [(z, 0) for z in range(tall)]
    for z in range(tall - 1, -1, -1):
        row = list(range(1, wide))
        ring += [(z, y) for y in (row if (tall - 1 - z) % 2 == 0 else row[::-1])]
    if (tall - 1) % 2 == 0 or wide == 2:
        return [z * wide + y for z, y in ring]
    return [z * wide + y for z, y in ring]


def vmem_specs(count):
    return [pl.BlockSpec(memory_space=pltpu.VMEM)] * count


def compute_params():
    return pltpu.CompilerParams(vmem_limit_bytes=VMEM_LIMIT)


def place_of(place):
    context = lax.axis_index("context")
    at = jnp.int32(0)
    for chip, spot in enumerate(place):
        at = jnp.where(context // 2 == chip, jnp.int32(spot), at)
    return at, context % 2


def where_kernel(
    n_tensor, rows_here, spans_ref, lengths_ref, freq_ref, cos_ref, sin_ref, low_ref, high_ref, orig_ref
):
    context, tensor = lax.axis_index("context"), lax.axis_index("tensor")
    rows = rows_here * n_tensor
    spans = rows // SPAN

    def shift(values, size):
        return lax.shift_right_logical(values, jnp.int32(size.bit_length() - 1))

    def inside_of(row):
        row = row & (rows - 1)
        turned = (tensor + shift(row, rows_here)) & (n_tensor - 1)
        return turned * rows_here + (row & (rows_here - 1))

    def initial(owner, inside):
        source = jnp.zeros_like(inside)
        for k in range(spans):
            source = jnp.where(shift(inside, SPAN) == k, spans_ref[owner * spans + k], source)
        return source * SPAN + (inside & (SPAN - 1))

    row = lax.broadcasted_iota(jnp.int32, cos_ref.shape, 0)
    inside = inside_of(row)
    orig = jnp.where(row < rows, initial(context, inside), initial(context ^ 1, inside))
    start, end = jnp.zeros_like(orig), jnp.int32(0)
    for i in range(lengths_ref.shape[0]):
        end = end + lengths_ref[i]
        start = jnp.where(orig >= end, end, start)
    low_ref[...] = start[:, :1]
    high_ref[...] = orig[:, :1]
    angle = (orig - start).astype(jnp.float32) * freq_ref[...]
    lane = lax.broadcasted_iota(jnp.int32, cos_ref.shape, 1)
    cos_ref[...] = jnp.cos(angle)
    sine = jnp.sin(angle)
    sin_ref[...] = jnp.where(lane < HD // 2, -sine, sine)
    inside = inside_of(lax.broadcasted_iota(jnp.int32, (1, rows), 1))
    for chip in range(orig_ref.shape[1] // rows):
        owner = 2 * chip + context % 2
        orig_ref[:, chip * rows : (chip + 1) * rows] = initial(owner, inside)


def norm_kernel(place, chips, hidden_ref, gain_ref, out_ref):
    at, core = place_of(place)
    wide = hidden_ref[...].astype(jnp.float32)
    meansq = jnp.mean(wide * wide, axis=-1, keepdims=True)
    scaled = wide * lax.rsqrt(meansq + 1e-05)
    lanes = gain_ref.shape[1]
    normed = jnp.concatenate(
        [
            (
                scaled[:, i * lanes : (i + 1) * lanes]
                * gain_ref[i : i + 1, :].astype(jnp.float32)
            ).astype(jnp.bfloat16)
            for i in range(gain_ref.shape[0])
        ],
        axis=1,
    )
    block = out_ref.shape[3]
    for even in range(2):

        @pl.when(core == even)
        def _():
            for chip in range(chips):
                slot = lax.rem(place[chip] + chips - at, chips)
                for side in range(2):
                    column = (2 * chip + side) * block
                    out_ref[side ^ even, slot] = normed[:, column : column + block]


def take_ring(refs, chips):
    refs = list(refs)
    if chips % 2:
        return [(ref,) for ref in refs]
    half = chips // 2
    return [(r,) for r in refs[:half]] + [tuple(refs[half : half + 2])] + [
        (r,) for r in refs[half + 2 :]
    ]


def project_kernel(chips, groups, *refs):
    rows_refs, refs = refs[:groups], refs[groups:]
    weight_refs, (mine_ref, theirs_ref, queries_ref) = refs[:-3], refs[-3:]
    half = groups // 2
    weights = take_ring(weight_refs, chips)
    total = None
    for slot in range(chips):
        rows = jnp.concatenate(
            [ref[group // half, slot] for group, ref in enumerate(rows_refs)], axis=0
        )
        start = 0
        for ref in weights[slot]:
            depth = ref.shape[0]
            part = jnp.dot(
                rows[:, start : start + depth], ref[...], preferred_element_type=jnp.float32
            )
            total = part if total is None else total + part
            start += depth
    count = mine_ref.shape[0]
    mine_ref[...] = total[:count, HEAD_COLS:]
    theirs_ref[...] = total[count:, HEAD_COLS:]
    queries_ref[...] = total[:, :HEAD_COLS]


def turn(values, cosine, sine):
    return values * cosine + pltpu.roll(values, HD // 2, 1) * sine


def keys_kernel(chips, mine_ref, theirs_ref, cosine_ref, sine_ref, out_ref):
    rows = out_ref.shape[0] // chips
    cosine, sine = cosine_ref[:rows, :], sine_ref[:rows, :]
    total = mine_ref[...] + theirs_ref[...]
    keys = turn(total[:, :HD], cosine, sine).astype(jnp.bfloat16)
    values = total[:, HD:].astype(jnp.bfloat16)
    for chip in range(chips):
        out_ref[chip * rows : (chip + 1) * rows, :HD] = keys
        out_ref[chip * rows : (chip + 1) * rows, HD:] = values


def attend_kernel(
    mine_ref,
    theirs_ref,
    cosine_ref,
    sine_ref,
    low_ref,
    high_ref,
    orig_ref,
    kv_ref,
    out_ref,
):
    keys = kv_ref[:, :HD]
    values = kv_ref[:, HD:]
    orig = orig_ref[...]
    allowed = (orig >= low_ref[...]) & (orig <= high_ref[...])
    scale = 1.0 / HD**0.5
    rows = out_ref.shape[0]
    half = rows // 2
    lane = lax.broadcasted_iota(jnp.int32, (rows, HD), 1)
    stats = jnp.zeros((rows, HD), jnp.float32)
    for head in range(QH_DEV):
        columns = slice(head * HD, (head + 1) * HD)
        query = jnp.concatenate(
            [
                mine_ref[:half, columns] + theirs_ref[half:, columns],
                mine_ref[half:, columns] + theirs_ref[:half, columns],
            ],
            axis=0,
        )
        query = turn(query, cosine_ref[...], sine_ref[...]).astype(jnp.bfloat16)
        scores = lax.dot_general(
            query, keys, (((1,), (1,)), ((), ())), preferred_element_type=jnp.float32
        )
        scores = jnp.where(allowed, scores * scale, -1e30)
        top = jnp.max(scores, axis=-1, keepdims=True)
        expo = jnp.where(allowed, jnp.exp(scores - top), 0.0)
        total = jnp.sum(expo, axis=-1, keepdims=True)
        out_ref[:, columns] = jnp.dot(
            expo.astype(jnp.bfloat16), values, preferred_element_type=jnp.float32
        )
        stats = jnp.where(lane == 2 * head, total, stats)
        stats = jnp.where(lane == 2 * head + 1, top, stats)
    out_ref[:, HEAD_COLS:] = stats


def output_kernel(groups, pieces_of, mine_ref, theirs_ref, *refs):
    weight_refs, out_refs = refs[:-groups], refs[-groups:]
    chip_rows = mine_ref.shape[0]
    half = chip_rows // 2

    def swapped(columns):
        return jnp.concatenate([theirs_ref[half:, columns], theirs_ref[:half, columns]], axis=0)

    pieces = []
    for head in range(QH_DEV):
        columns = slice(head * HD, (head + 1) * HD)
        at = HEAD_COLS + 2 * head
        total, top = mine_ref[:, at : at + 1], mine_ref[:, at + 1 : at + 2]
        other_total, other_top = swapped(slice(at, at + 1)), swapped(slice(at + 1, at + 2))
        peak = jnp.maximum(top, other_top)
        factor, other_factor = jnp.exp(top - peak), jnp.exp(other_top - peak)
        product = mine_ref[:, columns] * factor + swapped(columns) * other_factor
        pieces.append(
            (product / (total * factor + other_total * other_factor)).astype(jnp.bfloat16)
        )
    mixed = jnp.concatenate(pieces, axis=1)
    rows = chip_rows // groups
    weight_refs = iter(weight_refs)
    for slot, pieces in enumerate(pieces_of):
        start, total = 0, None
        for _ in range(pieces):
            ref = next(weight_refs)
            depth = ref.shape[0]
            part = jnp.dot(
                mixed[:, start : start + depth], ref[...], preferred_element_type=jnp.float32
            )
            total = part if total is None else total + part
            start += depth
        total = total.astype(jnp.bfloat16)
        for group in range(groups):
            out_refs[group][slot] = total[group * rows : (group + 1) * rows]


def sum_kernel(place, chips, groups, near, token_ref, *refs):
    near_refs, far_refs, out_ref = refs[:groups], refs[groups : 2 * groups], refs[2 * groups]
    at, core = place_of(place)
    block = near_refs[0].shape[2]
    half = groups // 2

    def added(part, slot):
        turn_at = lax.rem(slot + near // 2, chips)
        total = None
        for group in range(part * half, (part + 1) * half):
            rows = jnp.where(
                turn_at < near,
                near_refs[group][jnp.minimum(turn_at, near - 1)].astype(jnp.float32),
                far_refs[group][jnp.maximum(turn_at - near, 0)].astype(jnp.float32),
            )
            total = rows if total is None else total + rows
        return total.astype(jnp.bfloat16)

    for even in range(2):

        @pl.when(core == even)
        def _():
            for chip in range(chips):
                slot = lax.rem(place[chip] + chips - at, chips)
                for side in range(2):
                    column = (2 * chip + side) * block
                    out_ref[:, column : column + block] = added(side ^ even, slot)


def per_device(n_context, n_tensor, hidden_rows, norm_gain, w_qkv, w_out, doc_lengths, span_order):
    chips = n_context // 2
    ring = ring_of_chips(chips)
    place = [ring.index(chip) for chip in range(chips)]
    groups = 2 * n_tensor
    rows_here, width = hidden_rows.shape
    tokens_here = rows_here * n_tensor
    block = width // n_context
    context = lax.axis_index("context")
    tensor = lax.axis_index("tensor")
    ahead = [
        (ring[i] * 2 + k, ring[(i + 1) % chips] * 2 + k) for i in range(chips) for k in range(2)
    ]
    back = [(b, a) for a, b in ahead]
    sibling = [(c, c ^ 1) for c in range(n_context)]

    same_core = [[2 * chip + k for chip in range(chips)] for k in range(2)]
    token = [doc_lengths]

    def ordered(values):
        held = lax.optimization_barrier((*values, token[0]))
        token[0] = held[-1]
        return list(held[:-1])

    class Ring:
        def __init__(self, mine):
            self.up, self.down = [mine], [mine]
            self.middle = []

        def step(self, earlier=()):
            up, down, *earlier = ordered((self.up[-1], self.down[-1], *earlier))
            if len(self.up) <= (chips - 1) // 2:
                self.up.append(lax.ppermute(up, "context", ahead))
                self.down.append(lax.ppermute(down, "context", back))
            elif chips % 2 == 0 and not self.middle:
                half = up.shape[0] // 2
                self.middle = [
                    lax.ppermute(up[:half], "context", ahead),
                    lax.ppermute(down[half:], "context", back),
                ]
            return earlier

        def done(self):
            return len(self.up) > (chips - 1) // 2 and (chips % 2 == 1 or bool(self.middle))

        def finish(self):
            while not self.done():
                self.step()
            return self.down + self.middle + self.up[:0:-1]

        def block(self, slot):
            slot %= chips
            if chips % 2 == 0 and slot == chips // 2:
                return tuple(self.middle)
            return (self.down[slot] if slot <= chips // 2 else self.up[chips - slot],)

    def member(e, d):
        return [
            (c * n_tensor + t, (c ^ e) * n_tensor + (t - d) % n_tensor)
            for c in range(n_context)
            for t in range(n_tensor)
        ]

    smem, vmem = pl.BlockSpec(memory_space=pltpu.SMEM), pl.BlockSpec(memory_space=pltpu.VMEM)
    freq = rope_theta ** (-(np.arange(HD // 2, dtype=np.float64) * 2.0 / HD))
    freq = np.concatenate([freq, freq]).astype(np.float32)[None, :]
    table = jax.ShapeDtypeStruct((2 * tokens_here, HD), jnp.float32)
    bound = jax.ShapeDtypeStruct((2 * tokens_here, 1), jnp.int32)
    cosine, sine, query_start, query_orig, key_orig = pl.pallas_call(
        functools.partial(where_kernel, n_tensor, rows_here),
        out_shape=[
            table,
            table,
            bound,
            bound,
            jax.ShapeDtypeStruct((1, chips * tokens_here), jnp.int32),
        ],
        in_specs=[smem, smem, vmem],
        out_specs=vmem_specs(5),
        compiler_params=compute_params(),
        name="where",
    )(span_order, doc_lengths, jnp.asarray(freq))

    qkv_ring = Ring(w_qkv)
    qkv_ring.step()
    normed = pl.pallas_call(
        functools.partial(norm_kernel, place, chips),
        out_shape=jax.ShapeDtypeStruct((2, chips, rows_here, block), jnp.bfloat16),
        in_specs=vmem_specs(2),
        out_specs=vmem_specs(1)[0],
        compiler_params=compute_params(),
        name="norm",
    )(hidden_rows, norm_gain.reshape(-1, HD))
    normed = [normed] + [
        lax.ppermute(
            normed, "tensor", [(t, (t - d) % n_tensor) for t in range(n_tensor)]
        )
        for d in range(1, n_tensor)
    ]
    normed += [lax.ppermute(rows, "context", sibling) for rows in normed]

    qkv_ring.step()
    cosine, sine, query_start, query_orig, key_orig = ordered(
        (cosine, sine, query_start, query_orig, key_orig)
    )
    qkv_ring.step()
    normed = qkv_ring.step(normed)
    while not qkv_ring.done():
        qkv_ring.step()

    out_ring = Ring(w_out)
    out_ring.step()
    blocks = qkv_ring.finish()
    mine, theirs, queries = pl.pallas_call(
        functools.partial(project_kernel, chips, groups),
        out_shape=[
            jax.ShapeDtypeStruct((tokens_here, 2 * HD), jnp.float32),
            jax.ShapeDtypeStruct((tokens_here, 2 * HD), jnp.float32),
            jax.ShapeDtypeStruct((2 * tokens_here, HEAD_COLS), jnp.float32),
        ],
        in_specs=vmem_specs(groups + len(blocks)),
        out_specs=vmem_specs(3),
        compiler_params=compute_params(),
        name="project",
    )(*ordered((*normed, *blocks)))
    theirs = lax.ppermute(theirs, "context", sibling)
    queries_theirs = lax.ppermute(queries, "context", sibling)
    mine, theirs = ordered((mine, theirs))
    kv = pl.pallas_call(
        functools.partial(keys_kernel, chips),
        out_shape=jax.ShapeDtypeStruct((chips * tokens_here, 2 * HD), jnp.bfloat16),
        in_specs=vmem_specs(4),
        out_specs=vmem_specs(1)[0],
        compiler_params=compute_params(),
        name="keys",
    )(mine, theirs, cosine, sine)
    (kv,) = ordered((kv,))
    kv = lax.all_to_all(
        kv, "context", split_axis=0, concat_axis=0, axis_index_groups=same_core, tiled=True
    )
    (kv,) = ordered((kv,))

    mixed = pl.pallas_call(
        attend_kernel,
        out_shape=jax.ShapeDtypeStruct((2 * tokens_here, HEAD_COLS + HD), jnp.float32),
        in_specs=vmem_specs(8),
        out_specs=vmem_specs(1)[0],
        compiler_params=compute_params(),
        name="attend",
    )(
        queries,
        queries_theirs,
        cosine,
        sine,
        query_start,
        query_orig,
        key_orig,
        kv,
    )
    out_ring.step()
    (mixed,) = ordered((mixed,))
    mixed_theirs = lax.ppermute(mixed, "context", sibling)

    out_block = w_out.shape[1]

    def output(slots, name):
        blocks = [out_ring.block(slot) for slot in slots]
        flat = [piece for pieces in blocks for piece in pieces]
        parts = pl.pallas_call(
            functools.partial(output_kernel, groups, [len(pieces) for pieces in blocks]),
            out_shape=[jax.ShapeDtypeStruct((len(slots), rows_here, out_block), jnp.bfloat16)]
            * groups,
            in_specs=vmem_specs(2 + len(flat)),
            out_specs=vmem_specs(groups),
            compiler_params=compute_params(),
            name=name,
        )(mixed, mixed_theirs, *flat)
        parts = ordered(parts)
        arrived = []
        for e in range(2):
            for d in range(n_tensor):
                part = parts[e * n_tensor + d]
                if e or d:
                    part = lax.ppermute(part, ("context", "tensor"), member(e, -d))
                arrived.append(part)
        return arrived

    reach = max(chips // 2 - 2, 0)
    while len(out_ring.up) <= reach:
        out_ring.step()
    near = 2 * reach + 1
    arrived = output(list(range(-reach, reach + 1)), "output_near")
    while not out_ring.done():
        out_ring.step()
    arrived += output(list(range(reach + 1, chips - reach)), "output_far")
    return pl.pallas_call(
        functools.partial(sum_kernel, place, chips, groups, near),
        out_shape=jax.ShapeDtypeStruct((rows_here, n_context * out_block), jnp.bfloat16),
        in_specs=[pl.BlockSpec(memory_space=pl.ANY)] + vmem_specs(2 * groups),
        out_specs=vmem_specs(1)[0],
        compiler_params=compute_params(),
        name="sum",
    )(token[0], *arrived)


def solution(mesh):
    placed = (
        P(("context", "tensor"), None),
        P(),
        P("context", "tensor"),
        P("tensor", "context"),
        P(),
        P(),
    )
    return jax.shard_map(
        functools.partial(per_device, mesh.shape["context"], mesh.shape["tensor"]),
        mesh=mesh,
        in_specs=placed,
        out_specs=P(("context", "tensor"), None),
        check_vma=False,
    )
```

```python
import functools

import jax
import jax.numpy as jnp
import numpy as np
from jax import lax
from jax.experimental import pallas as pl
from jax.experimental.pallas import tpu as pltpu
from jax.sharding import PartitionSpec as P

HD = 128
QH_DEV = 4
SPAN = 64
HEAD_COLS = QH_DEV * HD
VMEM_LIMIT = 24 * 1024 * 1024

rope_theta = 500000.0


def ring_of_chips(count):
    wide = 1
    while (wide * 2) * (wide * 2) <= count:
        wide *= 2
    tall = count // wide
    if wide < 2:
        return list(range(count))
    ring = [(z, 0) for z in range(tall)]
    for z in range(tall - 1, -1, -1):
        row = list(range(1, wide))
        ring += [(z, y) for y in (row if (tall - 1 - z) % 2 == 0 else row[::-1])]
    if (tall - 1) % 2 == 0 or wide == 2:
        return [z * wide + y for z, y in ring]
    return [z * wide + y for z, y in ring]


def vmem_specs(count):
    return [pl.BlockSpec(memory_space=pltpu.VMEM)] * count


def compute_params():
    return pltpu.CompilerParams(vmem_limit_bytes=VMEM_LIMIT)


def place_of(place):
    context = lax.axis_index("context")
    at = jnp.int32(0)
    for chip, spot in enumerate(place):
        at = jnp.where(context // 2 == chip, jnp.int32(spot), at)
    return at, context % 2


def where_kernel(
    ring,
    place,
    n_tensor,
    rows_here,
    spans_ref,
    lengths_ref,
    freq_ref,
    cos_ref,
    sin_ref,
    low_ref,
    high_ref,
    orig_ref,
):
    context, tensor = lax.axis_index("context"), lax.axis_index("tensor")
    rows = rows_here * n_tensor
    spans = rows // SPAN

    def shift(values, size):
        return lax.shift_right_logical(values, jnp.int32(size.bit_length() - 1))

    def inside_of(row):
        row = row & (rows - 1)
        turned = (tensor + shift(row, rows_here)) & (n_tensor - 1)
        return turned * rows_here + (row & (rows_here - 1))

    def initial(owner, inside):
        source = jnp.zeros_like(inside)
        for k in range(spans):
            source = jnp.where(shift(inside, SPAN) == k, spans_ref[owner * spans + k], source)
        return source * SPAN + (inside & (SPAN - 1))

    row = lax.broadcasted_iota(jnp.int32, cos_ref.shape, 0)
    inside = inside_of(row)
    orig = jnp.where(row < rows, initial(context, inside), initial(context ^ 1, inside))
    start, end = jnp.zeros_like(orig), jnp.int32(0)
    for i in range(lengths_ref.shape[0]):
        end = end + lengths_ref[i]
        start = jnp.where(orig >= end, end, start)
    low_ref[...] = start[:, :1]
    high_ref[...] = orig[:, :1]
    angle = (orig - start).astype(jnp.float32) * freq_ref[...]
    lane = lax.broadcasted_iota(jnp.int32, cos_ref.shape, 1)
    cos_ref[...] = jnp.cos(angle)
    sine = jnp.sin(angle)
    sin_ref[...] = jnp.where(lane < HD // 2, -sine, sine)
    inside = inside_of(lax.broadcasted_iota(jnp.int32, (1, rows), 1))
    at, core = place_of(place)
    for slot in range(len(ring)):
        spot = lax.rem(at + slot, len(ring))
        chip = jnp.int32(0)
        for i, at_spot in enumerate(ring):
            chip = jnp.where(spot == i, jnp.int32(at_spot), chip)
        owner = 2 * chip + core
        orig_ref[:, slot * rows : (slot + 1) * rows] = initial(owner, inside)


def norm_kernel(place, chips, hidden_ref, gain_ref, out_ref):
    at, core = place_of(place)
    wide = hidden_ref[...].astype(jnp.float32)
    meansq = jnp.mean(wide * wide, axis=-1, keepdims=True)
    scaled = wide * lax.rsqrt(meansq + 1e-05)
    lanes = gain_ref.shape[1]
    normed = jnp.concatenate(
        [
            (
                scaled[:, i * lanes : (i + 1) * lanes]
                * gain_ref[i : i + 1, :].astype(jnp.float32)
            ).astype(jnp.bfloat16)
            for i in range(gain_ref.shape[0])
        ],
        axis=1,
    )
    block = out_ref.shape[3]
    for even in range(2):

        @pl.when(core == even)
        def _():
            for chip in range(chips):
                slot = lax.rem(place[chip] + chips - at, chips)
                for side in range(2):
                    column = (2 * chip + side) * block
                    out_ref[side ^ even, slot] = normed[:, column : column + block]


def take_ring(refs, chips):
    refs = list(refs)
    if chips % 2:
        return [(ref,) for ref in refs]
    half = chips // 2
    return [(r,) for r in refs[:half]] + [tuple(refs[half : half + 2])] + [
        (r,) for r in refs[half + 2 :]
    ]


def project_kernel(chips, groups, *refs):
    rows_refs, refs = refs[:groups], refs[groups:]
    weight_refs, (mine_ref, theirs_ref, queries_ref) = refs[:-3], refs[-3:]
    half = groups // 2
    weights = take_ring(weight_refs, chips)
    total = None
    for slot in range(chips):
        rows = jnp.concatenate(
            [ref[group // half, slot] for group, ref in enumerate(rows_refs)], axis=0
        )
        start = 0
        for ref in weights[slot]:
            depth = ref.shape[0]
            part = jnp.dot(
                rows[:, start : start + depth], ref[...], preferred_element_type=jnp.float32
            )
            total = part if total is None else total + part
            start += depth
    count = mine_ref.shape[0]
    mine_ref[...] = total[:count, HEAD_COLS:]
    theirs_ref[...] = total[count:, HEAD_COLS:]
    queries_ref[...] = total[:, :HEAD_COLS]


def turn(values, cosine, sine):
    return values * cosine + pltpu.roll(values, HD // 2, 1) * sine


def keys_kernel(mine_ref, theirs_ref, cosine_ref, sine_ref, out_ref):
    rows = out_ref.shape[0]
    total = mine_ref[...] + theirs_ref[...]
    out_ref[:, :HD] = turn(total[:, :HD], cosine_ref[:rows, :], sine_ref[:rows, :]).astype(
        jnp.bfloat16
    )
    out_ref[:, HD:] = total[:, HD:].astype(jnp.bfloat16)


def attend_kernel(
    mine_ref,
    theirs_ref,
    cosine_ref,
    sine_ref,
    low_ref,
    high_ref,
    orig_ref,
    *refs,
):
    block_refs, (out_ref, keys_ref, values_ref) = refs[:-3], refs[-3:]
    start = 0
    for ref in block_refs:
        keys_ref[start : start + ref.shape[0], :] = ref[:, :HD]
        values_ref[start : start + ref.shape[0], :] = ref[:, HD:]
        start += ref.shape[0]
    keys = keys_ref[...]
    values = values_ref[...]
    orig = orig_ref[...]
    allowed = (orig >= low_ref[...]) & (orig <= high_ref[...])
    scale = 1.0 / HD**0.5
    rows = out_ref.shape[0]
    half = rows // 2
    lane = lax.broadcasted_iota(jnp.int32, (rows, HD), 1)
    stats = jnp.zeros((rows, HD), jnp.float32)
    for head in range(QH_DEV):
        columns = slice(head * HD, (head + 1) * HD)
        query = jnp.concatenate(
            [
                mine_ref[:half, columns] + theirs_ref[half:, columns],
                mine_ref[half:, columns] + theirs_ref[:half, columns],
            ],
            axis=0,
        )
        query = turn(query, cosine_ref[...], sine_ref[...]).astype(jnp.bfloat16)
        scores = lax.dot_general(
            query, keys, (((1,), (1,)), ((), ())), preferred_element_type=jnp.float32
        )
        scores = jnp.where(allowed, scores * scale, -1e30)
        top = jnp.max(scores, axis=-1, keepdims=True)
        expo = jnp.where(allowed, jnp.exp(scores - top), 0.0)
        total = jnp.sum(expo, axis=-1, keepdims=True)
        out_ref[:, columns] = jnp.dot(
            expo.astype(jnp.bfloat16), values, preferred_element_type=jnp.float32
        )
        stats = jnp.where(lane == 2 * head, total, stats)
        stats = jnp.where(lane == 2 * head + 1, top, stats)
    out_ref[:, HEAD_COLS:] = stats


def output_kernel(chips, groups, mine_ref, theirs_ref, *refs):
    weight_refs, out_refs = refs[:-groups], refs[-groups:]
    weights = take_ring(weight_refs, chips)
    chip_rows = mine_ref.shape[0]
    half = chip_rows // 2

    def swapped(columns):
        return jnp.concatenate([theirs_ref[half:, columns], theirs_ref[:half, columns]], axis=0)

    pieces = []
    for head in range(QH_DEV):
        columns = slice(head * HD, (head + 1) * HD)
        at = HEAD_COLS + 2 * head
        total, top = mine_ref[:, at : at + 1], mine_ref[:, at + 1 : at + 2]
        other_total, other_top = swapped(slice(at, at + 1)), swapped(slice(at + 1, at + 2))
        peak = jnp.maximum(top, other_top)
        factor, other_factor = jnp.exp(top - peak), jnp.exp(other_top - peak)
        product = mine_ref[:, columns] * factor + swapped(columns) * other_factor
        pieces.append(
            (product / (total * factor + other_total * other_factor)).astype(jnp.bfloat16)
        )
    mixed = jnp.concatenate(pieces, axis=1)
    rows = chip_rows // groups
    for slot in range(chips):
        start, total = 0, None
        for ref in weights[slot]:
            depth = ref.shape[0]
            part = jnp.dot(
                mixed[:, start : start + depth], ref[...], preferred_element_type=jnp.float32
            )
            total = part if total is None else total + part
            start += depth
        total = total.astype(jnp.bfloat16)
        for group in range(groups):
            out_refs[group][slot] = total[group * rows : (group + 1) * rows]


def sum_kernel(place, chips, groups, token_ref, *refs):
    part_refs, out_ref = refs[:groups], refs[groups]
    at, core = place_of(place)
    block = part_refs[0].shape[2]
    half = groups // 2

    def added(part, slot):
        total = part_refs[part * half][slot].astype(jnp.float32)
        for ref in part_refs[part * half + 1 : (part + 1) * half]:
            total += ref[slot].astype(jnp.float32)
        return total.astype(jnp.bfloat16)

    for even in range(2):

        @pl.when(core == even)
        def _():
            for chip in range(chips):
                slot = lax.rem(place[chip] + chips - at, chips)
                for side in range(2):
                    column = (2 * chip + side) * block
                    out_ref[:, column : column + block] = added(side ^ even, slot)


def per_device(n_context, n_tensor, hidden_rows, norm_gain, w_qkv, w_out, doc_lengths, span_order):
    chips = n_context // 2
    ring = ring_of_chips(chips)
    place = [ring.index(chip) for chip in range(chips)]
    groups = 2 * n_tensor
    rows_here, width = hidden_rows.shape
    tokens_here = rows_here * n_tensor
    block = width // n_context
    context = lax.axis_index("context")
    tensor = lax.axis_index("tensor")
    ahead = [
        (ring[i] * 2 + k, ring[(i + 1) % chips] * 2 + k) for i in range(chips) for k in range(2)
    ]
    back = [(b, a) for a, b in ahead]
    sibling = [(c, c ^ 1) for c in range(n_context)]

    token = [doc_lengths]

    def ordered(values):
        held = lax.optimization_barrier((*values, token[0]))
        token[0] = held[-1]
        return list(held[:-1])

    class Ring:
        def __init__(self, mine):
            self.up, self.down = [mine], [mine]
            self.middle = []

        def step(self, earlier=()):
            up, down, *earlier = ordered((self.up[-1], self.down[-1], *earlier))
            if len(self.up) <= (chips - 1) // 2:
                self.up.append(lax.ppermute(up, "context", ahead))
                self.down.append(lax.ppermute(down, "context", back))
            elif chips % 2 == 0 and not self.middle:
                half = up.shape[0] // 2
                self.middle = [
                    lax.ppermute(up[:half], "context", ahead),
                    lax.ppermute(down[half:], "context", back),
                ]
            return earlier

        def done(self):
            return len(self.up) > (chips - 1) // 2 and (chips % 2 == 1 or bool(self.middle))

        def finish(self):
            while not self.done():
                self.step()
            return self.down + self.middle + self.up[:0:-1]

    def member(e, d):
        return [
            (c * n_tensor + t, (c ^ e) * n_tensor + (t - d) % n_tensor)
            for c in range(n_context)
            for t in range(n_tensor)
        ]

    smem, vmem = pl.BlockSpec(memory_space=pltpu.SMEM), pl.BlockSpec(memory_space=pltpu.VMEM)
    freq = rope_theta ** (-(np.arange(HD // 2, dtype=np.float64) * 2.0 / HD))
    freq = np.concatenate([freq, freq]).astype(np.float32)[None, :]
    table = jax.ShapeDtypeStruct((2 * tokens_here, HD), jnp.float32)
    bound = jax.ShapeDtypeStruct((2 * tokens_here, 1), jnp.int32)
    cosine, sine, query_start, query_orig, key_orig = pl.pallas_call(
        functools.partial(where_kernel, ring, place, n_tensor, rows_here),
        out_shape=[
            table,
            table,
            bound,
            bound,
            jax.ShapeDtypeStruct((1, chips * tokens_here), jnp.int32),
        ],
        in_specs=[smem, smem, vmem],
        out_specs=vmem_specs(5),
        compiler_params=compute_params(),
        name="where",
    )(span_order, doc_lengths, jnp.asarray(freq))

    qkv_ring = Ring(w_qkv)
    qkv_ring.step()
    normed = pl.pallas_call(
        functools.partial(norm_kernel, place, chips),
        out_shape=jax.ShapeDtypeStruct((2, chips, rows_here, block), jnp.bfloat16),
        in_specs=vmem_specs(2),
        out_specs=vmem_specs(1)[0],
        compiler_params=compute_params(),
        name="norm",
    )(hidden_rows, norm_gain.reshape(-1, HD))
    normed = [normed] + [
        lax.ppermute(
            normed, "tensor", [(t, (t - d) % n_tensor) for t in range(n_tensor)]
        )
        for d in range(1, n_tensor)
    ]
    normed += [lax.ppermute(rows, "context", sibling) for rows in normed]

    qkv_ring.step()
    cosine, sine, query_start, query_orig, key_orig = ordered(
        (cosine, sine, query_start, query_orig, key_orig)
    )
    qkv_ring.step()
    normed = qkv_ring.step(normed)
    while not qkv_ring.done():
        qkv_ring.step()

    out_ring = Ring(w_out)
    out_ring.step()
    blocks = qkv_ring.finish()
    mine, theirs, queries = pl.pallas_call(
        functools.partial(project_kernel, chips, groups),
        out_shape=[
            jax.ShapeDtypeStruct((tokens_here, 2 * HD), jnp.float32),
            jax.ShapeDtypeStruct((tokens_here, 2 * HD), jnp.float32),
            jax.ShapeDtypeStruct((2 * tokens_here, HEAD_COLS), jnp.float32),
        ],
        in_specs=vmem_specs(groups + len(blocks)),
        out_specs=vmem_specs(3),
        compiler_params=compute_params(),
        name="project",
    )(*ordered((*normed, *blocks)))
    theirs = lax.ppermute(theirs, "context", sibling)
    queries_theirs = lax.ppermute(queries, "context", sibling)
    mine, theirs = ordered((mine, theirs))
    out_ring.step()
    kv = pl.pallas_call(
        keys_kernel,
        out_shape=jax.ShapeDtypeStruct((tokens_here, 2 * HD), jnp.bfloat16),
        in_specs=vmem_specs(4),
        out_specs=vmem_specs(1)[0],
        compiler_params=compute_params(),
        name="keys",
    )(mine, theirs, cosine, sine)
    kv_ring = Ring(kv)
    kv_ring.step()
    kv_ring.step()
    out_ring.step()
    while not kv_ring.done():
        kv_ring.step()
    while not out_ring.done():
        out_ring.step()
    kv_blocks = ordered(kv_ring.finish())

    mixed = pl.pallas_call(
        attend_kernel,
        out_shape=jax.ShapeDtypeStruct((2 * tokens_here, HEAD_COLS + HD), jnp.float32),
        in_specs=vmem_specs(7 + len(kv_blocks)),
        out_specs=vmem_specs(1)[0],
        scratch_shapes=[pltpu.VMEM((chips * tokens_here, HD), jnp.bfloat16)] * 2,
        compiler_params=compute_params(),
        name="attend",
    )(
        queries,
        queries_theirs,
        cosine,
        sine,
        query_start,
        query_orig,
        key_orig,
        *kv_blocks,
    )
    mixed, *out_ring.middle = ordered((mixed, *out_ring.middle))
    mixed_theirs = lax.ppermute(mixed, "context", sibling)

    out_block = w_out.shape[1]

    blocks = out_ring.finish()
    parts = pl.pallas_call(
        functools.partial(output_kernel, chips, groups),
        out_shape=[jax.ShapeDtypeStruct((chips, rows_here, out_block), jnp.bfloat16)] * groups,
        in_specs=vmem_specs(2 + len(blocks)),
        out_specs=vmem_specs(groups),
        compiler_params=compute_params(),
        name="output",
    )(mixed, mixed_theirs, *blocks)
    arrived = []
    for e in range(2):
        for d in range(n_tensor):
            part = parts[e * n_tensor + d]
            if e or d:
                part = lax.ppermute(part, ("context", "tensor"), member(e, -d))
            arrived.append(part)
    return pl.pallas_call(
        functools.partial(sum_kernel, place, chips, groups),
        out_shape=jax.ShapeDtypeStruct((rows_here, n_context * out_block), jnp.bfloat16),
        in_specs=[pl.BlockSpec(memory_space=pl.ANY)] + vmem_specs(groups),
        out_specs=vmem_specs(1)[0],
        compiler_params=compute_params(),
        name="sum",
    )(token[0], *arrived)


def solution(mesh):
    placed = (
        P(("context", "tensor"), None),
        P(),
        P("context", "tensor"),
        P("tensor", "context"),
        P(),
        P(),
    )
    return jax.shard_map(
        functools.partial(per_device, mesh.shape["context"], mesh.shape["tensor"]),
        mesh=mesh,
        in_specs=placed,
        out_specs=P(("context", "tensor"), None),
        check_vma=False,
    )
```

```python
import functools

import jax
import jax.numpy as jnp
import numpy as np
from jax import lax
from jax.experimental import pallas as pl
from jax.experimental.pallas import tpu as pltpu
from jax.sharding import PartitionSpec as P

HD = 128
QH_DEV = 4
SPAN = 64
HEAD_COLS = QH_DEV * HD
VMEM_LIMIT = 24 * 1024 * 1024

rope_theta = 500000.0


def ring_of_chips(count):
    wide = 1
    while (wide * 2) * (wide * 2) <= count:
        wide *= 2
    tall = count // wide
    if wide < 2:
        return list(range(count))
    ring = [(z, 0) for z in range(tall)]
    for z in range(tall - 1, -1, -1):
        row = list(range(1, wide))
        ring += [(z, y) for y in (row if (tall - 1 - z) % 2 == 0 else row[::-1])]
    if (tall - 1) % 2 == 0 or wide == 2:
        return [z * wide + y for z, y in ring]
    return [z * wide + y for z, y in ring]


def vmem_specs(count):
    return [pl.BlockSpec(memory_space=pltpu.VMEM)] * count


def compute_params():
    return pltpu.CompilerParams(vmem_limit_bytes=VMEM_LIMIT)


def place_of(place):
    context = lax.axis_index("context")
    at = jnp.int32(0)
    for chip, spot in enumerate(place):
        at = jnp.where(context // 2 == chip, jnp.int32(spot), at)
    return at, context % 2


def where_kernel(
    ring,
    place,
    n_tensor,
    rows_here,
    spans_ref,
    lengths_ref,
    freq_ref,
    cos_ref,
    sin_ref,
    low_ref,
    high_ref,
    orig_ref,
):
    context, tensor = lax.axis_index("context"), lax.axis_index("tensor")
    rows = rows_here * n_tensor
    spans = rows // SPAN

    def shift(values, size):
        return lax.shift_right_logical(values, jnp.int32(size.bit_length() - 1))

    def inside_of(row):
        row = row & (rows - 1)
        turned = (tensor + shift(row, rows_here)) & (n_tensor - 1)
        return turned * rows_here + (row & (rows_here - 1))

    def initial(owner, inside):
        source = jnp.zeros_like(inside)
        for k in range(spans):
            source = jnp.where(shift(inside, SPAN) == k, spans_ref[owner * spans + k], source)
        return source * SPAN + (inside & (SPAN - 1))

    row = lax.broadcasted_iota(jnp.int32, cos_ref.shape, 0)
    inside = inside_of(row)
    orig = jnp.where(row < rows, initial(context, inside), initial(context ^ 1, inside))
    start, end = jnp.zeros_like(orig), jnp.int32(0)
    for i in range(lengths_ref.shape[0]):
        end = end + lengths_ref[i]
        start = jnp.where(orig >= end, end, start)
    low_ref[...] = start[:, :1]
    high_ref[...] = orig[:, :1]
    angle = (orig - start).astype(jnp.float32) * freq_ref[...]
    lane = lax.broadcasted_iota(jnp.int32, cos_ref.shape, 1)
    cos_ref[...] = jnp.cos(angle)
    sine = jnp.sin(angle)
    sin_ref[...] = jnp.where(lane < HD // 2, -sine, sine)
    inside = inside_of(lax.broadcasted_iota(jnp.int32, (1, rows), 1))
    at, core = place_of(place)
    for slot in range(len(ring)):
        spot = lax.rem(at + slot, len(ring))
        chip = jnp.int32(0)
        for i, at_spot in enumerate(ring):
            chip = jnp.where(spot == i, jnp.int32(at_spot), chip)
        owner = 2 * chip + core
        orig_ref[:, slot * rows : (slot + 1) * rows] = initial(owner, inside)


def norm_kernel(place, chips, hidden_ref, gain_ref, out_ref):
    at, core = place_of(place)
    wide = hidden_ref[...].astype(jnp.float32)
    meansq = jnp.mean(wide * wide, axis=-1, keepdims=True)
    scaled = wide * lax.rsqrt(meansq + 1e-05)
    lanes = gain_ref.shape[1]
    normed = jnp.concatenate(
        [
            (
                scaled[:, i * lanes : (i + 1) * lanes]
                * gain_ref[i : i + 1, :].astype(jnp.float32)
            ).astype(jnp.bfloat16)
            for i in range(gain_ref.shape[0])
        ],
        axis=1,
    )
    block = out_ref.shape[3]
    for even in range(2):

        @pl.when(core == even)
        def _():
            for chip in range(chips):
                slot = lax.rem(place[chip] + chips - at, chips)
                for side in range(2):
                    column = (2 * chip + side) * block
                    out_ref[side ^ even, slot] = normed[:, column : column + block]


def take_ring(refs, chips):
    refs = list(refs)
    if chips % 2:
        return [(ref,) for ref in refs]
    half = chips // 2
    return [(r,) for r in refs[:half]] + [tuple(refs[half : half + 2])] + [
        (r,) for r in refs[half + 2 :]
    ]


def project_kernel(chips, groups, *refs):
    rows_refs, refs = refs[:groups], refs[groups:]
    weight_refs, (mine_ref, theirs_ref, queries_ref) = refs[:-3], refs[-3:]
    half = groups // 2
    weights = take_ring(weight_refs, chips)
    total = None
    for slot in range(chips):
        rows = jnp.concatenate(
            [ref[group // half, slot] for group, ref in enumerate(rows_refs)], axis=0
        )
        start = 0
        for ref in weights[slot]:
            depth = ref.shape[0]
            part = jnp.dot(
                rows[:, start : start + depth], ref[...], preferred_element_type=jnp.float32
            )
            total = part if total is None else total + part
            start += depth
    count = mine_ref.shape[0]
    mine_ref[...] = total[:count, HEAD_COLS:]
    theirs_ref[...] = total[count:, HEAD_COLS:]
    queries_ref[...] = total[:, :HEAD_COLS]


def turn(values, cosine, sine):
    return values * cosine + pltpu.roll(values, HD // 2, 1) * sine


def keys_kernel(mine_ref, theirs_ref, cosine_ref, sine_ref, out_ref):
    rows = out_ref.shape[0]
    total = mine_ref[...] + theirs_ref[...]
    out_ref[:, :HD] = turn(total[:, :HD], cosine_ref[:rows, :], sine_ref[:rows, :]).astype(
        jnp.bfloat16
    )
    out_ref[:, HD:] = total[:, HD:].astype(jnp.bfloat16)


def attend_kernel(
    mine_ref,
    theirs_ref,
    cosine_ref,
    sine_ref,
    low_ref,
    high_ref,
    orig_ref,
    *refs,
):
    block_refs, (out_ref, keys_ref, values_ref) = refs[:-3], refs[-3:]
    start = 0
    for ref in block_refs:
        keys_ref[start : start + ref.shape[0], :] = ref[:, :HD]
        values_ref[start : start + ref.shape[0], :] = ref[:, HD:]
        start += ref.shape[0]
    keys = keys_ref[...]
    values = values_ref[...]
    orig = orig_ref[...]
    allowed = (orig >= low_ref[...]) & (orig <= high_ref[...])
    scale = 1.0 / HD**0.5
    rows = out_ref.shape[0]
    half = rows // 2
    lane = lax.broadcasted_iota(jnp.int32, (rows, HD), 1)
    stats = jnp.zeros((rows, HD), jnp.float32)
    for head in range(QH_DEV):
        columns = slice(head * HD, (head + 1) * HD)
        query = jnp.concatenate(
            [
                mine_ref[:half, columns] + theirs_ref[half:, columns],
                mine_ref[half:, columns] + theirs_ref[:half, columns],
            ],
            axis=0,
        )
        query = turn(query, cosine_ref[...], sine_ref[...]).astype(jnp.bfloat16)
        scores = lax.dot_general(
            query, keys, (((1,), (1,)), ((), ())), preferred_element_type=jnp.float32
        )
        scores = jnp.where(allowed, scores * scale, -1e30)
        top = jnp.max(scores, axis=-1, keepdims=True)
        expo = jnp.where(allowed, jnp.exp(scores - top), 0.0)
        total = jnp.sum(expo, axis=-1, keepdims=True)
        out_ref[:, columns] = jnp.dot(
            expo.astype(jnp.bfloat16), values, preferred_element_type=jnp.float32
        )
        stats = jnp.where(lane == 2 * head, total, stats)
        stats = jnp.where(lane == 2 * head + 1, top, stats)
    out_ref[:, HEAD_COLS:] = stats


def output_kernel(chips, groups, mine_ref, theirs_ref, *refs):
    weight_refs, out_refs = refs[:-groups], refs[-groups:]
    weights = take_ring(weight_refs, chips)
    chip_rows = mine_ref.shape[0]
    half = chip_rows // 2

    def swapped(columns):
        return jnp.concatenate([theirs_ref[half:, columns], theirs_ref[:half, columns]], axis=0)

    pieces = []
    for head in range(QH_DEV):
        columns = slice(head * HD, (head + 1) * HD)
        at = HEAD_COLS + 2 * head
        total, top = mine_ref[:, at : at + 1], mine_ref[:, at + 1 : at + 2]
        other_total, other_top = swapped(slice(at, at + 1)), swapped(slice(at + 1, at + 2))
        peak = jnp.maximum(top, other_top)
        factor, other_factor = jnp.exp(top - peak), jnp.exp(other_top - peak)
        product = mine_ref[:, columns] * factor + swapped(columns) * other_factor
        pieces.append(
            (product / (total * factor + other_total * other_factor)).astype(jnp.bfloat16)
        )
    mixed = jnp.concatenate(pieces, axis=1)
    rows = chip_rows // groups
    for slot in range(chips):
        start, total = 0, None
        for ref in weights[slot]:
            depth = ref.shape[0]
            part = jnp.dot(
                mixed[:, start : start + depth], ref[...], preferred_element_type=jnp.float32
            )
            total = part if total is None else total + part
            start += depth
        total = total.astype(jnp.bfloat16)
        for group in range(groups):
            out_refs[group][slot] = total[group * rows : (group + 1) * rows]


def sum_kernel(place, chips, groups, token_ref, *refs):
    part_refs, out_ref = refs[:groups], refs[groups]
    at, core = place_of(place)
    block = part_refs[0].shape[2]
    half = groups // 2

    def added(part, slot):
        total = part_refs[part * half][slot].astype(jnp.float32)
        for ref in part_refs[part * half + 1 : (part + 1) * half]:
            total += ref[slot].astype(jnp.float32)
        return total.astype(jnp.bfloat16)

    for even in range(2):

        @pl.when(core == even)
        def _():
            for chip in range(chips):
                slot = lax.rem(place[chip] + chips - at, chips)
                for side in range(2):
                    column = (2 * chip + side) * block
                    out_ref[:, column : column + block] = added(side ^ even, slot)


def per_device(n_context, n_tensor, hidden_rows, norm_gain, w_qkv, w_out, doc_lengths, span_order):
    chips = n_context // 2
    ring = ring_of_chips(chips)
    place = [ring.index(chip) for chip in range(chips)]
    groups = 2 * n_tensor
    rows_here, width = hidden_rows.shape
    tokens_here = rows_here * n_tensor
    block = width // n_context
    context = lax.axis_index("context")
    tensor = lax.axis_index("tensor")
    ahead = [
        (ring[i] * 2 + k, ring[(i + 1) % chips] * 2 + k) for i in range(chips) for k in range(2)
    ]
    back = [(b, a) for a, b in ahead]
    sibling = [(c, c ^ 1) for c in range(n_context)]

    token = [doc_lengths]

    def ordered(values):
        held = lax.optimization_barrier((*values, token[0]))
        token[0] = held[-1]
        return list(held[:-1])

    class Ring:
        def __init__(self, mine):
            self.up, self.down = [mine], [mine]
            self.middle = []

        def step(self, earlier=()):
            up, down, *earlier = ordered((self.up[-1], self.down[-1], *earlier))
            if len(self.up) <= (chips - 1) // 2:
                self.up.append(lax.ppermute(up, "context", ahead))
                self.down.append(lax.ppermute(down, "context", back))
            elif chips % 2 == 0 and not self.middle:
                half = up.shape[0] // 2
                self.middle = [
                    lax.ppermute(up[:half], "context", ahead),
                    lax.ppermute(down[half:], "context", back),
                ]
            return earlier

        def done(self):
            return len(self.up) > (chips - 1) // 2 and (chips % 2 == 1 or bool(self.middle))

        def finish(self):
            while not self.done():
                self.step()
            return self.down + self.middle + self.up[:0:-1]

    def member(e, d):
        return [
            (c * n_tensor + t, (c ^ e) * n_tensor + (t - d) % n_tensor)
            for c in range(n_context)
            for t in range(n_tensor)
        ]

    smem, vmem = pl.BlockSpec(memory_space=pltpu.SMEM), pl.BlockSpec(memory_space=pltpu.VMEM)
    freq = rope_theta ** (-(np.arange(HD // 2, dtype=np.float64) * 2.0 / HD))
    freq = np.concatenate([freq, freq]).astype(np.float32)[None, :]
    table = jax.ShapeDtypeStruct((2 * tokens_here, HD), jnp.float32)
    bound = jax.ShapeDtypeStruct((2 * tokens_here, 1), jnp.int32)
    cosine, sine, query_start, query_orig, key_orig = pl.pallas_call(
        functools.partial(where_kernel, ring, place, n_tensor, rows_here),
        out_shape=[
            table,
            table,
            bound,
            bound,
            jax.ShapeDtypeStruct((1, chips * tokens_here), jnp.int32),
        ],
        in_specs=[smem, smem, vmem],
        out_specs=vmem_specs(5),
        compiler_params=compute_params(),
        name="where",
    )(span_order, doc_lengths, jnp.asarray(freq))

    qkv_ring = Ring(w_qkv)
    qkv_ring.step()
    normed = pl.pallas_call(
        functools.partial(norm_kernel, place, chips),
        out_shape=jax.ShapeDtypeStruct((2, chips, rows_here, block), jnp.bfloat16),
        in_specs=vmem_specs(2),
        out_specs=vmem_specs(1)[0],
        compiler_params=compute_params(),
        name="norm",
    )(hidden_rows, norm_gain.reshape(-1, HD))
    normed = [normed] + [
        lax.ppermute(
            normed, "tensor", [(t, (t - d) % n_tensor) for t in range(n_tensor)]
        )
        for d in range(1, n_tensor)
    ]
    normed += [lax.ppermute(rows, "context", sibling) for rows in normed]

    qkv_ring.step()
    cosine, sine, query_start, query_orig, key_orig = ordered(
        (cosine, sine, query_start, query_orig, key_orig)
    )
    qkv_ring.step()
    normed = qkv_ring.step(normed)
    while not qkv_ring.done():
        qkv_ring.step()

    out_ring = Ring(w_out)
    out_ring.step()
    blocks = qkv_ring.finish()
    mine, theirs, queries = pl.pallas_call(
        functools.partial(project_kernel, chips, groups),
        out_shape=[
            jax.ShapeDtypeStruct((tokens_here, 2 * HD), jnp.float32),
            jax.ShapeDtypeStruct((tokens_here, 2 * HD), jnp.float32),
            jax.ShapeDtypeStruct((2 * tokens_here, HEAD_COLS), jnp.float32),
        ],
        in_specs=vmem_specs(groups + len(blocks)),
        out_specs=vmem_specs(3),
        compiler_params=compute_params(),
        name="project",
    )(*ordered((*normed, *blocks)))
    theirs = lax.ppermute(theirs, "context", sibling)
    queries_theirs = lax.ppermute(queries, "context", sibling)
    mine, theirs = ordered((mine, theirs))
    kv = pl.pallas_call(
        keys_kernel,
        out_shape=jax.ShapeDtypeStruct((tokens_here, 2 * HD), jnp.bfloat16),
        in_specs=vmem_specs(4),
        out_specs=vmem_specs(1)[0],
        compiler_params=compute_params(),
        name="keys",
    )(mine, theirs, cosine, sine)
    kv_ring = Ring(kv)
    kv_ring.step()
    kv_ring.step()
    out_ring.step()
    while not kv_ring.done():
        kv_ring.step()
    while len(out_ring.up) <= (chips - 1) // 2:
        out_ring.step()
    kv_blocks = ordered(kv_ring.finish())
    while not out_ring.done():
        out_ring.step()

    mixed = pl.pallas_call(
        attend_kernel,
        out_shape=jax.ShapeDtypeStruct((2 * tokens_here, HEAD_COLS + HD), jnp.float32),
        in_specs=vmem_specs(7 + len(kv_blocks)),
        out_specs=vmem_specs(1)[0],
        scratch_shapes=[pltpu.VMEM((chips * tokens_here, HD), jnp.bfloat16)] * 2,
        compiler_params=compute_params(),
        name="attend",
    )(
        queries,
        queries_theirs,
        cosine,
        sine,
        query_start,
        query_orig,
        key_orig,
        *kv_blocks,
    )
    mixed, *out_ring.middle = ordered((mixed, *out_ring.middle))
    mixed_theirs = lax.ppermute(mixed, "context", sibling)

    out_block = w_out.shape[1]

    blocks = out_ring.finish()
    parts = pl.pallas_call(
        functools.partial(output_kernel, chips, groups),
        out_shape=[jax.ShapeDtypeStruct((chips, rows_here, out_block), jnp.bfloat16)] * groups,
        in_specs=vmem_specs(2 + len(blocks)),
        out_specs=vmem_specs(groups),
        compiler_params=compute_params(),
        name="output",
    )(mixed, mixed_theirs, *blocks)
    arrived = []
    for e in range(2):
        for d in range(n_tensor):
            part = parts[e * n_tensor + d]
            if e or d:
                part = lax.ppermute(part, ("context", "tensor"), member(e, -d))
            arrived.append(part)
    return pl.pallas_call(
        functools.partial(sum_kernel, place, chips, groups),
        out_shape=jax.ShapeDtypeStruct((rows_here, n_context * out_block), jnp.bfloat16),
        in_specs=[pl.BlockSpec(memory_space=pl.ANY)] + vmem_specs(groups),
        out_specs=vmem_specs(1)[0],
        compiler_params=compute_params(),
        name="sum",
    )(token[0], *arrived)


def solution(mesh):
    placed = (
        P(("context", "tensor"), None),
        P(),
        P("context", "tensor"),
        P("tensor", "context"),
        P(),
        P(),
    )
    return jax.shard_map(
        functools.partial(per_device, mesh.shape["context"], mesh.shape["tensor"]),
        mesh=mesh,
        in_specs=placed,
        out_specs=P(("context", "tensor"), None),
        check_vma=False,
    )
```

```python
import functools

import jax
import jax.numpy as jnp
import numpy as np
from jax import lax
from jax.experimental import pallas as pl
from jax.experimental.pallas import tpu as pltpu
from jax.sharding import PartitionSpec as P

HD = 128
QH_DEV = 4
SPAN = 64
HEAD_COLS = QH_DEV * HD
VMEM_LIMIT = 24 * 1024 * 1024

rope_theta = 500000.0


def ring_of_chips(count):
    wide = 1
    while (wide * 2) * (wide * 2) <= count:
        wide *= 2
    tall = count // wide
    if wide < 2:
        return list(range(count))
    ring = [(z, 0) for z in range(tall)]
    for z in range(tall - 1, -1, -1):
        row = list(range(1, wide))
        ring += [(z, y) for y in (row if (tall - 1 - z) % 2 == 0 else row[::-1])]
    if (tall - 1) % 2 == 0 or wide == 2:
        return [z * wide + y for z, y in ring]
    return [z * wide + y for z, y in ring]


def vmem_specs(count):
    return [pl.BlockSpec(memory_space=pltpu.VMEM)] * count


def compute_params():
    return pltpu.CompilerParams(vmem_limit_bytes=VMEM_LIMIT)


def place_of(place):
    context = lax.axis_index("context")
    at = jnp.int32(0)
    for chip, spot in enumerate(place):
        at = jnp.where(context // 2 == chip, jnp.int32(spot), at)
    return at, context % 2


def where_kernel(
    n_tensor, rows_here, spans_ref, lengths_ref, freq_ref, cos_ref, sin_ref, low_ref, high_ref, orig_ref
):
    context, tensor = lax.axis_index("context"), lax.axis_index("tensor")
    rows = rows_here * n_tensor
    spans = rows // SPAN

    def shift(values, size):
        return lax.shift_right_logical(values, jnp.int32(size.bit_length() - 1))

    def inside_of(row):
        row = row & (rows - 1)
        turned = (tensor + shift(row, rows_here)) & (n_tensor - 1)
        return turned * rows_here + (row & (rows_here - 1))

    def initial(owner, inside):
        source = jnp.zeros_like(inside)
        for k in range(spans):
            source = jnp.where(shift(inside, SPAN) == k, spans_ref[owner * spans + k], source)
        return source * SPAN + (inside & (SPAN - 1))

    row = lax.broadcasted_iota(jnp.int32, cos_ref.shape, 0)
    inside = inside_of(row)
    orig = jnp.where(row < rows, initial(context, inside), initial(context ^ 1, inside))
    start, end = jnp.zeros_like(orig), jnp.int32(0)
    for i in range(lengths_ref.shape[0]):
        end = end + lengths_ref[i]
        start = jnp.where(orig >= end, end, start)
    low_ref[...] = start[:, :1]
    high_ref[...] = orig[:, :1]
    angle = (orig - start).astype(jnp.float32) * freq_ref[...]
    lane = lax.broadcasted_iota(jnp.int32, cos_ref.shape, 1)
    cos_ref[...] = jnp.cos(angle)
    sine = jnp.sin(angle)
    sin_ref[...] = jnp.where(lane < HD // 2, -sine, sine)
    inside = inside_of(lax.broadcasted_iota(jnp.int32, (1, rows), 1))
    for chip in range(orig_ref.shape[1] // rows):
        owner = 2 * chip + context % 2
        orig_ref[:, chip * rows : (chip + 1) * rows] = initial(owner, inside)


def norm_kernel(place, chips, hidden_ref, gain_ref, out_ref):
    at, core = place_of(place)
    wide = hidden_ref[...].astype(jnp.float32)
    meansq = jnp.mean(wide * wide, axis=-1, keepdims=True)
    scaled = wide * lax.rsqrt(meansq + 1e-05)
    lanes = gain_ref.shape[1]
    normed = jnp.concatenate(
        [
            (
                scaled[:, i * lanes : (i + 1) * lanes]
                * gain_ref[i : i + 1, :].astype(jnp.float32)
            ).astype(jnp.bfloat16)
            for i in range(gain_ref.shape[0])
        ],
        axis=1,
    )
    block = out_ref.shape[3]
    for even in range(2):

        @pl.when(core == even)
        def _():
            for chip in range(chips):
                slot = lax.rem(place[chip] + chips - at, chips)
                for side in range(2):
                    column = (2 * chip + side) * block
                    out_ref[side ^ even, slot] = normed[:, column : column + block]


def take_ring(refs, chips):
    refs = list(refs)
    if chips % 2:
        return [(ref,) for ref in refs]
    half = chips // 2
    return [(r,) for r in refs[:half]] + [tuple(refs[half : half + 2])] + [
        (r,) for r in refs[half + 2 :]
    ]


def project_kernel(chips, groups, *refs):
    rows_refs, refs = refs[:groups], refs[groups:]
    weight_refs, (mine_ref, theirs_ref, queries_ref) = refs[:-3], refs[-3:]
    half = groups // 2
    weights = take_ring(weight_refs, chips)
    total = None
    for slot in range(chips):
        rows = jnp.concatenate(
            [ref[group // half, slot] for group, ref in enumerate(rows_refs)], axis=0
        )
        start = 0
        for ref in weights[slot]:
            depth = ref.shape[0]
            part = jnp.dot(
                rows[:, start : start + depth], ref[...], preferred_element_type=jnp.float32
            )
            total = part if total is None else total + part
            start += depth
    count = mine_ref.shape[0]
    mine_ref[...] = total[:count, HEAD_COLS:]
    theirs_ref[...] = total[count:, HEAD_COLS:]
    queries_ref[...] = total[:, :HEAD_COLS]


def turn(values, cosine, sine):
    return values * cosine + pltpu.roll(values, HD // 2, 1) * sine


def keys_kernel(chips, mine_ref, theirs_ref, cosine_ref, sine_ref, out_ref):
    rows = out_ref.shape[0] // chips
    cosine, sine = cosine_ref[:rows, :], sine_ref[:rows, :]
    total = mine_ref[...] + theirs_ref[...]
    keys = turn(total[:, :HD], cosine, sine).astype(jnp.bfloat16)
    values = total[:, HD:].astype(jnp.bfloat16)
    for chip in range(chips):
        out_ref[chip * rows : (chip + 1) * rows, :HD] = keys
        out_ref[chip * rows : (chip + 1) * rows, HD:] = values


def attend_kernel(
    mine_ref,
    theirs_ref,
    cosine_ref,
    sine_ref,
    low_ref,
    high_ref,
    orig_ref,
    kv_ref,
    out_ref,
):
    keys = kv_ref[:, :HD]
    values = kv_ref[:, HD:]
    orig = orig_ref[...]
    allowed = (orig >= low_ref[...]) & (orig <= high_ref[...])
    scale = 1.0 / HD**0.5
    rows = out_ref.shape[0]
    half = rows // 2
    lane = lax.broadcasted_iota(jnp.int32, (rows, HD), 1)
    stats = jnp.zeros((rows, HD), jnp.float32)
    for head in range(QH_DEV):
        columns = slice(head * HD, (head + 1) * HD)
        query = jnp.concatenate(
            [
                mine_ref[:half, columns] + theirs_ref[half:, columns],
                mine_ref[half:, columns] + theirs_ref[:half, columns],
            ],
            axis=0,
        )
        query = turn(query, cosine_ref[...], sine_ref[...]).astype(jnp.bfloat16)
        scores = lax.dot_general(
            query, keys, (((1,), (1,)), ((), ())), preferred_element_type=jnp.float32
        )
        scores = jnp.where(allowed, scores * scale, -1e30)
        top = jnp.max(scores, axis=-1, keepdims=True)
        expo = jnp.where(allowed, jnp.exp(scores - top), 0.0)
        total = jnp.sum(expo, axis=-1, keepdims=True)
        out_ref[:, columns] = jnp.dot(
            expo.astype(jnp.bfloat16), values, preferred_element_type=jnp.float32
        )
        stats = jnp.where(lane == 2 * head, total, stats)
        stats = jnp.where(lane == 2 * head + 1, top, stats)
    out_ref[:, HEAD_COLS:] = stats


def output_kernel(groups, pieces_of, mine_ref, theirs_ref, *refs):
    weight_refs, out_refs = refs[:-groups], refs[-groups:]
    chip_rows = mine_ref.shape[0]
    half = chip_rows // 2

    def swapped(columns):
        return jnp.concatenate([theirs_ref[half:, columns], theirs_ref[:half, columns]], axis=0)

    pieces = []
    for head in range(QH_DEV):
        columns = slice(head * HD, (head + 1) * HD)
        at = HEAD_COLS + 2 * head
        total, top = mine_ref[:, at : at + 1], mine_ref[:, at + 1 : at + 2]
        other_total, other_top = swapped(slice(at, at + 1)), swapped(slice(at + 1, at + 2))
        peak = jnp.maximum(top, other_top)
        factor, other_factor = jnp.exp(top - peak), jnp.exp(other_top - peak)
        product = mine_ref[:, columns] * factor + swapped(columns) * other_factor
        pieces.append(
            (product / (total * factor + other_total * other_factor)).astype(jnp.bfloat16)
        )
    mixed = jnp.concatenate(pieces, axis=1)
    rows = chip_rows // groups
    weight_refs = iter(weight_refs)
    for slot, pieces in enumerate(pieces_of):
        start, total = 0, None
        for _ in range(pieces):
            ref = next(weight_refs)
            depth = ref.shape[0]
            part = jnp.dot(
                mixed[:, start : start + depth], ref[...], preferred_element_type=jnp.float32
            )
            total = part if total is None else total + part
            start += depth
        total = total.astype(jnp.bfloat16)
        for group in range(groups):
            out_refs[group][slot] = total[group * rows : (group + 1) * rows]


def sum_kernel(place, chips, groups, near, token_ref, *refs):
    near_refs, far_refs, out_ref = refs[:groups], refs[groups : 2 * groups], refs[2 * groups]
    at, core = place_of(place)
    block = near_refs[0].shape[2]
    half = groups // 2

    def added(part, slot):
        turn_at = lax.rem(slot + near // 2, chips)
        total = None
        for group in range(part * half, (part + 1) * half):
            rows = jnp.where(
                turn_at < near,
                near_refs[group][jnp.minimum(turn_at, near - 1)].astype(jnp.float32),
                far_refs[group][jnp.maximum(turn_at - near, 0)].astype(jnp.float32),
            )
            total = rows if total is None else total + rows
        return total.astype(jnp.bfloat16)

    for even in range(2):

        @pl.when(core == even)
        def _():
            for chip in range(chips):
                slot = lax.rem(place[chip] + chips - at, chips)
                for side in range(2):
                    column = (2 * chip + side) * block
                    out_ref[:, column : column + block] = added(side ^ even, slot)


def per_device(n_context, n_tensor, hidden_rows, norm_gain, w_qkv, w_out, doc_lengths, span_order):
    chips = n_context // 2
    ring = ring_of_chips(chips)
    place = [ring.index(chip) for chip in range(chips)]
    groups = 2 * n_tensor
    rows_here, width = hidden_rows.shape
    tokens_here = rows_here * n_tensor
    block = width // n_context
    context = lax.axis_index("context")
    tensor = lax.axis_index("tensor")
    ahead = [
        (ring[i] * 2 + k, ring[(i + 1) % chips] * 2 + k) for i in range(chips) for k in range(2)
    ]
    back = [(b, a) for a, b in ahead]
    sibling = [(c, c ^ 1) for c in range(n_context)]

    same_core = [[2 * chip + k for chip in range(chips)] for k in range(2)]
    token = [doc_lengths]

    def ordered(values):
        held = lax.optimization_barrier((*values, token[0]))
        token[0] = held[-1]
        return list(held[:-1])

    class Ring:
        def __init__(self, mine):
            self.up, self.down = [mine], [mine]
            self.middle = []

        def step(self, earlier=()):
            up, down, *earlier = ordered((self.up[-1], self.down[-1], *earlier))
            if len(self.up) <= (chips - 1) // 2:
                self.up.append(lax.ppermute(up, "context", ahead))
                self.down.append(lax.ppermute(down, "context", back))
            elif chips % 2 == 0 and not self.middle:
                half = up.shape[0] // 2
                self.middle = [
                    lax.ppermute(up[:half], "context", ahead),
                    lax.ppermute(down[half:], "context", back),
                ]
            return earlier

        def done(self):
            return len(self.up) > (chips - 1) // 2 and (chips % 2 == 1 or bool(self.middle))

        def finish(self):
            while not self.done():
                self.step()
            return self.down + self.middle + self.up[:0:-1]

        def block(self, slot):
            slot %= chips
            if chips % 2 == 0 and slot == chips // 2:
                return tuple(self.middle)
            return (self.down[slot] if slot <= chips // 2 else self.up[chips - slot],)

    def member(e, d):
        return [
            (c * n_tensor + t, (c ^ e) * n_tensor + (t - d) % n_tensor)
            for c in range(n_context)
            for t in range(n_tensor)
        ]

    smem, vmem = pl.BlockSpec(memory_space=pltpu.SMEM), pl.BlockSpec(memory_space=pltpu.VMEM)
    freq = rope_theta ** (-(np.arange(HD // 2, dtype=np.float64) * 2.0 / HD))
    freq = np.concatenate([freq, freq]).astype(np.float32)[None, :]
    table = jax.ShapeDtypeStruct((2 * tokens_here, HD), jnp.float32)
    bound = jax.ShapeDtypeStruct((2 * tokens_here, 1), jnp.int32)
    cosine, sine, query_start, query_orig, key_orig = pl.pallas_call(
        functools.partial(where_kernel, n_tensor, rows_here),
        out_shape=[
            table,
            table,
            bound,
            bound,
            jax.ShapeDtypeStruct((1, chips * tokens_here), jnp.int32),
        ],
        in_specs=[smem, smem, vmem],
        out_specs=vmem_specs(5),
        compiler_params=compute_params(),
        name="where",
    )(span_order, doc_lengths, jnp.asarray(freq))

    qkv_ring = Ring(w_qkv)
    qkv_ring.step()
    normed = pl.pallas_call(
        functools.partial(norm_kernel, place, chips),
        out_shape=jax.ShapeDtypeStruct((2, chips, rows_here, block), jnp.bfloat16),
        in_specs=vmem_specs(2),
        out_specs=vmem_specs(1)[0],
        compiler_params=compute_params(),
        name="norm",
    )(hidden_rows, norm_gain.reshape(-1, HD))
    normed = [normed] + [
        lax.ppermute(
            normed, "tensor", [(t, (t - d) % n_tensor) for t in range(n_tensor)]
        )
        for d in range(1, n_tensor)
    ]
    normed += [lax.ppermute(rows, "context", sibling) for rows in normed]

    qkv_ring.step()
    cosine, sine, query_start, query_orig, key_orig = ordered(
        (cosine, sine, query_start, query_orig, key_orig)
    )
    qkv_ring.step()
    normed = qkv_ring.step(normed)
    while not qkv_ring.done():
        qkv_ring.step()

    out_ring = Ring(w_out)
    out_ring.step()
    blocks = qkv_ring.finish()
    mine, theirs, queries = pl.pallas_call(
        functools.partial(project_kernel, chips, groups),
        out_shape=[
            jax.ShapeDtypeStruct((tokens_here, 2 * HD), jnp.float32),
            jax.ShapeDtypeStruct((tokens_here, 2 * HD), jnp.float32),
            jax.ShapeDtypeStruct((2 * tokens_here, HEAD_COLS), jnp.float32),
        ],
        in_specs=vmem_specs(groups + len(blocks)),
        out_specs=vmem_specs(3),
        compiler_params=compute_params(),
        name="project",
    )(*ordered((*normed, *blocks)))
    theirs = lax.ppermute(theirs, "context", sibling)
    queries_theirs = lax.ppermute(queries, "context", sibling)
    mine, theirs = ordered((mine, theirs))
    kv = pl.pallas_call(
        functools.partial(keys_kernel, chips),
        out_shape=jax.ShapeDtypeStruct((chips * tokens_here, 2 * HD), jnp.bfloat16),
        in_specs=vmem_specs(4),
        out_specs=vmem_specs(1)[0],
        compiler_params=compute_params(),
        name="keys",
    )(mine, theirs, cosine, sine)
    (kv,) = ordered((kv,))
    kv = lax.all_to_all(
        kv, "context", split_axis=0, concat_axis=0, axis_index_groups=same_core, tiled=True
    )
    out_ring.step()
    out_ring.step()
    (kv,) = ordered((kv,))

    mixed = pl.pallas_call(
        attend_kernel,
        out_shape=jax.ShapeDtypeStruct((2 * tokens_here, HEAD_COLS + HD), jnp.float32),
        in_specs=vmem_specs(8),
        out_specs=vmem_specs(1)[0],
        compiler_params=compute_params(),
        name="attend",
    )(
        queries,
        queries_theirs,
        cosine,
        sine,
        query_start,
        query_orig,
        key_orig,
        kv,
    )
    (mixed,) = ordered((mixed,))
    mixed_theirs = lax.ppermute(mixed, "context", sibling)

    out_block = w_out.shape[1]

    def output(slots, name):
        blocks = [out_ring.block(slot) for slot in slots]
        flat = [piece for pieces in blocks for piece in pieces]
        parts = pl.pallas_call(
            functools.partial(output_kernel, groups, [len(pieces) for pieces in blocks]),
            out_shape=[jax.ShapeDtypeStruct((len(slots), rows_here, out_block), jnp.bfloat16)]
            * groups,
            in_specs=vmem_specs(2 + len(flat)),
            out_specs=vmem_specs(groups),
            compiler_params=compute_params(),
            name=name,
        )(mixed, mixed_theirs, *flat)
        parts = ordered(parts)
        arrived = []
        for e in range(2):
            for d in range(n_tensor):
                part = parts[e * n_tensor + d]
                if e or d:
                    part = lax.ppermute(part, ("context", "tensor"), member(e, -d))
                arrived.append(part)
        return arrived

    reach = max(chips // 2 - 2, 0)
    while len(out_ring.up) <= reach:
        out_ring.step()
    near = 2 * reach + 1
    arrived = output(list(range(-reach, reach + 1)), "output_near")
    while not out_ring.done():
        out_ring.step()
    arrived += output(list(range(reach + 1, chips - reach)), "output_far")
    return pl.pallas_call(
        functools.partial(sum_kernel, place, chips, groups, near),
        out_shape=jax.ShapeDtypeStruct((rows_here, n_context * out_block), jnp.bfloat16),
        in_specs=[pl.BlockSpec(memory_space=pl.ANY)] + vmem_specs(2 * groups),
        out_specs=vmem_specs(1)[0],
        compiler_params=compute_params(),
        name="sum",
    )(token[0], *arrived)


def solution(mesh):
    placed = (
        P(("context", "tensor"), None),
        P(),
        P("context", "tensor"),
        P("tensor", "context"),
        P(),
        P(),
    )
    return jax.shard_map(
        functools.partial(per_device, mesh.shape["context"], mesh.shape["tensor"]),
        mesh=mesh,
        in_specs=placed,
        out_specs=P(("context", "tensor"), None),
        check_vma=False,
    )
```

```python
import functools

import jax
import jax.numpy as jnp
import numpy as np
from jax import lax
from jax.experimental import pallas as pl
from jax.experimental.pallas import tpu as pltpu
from jax.sharding import PartitionSpec as P

HD = 128
QH_DEV = 4
SPAN = 64
HEAD_COLS = QH_DEV * HD
VMEM_LIMIT = 24 * 1024 * 1024

rope_theta = 500000.0


def ring_of_chips(count):
    wide = 1
    while (wide * 2) * (wide * 2) <= count:
        wide *= 2
    tall = count // wide
    if wide < 2:
        return list(range(count))
    ring = [(z, 0) for z in range(tall)]
    for z in range(tall - 1, -1, -1):
        row = list(range(1, wide))
        ring += [(z, y) for y in (row if (tall - 1 - z) % 2 == 0 else row[::-1])]
    if (tall - 1) % 2 == 0 or wide == 2:
        return [z * wide + y for z, y in ring]
    return [z * wide + y for z, y in ring]


def vmem_specs(count):
    return [pl.BlockSpec(memory_space=pltpu.VMEM)] * count


def compute_params():
    return pltpu.CompilerParams(vmem_limit_bytes=VMEM_LIMIT)


def place_of(place):
    context = lax.axis_index("context")
    at = jnp.int32(0)
    for chip, spot in enumerate(place):
        at = jnp.where(context // 2 == chip, jnp.int32(spot), at)
    return at, context % 2


def where_kernel(
    n_tensor, rows_here, spans_ref, lengths_ref, freq_ref, cos_ref, sin_ref, low_ref, high_ref, orig_ref
):
    context, tensor = lax.axis_index("context"), lax.axis_index("tensor")
    rows = rows_here * n_tensor
    spans = rows // SPAN

    def shift(values, size):
        return lax.shift_right_logical(values, jnp.int32(size.bit_length() - 1))

    def inside_of(row):
        row = row & (rows - 1)
        turned = (tensor + shift(row, rows_here)) & (n_tensor - 1)
        return turned * rows_here + (row & (rows_here - 1))

    def initial(owner, inside):
        source = jnp.zeros_like(inside)
        for k in range(spans):
            source = jnp.where(shift(inside, SPAN) == k, spans_ref[owner * spans + k], source)
        return source * SPAN + (inside & (SPAN - 1))

    row = lax.broadcasted_iota(jnp.int32, cos_ref.shape, 0)
    inside = inside_of(row)
    orig = jnp.where(row < rows, initial(context, inside), initial(context ^ 1, inside))
    start, end = jnp.zeros_like(orig), jnp.int32(0)
    for i in range(lengths_ref.shape[0]):
        end = end + lengths_ref[i]
        start = jnp.where(orig >= end, end, start)
    low_ref[...] = start[:, :1]
    high_ref[...] = orig[:, :1]
    angle = (orig - start).astype(jnp.float32) * freq_ref[...]
    lane = lax.broadcasted_iota(jnp.int32, cos_ref.shape, 1)
    cos_ref[...] = jnp.cos(angle)
    sine = jnp.sin(angle)
    sin_ref[...] = jnp.where(lane < HD // 2, -sine, sine)
    inside = inside_of(lax.broadcasted_iota(jnp.int32, (1, rows), 1))
    for chip in range(orig_ref.shape[1] // rows):
        owner = 2 * chip + context % 2
        orig_ref[:, chip * rows : (chip + 1) * rows] = initial(owner, inside)


def norm_kernel(place, chips, hidden_ref, gain_ref, out_ref):
    at, core = place_of(place)
    wide = hidden_ref[...].astype(jnp.float32)
    meansq = jnp.mean(wide * wide, axis=-1, keepdims=True)
    scaled = wide * lax.rsqrt(meansq + 1e-05)
    lanes = gain_ref.shape[1]
    normed = jnp.concatenate(
        [
            (
                scaled[:, i * lanes : (i + 1) * lanes]
                * gain_ref[i : i + 1, :].astype(jnp.float32)
            ).astype(jnp.bfloat16)
            for i in range(gain_ref.shape[0])
        ],
        axis=1,
    )
    block = out_ref.shape[3]
    for even in range(2):

        @pl.when(core == even)
        def _():
            for chip in range(chips):
                slot = lax.rem(place[chip] + chips - at, chips)
                for side in range(2):
                    column = (2 * chip + side) * block
                    out_ref[side ^ even, slot] = normed[:, column : column + block]


def take_ring(refs, chips):
    refs = list(refs)
    if chips % 2:
        return [(ref,) for ref in refs]
    half = chips // 2
    return [(r,) for r in refs[:half]] + [tuple(refs[half : half + 2])] + [
        (r,) for r in refs[half + 2 :]
    ]


def project_kernel(chips, groups, *refs):
    rows_refs, refs = refs[:groups], refs[groups:]
    weight_refs, (mine_ref, theirs_ref, queries_ref) = refs[:-3], refs[-3:]
    half = groups // 2
    weights = take_ring(weight_refs, chips)
    total = None
    for slot in range(chips):
        rows = jnp.concatenate(
            [ref[group // half, slot] for group, ref in enumerate(rows_refs)], axis=0
        )
        start = 0
        for ref in weights[slot]:
            depth = ref.shape[0]
            part = jnp.dot(
                rows[:, start : start + depth], ref[...], preferred_element_type=jnp.float32
            )
            total = part if total is None else total + part
            start += depth
    count = mine_ref.shape[0]
    mine_ref[...] = total[:count, HEAD_COLS:]
    theirs_ref[...] = total[count:, HEAD_COLS:]
    queries_ref[...] = total[:, :HEAD_COLS]


def turn(values, cosine, sine):
    return values * cosine + pltpu.roll(values, HD // 2, 1) * sine


def keys_kernel(chips, mine_ref, theirs_ref, cosine_ref, sine_ref, out_ref):
    rows = out_ref.shape[0] // chips
    cosine, sine = cosine_ref[:rows, :], sine_ref[:rows, :]
    total = mine_ref[...] + theirs_ref[...]
    keys = turn(total[:, :HD], cosine, sine).astype(jnp.bfloat16)
    values = total[:, HD:].astype(jnp.bfloat16)
    for chip in range(chips):
        out_ref[chip * rows : (chip + 1) * rows, :HD] = keys
        out_ref[chip * rows : (chip + 1) * rows, HD:] = values


def attend_kernel(
    mine_ref,
    theirs_ref,
    cosine_ref,
    sine_ref,
    low_ref,
    high_ref,
    orig_ref,
    kv_ref,
    out_ref,
    sent_ref,
    stats_ref,
):
    keys = kv_ref[:, :HD]
    values = kv_ref[:, HD:]
    orig = orig_ref[...]
    allowed = (orig >= low_ref[...]) & (orig <= high_ref[...])
    scale = 1.0 / HD**0.5
    rows = out_ref.shape[0]
    half = rows // 2
    lane = lax.broadcasted_iota(jnp.int32, (rows, HD), 1)
    stats = jnp.zeros((rows, HD), jnp.float32)
    for head in range(QH_DEV):
        columns = slice(head * HD, (head + 1) * HD)
        query = jnp.concatenate(
            [
                mine_ref[:half, columns] + theirs_ref[half:, columns],
                mine_ref[half:, columns] + theirs_ref[:half, columns],
            ],
            axis=0,
        )
        query = turn(query, cosine_ref[...], sine_ref[...]).astype(jnp.bfloat16)
        scores = lax.dot_general(
            query, keys, (((1,), (1,)), ((), ())), preferred_element_type=jnp.float32
        )
        scores = jnp.where(allowed, scores * scale, -1e30)
        top = jnp.max(scores, axis=-1, keepdims=True)
        expo = jnp.where(allowed, jnp.exp(scores - top), 0.0)
        total = jnp.sum(expo, axis=-1, keepdims=True)
        product = jnp.dot(expo.astype(jnp.bfloat16), values, preferred_element_type=jnp.float32)
        out_ref[:, columns] = product
        sent_ref[:, columns] = product.astype(jnp.bfloat16)
        stats = jnp.where(lane == 2 * head, total, stats)
        stats = jnp.where(lane == 2 * head + 1, top, stats)
    stats_ref[...] = stats


def output_kernel(
    groups, pieces_of, mine_ref, stats_ref, theirs_ref, their_stats_ref, *refs
):
    weight_refs, out_refs = refs[:-groups], refs[-groups:]
    chip_rows = mine_ref.shape[0]
    half = chip_rows // 2

    def swapped(ref, columns):
        return jnp.concatenate([ref[half:, columns], ref[:half, columns]], axis=0)

    pieces = []
    for head in range(QH_DEV):
        columns = slice(head * HD, (head + 1) * HD)
        sums, tops = slice(2 * head, 2 * head + 1), slice(2 * head + 1, 2 * head + 2)
        total, top = stats_ref[:, sums], stats_ref[:, tops]
        other_total, other_top = swapped(their_stats_ref, sums), swapped(their_stats_ref, tops)
        peak = jnp.maximum(top, other_top)
        factor, other_factor = jnp.exp(top - peak), jnp.exp(other_top - peak)
        other = swapped(theirs_ref, columns).astype(jnp.float32)
        product = mine_ref[:, columns] * factor + other * other_factor
        pieces.append(
            (product / (total * factor + other_total * other_factor)).astype(jnp.bfloat16)
        )
    mixed = jnp.concatenate(pieces, axis=1)
    rows = chip_rows // groups
    weight_refs = iter(weight_refs)
    for slot, pieces in enumerate(pieces_of):
        start, total = 0, None
        for _ in range(pieces):
            ref = next(weight_refs)
            depth = ref.shape[0]
            part = jnp.dot(
                mixed[:, start : start + depth], ref[...], preferred_element_type=jnp.float32
            )
            total = part if total is None else total + part
            start += depth
        total = total.astype(jnp.bfloat16)
        for group in range(groups):
            out_refs[group][slot] = total[group * rows : (group + 1) * rows]


def sum_kernel(place, chips, groups, near, token_ref, *refs):
    near_refs, far_refs, out_ref = refs[:groups], refs[groups : 2 * groups], refs[2 * groups]
    at, core = place_of(place)
    block = near_refs[0].shape[2]
    half = groups // 2

    def added(part, slot):
        turn_at = lax.rem(slot + near // 2, chips)
        total = None
        for group in range(part * half, (part + 1) * half):
            rows = jnp.where(
                turn_at < near,
                near_refs[group][jnp.minimum(turn_at, near - 1)].astype(jnp.float32),
                far_refs[group][jnp.maximum(turn_at - near, 0)].astype(jnp.float32),
            )
            total = rows if total is None else total + rows
        return total.astype(jnp.bfloat16)

    for even in range(2):

        @pl.when(core == even)
        def _():
            for chip in range(chips):
                slot = lax.rem(place[chip] + chips - at, chips)
                for side in range(2):
                    column = (2 * chip + side) * block
                    out_ref[:, column : column + block] = added(side ^ even, slot)


def per_device(n_context, n_tensor, hidden_rows, norm_gain, w_qkv, w_out, doc_lengths, span_order):
    chips = n_context // 2
    ring = ring_of_chips(chips)
    place = [ring.index(chip) for chip in range(chips)]
    groups = 2 * n_tensor
    rows_here, width = hidden_rows.shape
    tokens_here = rows_here * n_tensor
    block = width // n_context
    context = lax.axis_index("context")
    tensor = lax.axis_index("tensor")
    ahead = [
        (ring[i] * 2 + k, ring[(i + 1) % chips] * 2 + k) for i in range(chips) for k in range(2)
    ]
    back = [(b, a) for a, b in ahead]
    sibling = [(c, c ^ 1) for c in range(n_context)]

    same_core = [[2 * chip + k for chip in range(chips)] for k in range(2)]
    token = [doc_lengths]

    def ordered(values):
        held = lax.optimization_barrier((*values, token[0]))
        token[0] = held[-1]
        return list(held[:-1])

    class Ring:
        def __init__(self, mine):
            self.up, self.down = [mine], [mine]
            self.middle = []

        def step(self, earlier=()):
            up, down, *earlier = ordered((self.up[-1], self.down[-1], *earlier))
            if len(self.up) <= (chips - 1) // 2:
                self.up.append(lax.ppermute(up, "context", ahead))
                self.down.append(lax.ppermute(down, "context", back))
            elif chips % 2 == 0 and not self.middle:
                half = up.shape[0] // 2
                self.middle = [
                    lax.ppermute(up[:half], "context", ahead),
                    lax.ppermute(down[half:], "context", back),
                ]
            return earlier

        def done(self):
            return len(self.up) > (chips - 1) // 2 and (chips % 2 == 1 or bool(self.middle))

        def finish(self):
            while not self.done():
                self.step()
            return self.down + self.middle + self.up[:0:-1]

        def block(self, slot):
            slot %= chips
            if chips % 2 == 0 and slot == chips // 2:
                return tuple(self.middle)
            return (self.down[slot] if slot <= chips // 2 else self.up[chips - slot],)

    def member(e, d):
        return [
            (c * n_tensor + t, (c ^ e) * n_tensor + (t - d) % n_tensor)
            for c in range(n_context)
            for t in range(n_tensor)
        ]

    smem, vmem = pl.BlockSpec(memory_space=pltpu.SMEM), pl.BlockSpec(memory_space=pltpu.VMEM)
    freq = rope_theta ** (-(np.arange(HD // 2, dtype=np.float64) * 2.0 / HD))
    freq = np.concatenate([freq, freq]).astype(np.float32)[None, :]
    table = jax.ShapeDtypeStruct((2 * tokens_here, HD), jnp.float32)
    bound = jax.ShapeDtypeStruct((2 * tokens_here, 1), jnp.int32)
    cosine, sine, query_start, query_orig, key_orig = pl.pallas_call(
        functools.partial(where_kernel, n_tensor, rows_here),
        out_shape=[
            table,
            table,
            bound,
            bound,
            jax.ShapeDtypeStruct((1, chips * tokens_here), jnp.int32),
        ],
        in_specs=[smem, smem, vmem],
        out_specs=vmem_specs(5),
        compiler_params=compute_params(),
        name="where",
    )(span_order, doc_lengths, jnp.asarray(freq))

    qkv_ring = Ring(w_qkv)
    qkv_ring.step()
    normed = pl.pallas_call(
        functools.partial(norm_kernel, place, chips),
        out_shape=jax.ShapeDtypeStruct((2, chips, rows_here, block), jnp.bfloat16),
        in_specs=vmem_specs(2),
        out_specs=vmem_specs(1)[0],
        compiler_params=compute_params(),
        name="norm",
    )(hidden_rows, norm_gain.reshape(-1, HD))
    normed = [normed] + [
        lax.ppermute(
            normed, "tensor", [(t, (t - d) % n_tensor) for t in range(n_tensor)]
        )
        for d in range(1, n_tensor)
    ]
    normed += [lax.ppermute(rows, "context", sibling) for rows in normed]

    qkv_ring.step()
    cosine, sine, query_start, query_orig, key_orig = ordered(
        (cosine, sine, query_start, query_orig, key_orig)
    )
    qkv_ring.step()
    normed = qkv_ring.step(normed)
    while not qkv_ring.done():
        qkv_ring.step()

    out_ring = Ring(w_out)
    out_ring.step()
    blocks = qkv_ring.finish()
    mine, theirs, queries = pl.pallas_call(
        functools.partial(project_kernel, chips, groups),
        out_shape=[
            jax.ShapeDtypeStruct((tokens_here, 2 * HD), jnp.float32),
            jax.ShapeDtypeStruct((tokens_here, 2 * HD), jnp.float32),
            jax.ShapeDtypeStruct((2 * tokens_here, HEAD_COLS), jnp.float32),
        ],
        in_specs=vmem_specs(groups + len(blocks)),
        out_specs=vmem_specs(3),
        compiler_params=compute_params(),
        name="project",
    )(*ordered((*normed, *blocks)))
    theirs = lax.ppermute(theirs, "context", sibling)
    queries_theirs = lax.ppermute(queries, "context", sibling)
    out_ring.step()
    mine, theirs = ordered((mine, theirs))
    kv = pl.pallas_call(
        functools.partial(keys_kernel, chips),
        out_shape=jax.ShapeDtypeStruct((chips * tokens_here, 2 * HD), jnp.bfloat16),
        in_specs=vmem_specs(4),
        out_specs=vmem_specs(1)[0],
        compiler_params=compute_params(),
        name="keys",
    )(mine, theirs, cosine, sine)
    (kv,) = ordered((kv,))
    kv = lax.all_to_all(
        kv, "context", split_axis=0, concat_axis=0, axis_index_groups=same_core, tiled=True
    )
    out_ring.step()
    (kv,) = ordered((kv,))

    mixed, sent, stats = pl.pallas_call(
        attend_kernel,
        out_shape=[
            jax.ShapeDtypeStruct((2 * tokens_here, HEAD_COLS), jnp.float32),
            jax.ShapeDtypeStruct((2 * tokens_here, HEAD_COLS), jnp.bfloat16),
            jax.ShapeDtypeStruct((2 * tokens_here, HD), jnp.float32),
        ],
        in_specs=vmem_specs(8),
        out_specs=vmem_specs(3),
        compiler_params=compute_params(),
        name="attend",
    )(
        queries,
        queries_theirs,
        cosine,
        sine,
        query_start,
        query_orig,
        key_orig,
        kv,
    )
    sent, stats = ordered((sent, stats))
    sent = lax.ppermute(sent, "context", sibling)
    their_stats = lax.ppermute(stats, "context", sibling)
    while not out_ring.done():
        out_ring.step()

    out_block = w_out.shape[1]

    def output(slots, name):
        blocks = [out_ring.block(slot) for slot in slots]
        flat = [piece for pieces in blocks for piece in pieces]
        parts = pl.pallas_call(
            functools.partial(output_kernel, groups, [len(pieces) for pieces in blocks]),
            out_shape=[jax.ShapeDtypeStruct((len(slots), rows_here, out_block), jnp.bfloat16)]
            * groups,
            in_specs=vmem_specs(4 + len(flat)),
            out_specs=vmem_specs(groups),
            compiler_params=compute_params(),
            name=name,
        )(mixed, stats, sent, their_stats, *flat)
        held = ordered((*parts, *out_ring.middle))
        parts, out_ring.middle = held[: len(parts)], held[len(parts) :]
        arrived = []
        for e in range(2):
            for d in range(n_tensor):
                part = parts[e * n_tensor + d]
                if e or d:
                    part = lax.ppermute(part, ("context", "tensor"), member(e, -d))
                arrived.append(part)
        return arrived

    reach = (chips - 1) // 2
    near = 2 * reach + 1
    arrived = output(list(range(-reach, reach + 1)), "output_near")
    arrived += output(list(range(reach + 1, chips - reach)), "output_far")
    return pl.pallas_call(
        functools.partial(sum_kernel, place, chips, groups, near),
        out_shape=jax.ShapeDtypeStruct((rows_here, n_context * out_block), jnp.bfloat16),
        in_specs=[pl.BlockSpec(memory_space=pl.ANY)] + vmem_specs(2 * groups),
        out_specs=vmem_specs(1)[0],
        compiler_params=compute_params(),
        name="sum",
    )(token[0], *arrived)


def solution(mesh):
    placed = (
        P(("context", "tensor"), None),
        P(),
        P("context", "tensor"),
        P("tensor", "context"),
        P(),
        P(),
    )
    return jax.shard_map(
        functools.partial(per_device, mesh.shape["context"], mesh.shape["tensor"]),
        mesh=mesh,
        in_specs=placed,
        out_specs=P(("context", "tensor"), None),
        check_vma=False,
    )
```

```python
import functools

import jax
import jax.numpy as jnp
import numpy as np
from jax import lax
from jax.experimental import pallas as pl
from jax.experimental.pallas import tpu as pltpu
from jax.sharding import PartitionSpec as P

HD = 128
QH_DEV = 4
SPAN = 64
HEAD_COLS = QH_DEV * HD
VMEM_LIMIT = 24 * 1024 * 1024

rope_theta = 500000.0


def ring_of_chips(count):
    wide = 1
    while (wide * 2) * (wide * 2) <= count:
        wide *= 2
    tall = count // wide
    if wide < 2:
        return list(range(count))
    ring = [(z, 0) for z in range(tall)]
    for z in range(tall - 1, -1, -1):
        row = list(range(1, wide))
        ring += [(z, y) for y in (row if (tall - 1 - z) % 2 == 0 else row[::-1])]
    if (tall - 1) % 2 == 0 or wide == 2:
        return [z * wide + y for z, y in ring]
    return [z * wide + y for z, y in ring]


def vmem_specs(count):
    return [pl.BlockSpec(memory_space=pltpu.VMEM)] * count


def compute_params():
    return pltpu.CompilerParams(vmem_limit_bytes=VMEM_LIMIT)


def place_of(place):
    context = lax.axis_index("context")
    at = jnp.int32(0)
    for chip, spot in enumerate(place):
        at = jnp.where(context // 2 == chip, jnp.int32(spot), at)
    return at, context % 2


def where_kernel(
    n_tensor, rows_here, spans_ref, lengths_ref, freq_ref, cos_ref, sin_ref, low_ref, high_ref, orig_ref
):
    context, tensor = lax.axis_index("context"), lax.axis_index("tensor")
    rows = rows_here * n_tensor
    spans = rows // SPAN

    def shift(values, size):
        return lax.shift_right_logical(values, jnp.int32(size.bit_length() - 1))

    def inside_of(row):
        row = row & (rows - 1)
        turned = (tensor + shift(row, rows_here)) & (n_tensor - 1)
        return turned * rows_here + (row & (rows_here - 1))

    def initial(owner, inside):
        source = jnp.zeros_like(inside)
        for k in range(spans):
            source = jnp.where(shift(inside, SPAN) == k, spans_ref[owner * spans + k], source)
        return source * SPAN + (inside & (SPAN - 1))

    row = lax.broadcasted_iota(jnp.int32, cos_ref.shape, 0)
    inside = inside_of(row)
    orig = jnp.where(row < rows, initial(context, inside), initial(context ^ 1, inside))
    start, end = jnp.zeros_like(orig), jnp.int32(0)
    for i in range(lengths_ref.shape[0]):
        end = end + lengths_ref[i]
        start = jnp.where(orig >= end, end, start)
    low_ref[...] = start[:, :1]
    high_ref[...] = orig[:, :1]
    angle = (orig - start).astype(jnp.float32) * freq_ref[...]
    lane = lax.broadcasted_iota(jnp.int32, cos_ref.shape, 1)
    cos_ref[...] = jnp.cos(angle)
    sine = jnp.sin(angle)
    sin_ref[...] = jnp.where(lane < HD // 2, -sine, sine)
    inside = inside_of(lax.broadcasted_iota(jnp.int32, (1, rows), 1))
    for chip in range(orig_ref.shape[1] // rows):
        owner = 2 * chip + context % 2
        orig_ref[:, chip * rows : (chip + 1) * rows] = initial(owner, inside)


def norm_kernel(place, chips, hidden_ref, gain_ref, out_ref):
    at, core = place_of(place)
    wide = hidden_ref[...].astype(jnp.float32)
    meansq = jnp.mean(wide * wide, axis=-1, keepdims=True)
    scaled = wide * lax.rsqrt(meansq + 1e-05)
    lanes = gain_ref.shape[1]
    normed = jnp.concatenate(
        [
            (
                scaled[:, i * lanes : (i + 1) * lanes]
                * gain_ref[i : i + 1, :].astype(jnp.float32)
            ).astype(jnp.bfloat16)
            for i in range(gain_ref.shape[0])
        ],
        axis=1,
    )
    block = out_ref.shape[3]
    for even in range(2):

        @pl.when(core == even)
        def _():
            for chip in range(chips):
                slot = lax.rem(place[chip] + chips - at, chips)
                for side in range(2):
                    column = (2 * chip + side) * block
                    out_ref[side ^ even, slot] = normed[:, column : column + block]


def take_ring(refs, chips):
    refs = list(refs)
    if chips % 2:
        return [(ref,) for ref in refs]
    half = chips // 2
    return [(r,) for r in refs[:half]] + [tuple(refs[half : half + 2])] + [
        (r,) for r in refs[half + 2 :]
    ]


def project_kernel(chips, groups, *refs):
    rows_refs, refs = refs[:groups], refs[groups:]
    weight_refs, (mine_ref, theirs_ref, queries_ref) = refs[:-3], refs[-3:]
    half = groups // 2
    weights = take_ring(weight_refs, chips)
    total = None
    for slot in range(chips):
        rows = jnp.concatenate(
            [ref[group // half, slot] for group, ref in enumerate(rows_refs)], axis=0
        )
        start = 0
        for ref in weights[slot]:
            depth = ref.shape[0]
            part = jnp.dot(
                rows[:, start : start + depth], ref[...], preferred_element_type=jnp.float32
            )
            total = part if total is None else total + part
            start += depth
    count = mine_ref.shape[0]
    mine_ref[...] = total[:count, HEAD_COLS:]
    theirs_ref[...] = total[count:, HEAD_COLS:]
    queries_ref[...] = total[:, :HEAD_COLS]


def turn(values, cosine, sine):
    return values * cosine + pltpu.roll(values, HD // 2, 1) * sine


def keys_kernel(chips, mine_ref, theirs_ref, cosine_ref, sine_ref, out_ref):
    rows = out_ref.shape[0] // chips
    cosine, sine = cosine_ref[:rows, :], sine_ref[:rows, :]
    total = mine_ref[...] + theirs_ref[...]
    keys = turn(total[:, :HD], cosine, sine).astype(jnp.bfloat16)
    values = total[:, HD:].astype(jnp.bfloat16)
    for chip in range(chips):
        out_ref[chip * rows : (chip + 1) * rows, :HD] = keys
        out_ref[chip * rows : (chip + 1) * rows, HD:] = values


def attend_kernel(
    mine_ref,
    theirs_ref,
    cosine_ref,
    sine_ref,
    low_ref,
    high_ref,
    orig_ref,
    kv_ref,
    out_ref,
):
    keys = kv_ref[:, :HD]
    values = kv_ref[:, HD:]
    orig = orig_ref[...]
    allowed = (orig >= low_ref[...]) & (orig <= high_ref[...])
    scale = 1.0 / HD**0.5
    rows = out_ref.shape[0]
    half = rows // 2
    lane = lax.broadcasted_iota(jnp.int32, (rows, HD), 1)
    stats = jnp.zeros((rows, HD), jnp.float32)
    for head in range(QH_DEV):
        columns = slice(head * HD, (head + 1) * HD)
        query = jnp.concatenate(
            [
                mine_ref[:half, columns] + theirs_ref[half:, columns],
                mine_ref[half:, columns] + theirs_ref[:half, columns],
            ],
            axis=0,
        )
        query = turn(query, cosine_ref[...], sine_ref[...]).astype(jnp.bfloat16)
        scores = lax.dot_general(
            query, keys, (((1,), (1,)), ((), ())), preferred_element_type=jnp.float32
        )
        scores = jnp.where(allowed, scores * scale, -1e30)
        top = jnp.max(scores, axis=-1, keepdims=True)
        expo = jnp.where(allowed, jnp.exp(scores - top), 0.0)
        total = jnp.sum(expo, axis=-1, keepdims=True)
        out_ref[:, columns] = jnp.dot(
            expo.astype(jnp.bfloat16), values, preferred_element_type=jnp.float32
        )
        stats = jnp.where(lane == 2 * head, total, stats)
        stats = jnp.where(lane == 2 * head + 1, top, stats)
    out_ref[:, HEAD_COLS:] = stats


def output_kernel(groups, pieces_of, mine_ref, theirs_ref, *refs):
    weight_refs, out_refs = refs[:-groups], refs[-groups:]
    chip_rows = mine_ref.shape[0]
    half = chip_rows // 2

    def swapped(columns):
        return jnp.concatenate([theirs_ref[half:, columns], theirs_ref[:half, columns]], axis=0)

    pieces = []
    for head in range(QH_DEV):
        columns = slice(head * HD, (head + 1) * HD)
        at = HEAD_COLS + 2 * head
        total, top = mine_ref[:, at : at + 1], mine_ref[:, at + 1 : at + 2]
        other_total, other_top = swapped(slice(at, at + 1)), swapped(slice(at + 1, at + 2))
        peak = jnp.maximum(top, other_top)
        factor, other_factor = jnp.exp(top - peak), jnp.exp(other_top - peak)
        product = mine_ref[:, columns] * factor + swapped(columns) * other_factor
        pieces.append(
            (product / (total * factor + other_total * other_factor)).astype(jnp.bfloat16)
        )
    mixed = jnp.concatenate(pieces, axis=1)
    rows = chip_rows // groups
    weight_refs = iter(weight_refs)
    for slot, pieces in enumerate(pieces_of):
        start, total = 0, None
        for _ in range(pieces):
            ref = next(weight_refs)
            depth = ref.shape[0]
            part = jnp.dot(
                mixed[:, start : start + depth], ref[...], preferred_element_type=jnp.float32
            )
            total = part if total is None else total + part
            start += depth
        total = total.astype(jnp.bfloat16)
        for group in range(groups):
            out_refs[group][slot] = total[group * rows : (group + 1) * rows]


def sum_kernel(place, chips, groups, near, token_ref, *refs):
    near_refs, far_refs, out_ref = refs[:groups], refs[groups : 2 * groups], refs[2 * groups]
    at, core = place_of(place)
    block = near_refs[0].shape[2]
    half = groups // 2

    def added(part, slot):
        turn_at = lax.rem(slot + near // 2, chips)
        total = None
        for group in range(part * half, (part + 1) * half):
            rows = jnp.where(
                turn_at < near,
                near_refs[group][jnp.minimum(turn_at, near - 1)].astype(jnp.float32),
                far_refs[group][jnp.maximum(turn_at - near, 0)].astype(jnp.float32),
            )
            total = rows if total is None else total + rows
        return total.astype(jnp.bfloat16)

    for even in range(2):

        @pl.when(core == even)
        def _():
            for chip in range(chips):
                slot = lax.rem(place[chip] + chips - at, chips)
                for side in range(2):
                    column = (2 * chip + side) * block
                    out_ref[:, column : column + block] = added(side ^ even, slot)


def per_device(n_context, n_tensor, hidden_rows, norm_gain, w_qkv, w_out, doc_lengths, span_order):
    chips = n_context // 2
    ring = ring_of_chips(chips)
    place = [ring.index(chip) for chip in range(chips)]
    groups = 2 * n_tensor
    rows_here, width = hidden_rows.shape
    tokens_here = rows_here * n_tensor
    block = width // n_context
    context = lax.axis_index("context")
    tensor = lax.axis_index("tensor")
    ahead = [
        (ring[i] * 2 + k, ring[(i + 1) % chips] * 2 + k) for i in range(chips) for k in range(2)
    ]
    back = [(b, a) for a, b in ahead]
    sibling = [(c, c ^ 1) for c in range(n_context)]

    same_core = [[2 * chip + k for chip in range(chips)] for k in range(2)]
    token = [doc_lengths]

    def ordered(values):
        held = lax.optimization_barrier((*values, token[0]))
        token[0] = held[-1]
        return list(held[:-1])

    class Ring:
        def __init__(self, mine):
            self.up, self.down = [mine], [mine]
            self.middle = []

        def step(self, earlier=()):
            up, down, *earlier = ordered((self.up[-1], self.down[-1], *earlier))
            if len(self.up) <= (chips - 1) // 2:
                self.up.append(lax.ppermute(up, "context", ahead))
                self.down.append(lax.ppermute(down, "context", back))
            elif chips % 2 == 0 and not self.middle:
                half = up.shape[0] // 2
                self.middle = [
                    lax.ppermute(up[:half], "context", ahead),
                    lax.ppermute(down[half:], "context", back),
                ]
            return earlier

        def done(self):
            return len(self.up) > (chips - 1) // 2 and (chips % 2 == 1 or bool(self.middle))

        def finish(self):
            while not self.done():
                self.step()
            return self.down + self.middle + self.up[:0:-1]

        def block(self, slot):
            slot %= chips
            if chips % 2 == 0 and slot == chips // 2:
                return tuple(self.middle)
            return (self.down[slot] if slot <= chips // 2 else self.up[chips - slot],)

    def member(e, d):
        return [
            (c * n_tensor + t, (c ^ e) * n_tensor + (t - d) % n_tensor)
            for c in range(n_context)
            for t in range(n_tensor)
        ]

    smem, vmem = pl.BlockSpec(memory_space=pltpu.SMEM), pl.BlockSpec(memory_space=pltpu.VMEM)
    freq = rope_theta ** (-(np.arange(HD // 2, dtype=np.float64) * 2.0 / HD))
    freq = np.concatenate([freq, freq]).astype(np.float32)[None, :]
    table = jax.ShapeDtypeStruct((2 * tokens_here, HD), jnp.float32)
    bound = jax.ShapeDtypeStruct((2 * tokens_here, 1), jnp.int32)
    cosine, sine, query_start, query_orig, key_orig = pl.pallas_call(
        functools.partial(where_kernel, n_tensor, rows_here),
        out_shape=[
            table,
            table,
            bound,
            bound,
            jax.ShapeDtypeStruct((1, chips * tokens_here), jnp.int32),
        ],
        in_specs=[smem, smem, vmem],
        out_specs=vmem_specs(5),
        compiler_params=compute_params(),
        name="where",
    )(span_order, doc_lengths, jnp.asarray(freq))

    qkv_ring = Ring(w_qkv)
    qkv_ring.step()
    normed = pl.pallas_call(
        functools.partial(norm_kernel, place, chips),
        out_shape=jax.ShapeDtypeStruct((2, chips, rows_here, block), jnp.bfloat16),
        in_specs=vmem_specs(2),
        out_specs=vmem_specs(1)[0],
        compiler_params=compute_params(),
        name="norm",
    )(hidden_rows, norm_gain.reshape(-1, HD))
    normed = [normed] + [
        lax.ppermute(
            normed, "tensor", [(t, (t - d) % n_tensor) for t in range(n_tensor)]
        )
        for d in range(1, n_tensor)
    ]
    normed += [lax.ppermute(rows, "context", sibling) for rows in normed]

    qkv_ring.step()
    cosine, sine, query_start, query_orig, key_orig = ordered(
        (cosine, sine, query_start, query_orig, key_orig)
    )
    qkv_ring.step()
    normed = qkv_ring.step(normed)
    while not qkv_ring.done():
        qkv_ring.step()

    out_ring = Ring(w_out)
    out_ring.step()
    blocks = qkv_ring.finish()
    mine, theirs, queries = pl.pallas_call(
        functools.partial(project_kernel, chips, groups),
        out_shape=[
            jax.ShapeDtypeStruct((tokens_here, 2 * HD), jnp.float32),
            jax.ShapeDtypeStruct((tokens_here, 2 * HD), jnp.float32),
            jax.ShapeDtypeStruct((2 * tokens_here, HEAD_COLS), jnp.float32),
        ],
        in_specs=vmem_specs(groups + len(blocks)),
        out_specs=vmem_specs(3),
        compiler_params=compute_params(),
        name="project",
    )(*ordered((*normed, *blocks)))
    theirs = lax.ppermute(theirs, "context", sibling)
    queries_theirs = lax.ppermute(queries, "context", sibling)
    out_ring.step()
    mine, theirs = ordered((mine, theirs))
    kv = pl.pallas_call(
        functools.partial(keys_kernel, chips),
        out_shape=jax.ShapeDtypeStruct((chips * tokens_here, 2 * HD), jnp.bfloat16),
        in_specs=vmem_specs(4),
        out_specs=vmem_specs(1)[0],
        compiler_params=compute_params(),
        name="keys",
    )(mine, theirs, cosine, sine)
    (kv,) = ordered((kv,))
    kv = lax.all_to_all(
        kv, "context", split_axis=0, concat_axis=0, axis_index_groups=same_core, tiled=True
    )
    out_ring.step()
    (kv,) = ordered((kv,))

    mixed = pl.pallas_call(
        attend_kernel,
        out_shape=jax.ShapeDtypeStruct((2 * tokens_here, HEAD_COLS + HD), jnp.float32),
        in_specs=vmem_specs(8),
        out_specs=vmem_specs(1)[0],
        compiler_params=compute_params(),
        name="attend",
    )(
        queries,
        queries_theirs,
        cosine,
        sine,
        query_start,
        query_orig,
        key_orig,
        kv,
    )
    (mixed,) = ordered((mixed,))
    mixed_theirs = lax.ppermute(mixed, "context", sibling)

    out_block = w_out.shape[1]

    def output(slots, name):
        blocks = [out_ring.block(slot) for slot in slots]
        flat = [piece for pieces in blocks for piece in pieces]
        parts = pl.pallas_call(
            functools.partial(output_kernel, groups, [len(pieces) for pieces in blocks]),
            out_shape=[jax.ShapeDtypeStruct((len(slots), rows_here, out_block), jnp.bfloat16)]
            * groups,
            in_specs=vmem_specs(2 + len(flat)),
            out_specs=vmem_specs(groups),
            compiler_params=compute_params(),
            name=name,
        )(mixed, mixed_theirs, *flat)
        parts = ordered(parts)
        arrived = []
        for e in range(2):
            for d in range(n_tensor):
                part = parts[e * n_tensor + d]
                if e or d:
                    part = lax.ppermute(part, ("context", "tensor"), member(e, -d))
                arrived.append(part)
        return arrived

    reach = max(chips // 2 - 2, 0)
    while len(out_ring.up) <= reach:
        out_ring.step()
    near = 2 * reach + 1
    arrived = output(list(range(-reach, reach + 1)), "output_near")
    while not out_ring.done():
        out_ring.step()
    arrived += output(list(range(reach + 1, chips - reach)), "output_far")
    return pl.pallas_call(
        functools.partial(sum_kernel, place, chips, groups, near),
        out_shape=jax.ShapeDtypeStruct((rows_here, n_context * out_block), jnp.bfloat16),
        in_specs=[pl.BlockSpec(memory_space=pl.ANY)] + vmem_specs(2 * groups),
        out_specs=vmem_specs(1)[0],
        compiler_params=compute_params(),
        name="sum",
    )(token[0], *arrived)


def solution(mesh):
    placed = (
        P(("context", "tensor"), None),
        P(),
        P("context", "tensor"),
        P("tensor", "context"),
        P(),
        P(),
    )
    return jax.shard_map(
        functools.partial(per_device, mesh.shape["context"], mesh.shape["tensor"]),
        mesh=mesh,
        in_specs=placed,
        out_specs=P(("context", "tensor"), None),
        check_vma=False,
    )
```
